32 devices in a mesh: leaf: 16 (over z, y, x), cols: 2 (over core).
Axes of the slice: x: 2, y: 2, z: 4, core: 2. Of those that a mesh axis runs over, the one named last changes fastest.
Arguments:
- points: float32 [3, 32768], P(None, 'leaf'), may hold values from 0 to 1
- samples: float32 [256, 32768], P('cols', 'leaf'), may hold values from -6 to 6
- sketch: float32 [32, 256], P(None, 'cols'), may hold values from -0.375 to 0.375
- far_requests: int32 [16, 16, 8], P('leaf'), may hold values from 0 to 31, as said below
- far_slots: int32 [512, 16], P('leaf'), may hold values from 0 to 127, as said below
- far_count: int32 [512], P('leaf'), may hold values from 1 to 16, as said below
- near_mask: int32 [512, 3], P('leaf'), may hold values 0 or 1
Outputs:
- far_sample: float32 [256, 32768], P('cols', 'leaf')
- near_sample: float32 [256, 32768], P('cols', 'leaf')
- leaf_basis: float32 [32, 32768], P(None, 'leaf')
- branch_samples: float32 [512, 256], P('leaf', 'cols')
- top_transfer: float32 [15, 64, 32], replicated
- root_sample: float32 [32, 256], P(None, 'cols')
The draws below stay inside these ranges and needn't reach their ends.
Inputs may be any that keep to these rules, and one draw needn't show every extreme that they name: far_requests[e, d, c] is a leaf counted on device d of leaf (0 for its first); the 8 entries of each [e, d] are distinct. far_slots[i, f] names slot far_slots[i, f] mod 8 of the clusters fetched from device far_slots[i, f] // 8; only entries f < far_count[i] are used; among the 512 entries (used or not) of the leaves of one device, no device is named by more than 32 entries, and some device by exactly 32. `far_count`: used entries of each leaf's far-field list.
All inputs are finite; a program needn't handle non-finite values. No bound on the sum of `near_mask` on one device may be relied on, other than what follows from the above.
Results may differ from the reference program's by a relative error of at most 0.0003.
Values sent between devices are 32-bit elements; how exact they have to be, the bound alone decides.
No kernel may reach another device: no remote copies, remote signals or barrier semaphores. Data moves between devices by JAX's collectives and lax.ppermute only.
A program may use at most 64 MiB of HBM per device.

```python
import math
import jax
import jax.numpy as jnp
from jax import lax

LEAF = 64
SAMPLES = 256
RANK = 32
FAR = 16
NS = 1
CAP = 8
LEAVES_DEV = 32
LEAVES = 512
NPTS = 32768
N_LEAF = 16


def draw_far_requests(key, part):
    key = jax.random.fold_in(key, 11)
    scores = jax.random.randint(key, (N_LEAF, N_LEAF, LEAVES_DEV), 0, 1 << 18)
    scores = scores * LEAVES_DEV + jnp.arange(LEAVES_DEV, dtype=jnp.int32)
    unused, chosen = jax.lax.top_k(scores, CAP)
    return chosen.astype(jnp.int32)


def draw_far_slots(key, part):
    key = jax.random.fold_in(key, 37)
    order_key, slot_key = jax.random.split(key, 2)
    scores = jax.random.randint(order_key, (N_LEAF, N_LEAF), 0, 1 << 18)
    scores = scores * N_LEAF + jnp.arange(N_LEAF, dtype=jnp.int32)[None, :]
    orders = jnp.argsort(scores, axis=1, stable=True).astype(jnp.int32)
    entry_ids = jnp.arange(LEAVES_DEV * FAR, dtype=jnp.int32) % N_LEAF
    owners = jnp.take(orders, entry_ids, axis=1)
    slot_ids = jax.random.randint(slot_key, (N_LEAF, LEAVES_DEV * FAR), 0, CAP)
    return (owners * CAP + slot_ids).reshape(LEAVES, FAR).astype(jnp.int32)


def draw_far_count(key, part):
    key = jax.random.fold_in(key, 23)
    first_key, second_key, third_key, fourth_key = jax.random.split(key, 4)
    levels = jax.random.randint(first_key, (N_LEAF,), 1, 5)
    busiest = jax.random.randint(second_key, (), 0, N_LEAF)
    levels = jnp.where(jnp.arange(N_LEAF, dtype=jnp.int32) == busiest, 4, levels)
    highest_count = jnp.maximum(1, FAR * levels // 4)
    leaf_highest = jnp.repeat(highest_count, LEAVES_DEV)
    chosen_leaf = jnp.repeat(jax.random.randint(third_key, (N_LEAF,), 0, LEAVES_DEV), LEAVES_DEV)
    local_ids = jnp.arange(LEAVES, dtype=jnp.int32) % LEAVES_DEV
    counts = 1 + jax.random.randint(fourth_key, (LEAVES,), 0, 1 << 20) % leaf_highest
    return jnp.where(local_ids == chosen_leaf, leaf_highest, counts).astype(jnp.int32)


def plant(array, key, low, high):
    longest = array.shape.index(max(array.shape))
    spots = []
    for shift in (0, 1):
        where = [jax.random.randint(jax.random.fold_in(key, axis), (), 0, length) for axis, length in enumerate(array.shape)]
        where[longest] = (where[longest] + shift) % array.shape[longest]
        spots.append(tuple(where))
    return array.at[spots[0]].set(low).at[spots[1]].set(high)


def steps_of(rng, dims, pieces, least, top_value):
    def one(axis_at, parts):
        steps = jax.random.uniform(jax.random.fold_in(jax.random.fold_in(rng, 6), axis_at), (parts,), jnp.float32, least / len(pieces), top_value / len(pieces))
        return jnp.repeat(jnp.exp(steps), dims[axis_at] // parts).reshape((-1,) + (1,) * (len(dims) - axis_at - 1))

    factor_of = one(*pieces[0])
    for cut in pieces[1:]:
        factor_of = factor_of * one(*cut)
    return factor_of


def noise(key, dims, spread, bound, shards=(), kind=jnp.bfloat16):
    loudness = steps_of(key, dims, shards, -0.22, 0.18) if shards else 1.0
    result = jax.random.normal(key, dims, jnp.float32) * spread * loudness
    return jnp.minimum(jnp.maximum(result, -bound), bound).astype(kind)


def setup_inputs(seed: int = 0) -> dict:
    splits = jax.random.split(jax.random.key(seed), 8)
    return {
        "points": jnp.clip(1.0 * jax.random.uniform(splits[0], (3, NPTS), jnp.float32) ** steps_of(splits[0], (3, NPTS), ((1, 16),), -0.2, 0.2), 0.0, 1.0),
        "samples": noise(splits[1], (SAMPLES, NPTS), 1.0, 6.0, ((0, 2), (1, 16)), jnp.float32),
        "sketch": noise(splits[2], (RANK, SAMPLES), SAMPLES ** -0.5, 0.375, ((1, 2),), jnp.float32),
        "far_requests": draw_far_requests(jax.random.fold_in(splits[7], 71), 0),
        "far_slots": draw_far_slots(jax.random.fold_in(splits[7], 71), 0),
        "far_count": draw_far_count(jax.random.fold_in(splits[7], 71), 0),
        "near_mask": plant((jax.random.randint(splits[6], (LEAVES, 2 * NS + 1), 0, 4) < 3).astype(jnp.int32), jax.random.fold_in(splits[6], 1), 0, 1),
    }


length_scale = 0.3
shift_share = 0.05
highest = lax.Precision.HIGHEST

def kernel_block(source_coords, target_coords):
    differences = source_coords[:, :, :, None] - target_coords[:, :, None, :]
    return jnp.exp(-jnp.sqrt(lax.optimization_barrier(jnp.sum(differences * differences, axis=1))) / length_scale)

def compress(sample_block, sketch):
    sketched = jnp.einsum('nms,rs->nmr', sample_block, sketch, precision=highest)
    gram_matrix = jnp.einsum('nmr,nmq->nrq', sketched, sketched, precision=highest)
    order_size = gram_matrix.shape[-1]
    trace_sum = jnp.trace(gram_matrix, axis1=1, axis2=2)
    shifted = gram_matrix + (shift_share * trace_sum / order_size + 1e-06)[:, None, None] * jnp.eye(order_size, dtype=jnp.float32)
    lower_factor = jnp.linalg.cholesky(shifted)
    basis_t = jax.scipy.linalg.solve_triangular(lower_factor, jnp.swapaxes(sketched, 1, 2), lower=True)
    projected = jnp.einsum('nrm,nms->nrs', basis_t, sample_block, precision=highest)
    return (basis_t, projected)

def reference(points, samples, sketch, far_requests, far_slots, far_count, near_mask):
    coords = jnp.transpose(points.reshape(3, LEAVES, LEAF), (1, 0, 2))
    sample_blocks = jnp.transpose(samples.reshape(SAMPLES, LEAVES, LEAF), (1, 0, 2))
    leaf_ids = jnp.arange(LEAVES, dtype=jnp.int32)
    device_ids = leaf_ids // LEAVES_DEV
    owners = far_slots // CAP
    positions = far_slots % CAP
    sources = (owners * LEAVES_DEV + far_requests[device_ids[:, None], owners, positions]).astype(jnp.int32)
    valid_mask = (jnp.arange(FAR, dtype=jnp.int32)[None, :] < far_count[:, None]).astype(jnp.float32)
    near_weights = near_mask.astype(jnp.float32)
    pad_coords = jnp.pad(coords, ((NS, NS), (0, 0), (0, 0)))
    pad_samples = jnp.pad(sample_blocks, ((NS, NS), (0, 0), (0, 0)))
    block_size = math.gcd(LEAVES, 256)
    block_count = LEAVES // block_size

    def one_block(inputs):
        target, source_ids, weights, first_ids, near_block = inputs
        start = jnp.zeros((block_size, SAMPLES, LEAF), jnp.float32)

        def far_step(accumulated, step_inputs):
            picked, scale = step_inputs
            kernel_vals = kernel_block(coords[picked], target) * scale[:, None, None]
            term = jnp.einsum('bsp,bpq->bsq', sample_blocks[picked], kernel_vals, precision=highest)
            return (accumulated + term, None)
        far_part, _ = lax.scan(far_step, start, (source_ids.T, weights.T))
        near_part = start
        for offset in range(2 * NS + 1):
            picked = first_ids + offset
            kernel_vals = kernel_block(pad_coords[picked], target) * near_block[:, offset][:, None, None]
            near_part = near_part + jnp.einsum('bsp,bpq->bsq', pad_samples[picked], kernel_vals, precision=highest)
        return (far_part, near_part)
    far_all, near_all = lax.map(one_block, (coords.reshape(block_count, block_size, 3, LEAF), sources.reshape(block_count, block_size, FAR), valid_mask.reshape(block_count, block_size, FAR), leaf_ids.reshape(block_count, block_size), near_weights.reshape(block_count, block_size, 2 * NS + 1)))
    far_all = far_all.reshape(LEAVES, SAMPLES, LEAF)
    near_all = near_all.reshape(LEAVES, SAMPLES, LEAF)
    far_sample = jnp.transpose(far_all, (1, 0, 2)).reshape(SAMPLES, NPTS)
    near_sample = jnp.transpose(near_all, (1, 0, 2)).reshape(SAMPLES, NPTS)
    sample_rows = jnp.transpose(far_all, (0, 2, 1))
    basis_t, current = compress(sample_rows, sketch)
    leaf_basis = jnp.transpose(basis_t, (1, 0, 2)).reshape(RANK, NPTS)
    while current.shape[0] > N_LEAF:
        unused, current = compress(current.reshape(current.shape[0] // 2, 2 * RANK, SAMPLES), sketch)
    branch_samples = current.reshape(N_LEAF * RANK, SAMPLES)
    transfers = []
    while current.shape[0] > 1:
        transfer_t, current = compress(current.reshape(current.shape[0] // 2, 2 * RANK, SAMPLES), sketch)
        transfers.append(jnp.swapaxes(transfer_t, 1, 2))
    top_transfer = jnp.concatenate(transfers, axis=0)
    root_sample = current[0]
    return (far_sample, near_sample, leaf_basis, branch_samples, top_transfer, root_sample)
```

```python
import functools
import math

import jax
import jax.numpy as jnp
import numpy as np
from jax import lax
from jax.experimental import pallas as pl
from jax.experimental.pallas import tpu as pltpu
from jax.sharding import PartitionSpec as P

LEAF = 64
FAR = 16
GROUP = 4
BATCH = 16
LANES = 128

length_scale = 0.3
shift_share = 0.05
highest = lax.Precision.HIGHEST
exponent_scale = -math.log2(math.e) / length_scale
vmem_bytes = 56 * 1024 * 1024

nt_dims = (((1,), (1,)), ((), ()))


def halves(value):
    high = value.astype(jnp.bfloat16)
    low = (value - high.astype(jnp.float32)).astype(jnp.bfloat16)
    return high, low


def dot(a, b):
    return jnp.dot(a, b, preferred_element_type=jnp.float32)


def dot_nt(a, b):
    return lax.dot_general(a, b, nt_dims, preferred_element_type=jnp.float32)


def kernel_half(source_rows, target, lane, valid):
    total = None
    for axis in range(3):
        difference = source_rows[axis : axis + 1, :] - target[:, axis : axis + 1]
        square = difference * difference
        total = square if total is None else total + square
    distance = total * lax.rsqrt(jnp.maximum(total, 1e-30))
    values = jnp.exp2(distance * exponent_scale)
    return jnp.where(lane < valid, values, 0.0)


def blocks_body(
    total_ref, leaf_ref, count_ref, slot_ref,
    packed_ref, target_ref,
    high_ref, low_ref, sketched_ref, gram_ref,
    *, rank,
):
    step = pl.program_id(0)
    lane = lax.broadcasted_iota(jnp.int32, (1, LANES), 1)
    first = lane < LEAF

    @pl.when(step == 0)
    def _():
        sketched_ref[...] = jnp.zeros_like(sketched_ref)

    @pl.when(step * BATCH < total_ref[0])
    def _():
        for member in range(BATCH):
            group = step * BATCH + member
            leaf = leaf_ref[group]
            count = count_ref[group]
            slots = [slot_ref[group * GROUP + e] for e in range(GROUP)]
            target = target_ref[leaf]
            z_parts = []
            for half in range(GROUP // 2):
                left = packed_ref[slots[2 * half]]
                right = packed_ref[slots[2 * half + 1]]
                both = jnp.where(first, left, right)
                values = kernel_half(both[rank : rank + 3], target, lane, (count - 2 * half) * LEAF)
                high, low = halves(values)
                high_ref[member, :, half * LANES : (half + 1) * LANES] = high
                low_ref[member, :, half * LANES : (half + 1) * LANES] = low
                z_parts.append(both[:rank])
            z_high, z_low = halves(jnp.concatenate(z_parts, axis=1))
            k_high = high_ref[member]
            k_low = low_ref[member]
            update = dot_nt(z_high, k_high) + (dot_nt(z_low, k_high) + dot_nt(z_high, k_low))
            sketched_ref[leaf] += update

    @pl.when(step == pl.num_programs(0) - 1)
    def _():
        for leaf in range(gram_ref.shape[0]):
            block = sketched_ref[leaf]
            gram_ref[leaf] = lax.dot_general(
                block, block, nt_dims, precision=highest, preferred_element_type=jnp.float32
            )


def kernel_blocks(total, group_leaf, group_count, group_slots, packed, targets, rank):
    leaves = targets.shape[0]
    groups = group_leaf.shape[0]
    steps = groups // BATCH

    def block_index(step, total_ref, *unused):
        last = (total_ref[0] - 1) // BATCH
        return (jnp.minimum(step, last), 0, 0)

    whole = lambda *unused: (0, 0, 0)
    return pl.pallas_call(
        functools.partial(blocks_body, rank=rank),
        grid_spec=pltpu.PrefetchScalarGridSpec(
            num_scalar_prefetch=4,
            grid=(steps,),
            in_specs=[
                pl.BlockSpec(packed.shape, whole),
                pl.BlockSpec(targets.shape, whole),
            ],
            out_specs=[
                pl.BlockSpec((BATCH, LEAF, GROUP * LEAF), block_index),
                pl.BlockSpec((BATCH, LEAF, GROUP * LEAF), block_index),
                pl.BlockSpec((leaves, rank, LEAF), whole),
                pl.BlockSpec((leaves, rank, rank), whole),
            ],
        ),
        out_shape=[
            jax.ShapeDtypeStruct((groups, LEAF, GROUP * LEAF), jnp.bfloat16),
            jax.ShapeDtypeStruct((groups, LEAF, GROUP * LEAF), jnp.bfloat16),
            jax.ShapeDtypeStruct((leaves, rank, LEAF), jnp.float32),
            jax.ShapeDtypeStruct((leaves, rank, rank), jnp.float32),
        ],
        compiler_params=pltpu.CompilerParams(vmem_limit_bytes=vmem_bytes),
        name="kernel_blocks",
        cost_estimate=pl.CostEstimate(
            flops=2 * 10**10, bytes_accessed=2 * 10**7, transcendentals=0
        ),
    )(total, group_leaf, group_count, group_slots, packed, targets)


def far_body(
    total_ref, leaf_ref, slot_ref,
    fetched_ref, high_ref, low_ref, weights_ref,
    out_ref, projected_ref,
    s_high, s_low, acc,
):
    step = pl.program_id(0)
    samp_dev = fetched_ref.shape[2]

    @pl.when(step == 0)
    def _():
        acc[...] = jnp.zeros_like(acc)

        def split(slot, carry):
            s_high[slot], s_low[slot] = halves(fetched_ref[slot])
            return carry

        lax.fori_loop(0, fetched_ref.shape[0], split, 0, unroll=8)

    @pl.when(step * BATCH < total_ref[0])
    def _():
        for member in range(BATCH):
            group = step * BATCH + member
            leaf = leaf_ref[group]
            slots = [slot_ref[group * GROUP + e] for e in range(GROUP)]
            rows_high = jnp.concatenate([s_high[slot] for slot in slots], axis=0)
            rows_low = jnp.concatenate([s_low[slot] for slot in slots], axis=0)
            k_high = high_ref[member]
            k_low = low_ref[member]
            acc[leaf] += dot(k_high, rows_high) + (dot(k_high, rows_low) + dot(k_low, rows_high))

    @pl.when(step == pl.num_programs(0) - 1)
    def _():
        leaves = acc.shape[0]
        rows = acc[...].reshape(leaves * LEAF, samp_dev)
        projected_ref[...] = jnp.dot(
            weights_ref[...], rows, precision=highest, preferred_element_type=jnp.float32
        )
        for pair in range(leaves // 2):
            block = acc[2 * pair : 2 * pair + 2].reshape(2 * LEAF, samp_dev)
            out_ref[:, 2 * pair * LEAF : 2 * (pair + 1) * LEAF] = block.T


def far_products(total, group_leaf, group_slots, fetched, high, low, weights):
    slots, unused, samp_dev = fetched.shape
    groups = group_leaf.shape[0]
    points_dev = weights.shape[1]
    leaves = points_dev // LEAF
    steps = groups // BATCH

    def block_index(step, total_ref, *unused):
        last = (total_ref[0] - 1) // BATCH
        return (jnp.minimum(step, last), 0, 0)

    return pl.pallas_call(
        far_body,
        grid_spec=pltpu.PrefetchScalarGridSpec(
            num_scalar_prefetch=3,
            grid=(steps,),
            in_specs=[
                pl.BlockSpec(fetched.shape, lambda *unused: (0, 0, 0), pipeline_mode=pl.Buffered(1)),
                pl.BlockSpec((BATCH, LEAF, GROUP * LEAF), block_index),
                pl.BlockSpec((BATCH, LEAF, GROUP * LEAF), block_index),
                pl.BlockSpec(weights.shape, lambda *unused: (0, 0), pipeline_mode=pl.Buffered(1)),
            ],
            out_specs=[
                pl.BlockSpec((samp_dev, points_dev), lambda *unused: (0, 0)),
                pl.BlockSpec((weights.shape[0], samp_dev), lambda *unused: (0, 0)),
            ],
            scratch_shapes=[
                pltpu.VMEM((slots, LEAF, samp_dev), jnp.bfloat16),
                pltpu.VMEM((slots, LEAF, samp_dev), jnp.bfloat16),
                pltpu.VMEM((leaves, LEAF, samp_dev), jnp.float32),
            ],
        ),
        out_shape=[
            jax.ShapeDtypeStruct((samp_dev, points_dev), jnp.float32),
            jax.ShapeDtypeStruct((weights.shape[0], samp_dev), jnp.float32),
        ],
        compiler_params=pltpu.CompilerParams(vmem_limit_bytes=vmem_bytes),
        name="far_products",
        cost_estimate=pl.CostEstimate(
            flops=10**10, bytes_accessed=2 * 10**7, transcendentals=0
        ),
    )(total, group_leaf, group_slots, fetched, high, low, weights)


NEAR_LEAVES = 8


def near_body(mask_ref, rows_ref, coords_ref, target_ref, out_ref):
    step = pl.program_id(0)
    samp_dev = rows_ref.shape[2]
    lane = lax.broadcasted_iota(jnp.int32, (1, LANES), 1)
    first = lane < LEAF
    for pair in range(NEAR_LEAVES // 2):
        results = []
        for member in range(2):
            leaf = step * NEAR_LEAVES + 2 * pair + member
            target = target_ref[leaf]
            k_high = []
            k_low = []
            for half in range(2):
                both = jnp.where(first, coords_ref[leaf + 2 * half], coords_ref[leaf + 2 * half + 1])
                values = kernel_half(both, target, lane, LANES)
                left = mask_ref[leaf * 3 + 2 * half].astype(jnp.float32)
                if half == 0:
                    right = mask_ref[leaf * 3 + 1].astype(jnp.float32)
                else:
                    right = jnp.float32(0.0)
                high, low = halves(values * jnp.where(first, left, right))
                k_high.append(high)
                k_low.append(low)
            k_high = jnp.concatenate(k_high, axis=1)
            k_low = jnp.concatenate(k_low, axis=1)
            rows = rows_ref[pl.ds(leaf, 4)].reshape(4 * LEAF, samp_dev)
            rows_high, rows_low = halves(rows)
            results.append(
                dot(k_high, rows_high) + (dot(k_high, rows_low) + dot(k_low, rows_high))
            )
        block = jnp.concatenate(results, axis=0)
        out_ref[:, 2 * pair * LEAF : 2 * (pair + 1) * LEAF] = block.T


def near_products(mask, rows, coords, targets):
    leaves = targets.shape[0]
    samp_dev = rows.shape[2]
    whole = lambda *unused: (0, 0, 0)
    return pl.pallas_call(
        near_body,
        grid_spec=pltpu.PrefetchScalarGridSpec(
            num_scalar_prefetch=1,
            grid=(leaves // NEAR_LEAVES,),
            in_specs=[
                pl.BlockSpec(rows.shape, whole),
                pl.BlockSpec(coords.shape, whole),
                pl.BlockSpec(targets.shape, whole),
            ],
            out_specs=pl.BlockSpec((samp_dev, NEAR_LEAVES * LEAF), lambda step, *unused: (0, step)),
        ),
        out_shape=jax.ShapeDtypeStruct((samp_dev, leaves * LEAF), jnp.float32),
        compiler_params=pltpu.CompilerParams(vmem_limit_bytes=vmem_bytes),
        name="near_products",
        cost_estimate=pl.CostEstimate(
            flops=4 * 10**9, bytes_accessed=10**7, transcendentals=0
        ),
    )(mask, rows, coords, targets)


SUB = 8


def tree_body(gram_ref, inverse_ref, child_ref, current, *, rank, levels):
    tiles = rank // SUB
    row = lax.broadcasted_iota(jnp.int32, (SUB, LANES), 0)
    current[...] = gram_ref[...]

    def level_step(level, carry):
        trace = None
        for j in range(rank):
            entry = current[j, j : j + 1, :]
            trace = entry if trace is None else trace + entry
        shift = shift_share * trace / rank + 1e-06
        a = [
            {t: current[j, SUB * t : SUB * (t + 1), :] for t in range(j // SUB, tiles)}
            for j in range(rank)
        ]
        for j in range(rank):
            a[j][j // SUB] = a[j][j // SUB] + jnp.where(row == j % SUB, shift, 0.0)
        m = []
        scales = []
        for k in range(rank):
            tk, rk = k // SUB, k % SUB
            root = lax.rsqrt(a[k][tk][rk : rk + 1, :])
            scales.append(root)
            reciprocal = root * root
            column = {t: a[k][t] * reciprocal for t in range(tk, tiles)}
            column[tk] = jnp.where(row > rk, column[tk], 0.0)
            for j in range(k + 1, rank):
                factor = a[k][j // SUB][j % SUB : j % SUB + 1, :]
                for t in range(j // SUB, tiles):
                    a[j][t] = a[j][t] - column[t] * factor
            for c in range(k):
                factor = m[c][tk][rk : rk + 1, :]
                for t in range(tk, tiles):
                    m[c][t] = m[c][t] - column[t] * factor
            fresh = {t: -column[t] for t in range(tk, tiles)}
            fresh[tk] = jnp.where(row == rk, 1.0, fresh[tk])
            m.append(fresh)
        for t in range(tiles):
            scale = jnp.concatenate(scales[SUB * t : SUB * (t + 1)], axis=0)
            for c in range(rank):
                if t >= c // SUB:
                    inverse_ref[level, c, SUB * t : SUB * (t + 1), :] = m[c][t] * scale
                else:
                    inverse_ref[level, c, SUB * t : SUB * (t + 1), :] = jnp.zeros(
                        (SUB, LANES), jnp.float32
                    )
        for block in range(tiles):
            sums = [[None] * tiles for _ in range(SUB)]
            for k in range(SUB * (block + 1)):
                parts = [current[k, SUB * t : SUB * (t + 1), :] for t in range(tiles)]
                for r in range(max(0, k - SUB * block), SUB):
                    at = SUB * block + r
                    factor = inverse_ref[level, k, at : at + 1, :]
                    for t in range(tiles):
                        term = parts[t] * factor
                        sums[r][t] = term if sums[r][t] is None else sums[r][t] + term
            for r in range(SUB):
                for t in range(tiles):
                    child_ref[level, SUB * block + r, SUB * t : SUB * (t + 1), :] = sums[r][t]

        @pl.when(level < levels - 1)
        def _():
            reach = LANES - lax.shift_left(1, level)

            def gram_block(block, inner):
                offset = pl.multiple_of(block * SUB, SUB)
                sums = [[None] * tiles for _ in range(SUB)]
                for r in range(rank):
                    parts = [child_ref[level, r, SUB * t : SUB * (t + 1), :] for t in range(tiles)]
                    heads = child_ref[level, r, pl.ds(offset, SUB), :]
                    for q in range(SUB):
                        factor = heads[q : q + 1, :]
                        for t in range(tiles):
                            term = parts[t] * factor
                            sums[q][t] = term if sums[q][t] is None else sums[q][t] + term
                for q in range(SUB):
                    for t in range(tiles):
                        current[offset + q, SUB * t : SUB * (t + 1), :] = sums[q][t] + pltpu.roll(
                            sums[q][t], reach, 1
                        )
                return inner

            lax.fori_loop(0, tiles, gram_block, 0)

        return carry

    lax.fori_loop(0, levels, level_step, 0)


def tree_factors(gram_last, levels):
    rank = gram_last.shape[0]
    nodes = gram_last.shape[2]
    padded = jnp.pad(gram_last, ((0, 0), (0, 0), (0, LANES - nodes)))
    shape = jax.ShapeDtypeStruct((levels, rank, rank, LANES), jnp.float32)
    inverse, child = pl.pallas_call(
        functools.partial(tree_body, rank=rank, levels=levels),
        in_specs=[pl.BlockSpec(memory_space=pltpu.VMEM)],
        out_specs=[pl.BlockSpec(memory_space=pltpu.VMEM)] * 2,
        out_shape=[shape, shape],
        scratch_shapes=[pltpu.VMEM((rank, rank, LANES), jnp.float32)],
        compiler_params=pltpu.CompilerParams(vmem_limit_bytes=vmem_bytes),
        name="tree_factors",
        cost_estimate=pl.CostEstimate(
            flops=10**10, bytes_accessed=10**7, transcendentals=0
        ),
    )(padded)
    return (
        jnp.transpose(inverse[..., :nodes], (0, 3, 2, 1)),
        jnp.transpose(child[..., :nodes], (0, 3, 1, 2)),
    )


def exchange_sum(pieces, axis):
    count = pieces.shape[0]
    me = lax.axis_index(axis)
    mine = lax.dynamic_index_in_dim(pieces, me, 0, keepdims=False)
    for step in range(1, count):
        outgoing = lax.dynamic_index_in_dim(pieces, (me + step) % count, 0, keepdims=False)
        mine = mine + lax.ppermute(
            outgoing, axis, [(i, (i + step) % count) for i in range(count)]
        )
    return mine


def exchange_all(piece, axis):
    count = lax.axis_size(axis)
    me = lax.axis_index(axis)
    if count == 2:
        other = lax.ppermute(piece, axis, [(0, 1), (1, 0)])
        return jnp.stack([jnp.where(me == 0, piece, other), jnp.where(me == 0, other, piece)])
    result = jnp.zeros((count,) + piece.shape, piece.dtype)
    result = lax.dynamic_update_index_in_dim(result, piece, me, 0)
    for step in range(1, count):
        arrived = lax.ppermute(piece, axis, [(i, (i + step) % count) for i in range(count)])
        result = lax.dynamic_update_index_in_dim(result, arrived, (me - step) % count, 0)
    return result


def double_all(piece, axis):
    count = lax.axis_size(axis)
    me = lax.axis_index(axis)
    held = piece[None]
    stride = 1
    while stride < count:
        other = lax.ppermute(held, axis, [(i, i ^ stride) for i in range(count)])
        low = (me // stride) % 2 == 0
        held = jnp.concatenate([jnp.where(low, held, other), jnp.where(low, other, held)], axis=0)
        stride *= 2
    return held


def group_tables(far_slots, far_count):
    leaves = far_slots.shape[0]
    groups = leaves * FAR // GROUP
    per_leaf = (far_count + GROUP - 1) // GROUP
    before = jnp.arange(leaves)[:, None] >= jnp.arange(leaves)[None, :]
    ends = jnp.sum(jnp.where(before, per_leaf[None, :], 0), axis=1)
    total = ends[leaves - 1 :]
    ids = jnp.arange(groups, dtype=jnp.int32)
    leaf = jnp.minimum(jnp.sum((ends[None, :] <= ids[:, None]).astype(jnp.int32), axis=1), leaves - 1)
    hit = leaf[:, None] == jnp.arange(leaves)[None, :]
    start = jnp.sum(jnp.where(hit, (ends - per_leaf)[None, :], 0), axis=1)
    length = jnp.sum(jnp.where(hit, far_count[None, :], 0), axis=1)
    sub = ids - start
    count = jnp.where(ids < total, jnp.clip(length - GROUP * sub, 0, GROUP), 0)
    first = jnp.minimum(sub, FAR // GROUP - 1)
    slots = far_slots.reshape(leaves * FAR // GROUP, GROUP)[leaf * (FAR // GROUP) + first]
    return (
        total.astype(jnp.int32),
        leaf.astype(jnp.int32),
        count.astype(jnp.int32),
        slots.reshape(-1).astype(jnp.int32),
    )


def on_device(points, samples, sketch, far_requests, far_slots, far_count, near_mask):
    samp_dev = samples.shape[0]
    leaves = samples.shape[1] // LEAF
    rank = sketch.shape[0]
    branches = lax.axis_size("leaf")
    columns = lax.axis_size("cols")
    cap = far_requests.shape[2]
    slots = branches * cap
    share = rank // columns

    wanted = far_requests.reshape(branches, cap)
    asked_for = lax.all_to_all(wanted, "leaf", split_axis=0, concat_axis=0, tiled=True)

    coords = jnp.transpose(points.reshape(3, leaves, LEAF), (1, 0, 2))
    targets = jnp.transpose(coords, (0, 2, 1))
    rows = jnp.transpose(samples.reshape(samp_dev, leaves, LEAF), (1, 2, 0))

    z_part = jnp.dot(sketch, samples, precision=highest)
    z_mine = exchange_sum(z_part.reshape(columns, share, leaves * LEAF), "cols")
    z_mine = jnp.transpose(z_mine.reshape(share, leaves, LEAF), (1, 0, 2))
    small_width = -(-(share + 3) * LEAF // LANES) * LANES
    small = jnp.concatenate([z_mine.reshape(leaves, -1), coords.reshape(leaves, -1)], axis=1)
    small = jnp.pad(small, ((0, 0), (0, small_width - small.shape[1])))
    small_sent = small[asked_for.reshape(-1)].reshape(branches, cap, small_width)
    small_got = lax.all_to_all(small_sent, "leaf", split_axis=0, concat_axis=0, tiled=True)

    rows_sent = rows[asked_for.reshape(-1)].reshape(branches, cap, LEAF, samp_dev)
    rows_got = lax.all_to_all(rows_sent, "leaf", split_axis=0, concat_axis=0, tiled=True)
    fetched = rows_got.reshape(slots, LEAF, samp_dev)

    small_got = small_got.reshape(slots, small_width)
    z_all = exchange_all(small_got[:, : share * LEAF], "cols")
    z_all = jnp.transpose(z_all.reshape(columns, slots, share, LEAF), (1, 0, 2, 3))
    z_all = z_all.reshape(slots, rank, LEAF)
    c_all = small_got[:, share * LEAF : (share + 3) * LEAF].reshape(slots, 3, LEAF)
    packed = jnp.concatenate([z_all, c_all, jnp.zeros((slots, 5, LEAF), jnp.float32)], axis=1)
    packed = jnp.concatenate([packed, packed], axis=2)

    total, group_leaf, group_count, group_slots = group_tables(far_slots, far_count)
    high, low, sketched, gram = kernel_blocks(
        total, group_leaf, group_count, group_slots, packed, targets, rank
    )

    levels = leaves.bit_length()
    inverse, child = tree_factors(jnp.transpose(gram, (1, 2, 0)), levels)
    own_child = child[levels - 1, 0]
    children = double_all(own_child.reshape(rank * rank // LANES, LANES), "leaf")
    children = children.reshape(branches, rank, rank)

    pair_children = children.reshape(branches // 2, 2 * rank, rank)
    top_gram = jnp.einsum("nmr,nmq->rqn", pair_children, pair_children, precision=highest)
    top_levels = branches.bit_length() - 1
    top_inverse, top_child = tree_factors(top_gram, top_levels)
    transfers = []
    below = children
    for level in range(top_levels):
        inverse_here = top_inverse[level, :: 2**level]
        stacked = below.reshape(branches >> level + 1, 2 * rank, rank)
        transfers.append((stacked, inverse_here))
        below = top_child[level, :: 2**level]
    top_transfer = jnp.einsum(
        "nmq,nrq->nmr",
        jnp.concatenate([stacked for stacked, unused in transfers], axis=0),
        jnp.concatenate([here for unused, here in transfers], axis=0),
        precision=highest,
    )

    me = lax.axis_index("leaf")
    offset = 0
    path = None
    for level in range(top_levels):
        node = offset + (me >> level + 1)
        block = lax.dynamic_index_in_dim(top_transfer, node, 0, keepdims=False)
        side = (me >> level) % 2
        block = lax.dynamic_slice_in_dim(block, side * rank, rank, axis=0)
        path = block if path is None else jnp.dot(path, block, precision=highest)
        offset += branches >> level + 1

    ratio = jnp.einsum("lnrq,lnrc->lnqc", child, inverse, precision=highest)
    upper = inverse[levels - 1, :1]
    for level in range(levels - 2, -1, -1):
        upper = jnp.einsum(
            "nij,nbjk->nbik",
            upper,
            ratio[level, :: 2**level].reshape(upper.shape[0], 2, rank, rank),
            precision=highest,
        ).reshape(-1, rank, rank)
    weights = jnp.einsum("nij,njp->inp", upper, sketched, precision=highest)
    weights = weights.reshape(rank, leaves * LEAF)
    weights = jnp.concatenate(
        [weights, jnp.dot(path.T, weights, precision=highest)], axis=0
    )
    leaf_basis = jnp.einsum("nij,njp->inp", inverse[0], sketched, precision=highest)
    leaf_basis = leaf_basis.reshape(rank, leaves * LEAF)

    edge_rows = jnp.concatenate([rows[:1], rows[leaves - 1 :]], axis=0)
    edge_coords = jnp.concatenate([coords[:1], coords[leaves - 1 :]], axis=0)
    forward = [(i, i + 1) for i in range(branches - 1)]
    backward = [(target, source) for source, target in forward]
    rows_low = lax.ppermute(edge_rows[1], "leaf", forward)
    rows_high = lax.ppermute(edge_rows[0], "leaf", backward)
    coords_low = lax.ppermute(edge_coords[1], "leaf", forward)
    coords_high = lax.ppermute(edge_coords[0], "leaf", backward)
    near_rows = jnp.concatenate(
        [rows_low[None], rows, rows_high[None], jnp.zeros_like(rows_low)[None]], axis=0
    )
    near_coords = jnp.concatenate(
        [coords_low[None], coords, coords_high[None], jnp.zeros_like(coords_low)[None]], axis=0
    )
    near_coords = jnp.pad(near_coords, ((0, 0), (0, 5), (0, 0)))
    near_coords = jnp.concatenate([near_coords, near_coords], axis=2)
    near_sample = near_products(near_mask.reshape(-1), near_rows, near_coords, targets)

    far_sample, projected = far_products(
        total, group_leaf, group_slots, fetched, high, low, weights
    )
    branch_samples = projected[:rank]
    part = jnp.broadcast_to(projected[rank:][None], (branches, rank, samp_dev))
    parts = lax.all_to_all(part, "leaf", split_axis=0, concat_axis=0, tiled=True)
    root_sample = jnp.sum(parts, axis=0)
    return (far_sample, near_sample, leaf_basis, branch_samples, top_transfer, root_sample)


def solution(mesh):
    return jax.shard_map(
        on_device,
        mesh=mesh,
        in_specs=(
            P(None, "leaf"),
            P("cols", "leaf"),
            P(None, "cols"),
            P("leaf", None, None),
            P("leaf", None),
            P("leaf"),
            P("leaf", None),
        ),
        out_specs=(
            P("cols", "leaf"),
            P("cols", "leaf"),
            P(None, "leaf"),
            P("leaf", "cols"),
            P(),
            P(None, "cols"),
        ),
        check_vma=False,
    )
```

```python
import functools
import math

import jax
import jax.numpy as jnp
import numpy as np
from jax import lax
from jax.experimental import pallas as pl
from jax.experimental.pallas import tpu as pltpu
from jax.sharding import PartitionSpec as P

LEAF = 64
FAR = 16
GROUP = 4
BATCH = 16
LANES = 128
SUB = 8

length_scale = 0.3
shift_share = 0.05
highest = lax.Precision.HIGHEST
exponent_scale = -math.log2(math.e) / length_scale
vmem_bytes = 56 * 1024 * 1024

nt_dims = (((1,), (1,)), ((), ()))
tn_dims = (((0,), (0,)), ((), ()))


def halves(value):
    high = value.astype(jnp.bfloat16)
    low = (value - high.astype(jnp.float32)).astype(jnp.bfloat16)
    return high, low


def dot(a, b):
    return jnp.dot(a, b, preferred_element_type=jnp.float32)


def dot_exact(a, b):
    return jnp.dot(a, b, precision=highest, preferred_element_type=jnp.float32)


def dot_exact_nt(a, b):
    return lax.dot_general(a, b, nt_dims, precision=highest, preferred_element_type=jnp.float32)


def dot_nt(a, b):
    return lax.dot_general(a, b, nt_dims, preferred_element_type=jnp.float32)


def kernel_half(source_rows, target, lane, valid):
    total = None
    for axis in range(3):
        difference = source_rows[axis : axis + 1, :] - target[:, axis : axis + 1]
        square = difference * difference
        total = square if total is None else total + square
    distance = total * lax.rsqrt(jnp.maximum(total, 1e-30))
    values = jnp.exp2(distance * exponent_scale)
    return jnp.where(lane < valid, values, 0.0)


def blocks_body(
    total_ref, leaf_ref, count_ref, slot_ref, place_ref,
    own_ref, other_ref, coords_ref, target_ref,
    high_ref, low_ref, sketched_ref, gram_ref,
    packed,
    *, rank,
):
    step = pl.program_id(0)
    lane = lax.broadcasted_iota(jnp.int32, (1, LANES), 1)
    first = lane < LEAF

    @pl.when(step == 0)
    def _():
        sketched_ref[...] = jnp.zeros_like(sketched_ref)
        quarter = rank // 4
        own_at = pl.multiple_of(place_ref[0] * 2 * quarter, quarter)
        other_at = pl.multiple_of((1 - place_ref[0]) * 2 * quarter, quarter)

        def unpack(slot, carry):
            for ref, base in ((own_ref, own_at), (other_ref, other_at)):
                value = ref[pl.ds(pl.multiple_of(slot * quarter, quarter), quarter), :]
                turned = pltpu.roll(value, LEAF, 1)
                packed[slot, pl.ds(base, quarter), :] = jnp.where(first, value, turned)
                packed[slot, pl.ds(base + quarter, quarter), :] = jnp.where(first, turned, value)
            value = coords_ref[pl.ds(slot * 2, 2), :]
            turned = pltpu.roll(value, LEAF, 1)
            packed[slot, rank : rank + 1, :] = jnp.where(first, value, turned)[0:1]
            packed[slot, rank + 1 : rank + 2, :] = jnp.where(first, turned, value)[0:1]
            packed[slot, rank + 2 : rank + 3, :] = jnp.where(first, value, turned)[1:2]
            return carry

        lax.fori_loop(0, packed.shape[0], unpack, 0, unroll=4)

    @pl.when(step * BATCH < total_ref[0])
    def _():
        for member in range(BATCH):
            group = step * BATCH + member
            leaf = leaf_ref[group]
            count = count_ref[group]
            slots = [slot_ref[group * GROUP + e] for e in range(GROUP)]
            target = target_ref[leaf]
            z_parts = []
            for half in range(GROUP // 2):
                left = packed[slots[2 * half]]
                right = packed[slots[2 * half + 1]]
                both = jnp.where(first, left, right)
                values = kernel_half(both[rank : rank + 3], target, lane, (count - 2 * half) * LEAF)
                high, low = halves(values)
                high_ref[member, :, half * LANES : (half + 1) * LANES] = high
                low_ref[member, :, half * LANES : (half + 1) * LANES] = low
                z_parts.append(both[:rank])
            z_high, z_low = halves(jnp.concatenate(z_parts, axis=1))
            k_high = high_ref[member]
            k_low = low_ref[member]
            update = dot_nt(z_high, k_high) + (dot_nt(z_low, k_high) + dot_nt(z_high, k_low))
            sketched_ref[leaf] += update

    @pl.when(step == pl.num_programs(0) - 1)
    def _():
        for leaf in range(gram_ref.shape[0]):
            block = sketched_ref[leaf]
            gram_ref[leaf] = dot_exact_nt(block, block)


def kernel_blocks(total, group_leaf, group_count, group_slots, place, own, other, coords, targets, rank):
    leaves = targets.shape[0]
    groups = group_leaf.shape[0]
    slots = coords.shape[0] // 2
    steps = groups // BATCH

    def block_index(step, total_ref, *unused):
        last = (total_ref[0] - 1) // BATCH
        return (jnp.minimum(step, last), 0, 0)

    flat = lambda *unused: (0, 0)
    whole = lambda *unused: (0, 0, 0)
    once = pl.Buffered(1)
    return pl.pallas_call(
        functools.partial(blocks_body, rank=rank),
        grid_spec=pltpu.PrefetchScalarGridSpec(
            num_scalar_prefetch=5,
            grid=(steps,),
            in_specs=[
                pl.BlockSpec(own.shape, flat, pipeline_mode=once),
                pl.BlockSpec(other.shape, flat, pipeline_mode=once),
                pl.BlockSpec(coords.shape, flat, pipeline_mode=once),
                pl.BlockSpec(targets.shape, whole, pipeline_mode=once),
            ],
            out_specs=[
                pl.BlockSpec((BATCH, LEAF, GROUP * LEAF), block_index),
                pl.BlockSpec((BATCH, LEAF, GROUP * LEAF), block_index),
                pl.BlockSpec((leaves, rank, LEAF), whole),
                pl.BlockSpec((leaves, rank, rank), whole),
            ],
            scratch_shapes=[pltpu.VMEM((slots, rank + SUB, LANES), jnp.float32)],
        ),
        out_shape=[
            jax.ShapeDtypeStruct((groups, LEAF, GROUP * LEAF), jnp.bfloat16),
            jax.ShapeDtypeStruct((groups, LEAF, GROUP * LEAF), jnp.bfloat16),
            jax.ShapeDtypeStruct((leaves, rank, LEAF), jnp.float32),
            jax.ShapeDtypeStruct((leaves, rank, rank), jnp.float32),
        ],
        compiler_params=pltpu.CompilerParams(vmem_limit_bytes=vmem_bytes),
        name="kernel_blocks",
        cost_estimate=pl.CostEstimate(
            flops=2 * 10**10, bytes_accessed=2 * 10**7, transcendentals=0
        ),
    )(total, group_leaf, group_count, group_slots, place, own, other, coords, targets)


def far_body(
    total_ref, leaf_ref, slot_ref,
    fetched_ref, high_ref, low_ref, weights_ref, path_ref,
    out_ref, projected_ref, root_ref,
    s_high, s_low, acc,
):
    step = pl.program_id(0)
    samp_dev = fetched_ref.shape[2]

    @pl.when(step == 0)
    def _():
        acc[...] = jnp.zeros_like(acc)

        def split(slot, carry):
            s_high[slot], s_low[slot] = halves(fetched_ref[slot])
            return carry

        lax.fori_loop(0, fetched_ref.shape[0], split, 0, unroll=8)

    @pl.when(step * BATCH < total_ref[0])
    def _():
        for member in range(BATCH):
            group = step * BATCH + member
            leaf = leaf_ref[group]
            slots = [slot_ref[group * GROUP + e] for e in range(GROUP)]
            rows_high = jnp.concatenate([s_high[slot] for slot in slots], axis=0)
            rows_low = jnp.concatenate([s_low[slot] for slot in slots], axis=0)
            k_high = high_ref[member]
            k_low = low_ref[member]
            acc[leaf] += dot(k_high, rows_high) + (dot(k_high, rows_low) + dot(k_low, rows_high))

    @pl.when(step == pl.num_programs(0) - 1)
    def _():
        leaves = acc.shape[0]
        rows = acc[...].reshape(leaves * LEAF, samp_dev)
        projected = dot_exact(weights_ref[...], rows)
        projected_ref[...] = projected
        root_ref[...] = lax.dot_general(
            path_ref[...], projected, tn_dims, precision=highest, preferred_element_type=jnp.float32
        )
        for pair in range(leaves // 2):
            block = acc[2 * pair : 2 * pair + 2].reshape(2 * LEAF, samp_dev)
            out_ref[:, 2 * pair * LEAF : 2 * (pair + 1) * LEAF] = block.T


def far_products(total, group_leaf, group_slots, fetched, high, low, weights, path):
    slots, unused, samp_dev = fetched.shape
    groups = group_leaf.shape[0]
    points_dev = weights.shape[1]
    leaves = points_dev // LEAF
    steps = groups // BATCH

    def block_index(step, total_ref, *unused):
        last = (total_ref[0] - 1) // BATCH
        return (jnp.minimum(step, last), 0, 0)

    return pl.pallas_call(
        far_body,
        grid_spec=pltpu.PrefetchScalarGridSpec(
            num_scalar_prefetch=3,
            grid=(steps,),
            in_specs=[
                pl.BlockSpec(fetched.shape, lambda *unused: (0, 0, 0), pipeline_mode=pl.Buffered(1)),
                pl.BlockSpec((BATCH, LEAF, GROUP * LEAF), block_index),
                pl.BlockSpec((BATCH, LEAF, GROUP * LEAF), block_index),
                pl.BlockSpec(weights.shape, lambda *unused: (0, 0), pipeline_mode=pl.Buffered(1)),
                pl.BlockSpec(path.shape, lambda *unused: (0, 0), pipeline_mode=pl.Buffered(1)),
            ],
            out_specs=[
                pl.BlockSpec((samp_dev, points_dev), lambda *unused: (0, 0)),
                pl.BlockSpec((weights.shape[0], samp_dev), lambda *unused: (0, 0)),
                pl.BlockSpec((weights.shape[0], samp_dev), lambda *unused: (0, 0)),
            ],
            scratch_shapes=[
                pltpu.VMEM((slots, LEAF, samp_dev), jnp.bfloat16),
                pltpu.VMEM((slots, LEAF, samp_dev), jnp.bfloat16),
                pltpu.VMEM((leaves, LEAF, samp_dev), jnp.float32),
            ],
        ),
        out_shape=[
            jax.ShapeDtypeStruct((samp_dev, points_dev), jnp.float32),
            jax.ShapeDtypeStruct((weights.shape[0], samp_dev), jnp.float32),
            jax.ShapeDtypeStruct((weights.shape[0], samp_dev), jnp.float32),
        ],
        compiler_params=pltpu.CompilerParams(vmem_limit_bytes=vmem_bytes),
        name="far_products",
        cost_estimate=pl.CostEstimate(
            flops=10**10, bytes_accessed=2 * 10**7, transcendentals=0
        ),
    )(total, group_leaf, group_slots, fetched, high, low, weights, path)


NEAR_LEAVES = 8


def near_body(mask_ref, rows_ref, coords_ref, target_ref, out_ref):
    step = pl.program_id(0)
    samp_dev = rows_ref.shape[2]
    lane = lax.broadcasted_iota(jnp.int32, (1, LANES), 1)
    first = lane < LEAF
    for pair in range(NEAR_LEAVES // 2):
        results = []
        for member in range(2):
            leaf = step * NEAR_LEAVES + 2 * pair + member
            target = target_ref[leaf]
            k_high = []
            k_low = []
            for half in range(2):
                both = jnp.where(first, coords_ref[leaf + 2 * half], coords_ref[leaf + 2 * half + 1])
                values = kernel_half(both, target, lane, LANES)
                left = mask_ref[leaf * 3 + 2 * half].astype(jnp.float32)
                if half == 0:
                    right = mask_ref[leaf * 3 + 1].astype(jnp.float32)
                else:
                    right = jnp.float32(0.0)
                high, low = halves(values * jnp.where(first, left, right))
                k_high.append(high)
                k_low.append(low)
            k_high = jnp.concatenate(k_high, axis=1)
            k_low = jnp.concatenate(k_low, axis=1)
            rows = rows_ref[pl.ds(leaf, 4)].reshape(4 * LEAF, samp_dev)
            rows_high, rows_low = halves(rows)
            results.append(
                dot(k_high, rows_high) + (dot(k_high, rows_low) + dot(k_low, rows_high))
            )
        block = jnp.concatenate(results, axis=0)
        out_ref[:, 2 * pair * LEAF : 2 * (pair + 1) * LEAF] = block.T


def near_products(mask, rows, coords, targets):
    leaves = targets.shape[0]
    samp_dev = rows.shape[2]
    whole = lambda *unused: (0, 0, 0)
    return pl.pallas_call(
        near_body,
        grid_spec=pltpu.PrefetchScalarGridSpec(
            num_scalar_prefetch=1,
            grid=(leaves // NEAR_LEAVES,),
            in_specs=[
                pl.BlockSpec(rows.shape, whole),
                pl.BlockSpec(coords.shape, whole),
                pl.BlockSpec(targets.shape, whole),
            ],
            out_specs=pl.BlockSpec((samp_dev, NEAR_LEAVES * LEAF), lambda step, *unused: (0, step)),
        ),
        out_shape=jax.ShapeDtypeStruct((samp_dev, leaves * LEAF), jnp.float32),
        compiler_params=pltpu.CompilerParams(vmem_limit_bytes=vmem_bytes),
        name="near_products",
        cost_estimate=pl.CostEstimate(
            flops=4 * 10**9, bytes_accessed=10**7, transcendentals=0
        ),
    )(mask, rows, coords, targets)


def to_lanes(source, target, rank):
    nodes = source.shape[0] // rank
    target[...] = jnp.zeros_like(target)
    for r in range(rank):
        target[r, :, 0:nodes] = source[pl.ds(r, nodes, stride=rank), :].T


def from_lanes(columns, target, r, nodes, rank):
    target[pl.ds(r, nodes, stride=rank), :] = columns.T[0:nodes]


def eliminate(current, left, inverse, level, rank):
    tiles = rank // SUB
    row = lax.broadcasted_iota(jnp.int32, (SUB, LANES), 0)
    diagonal = [current[j, j : j + 1, :] for j in range(rank)]
    while len(diagonal) > 1:
        diagonal = [diagonal[i] + diagonal[i + 1] for i in range(0, len(diagonal), 2)]
    share = shift_share * diagonal[0] / rank
    shift = share + 1e-06
    a = [
        {t: current[j, SUB * t : SUB * (t + 1), :] for t in range(j // SUB, tiles)}
        for j in range(rank)
    ]
    for j in range(rank):
        a[j][j // SUB] = a[j][j // SUB] + jnp.where(row == j % SUB, shift, 0.0)
    m = []
    scales = []
    for k in range(rank):
        tk, rk = k // SUB, k % SUB
        root = lax.rsqrt(a[k][tk][rk : rk + 1, :])
        scales.append(root)
        reciprocal = root * root
        column = {t: a[k][t] * reciprocal for t in range(tk, tiles)}
        column[tk] = jnp.where(row > rk, column[tk], 0.0)
        for j in range(k + 1, rank):
            factor = a[k][j // SUB][j % SUB : j % SUB + 1, :]
            for t in range(j // SUB, tiles):
                a[j][t] = a[j][t] - column[t] * factor
        for c in range(k):
            factor = m[c][tk][rk : rk + 1, :]
            for t in range(tk, tiles):
                m[c][t] = m[c][t] - column[t] * factor
        fresh = {t: -column[t] for t in range(tk, tiles)}
        fresh[tk] = jnp.where(row == rk, 1.0, fresh[tk])
        m.append(fresh)
        if left is not None:
            for t in range(tiles):
                if t < tk:
                    value = jnp.zeros((SUB, LANES), jnp.float32)
                else:
                    value = a[k][t] * root
                if t == tk:
                    value = jnp.where(row >= rk, value, 0.0)
                left[k, SUB * t : SUB * (t + 1), :] = value
    for t in range(tiles):
        scale = jnp.concatenate(scales[SUB * t : SUB * (t + 1)], axis=0)
        for c in range(rank):
            value = m[c][t] * scale if t >= c // SUB else jnp.zeros((SUB, LANES), jnp.float32)
            inverse[c * rank + SUB * t : c * rank + SUB * (t + 1), :] = value
    return shift, share


def inverse_row(inverse, r, t, rank):
    return inverse[pl.ds(SUB * t * rank + r, SUB, stride=rank), :]


def pair_up(value, level):
    return value + pltpu.roll(value, LANES - lax.shift_left(1, level), 1)


def level_fast(level, levels, current, left, inverse, squared, ratio, child, lowest, rank, child_at):
    tiles = rank // SUB
    row = lax.broadcasted_iota(jnp.int32, (SUB, LANES), 0)
    shift, share = eliminate(current, left, inverse, level, rank)
    lowest[...] = jnp.minimum(lowest[...], share)

    for block in range(tiles):
        sums = [[None] * tiles for _ in range(SUB)]
        for r in range(SUB * block, rank):
            parts = [inverse_row(inverse, r, t, rank) for t in range(block, r // SUB + 1)]
            for q in range(SUB):
                if SUB * block + q > r:
                    continue
                factor = parts[0][q : q + 1, :]
                for t in range(block, r // SUB + 1):
                    term = parts[t - block] * factor
                    sums[q][t] = term if sums[q][t] is None else sums[q][t] + term
        for q in range(SUB):
            at = (SUB * block + q) * rank
            for t in range(block, tiles):
                squared[at + SUB * t : at + SUB * (t + 1), :] = sums[q][t]

    if child is not None:
        @pl.when(child_at(level))
        def _():
            for r in range(rank):
                for t in range(tiles):
                    value = left[r, SUB * t : SUB * (t + 1), :]
                    if t <= r // SUB:
                        value = value - shift * inverse_row(inverse, r, t, rank)
                    child[r, SUB * t : SUB * (t + 1), :] = value

    for q in range(rank):
        for t in range(tiles):
            if t >= q // SUB:
                value = squared[q * rank + SUB * t : q * rank + SUB * (t + 1), :]
            else:
                value = squared[pl.ds(SUB * t * rank + q, SUB, stride=rank), :]
            value = -shift * value
            if t == q // SUB:
                value = value + jnp.where(row == q % SUB, 1.0, 0.0)
            if ratio is not None:
                ratio[level, q, SUB * t : SUB * (t + 1), :] = value
            here = current[q, SUB * t : SUB * (t + 1), :] - shift * value
            current[q, SUB * t : SUB * (t + 1), :] = pair_up(here, level)


def level_plain(level, levels, current, left, inverse, squared, ratio, child, lowest, rank, child_at):
    tiles = rank // SUB
    eliminate(current, left, inverse, level, rank)

    def products(out, count, left_of, right_of):
        def block_step(block, carry):
            offset = pl.multiple_of(block * SUB, SUB)
            sums = [[None] * tiles for _ in range(SUB)]
            for r in range(count):
                parts = [left_of(r, t) for t in range(tiles)]
                heads = right_of(r, offset)
                for q in range(SUB):
                    for t in range(tiles):
                        term = parts[t] * heads[q : q + 1, :]
                        sums[q][t] = term if sums[q][t] is None else sums[q][t] + term
            for q in range(SUB):
                for t in range(tiles):
                    out(offset + q, t, sums[q][t])
            return carry

        lax.fori_loop(0, tiles, block_step, 0)

    def tile(t):
        return slice(SUB * t, SUB * (t + 1))

    def put_child(r, t, value):
        squared[pl.ds(pl.multiple_of(r * rank + SUB * t, SUB), SUB), :] = value

    products(
        put_child, rank,
        lambda k, t: current[k, tile(t), :],
        lambda k, offset: inverse[pl.ds(pl.multiple_of(k * rank + offset, SUB), SUB), :],
    )
    if child is not None:
        @pl.when(child_at(level))
        def _():
            for r in range(rank):
                for t in range(tiles):
                    child[r, tile(t), :] = squared[r * rank + SUB * t : r * rank + SUB * (t + 1), :]

    def child_part(r, t):
        return squared[r * rank + SUB * t : r * rank + SUB * (t + 1), :]

    def put_current(q, t, value):
        current[q, tile(t), :] = pair_up(value, level)

    if ratio is not None:
        def put_ratio(c, t, value):
            ratio[level, c, tile(t), :] = value

        def inverse_head(r, offset):
            return inverse[pl.ds(offset * rank + r, SUB, stride=rank), :]

        products(put_ratio, rank, child_part, inverse_head)
    products(
        put_current, rank, child_part,
        lambda r, offset: squared[pl.ds(pl.multiple_of(r * rank + offset, SUB), SUB), :],
    )


def run_levels(source, levels, nodes, current, left, inverse, squared, ratio, child, lowest, rank, child_at, finish):
    lowest[...] = jnp.full((1, LANES), 1.0, jnp.float32)

    def sweep(level_step):
        to_lanes(source, current, rank)

        def body(level, carry):
            level_step(level, levels, current, left, inverse, squared, ratio, child, lowest, rank, child_at)
            finish(level)
            return carry

        lax.fori_loop(0, levels, body, 0)

    sweep(level_fast)
    lane = lax.broadcasted_iota(jnp.int32, (1, LANES), 1)
    least = jnp.min(jnp.where(lane < nodes, lowest[...], 1.0))

    @pl.when(least < 2e-06)
    def _():
        sweep(level_plain)


def branch_body(gram_ref, inverse_ref, ratio_ref, top_ref, child_ref, current, left, inverse, squared, child, lowest, *, rank, levels):
    nodes = gram_ref.shape[0] // rank

    def finish(level):
        @pl.when(level == 0)
        def _():
            for c in range(rank):
                inverse_ref[c] = inverse[c * rank : (c + 1) * rank, :]

        @pl.when(level == levels - 1)
        def _():
            for r in range(rank):
                child_ref[r : r + 1, :] = child[r].T[0:1, :]
                top_ref[r : r + 1, :] = jnp.concatenate(
                    [inverse_row(inverse, r, t, rank) for t in range(rank // SUB)], axis=0
                ).T[0:1, :]

    run_levels(
        gram_ref, levels, nodes, current, left, inverse, squared, ratio_ref, child, lowest, rank,
        lambda level: level == levels - 1, finish,
    )


vmem_spec = pl.BlockSpec(memory_space=pltpu.VMEM)


def tree_scratch(rank):
    return [
        pltpu.VMEM((rank, rank, LANES), jnp.float32),
        pltpu.VMEM((rank, rank, LANES), jnp.float32),
        pltpu.VMEM((rank * rank, LANES), jnp.float32),
        pltpu.VMEM((rank * rank, LANES), jnp.float32),
        pltpu.VMEM((rank, rank, LANES), jnp.float32),
        pltpu.VMEM((1, LANES), jnp.float32),
    ]


def branch_factors(gram, levels):
    leaves, rank, unused = gram.shape
    return pl.pallas_call(
        functools.partial(branch_body, rank=rank, levels=levels),
        in_specs=[vmem_spec],
        out_specs=[vmem_spec] * 4,
        out_shape=[
            jax.ShapeDtypeStruct((rank, rank, LANES), jnp.float32),
            jax.ShapeDtypeStruct((levels, rank, rank, LANES), jnp.float32),
            jax.ShapeDtypeStruct((rank, rank), jnp.float32),
            jax.ShapeDtypeStruct((rank, rank), jnp.float32),
        ],
        scratch_shapes=tree_scratch(rank),
        compiler_params=pltpu.CompilerParams(vmem_limit_bytes=vmem_bytes),
        name="branch_factors",
        cost_estimate=pl.CostEstimate(flops=10**10, bytes_accessed=10**7, transcendentals=0),
    )(gram.reshape(leaves * rank, rank))


def basis_body(inverse_ref, ratio_ref, top_ref, sketched_ref, weights_ref, basis_ref, natural, *, rank, levels):
    leaves = sketched_ref.shape[0]
    upper = [top_ref[...]]
    for level in range(levels - 2, -1, -1):
        stride = 2**level
        for c in range(rank):
            from_lanes(ratio_ref[level, c], natural, c, leaves, rank)
        fresh = []
        for node in range(leaves // stride):
            block = natural[node * stride * rank : (node * stride + 1) * rank, :]
            fresh.append(dot_exact(upper[node // 2], block))
        upper = fresh
    for r in range(rank):
        from_lanes(inverse_ref[r], natural, r, leaves, rank)
    for pair in range(leaves // 2):
        results = []
        for leaf in (2 * pair, 2 * pair + 1):
            block = sketched_ref[leaf]
            own = lax.dot_general(
                natural[leaf * rank : (leaf + 1) * rank, :], block, tn_dims,
                precision=highest, preferred_element_type=jnp.float32,
            )
            results.append(jnp.concatenate([dot_exact(upper[leaf], block), own], axis=0))
        both = jnp.concatenate(results, axis=1)
        weights_ref[:, pair * 2 * LEAF : (pair + 1) * 2 * LEAF] = both[:rank]
        basis_ref[:, pair * 2 * LEAF : (pair + 1) * 2 * LEAF] = both[rank:]


def bases(inverse, ratio, top, sketched):
    leaves, rank, unused = sketched.shape
    levels = ratio.shape[0]
    shape = jax.ShapeDtypeStruct((rank, leaves * LEAF), jnp.float32)
    return pl.pallas_call(
        functools.partial(basis_body, rank=rank, levels=levels),
        in_specs=[vmem_spec] * 4,
        out_specs=[vmem_spec] * 2,
        out_shape=[shape, shape],
        scratch_shapes=[pltpu.VMEM((leaves * rank, rank), jnp.float32)],
        compiler_params=pltpu.CompilerParams(vmem_limit_bytes=vmem_bytes),
        name="bases",
        cost_estimate=pl.CostEstimate(flops=5 * 10**9, bytes_accessed=10**7, transcendentals=0),
    )(inverse, ratio, top, sketched)


def top_body(place_ref, children_ref, transfer_ref, path_ref, source, current, left, inverse, squared, child, lowest, nat_inverse, nat_child, *, rank, levels):
    nodes = children_ref.shape[0] // 2
    for node in range(nodes):
        both = children_ref[2 * node : 2 * node + 2].reshape(2 * rank, rank)
        source[node * rank : (node + 1) * rank, :] = lax.dot_general(
            both, both, tn_dims, precision=highest, preferred_element_type=jnp.float32
        )

    def finish(level):
        for r in range(rank):
            from_lanes(child[r], nat_child.at[level], r, nodes, rank)
            from_lanes(inverse[r * rank : (r + 1) * rank, :], nat_inverse.at[level], r, nodes, rank)

    run_levels(
        source, levels, nodes, current, left, inverse, squared, None, child, lowest, rank,
        lambda level: level >= 0, finish,
    )
    offset = 0
    for level in range(levels):
        for node in range(nodes >> level):
            if level == 0:
                stacked = children_ref[2 * node : 2 * node + 2].reshape(2 * rank, rank)
            else:
                first = 2 * node << level - 1
                second = 2 * node + 1 << level - 1
                stacked = jnp.concatenate(
                    [
                        nat_child[level - 1, first * rank : (first + 1) * rank, :],
                        nat_child[level - 1, second * rank : (second + 1) * rank, :],
                    ],
                    axis=0,
                )
            at = (node << level) * rank
            transfer_ref[offset + node] = dot_exact(stacked, nat_inverse[level, at : at + rank, :])
        offset += nodes >> level
    me = place_ref[0]
    offset = 0
    path = None
    for level in range(levels):
        node = offset + lax.shift_right_logical(me, level + 1)
        side = lax.rem(lax.shift_right_logical(me, level), 2)
        block = transfer_ref[node, pl.ds(pl.multiple_of(side * rank, rank), rank), :]
        path = block if path is None else dot_exact(path, block)
        offset += nodes >> level
    path_ref[...] = path


def top_factors(children, place):
    branches, rank, unused = children.shape
    levels = branches.bit_length() - 1
    nodes = branches // 2
    natural = pltpu.VMEM((levels, nodes * rank, rank), jnp.float32)
    return pl.pallas_call(
        functools.partial(top_body, rank=rank, levels=levels),
        in_specs=[pl.BlockSpec(memory_space=pltpu.SMEM), vmem_spec],
        out_specs=[vmem_spec] * 2,
        out_shape=[
            jax.ShapeDtypeStruct((branches - 1, 2 * rank, rank), jnp.float32),
            jax.ShapeDtypeStruct((rank, rank), jnp.float32),
        ],
        scratch_shapes=[pltpu.VMEM((nodes * rank, rank), jnp.float32)]
        + tree_scratch(rank)
        + [natural, natural],
        compiler_params=pltpu.CompilerParams(vmem_limit_bytes=vmem_bytes),
        name="top_factors",
        cost_estimate=pl.CostEstimate(flops=10**10, bytes_accessed=10**7, transcendentals=0),
    )(place, children)


def exchange_sum(pieces, axis):
    count = pieces.shape[0]
    me = lax.axis_index(axis)
    mine = lax.dynamic_index_in_dim(pieces, me, 0, keepdims=False)
    for step in range(1, count):
        outgoing = lax.dynamic_index_in_dim(pieces, (me + step) % count, 0, keepdims=False)
        mine = mine + lax.ppermute(
            outgoing, axis, [(i, (i + step) % count) for i in range(count)]
        )
    return mine


def exchange_all(piece, axis):
    count = lax.axis_size(axis)
    me = lax.axis_index(axis)
    if count == 2:
        other = lax.ppermute(piece, axis, [(0, 1), (1, 0)])
        return jnp.stack([jnp.where(me == 0, piece, other), jnp.where(me == 0, other, piece)])
    result = jnp.zeros((count,) + piece.shape, piece.dtype)
    result = lax.dynamic_update_index_in_dim(result, piece, me, 0)
    for step in range(1, count):
        arrived = lax.ppermute(piece, axis, [(i, (i + step) % count) for i in range(count)])
        result = lax.dynamic_update_index_in_dim(result, arrived, (me - step) % count, 0)
    return result


def double_all(piece, axis):
    count = lax.axis_size(axis)
    me = lax.axis_index(axis)
    held = piece[None]
    stride = 1
    while stride < count:
        other = lax.ppermute(held, axis, [(i, i ^ stride) for i in range(count)])
        low = (me // stride) % 2 == 0
        held = jnp.concatenate([jnp.where(low, held, other), jnp.where(low, other, held)], axis=0)
        stride *= 2
    return held


def group_tables(far_slots, far_count):
    leaves = far_slots.shape[0]
    groups = leaves * FAR // GROUP
    per_leaf = (far_count + GROUP - 1) // GROUP
    before = jnp.arange(leaves)[:, None] >= jnp.arange(leaves)[None, :]
    ends = jnp.sum(jnp.where(before, per_leaf[None, :], 0), axis=1)
    total = ends[leaves - 1 :]
    ids = jnp.arange(groups, dtype=jnp.int32)
    leaf = jnp.minimum(jnp.sum((ends[None, :] <= ids[:, None]).astype(jnp.int32), axis=1), leaves - 1)
    hit = leaf[:, None] == jnp.arange(leaves)[None, :]
    start = jnp.sum(jnp.where(hit, (ends - per_leaf)[None, :], 0), axis=1)
    length = jnp.sum(jnp.where(hit, far_count[None, :], 0), axis=1)
    sub = ids - start
    count = jnp.where(ids < total, jnp.clip(length - GROUP * sub, 0, GROUP), 0)
    first = jnp.minimum(sub, FAR // GROUP - 1)
    slots = far_slots.reshape(leaves * FAR // GROUP, GROUP)[leaf * (FAR // GROUP) + first]
    return (
        total.astype(jnp.int32),
        leaf.astype(jnp.int32),
        count.astype(jnp.int32),
        slots.reshape(-1).astype(jnp.int32),
    )


def two_rows(values, rows):
    leaves = values.shape[1]
    split = jnp.transpose(values.reshape(2, rows, leaves, LEAF), (2, 1, 0, 3))
    return split.reshape(leaves, rows, 2 * LEAF)


def on_device(points, samples, sketch, far_requests, far_slots, far_count, near_mask):
    samp_dev = samples.shape[0]
    leaves = samples.shape[1] // LEAF
    rank = sketch.shape[0]
    branches = lax.axis_size("leaf")
    columns = lax.axis_size("cols")
    cap = far_requests.shape[2]
    slots = branches * cap
    share = rank // columns
    me = lax.axis_index("leaf").astype(jnp.int32).reshape(1)
    column = lax.axis_index("cols")

    wanted = far_requests.reshape(branches, cap)
    asked_for = lax.all_to_all(wanted, "leaf", split_axis=0, concat_axis=0, tiled=True)

    coords = jnp.transpose(points.reshape(3, leaves, LEAF), (1, 0, 2))
    targets = jnp.transpose(coords, (0, 2, 1))
    rows = jnp.transpose(samples.reshape(samp_dev, leaves, LEAF), (1, 2, 0))
    tables = group_tables(far_slots, far_count)

    z_part = jnp.dot(sketch, samples, precision=highest)
    z_mine = exchange_sum(z_part.reshape(columns, share, leaves * LEAF), "cols")
    z_rows = two_rows(z_mine.reshape(share, leaves, LEAF), share // 2)
    c_rows = two_rows(
        jnp.pad(points.reshape(3, leaves, LEAF)[jnp.array([0, 2, 1])], ((0, 1), (0, 0), (0, 0))), 2
    )
    asked_for, rows, z_rows, c_rows, tables = lax.optimization_barrier(
        (asked_for, rows, z_rows, c_rows, tables)
    )
    total, group_leaf, group_count, group_slots = tables
    picked = asked_for.reshape(-1)
    z_sent = z_rows[picked].reshape(branches, cap * share // 2, LANES)
    c_sent = c_rows[picked].reshape(branches, cap * 2, LANES)
    small_sent = jnp.concatenate([z_sent, c_sent], axis=1)
    small_got = lax.all_to_all(small_sent, "leaf", split_axis=0, concat_axis=0, tiled=True)

    rows_sent = rows[picked].reshape(branches, cap, LEAF, samp_dev)
    rows_got = lax.all_to_all(rows_sent, "leaf", split_axis=0, concat_axis=0, tiled=True)
    fetched = rows_got.reshape(slots, LEAF, samp_dev)

    z_own = small_got[:, : cap * share // 2].reshape(slots * share // 2, LANES)
    c_got = small_got[:, cap * share // 2 :].reshape(slots * 2, LANES)
    if columns == 2:
        z_other = lax.ppermute(z_own, "cols", [(0, 1), (1, 0)])
        place = column.astype(jnp.int32).reshape(1)
    else:
        z_all = exchange_all(z_own, "cols").reshape(columns, slots, share // 2, 2, LEAF)
        z_all = jnp.transpose(z_all, (1, 0, 3, 2, 4)).reshape(slots, 2, 2, rank // 4, LEAF)
        z_all = jnp.transpose(z_all, (1, 0, 3, 2, 4)).reshape(2, slots * rank // 4, LANES)
        z_own, z_other = z_all[0], z_all[1]
        place = jnp.zeros((1,), jnp.int32)

    high, low, sketched, gram = kernel_blocks(
        total, group_leaf, group_count, group_slots, place, z_own, z_other, c_got, targets, rank
    )

    levels = leaves.bit_length()
    inverse, ratio, top_inverse, own_child = branch_factors(gram, levels)
    children = double_all(own_child.reshape(rank * rank // LANES, LANES), "leaf")
    top_transfer, path = top_factors(children.reshape(branches, rank, rank), me)
    weights, leaf_basis = bases(inverse, ratio, top_inverse, sketched)

    edges = jnp.concatenate([rows[:1], rows[leaves - 1 :]], axis=0)
    edge_coords = jnp.concatenate([coords[:1], coords[leaves - 1 :]], axis=0)
    edge_coords = jnp.pad(edge_coords, ((0, 0), (0, 5), (0, samp_dev - LEAF))) if samp_dev >= LEAF else None
    forward = [(i, i + 1) for i in range(branches - 1)]
    backward = [(target, source) for source, target in forward]
    if edge_coords is not None:
        edges = jnp.concatenate([edges, edge_coords], axis=1)
        edges, unused = lax.optimization_barrier((edges, small_got))
        low_edge = lax.ppermute(edges[1], "leaf", forward)
        high_edge = lax.ppermute(edges[0], "leaf", backward)
        rows_low, rows_high = low_edge[:LEAF], high_edge[:LEAF]
        coords_low, coords_high = low_edge[LEAF : LEAF + 3, :LEAF], high_edge[LEAF : LEAF + 3, :LEAF]
    else:
        rows_low = lax.ppermute(edges[1], "leaf", forward)
        rows_high = lax.ppermute(edges[0], "leaf", backward)
        coords_low = lax.ppermute(coords[leaves - 1], "leaf", forward)
        coords_high = lax.ppermute(coords[0], "leaf", backward)
    near_rows = jnp.concatenate(
        [rows_low[None], rows, rows_high[None], jnp.zeros_like(rows_low)[None]], axis=0
    )
    near_coords = jnp.concatenate(
        [coords_low[None], coords, coords_high[None], jnp.zeros_like(coords_low)[None]], axis=0
    )
    near_coords = jnp.pad(near_coords, ((0, 0), (0, 5), (0, 0)))
    near_coords = jnp.concatenate([near_coords, near_coords], axis=2)
    near_sample = near_products(near_mask.reshape(-1), near_rows, near_coords, targets)

    far_sample, branch_samples, root_part = far_products(
        total, group_leaf, group_slots, fetched, high, low, weights, path
    )
    root_sample = lax.psum(root_part, "leaf")
    return (far_sample, near_sample, leaf_basis, branch_samples, top_transfer, root_sample)


def solution(mesh):
    return jax.shard_map(
        on_device,
        mesh=mesh,
        in_specs=(
            P(None, "leaf"),
            P("cols", "leaf"),
            P(None, "cols"),
            P("leaf", None, None),
            P("leaf", None),
            P("leaf"),
            P("leaf", None),
        ),
        out_specs=(
            P("cols", "leaf"),
            P("cols", "leaf"),
            P(None, "leaf"),
            P("leaf", "cols"),
            P(),
            P(None, "cols"),
        ),
        check_vma=False,
    )
```

```python
import functools
import math

import jax
import jax.numpy as jnp
import numpy as np
from jax import lax
from jax.experimental import pallas as pl
from jax.experimental.pallas import tpu as pltpu
from jax.sharding import PartitionSpec as P

LEAF = 64
FAR = 16
GROUP = 4
BATCH = 16
LANES = 128
SUB = 8

length_scale = 0.3
shift_share = 0.05
highest = lax.Precision.HIGHEST
exponent_scale = -math.log2(math.e) / length_scale
vmem_bytes = 56 * 1024 * 1024

nt_dims = (((1,), (1,)), ((), ()))
tn_dims = (((0,), (0,)), ((), ()))


def halves(value):
    high = value.astype(jnp.bfloat16)
    low = (value - high.astype(jnp.float32)).astype(jnp.bfloat16)
    return high, low


def dot(a, b):
    return jnp.dot(a, b, preferred_element_type=jnp.float32)


def dot_exact(a, b):
    return jnp.dot(a, b, precision=highest, preferred_element_type=jnp.float32)


def dot_exact_nt(a, b):
    return lax.dot_general(a, b, nt_dims, precision=highest, preferred_element_type=jnp.float32)


def dot_nt(a, b):
    return lax.dot_general(a, b, nt_dims, preferred_element_type=jnp.float32)


def kernel_half(source_rows, target, lane, valid):
    total = None
    for axis in range(3):
        difference = source_rows[axis : axis + 1, :] - target[:, axis : axis + 1]
        square = difference * difference
        total = square if total is None else total + square
    distance = total * lax.rsqrt(jnp.maximum(total, 1e-30))
    values = jnp.exp2(distance * exponent_scale)
    return jnp.where(lane < valid, values, 0.0)


def blocks_body(
    total_ref, leaf_ref, count_ref, slot_ref, place_ref,
    own_ref, other_ref, coords_ref, target_ref,
    high_ref, low_ref, sketched_ref, gram_ref,
    packed,
    *, rank,
):
    step = pl.program_id(0)
    lane = lax.broadcasted_iota(jnp.int32, (1, LANES), 1)
    first = lane < LEAF

    @pl.when(step == 0)
    def _():
        sketched_ref[...] = jnp.zeros_like(sketched_ref)
        quarter = rank // 4
        own_at = pl.multiple_of(place_ref[0] * 2 * quarter, quarter)
        other_at = pl.multiple_of((1 - place_ref[0]) * 2 * quarter, quarter)

        def unpack(slot, carry):
            for ref, base in ((own_ref, own_at), (other_ref, other_at)):
                value = ref[pl.ds(pl.multiple_of(slot * quarter, quarter), quarter), :]
                turned = pltpu.roll(value, LEAF, 1)
                packed[slot, pl.ds(base, quarter), :] = jnp.where(first, value, turned)
                packed[slot, pl.ds(base + quarter, quarter), :] = jnp.where(first, turned, value)
            value = coords_ref[pl.ds(slot * 2, 2), :]
            turned = pltpu.roll(value, LEAF, 1)
            packed[slot, rank : rank + 1, :] = jnp.where(first, value, turned)[0:1]
            packed[slot, rank + 1 : rank + 2, :] = jnp.where(first, turned, value)[0:1]
            packed[slot, rank + 2 : rank + 3, :] = jnp.where(first, value, turned)[1:2]
            return carry

        lax.fori_loop(0, packed.shape[0], unpack, 0, unroll=4)

    @pl.when(step * BATCH < total_ref[0])
    def _():
        for member in range(BATCH):
            group = step * BATCH + member
            leaf = leaf_ref[group]
            count = count_ref[group]
            slots = [slot_ref[group * GROUP + e] for e in range(GROUP)]
            target = target_ref[leaf]
            z_parts = []
            for half in range(GROUP // 2):
                left = packed[slots[2 * half]]
                right = packed[slots[2 * half + 1]]
                both = jnp.where(first, left, right)
                values = kernel_half(both[rank : rank + 3], target, lane, (count - 2 * half) * LEAF)
                high, low = halves(values)
                high_ref[member, :, half * LANES : (half + 1) * LANES] = high
                low_ref[member, :, half * LANES : (half + 1) * LANES] = low
                z_parts.append(both[:rank])
            z_high, z_low = halves(jnp.concatenate(z_parts, axis=1))
            k_high = high_ref[member]
            k_low = low_ref[member]
            update = dot_nt(z_high, k_high) + (dot_nt(z_low, k_high) + dot_nt(z_high, k_low))
            sketched_ref[leaf] += update

    @pl.when(step == pl.num_programs(0) - 1)
    def _():
        for leaf in range(gram_ref.shape[0]):
            block = sketched_ref[leaf]
            gram_ref[leaf] = dot_exact_nt(block, block)


def kernel_blocks(total, group_leaf, group_count, group_slots, place, own, other, coords, targets, rank):
    leaves = targets.shape[0]
    groups = group_leaf.shape[0]
    slots = coords.shape[0] // 2
    steps = groups // BATCH

    def block_index(step, total_ref, *unused):
        last = (total_ref[0] - 1) // BATCH
        return (jnp.minimum(step, last), 0, 0)

    flat = lambda *unused: (0, 0)
    whole = lambda *unused: (0, 0, 0)
    once = pl.Buffered(1)
    return pl.pallas_call(
        functools.partial(blocks_body, rank=rank),
        grid_spec=pltpu.PrefetchScalarGridSpec(
            num_scalar_prefetch=5,
            grid=(steps,),
            in_specs=[
                pl.BlockSpec(own.shape, flat, pipeline_mode=once),
                pl.BlockSpec(other.shape, flat, pipeline_mode=once),
                pl.BlockSpec(coords.shape, flat, pipeline_mode=once),
                pl.BlockSpec(targets.shape, whole, pipeline_mode=once),
            ],
            out_specs=[
                pl.BlockSpec((BATCH, LEAF, GROUP * LEAF), block_index),
                pl.BlockSpec((BATCH, LEAF, GROUP * LEAF), block_index),
                pl.BlockSpec((leaves, rank, LEAF), whole),
                pl.BlockSpec((leaves, rank, rank), whole),
            ],
            scratch_shapes=[pltpu.VMEM((slots, rank + SUB, LANES), jnp.float32)],
        ),
        out_shape=[
            jax.ShapeDtypeStruct((groups, LEAF, GROUP * LEAF), jnp.bfloat16),
            jax.ShapeDtypeStruct((groups, LEAF, GROUP * LEAF), jnp.bfloat16),
            jax.ShapeDtypeStruct((leaves, rank, LEAF), jnp.float32),
            jax.ShapeDtypeStruct((leaves, rank, rank), jnp.float32),
        ],
        compiler_params=pltpu.CompilerParams(vmem_limit_bytes=vmem_bytes),
        name="kernel_blocks",
        cost_estimate=pl.CostEstimate(
            flops=2 * 10**10, bytes_accessed=2 * 10**7, transcendentals=0
        ),
    )(total, group_leaf, group_count, group_slots, place, own, other, coords, targets)


def far_body(
    total_ref, leaf_ref, slot_ref,
    fetched_ref, high_ref, low_ref, weights_ref,
    out_ref, projected_ref, copies_ref,
    s_high, s_low, acc,
):
    step = pl.program_id(0)
    samp_dev = fetched_ref.shape[2]

    @pl.when(step == 0)
    def _():
        acc[...] = jnp.zeros_like(acc)

        def split(slot, carry):
            s_high[slot], s_low[slot] = halves(fetched_ref[slot])
            return carry

        lax.fori_loop(0, fetched_ref.shape[0], split, 0, unroll=8)

    @pl.when(step * BATCH < total_ref[0])
    def _():
        for member in range(BATCH):
            group = step * BATCH + member
            leaf = leaf_ref[group]
            slots = [slot_ref[group * GROUP + e] for e in range(GROUP)]
            rows_high = jnp.concatenate([s_high[slot] for slot in slots], axis=0)
            rows_low = jnp.concatenate([s_low[slot] for slot in slots], axis=0)
            k_high = high_ref[member]
            k_low = low_ref[member]
            acc[leaf] += dot(k_high, rows_high) + (dot(k_high, rows_low) + dot(k_low, rows_high))

    @pl.when(step == pl.num_programs(0) - 1)
    def _():
        leaves = acc.shape[0]
        rows = acc[...].reshape(leaves * LEAF, samp_dev)
        projected = dot_exact(weights_ref[...], rows)
        projected_ref[...] = projected
        for branch in range(copies_ref.shape[0]):
            copies_ref[branch] = projected
        for pair in range(leaves // 2):
            block = acc[2 * pair : 2 * pair + 2].reshape(2 * LEAF, samp_dev)
            out_ref[:, 2 * pair * LEAF : 2 * (pair + 1) * LEAF] = block.T


def far_products(total, group_leaf, group_slots, fetched, high, low, weights, branches):
    slots, unused, samp_dev = fetched.shape
    groups = group_leaf.shape[0]
    points_dev = weights.shape[1]
    leaves = points_dev // LEAF
    steps = groups // BATCH

    def block_index(step, total_ref, *unused):
        last = (total_ref[0] - 1) // BATCH
        return (jnp.minimum(step, last), 0, 0)

    return pl.pallas_call(
        far_body,
        grid_spec=pltpu.PrefetchScalarGridSpec(
            num_scalar_prefetch=3,
            grid=(steps,),
            in_specs=[
                pl.BlockSpec(fetched.shape, lambda *unused: (0, 0, 0), pipeline_mode=pl.Buffered(1)),
                pl.BlockSpec((BATCH, LEAF, GROUP * LEAF), block_index),
                pl.BlockSpec((BATCH, LEAF, GROUP * LEAF), block_index),
                pl.BlockSpec(weights.shape, lambda *unused: (0, 0), pipeline_mode=pl.Buffered(1)),
            ],
            out_specs=[
                pl.BlockSpec((samp_dev, points_dev), lambda *unused: (0, 0)),
                pl.BlockSpec((weights.shape[0], samp_dev), lambda *unused: (0, 0)),
                pl.BlockSpec((branches, weights.shape[0], samp_dev), lambda *unused: (0, 0, 0)),
            ],
            scratch_shapes=[
                pltpu.VMEM((slots, LEAF, samp_dev), jnp.bfloat16),
                pltpu.VMEM((slots, LEAF, samp_dev), jnp.bfloat16),
                pltpu.VMEM((leaves, LEAF, samp_dev), jnp.float32),
            ],
        ),
        out_shape=[
            jax.ShapeDtypeStruct((samp_dev, points_dev), jnp.float32),
            jax.ShapeDtypeStruct((weights.shape[0], samp_dev), jnp.float32),
            jax.ShapeDtypeStruct((branches, weights.shape[0], samp_dev), jnp.float32),
        ],
        compiler_params=pltpu.CompilerParams(vmem_limit_bytes=vmem_bytes),
        name="far_products",
        cost_estimate=pl.CostEstimate(
            flops=10**10, bytes_accessed=2 * 10**7, transcendentals=0
        ),
    )(total, group_leaf, group_slots, fetched, high, low, weights)


NEAR_LEAVES = 8


def near_body(mask_ref, rows_ref, coords_ref, target_ref, out_ref):
    step = pl.program_id(0)
    samp_dev = rows_ref.shape[2]
    lane = lax.broadcasted_iota(jnp.int32, (1, LANES), 1)
    first = lane < LEAF
    for pair in range(NEAR_LEAVES // 2):
        results = []
        for member in range(2):
            leaf = step * NEAR_LEAVES + 2 * pair + member
            target = target_ref[leaf]
            k_high = []
            k_low = []
            for half in range(2):
                both = jnp.where(first, coords_ref[leaf + 2 * half], coords_ref[leaf + 2 * half + 1])
                values = kernel_half(both, target, lane, LANES)
                left = mask_ref[leaf * 3 + 2 * half].astype(jnp.float32)
                if half == 0:
                    right = mask_ref[leaf * 3 + 1].astype(jnp.float32)
                else:
                    right = jnp.float32(0.0)
                high, low = halves(values * jnp.where(first, left, right))
                k_high.append(high)
                k_low.append(low)
            k_high = jnp.concatenate(k_high, axis=1)
            k_low = jnp.concatenate(k_low, axis=1)
            rows = rows_ref[pl.ds(leaf, 4)].reshape(4 * LEAF, samp_dev)
            rows_high, rows_low = halves(rows)
            results.append(
                dot(k_high, rows_high) + (dot(k_high, rows_low) + dot(k_low, rows_high))
            )
        block = jnp.concatenate(results, axis=0)
        out_ref[:, 2 * pair * LEAF : 2 * (pair + 1) * LEAF] = block.T


def near_products(mask, rows, coords, targets):
    leaves = targets.shape[0]
    samp_dev = rows.shape[2]
    whole = lambda *unused: (0, 0, 0)
    return pl.pallas_call(
        near_body,
        grid_spec=pltpu.PrefetchScalarGridSpec(
            num_scalar_prefetch=1,
            grid=(leaves // NEAR_LEAVES,),
            in_specs=[
                pl.BlockSpec(rows.shape, whole),
                pl.BlockSpec(coords.shape, whole),
                pl.BlockSpec(targets.shape, whole),
            ],
            out_specs=pl.BlockSpec((samp_dev, NEAR_LEAVES * LEAF), lambda step, *unused: (0, step)),
        ),
        out_shape=jax.ShapeDtypeStruct((samp_dev, leaves * LEAF), jnp.float32),
        compiler_params=pltpu.CompilerParams(vmem_limit_bytes=vmem_bytes),
        name="near_products",
        cost_estimate=pl.CostEstimate(
            flops=4 * 10**9, bytes_accessed=10**7, transcendentals=0
        ),
    )(mask, rows, coords, targets)


def to_lanes(source, target, rank):
    nodes = source.shape[0] // rank
    target[...] = jnp.zeros_like(target)
    for r in range(rank):
        target[r, :, 0:nodes] = source[pl.ds(r, nodes, stride=rank), :].T


def from_lanes(columns, target, r, nodes, rank):
    target[pl.ds(r, nodes, stride=rank), :] = columns.T[0:nodes]


def eliminate(current, left, inverse, level, rank):
    tiles = rank // SUB
    row = lax.broadcasted_iota(jnp.int32, (SUB, LANES), 0)
    diagonal = [current[j, j : j + 1, :] for j in range(rank)]
    while len(diagonal) > 1:
        diagonal = [diagonal[i] + diagonal[i + 1] for i in range(0, len(diagonal), 2)]
    share = shift_share * diagonal[0] / rank
    shift = share + 1e-06
    a = [
        {t: current[j, SUB * t : SUB * (t + 1), :] for t in range(j // SUB, tiles)}
        for j in range(rank)
    ]
    for j in range(rank):
        a[j][j // SUB] = a[j][j // SUB] + jnp.where(row == j % SUB, shift, 0.0)
    m = []
    scales = []
    for k in range(rank):
        tk, rk = k // SUB, k % SUB
        root = lax.rsqrt(a[k][tk][rk : rk + 1, :])
        scales.append(root)
        reciprocal = root * root
        column = {t: a[k][t] * reciprocal for t in range(tk, tiles)}
        column[tk] = jnp.where(row > rk, column[tk], 0.0)
        for j in range(k + 1, rank):
            factor = a[k][j // SUB][j % SUB : j % SUB + 1, :]
            for t in range(j // SUB, tiles):
                a[j][t] = a[j][t] - column[t] * factor
        for c in range(k):
            factor = m[c][tk][rk : rk + 1, :]
            for t in range(tk, tiles):
                m[c][t] = m[c][t] - column[t] * factor
        fresh = {t: -column[t] for t in range(tk, tiles)}
        fresh[tk] = jnp.where(row == rk, 1.0, fresh[tk])
        m.append(fresh)
        if left is not None:
            for t in range(tiles):
                if t < tk:
                    value = jnp.zeros((SUB, LANES), jnp.float32)
                else:
                    value = a[k][t] * root
                if t == tk:
                    value = jnp.where(row >= rk, value, 0.0)
                left[k, SUB * t : SUB * (t + 1), :] = value
    for t in range(tiles):
        scale = jnp.concatenate(scales[SUB * t : SUB * (t + 1)], axis=0)
        for c in range(rank):
            value = m[c][t] * scale if t >= c // SUB else jnp.zeros((SUB, LANES), jnp.float32)
            inverse[c * rank + SUB * t : c * rank + SUB * (t + 1), :] = value
    return shift, share


def inverse_row(inverse, r, t, rank):
    return inverse[pl.ds(SUB * t * rank + r, SUB, stride=rank), :]


def pair_up(value, level):
    return value + pltpu.roll(value, LANES - lax.shift_left(1, level), 1)


def level_fast(level, levels, current, left, inverse, squared, ratio, child, lowest, rank, child_at):
    tiles = rank // SUB
    row = lax.broadcasted_iota(jnp.int32, (SUB, LANES), 0)
    shift, share = eliminate(current, left, inverse, level, rank)
    lowest[...] = jnp.minimum(lowest[...], share)

    for block in range(tiles):
        sums = [[None] * tiles for _ in range(SUB)]
        for r in range(SUB * block, rank):
            parts = [inverse_row(inverse, r, t, rank) for t in range(block, r // SUB + 1)]
            for q in range(SUB):
                if SUB * block + q > r:
                    continue
                factor = parts[0][q : q + 1, :]
                for t in range(block, r // SUB + 1):
                    term = parts[t - block] * factor
                    sums[q][t] = term if sums[q][t] is None else sums[q][t] + term
        for q in range(SUB):
            at = (SUB * block + q) * rank
            for t in range(block, tiles):
                squared[at + SUB * t : at + SUB * (t + 1), :] = sums[q][t]

    if child is not None:
        @pl.when(child_at(level))
        def _():
            for r in range(rank):
                for t in range(tiles):
                    value = left[r, SUB * t : SUB * (t + 1), :]
                    if t <= r // SUB:
                        value = value - shift * inverse_row(inverse, r, t, rank)
                    child[r, SUB * t : SUB * (t + 1), :] = value

    for q in range(rank):
        for t in range(tiles):
            if t >= q // SUB:
                value = squared[q * rank + SUB * t : q * rank + SUB * (t + 1), :]
            else:
                value = squared[pl.ds(SUB * t * rank + q, SUB, stride=rank), :]
            value = -shift * value
            if t == q // SUB:
                value = value + jnp.where(row == q % SUB, 1.0, 0.0)
            if ratio is not None:
                ratio[level, q, SUB * t : SUB * (t + 1), :] = value
            here = current[q, SUB * t : SUB * (t + 1), :] - shift * value
            current[q, SUB * t : SUB * (t + 1), :] = pair_up(here, level)


def level_plain(level, levels, current, left, inverse, squared, ratio, child, lowest, rank, child_at):
    tiles = rank // SUB
    eliminate(current, left, inverse, level, rank)

    def products(out, count, left_of, right_of):
        def block_step(block, carry):
            offset = pl.multiple_of(block * SUB, SUB)
            sums = [[None] * tiles for _ in range(SUB)]
            for r in range(count):
                parts = [left_of(r, t) for t in range(tiles)]
                heads = right_of(r, offset)
                for q in range(SUB):
                    for t in range(tiles):
                        term = parts[t] * heads[q : q + 1, :]
                        sums[q][t] = term if sums[q][t] is None else sums[q][t] + term
            for q in range(SUB):
                for t in range(tiles):
                    out(offset + q, t, sums[q][t])
            return carry

        lax.fori_loop(0, tiles, block_step, 0)

    def tile(t):
        return slice(SUB * t, SUB * (t + 1))

    def put_child(r, t, value):
        squared[pl.ds(pl.multiple_of(r * rank + SUB * t, SUB), SUB), :] = value

    products(
        put_child, rank,
        lambda k, t: current[k, tile(t), :],
        lambda k, offset: inverse[pl.ds(pl.multiple_of(k * rank + offset, SUB), SUB), :],
    )
    if child is not None:
        @pl.when(child_at(level))
        def _():
            for r in range(rank):
                for t in range(tiles):
                    child[r, tile(t), :] = squared[r * rank + SUB * t : r * rank + SUB * (t + 1), :]

    def child_part(r, t):
        return squared[r * rank + SUB * t : r * rank + SUB * (t + 1), :]

    def put_current(q, t, value):
        current[q, tile(t), :] = pair_up(value, level)

    if ratio is not None:
        def put_ratio(c, t, value):
            ratio[level, c, tile(t), :] = value

        def inverse_head(r, offset):
            return inverse[pl.ds(offset * rank + r, SUB, stride=rank), :]

        products(put_ratio, rank, child_part, inverse_head)
    products(
        put_current, rank, child_part,
        lambda r, offset: squared[pl.ds(pl.multiple_of(r * rank + offset, SUB), SUB), :],
    )


def run_levels(source, levels, nodes, current, left, inverse, squared, ratio, child, lowest, rank, child_at, finish):
    lowest[...] = jnp.full((1, LANES), 1.0, jnp.float32)

    def sweep(level_step):
        to_lanes(source, current, rank)

        def body(level, carry):
            level_step(level, levels, current, left, inverse, squared, ratio, child, lowest, rank, child_at)
            finish(level)
            return carry

        lax.fori_loop(0, levels, body, 0)

    sweep(level_fast)
    lane = lax.broadcasted_iota(jnp.int32, (1, LANES), 1)
    least = jnp.min(jnp.where(lane < nodes, lowest[...], 1.0))

    @pl.when(least < 2e-06)
    def _():
        sweep(level_plain)


def branch_body(gram_ref, inverse_ref, ratio_ref, top_ref, child_ref, current, left, inverse, squared, child, lowest, *, rank, levels):
    nodes = gram_ref.shape[0] // rank

    def finish(level):
        @pl.when(level == 0)
        def _():
            for c in range(rank):
                inverse_ref[c] = inverse[c * rank : (c + 1) * rank, :]

        @pl.when(level == levels - 1)
        def _():
            for r in range(rank):
                child_ref[r : r + 1, :] = child[r].T[0:1, :]
                top_ref[r : r + 1, :] = jnp.concatenate(
                    [inverse_row(inverse, r, t, rank) for t in range(rank // SUB)], axis=0
                ).T[0:1, :]

    run_levels(
        gram_ref, levels, nodes, current, left, inverse, squared, ratio_ref, child, lowest, rank,
        lambda level: level == levels - 1, finish,
    )


vmem_spec = pl.BlockSpec(memory_space=pltpu.VMEM)


def tree_scratch(rank):
    return [
        pltpu.VMEM((rank, rank, LANES), jnp.float32),
        pltpu.VMEM((rank, rank, LANES), jnp.float32),
        pltpu.VMEM((rank * rank, LANES), jnp.float32),
        pltpu.VMEM((rank * rank, LANES), jnp.float32),
        pltpu.VMEM((rank, rank, LANES), jnp.float32),
        pltpu.VMEM((1, LANES), jnp.float32),
    ]


def branch_factors(gram, levels):
    leaves, rank, unused = gram.shape
    return pl.pallas_call(
        functools.partial(branch_body, rank=rank, levels=levels),
        in_specs=[vmem_spec],
        out_specs=[vmem_spec] * 4,
        out_shape=[
            jax.ShapeDtypeStruct((rank, rank, LANES), jnp.float32),
            jax.ShapeDtypeStruct((levels, rank, rank, LANES), jnp.float32),
            jax.ShapeDtypeStruct((rank, rank), jnp.float32),
            jax.ShapeDtypeStruct((rank, rank), jnp.float32),
        ],
        scratch_shapes=tree_scratch(rank),
        compiler_params=pltpu.CompilerParams(vmem_limit_bytes=vmem_bytes),
        name="branch_factors",
        cost_estimate=pl.CostEstimate(flops=10**10, bytes_accessed=10**7, transcendentals=0),
    )(gram.reshape(leaves * rank, rank))


def basis_body(inverse_ref, ratio_ref, top_ref, sketched_ref, weights_ref, basis_ref, natural, *, rank, levels):
    leaves = sketched_ref.shape[0]
    upper = [top_ref[...]]
    for level in range(levels - 2, -1, -1):
        stride = 2**level
        for c in range(rank):
            from_lanes(ratio_ref[level, c], natural, c, leaves, rank)
        fresh = []
        for node in range(leaves // stride):
            block = natural[node * stride * rank : (node * stride + 1) * rank, :]
            fresh.append(dot_exact(upper[node // 2], block))
        upper = fresh
    for r in range(rank):
        from_lanes(inverse_ref[r], natural, r, leaves, rank)
    for pair in range(leaves // 2):
        results = []
        for leaf in (2 * pair, 2 * pair + 1):
            block = sketched_ref[leaf]
            own = lax.dot_general(
                natural[leaf * rank : (leaf + 1) * rank, :], block, tn_dims,
                precision=highest, preferred_element_type=jnp.float32,
            )
            results.append(jnp.concatenate([dot_exact(upper[leaf], block), own], axis=0))
        both = jnp.concatenate(results, axis=1)
        weights_ref[:, pair * 2 * LEAF : (pair + 1) * 2 * LEAF] = both[:rank]
        basis_ref[:, pair * 2 * LEAF : (pair + 1) * 2 * LEAF] = both[rank:]


def bases(inverse, ratio, top, sketched):
    leaves, rank, unused = sketched.shape
    levels = ratio.shape[0]
    shape = jax.ShapeDtypeStruct((rank, leaves * LEAF), jnp.float32)
    return pl.pallas_call(
        functools.partial(basis_body, rank=rank, levels=levels),
        in_specs=[vmem_spec] * 4,
        out_specs=[vmem_spec] * 2,
        out_shape=[shape, shape],
        scratch_shapes=[pltpu.VMEM((leaves * rank, rank), jnp.float32)],
        compiler_params=pltpu.CompilerParams(vmem_limit_bytes=vmem_bytes),
        name="bases",
        cost_estimate=pl.CostEstimate(flops=5 * 10**9, bytes_accessed=10**7, transcendentals=0),
    )(inverse, ratio, top, sketched)


def top_body(children_ref, transfer_ref, paths_ref, source, current, left, inverse, squared, child, lowest, nat_inverse, nat_child, *, rank, levels):
    nodes = children_ref.shape[0] // 2
    for node in range(nodes):
        both = children_ref[2 * node : 2 * node + 2].reshape(2 * rank, rank)
        source[node * rank : (node + 1) * rank, :] = lax.dot_general(
            both, both, tn_dims, precision=highest, preferred_element_type=jnp.float32
        )

    def finish(level):
        for r in range(rank):
            from_lanes(child[r], nat_child.at[level], r, nodes, rank)
            from_lanes(inverse[r * rank : (r + 1) * rank, :], nat_inverse.at[level], r, nodes, rank)

    run_levels(
        source, levels, nodes, current, left, inverse, squared, None, child, lowest, rank,
        lambda level: level >= 0, finish,
    )
    offset = 0
    for level in range(levels):
        for node in range(nodes >> level):
            if level == 0:
                stacked = children_ref[2 * node : 2 * node + 2].reshape(2 * rank, rank)
            else:
                first = 2 * node << level - 1
                second = 2 * node + 1 << level - 1
                stacked = jnp.concatenate(
                    [
                        nat_child[level - 1, first * rank : (first + 1) * rank, :],
                        nat_child[level - 1, second * rank : (second + 1) * rank, :],
                    ],
                    axis=0,
                )
            at = (node << level) * rank
            transfer_ref[offset + node] = dot_exact(stacked, nat_inverse[level, at : at + rank, :])
        offset += nodes >> level
    above = [None]
    for level in range(levels - 1, -1, -1):
        offset -= nodes >> level
        fresh = []
        for node in range(nodes >> level):
            both = transfer_ref[offset + node]
            if above[0] is not None:
                both = dot_exact(both, above[node])
            fresh += [both[:rank], both[rank:]]
        above = fresh
    for branch in range(2 * nodes):
        paths_ref[branch * rank : (branch + 1) * rank, :] = above[branch]


def top_factors(children):
    branches, rank, unused = children.shape
    levels = branches.bit_length() - 1
    nodes = branches // 2
    natural = pltpu.VMEM((levels, nodes * rank, rank), jnp.float32)
    return pl.pallas_call(
        functools.partial(top_body, rank=rank, levels=levels),
        in_specs=[vmem_spec],
        out_specs=[vmem_spec] * 2,
        out_shape=[
            jax.ShapeDtypeStruct((branches - 1, 2 * rank, rank), jnp.float32),
            jax.ShapeDtypeStruct((branches * rank, rank), jnp.float32),
        ],
        scratch_shapes=[pltpu.VMEM((nodes * rank, rank), jnp.float32)]
        + tree_scratch(rank)
        + [natural, natural],
        compiler_params=pltpu.CompilerParams(vmem_limit_bytes=vmem_bytes),
        name="top_factors",
        cost_estimate=pl.CostEstimate(flops=10**10, bytes_accessed=10**7, transcendentals=0),
    )(children)


def exchange_sum(pieces, axis):
    count = pieces.shape[0]
    me = lax.axis_index(axis)
    mine = lax.dynamic_index_in_dim(pieces, me, 0, keepdims=False)
    for step in range(1, count):
        outgoing = lax.dynamic_index_in_dim(pieces, (me + step) % count, 0, keepdims=False)
        mine = mine + lax.ppermute(
            outgoing, axis, [(i, (i + step) % count) for i in range(count)]
        )
    return mine


def exchange_all(piece, axis):
    count = lax.axis_size(axis)
    me = lax.axis_index(axis)
    if count == 2:
        other = lax.ppermute(piece, axis, [(0, 1), (1, 0)])
        return jnp.stack([jnp.where(me == 0, piece, other), jnp.where(me == 0, other, piece)])
    result = jnp.zeros((count,) + piece.shape, piece.dtype)
    result = lax.dynamic_update_index_in_dim(result, piece, me, 0)
    for step in range(1, count):
        arrived = lax.ppermute(piece, axis, [(i, (i + step) % count) for i in range(count)])
        result = lax.dynamic_update_index_in_dim(result, arrived, (me - step) % count, 0)
    return result


def group_tables(far_slots, far_count):
    leaves = far_slots.shape[0]
    groups = leaves * FAR // GROUP
    per_leaf = (far_count + GROUP - 1) // GROUP
    before = jnp.arange(leaves)[:, None] >= jnp.arange(leaves)[None, :]
    ends = jnp.sum(jnp.where(before, per_leaf[None, :], 0), axis=1)
    total = ends[leaves - 1 :]
    ids = jnp.arange(groups, dtype=jnp.int32)
    leaf = jnp.minimum(jnp.sum((ends[None, :] <= ids[:, None]).astype(jnp.int32), axis=1), leaves - 1)
    hit = leaf[:, None] == jnp.arange(leaves)[None, :]
    start = jnp.sum(jnp.where(hit, (ends - per_leaf)[None, :], 0), axis=1)
    length = jnp.sum(jnp.where(hit, far_count[None, :], 0), axis=1)
    sub = ids - start
    count = jnp.where(ids < total, jnp.clip(length - GROUP * sub, 0, GROUP), 0)
    first = jnp.minimum(sub, FAR // GROUP - 1)
    slots = far_slots.reshape(leaves * FAR // GROUP, GROUP)[leaf * (FAR // GROUP) + first]
    return (
        total.astype(jnp.int32),
        leaf.astype(jnp.int32),
        count.astype(jnp.int32),
        slots.reshape(-1).astype(jnp.int32),
    )


def pack_body(picked_ref, z_ref, c_ref, out_ref, *, cap):
    z_rows = z_ref.shape[1]

    def one(branch, carry):
        for entry in range(cap):
            leaf = picked_ref[branch * cap + entry]
            out_ref[branch, z_rows * entry : z_rows * (entry + 1), :] = z_ref[leaf]
            at = z_rows * cap + 2 * entry
            out_ref[branch, at : at + 2, :] = c_ref[leaf]
        return carry

    lax.fori_loop(0, out_ref.shape[0], one, 0, unroll=2)


def packed_rows(picked, z_rows, c_rows, branches, cap):
    return pl.pallas_call(
        functools.partial(pack_body, cap=cap),
        in_specs=[pl.BlockSpec(memory_space=pltpu.SMEM), vmem_spec, vmem_spec],
        out_specs=vmem_spec,
        out_shape=jax.ShapeDtypeStruct((branches, cap * (z_rows.shape[1] + 2), LANES), jnp.float32),
        compiler_params=pltpu.CompilerParams(vmem_limit_bytes=vmem_bytes),
        name="packed_rows",
    )(picked, z_rows, c_rows)


def two_rows(values, rows):
    leaves = values.shape[1]
    split = jnp.transpose(values.reshape(2, rows, leaves, LEAF), (2, 1, 0, 3))
    return split.reshape(leaves, rows, 2 * LEAF)


def on_device(points, samples, sketch, far_requests, far_slots, far_count, near_mask):
    samp_dev = samples.shape[0]
    leaves = samples.shape[1] // LEAF
    rank = sketch.shape[0]
    branches = lax.axis_size("leaf")
    columns = lax.axis_size("cols")
    cap = far_requests.shape[2]
    slots = branches * cap
    share = rank // columns
    me = lax.axis_index("leaf")
    column = lax.axis_index("cols")

    wanted = far_requests.reshape(branches, cap)
    asked_for = lax.all_to_all(wanted, "leaf", split_axis=0, concat_axis=0, tiled=True)

    coords = jnp.transpose(points.reshape(3, leaves, LEAF), (1, 0, 2))
    targets = jnp.transpose(coords, (0, 2, 1))
    rows = jnp.transpose(samples.reshape(samp_dev, leaves, LEAF), (1, 2, 0))
    tables = group_tables(far_slots, far_count)

    z_part = jnp.dot(sketch, samples, precision=highest)
    z_mine = exchange_sum(z_part.reshape(columns, share, leaves * LEAF), "cols")
    z_rows = two_rows(z_mine.reshape(share, leaves, LEAF), share // 2)
    planes = points.reshape(3, leaves, LEAF)
    c_rows = two_rows(
        jnp.concatenate([planes[0:1], planes[2:3], planes[1:2], jnp.zeros_like(planes[0:1])], axis=0), 2
    )
    asked_for, rows, z_rows, c_rows = lax.optimization_barrier((asked_for, rows, z_rows, c_rows))
    picked = asked_for.reshape(-1)
    small_sent = packed_rows(picked, z_rows, c_rows, branches, cap)
    small_got = lax.all_to_all(small_sent, "leaf", split_axis=0, concat_axis=0, tiled=True)
    total, group_leaf, group_count, group_slots = group_tables(far_slots, far_count)

    forward = [(i, i + 1) for i in range(branches - 1)]
    backward = [(target, source) for source, target in forward]
    edges = jnp.concatenate([rows[:1], rows[leaves - 1 :]], axis=0)
    edge_coords = jnp.concatenate([coords[:1], coords[leaves - 1 :]], axis=0)
    width = max(samp_dev, LEAF)
    edges = jnp.concatenate(
        [
            jnp.pad(edges, ((0, 0), (0, 0), (0, width - samp_dev))),
            jnp.pad(edge_coords, ((0, 0), (0, 5), (0, width - LEAF))),
        ],
        axis=1,
    )
    edges, unused = lax.optimization_barrier((edges, small_sent))
    low_edge = lax.ppermute(edges[1], "leaf", forward)
    high_edge = lax.ppermute(edges[0], "leaf", backward)

    rows_sent = rows[picked].reshape(branches, cap, LEAF, samp_dev)
    rows_sent, low_edge, high_edge = lax.optimization_barrier((rows_sent, low_edge, high_edge))
    rows_got = lax.all_to_all(rows_sent, "leaf", split_axis=0, concat_axis=0, tiled=True)
    fetched = rows_got.reshape(slots, LEAF, samp_dev)

    z_own = small_got[:, : cap * share // 2].reshape(slots * share // 2, LANES)
    c_got = small_got[:, cap * share // 2 :].reshape(slots * 2, LANES)
    if columns == 2:
        z_other = lax.ppermute(z_own, "cols", [(0, 1), (1, 0)])
        place = column.astype(jnp.int32).reshape(1)
    else:
        z_all = exchange_all(z_own, "cols").reshape(columns, slots, share // 2, 2, LEAF)
        z_all = jnp.transpose(z_all, (1, 0, 3, 2, 4)).reshape(slots, 2, 2, rank // 4, LEAF)
        z_all = jnp.transpose(z_all, (1, 0, 3, 2, 4)).reshape(2, slots * rank // 4, LANES)
        z_own, z_other = z_all[0], z_all[1]
        place = jnp.zeros((1,), jnp.int32)

    high, low, sketched, gram = kernel_blocks(
        total, group_leaf, group_count, group_slots, place, z_own, z_other, c_got, targets, rank
    )

    levels = leaves.bit_length()
    inverse, ratio, top_inverse, own_child = branch_factors(gram, levels)
    weights, leaf_basis = bases(inverse, ratio, top_inverse, sketched)
    mine = jnp.arange(branches)[:, None, None] == me
    children = lax.psum(jnp.where(mine, own_child[None], 0.0), "leaf")

    rows_low, rows_high = low_edge[:LEAF, :samp_dev], high_edge[:LEAF, :samp_dev]
    coords_low, coords_high = low_edge[LEAF : LEAF + 3, :LEAF], high_edge[LEAF : LEAF + 3, :LEAF]
    near_rows = jnp.concatenate(
        [rows_low[None], rows, rows_high[None], jnp.zeros_like(rows_low)[None]], axis=0
    )
    near_coords = jnp.concatenate(
        [coords_low[None], coords, coords_high[None], jnp.zeros_like(coords_low)[None]], axis=0
    )
    near_coords = jnp.pad(near_coords, ((0, 0), (0, 5), (0, 0)))
    near_coords = jnp.concatenate([near_coords, near_coords], axis=2)
    near_sample = near_products(near_mask.reshape(-1), near_rows, near_coords, targets)

    far_sample, branch_samples, copies = far_products(
        total, group_leaf, group_slots, fetched, high, low, weights, branches
    )
    everyone = lax.all_to_all(copies, "leaf", split_axis=0, concat_axis=0, tiled=True)
    children, unused = lax.optimization_barrier((children, branch_samples))
    top_transfer, paths = top_factors(children)
    root_sample = lax.dot_general(
        paths, everyone.reshape(branches * rank, samp_dev), tn_dims, precision=highest
    )
    return (far_sample, near_sample, leaf_basis, branch_samples, top_transfer, root_sample)


def solution(mesh):
    return jax.shard_map(
        on_device,
        mesh=mesh,
        in_specs=(
            P(None, "leaf"),
            P("cols", "leaf"),
            P(None, "cols"),
            P("leaf", None, None),
            P("leaf", None),
            P("leaf"),
            P("leaf", None),
        ),
        out_specs=(
            P("cols", "leaf"),
            P("cols", "leaf"),
            P(None, "leaf"),
            P("leaf", "cols"),
            P(),
            P(None, "cols"),
        ),
        check_vma=False,
    )
```

```python
import functools
import math

import jax
import jax.numpy as jnp
import numpy as np
from jax import lax
from jax.experimental import pallas as pl
from jax.experimental.pallas import tpu as pltpu
from jax.sharding import PartitionSpec as P

LEAF = 64
FAR = 16
GROUP = 4
BATCH = 16
LANES = 128
SUB = 8

length_scale = 0.3
shift_share = 0.05
highest = lax.Precision.HIGHEST
exponent_scale = -math.log2(math.e) / length_scale
vmem_bytes = 56 * 1024 * 1024

nt_dims = (((1,), (1,)), ((), ()))
tn_dims = (((0,), (0,)), ((), ()))


def halves(value):
    high = value.astype(jnp.bfloat16)
    low = (value - high.astype(jnp.float32)).astype(jnp.bfloat16)
    return high, low


def dot(a, b):
    return jnp.dot(a, b, preferred_element_type=jnp.float32)


def dot_exact(a, b):
    return jnp.dot(a, b, precision=highest, preferred_element_type=jnp.float32)


def dot_exact_nt(a, b):
    return lax.dot_general(a, b, nt_dims, precision=highest, preferred_element_type=jnp.float32)


def dot_nt(a, b):
    return lax.dot_general(a, b, nt_dims, preferred_element_type=jnp.float32)


def kernel_half(source_rows, target, lane, valid):
    total = None
    for axis in range(3):
        difference = source_rows[axis : axis + 1, :] - target[:, axis : axis + 1]
        square = difference * difference
        total = square if total is None else total + square
    distance = total * lax.rsqrt(jnp.maximum(total, 1e-30))
    values = jnp.exp2(distance * exponent_scale)
    return jnp.where(lane < valid, values, 0.0)


def blocks_body(
    total_ref, leaf_ref, count_ref, slot_ref, place_ref,
    own_ref, other_ref, coords_ref, target_ref,
    high_ref, low_ref, sketched_ref, gram_ref,
    packed,
    *, rank, cap,
):
    step = pl.program_id(0)
    lane = lax.broadcasted_iota(jnp.int32, (1, LANES), 1)
    first = lane < LEAF

    @pl.when(step == 0)
    def _():
        sketched_ref[...] = jnp.zeros_like(sketched_ref)
        quarter = rank // 4
        slots = packed.shape[0]
        own_at = pl.multiple_of(place_ref[0] * 2 * quarter, quarter)
        other_at = pl.multiple_of((1 - place_ref[0]) * 2 * quarter, quarter)

        def unpack(peer, carry):
            for entry in range(2 * cap):
                slot = (entry // cap) * (slots // 2) + peer * cap + entry % cap
                at = pl.multiple_of((peer * 2 * cap + entry) * quarter, quarter)
                for ref, base in ((own_ref, own_at), (other_ref, other_at)):
                    value = ref[pl.ds(at, quarter), :]
                    turned = pltpu.roll(value, LEAF, 1)
                    packed[slot, pl.ds(base, quarter), :] = jnp.where(first, value, turned)
                    packed[slot, pl.ds(base + quarter, quarter), :] = jnp.where(first, turned, value)
                value = coords_ref[pl.ds((peer * 2 * cap + entry) * 2, 2), :]
                turned = pltpu.roll(value, LEAF, 1)
                packed[slot, rank : rank + 1, :] = jnp.where(first, value, turned)[0:1]
                packed[slot, rank + 1 : rank + 2, :] = jnp.where(first, turned, value)[0:1]
                packed[slot, rank + 2 : rank + 3, :] = jnp.where(first, value, turned)[1:2]
            return carry

        lax.fori_loop(0, slots // (2 * cap), unpack, 0)

    @pl.when(step * BATCH < total_ref[0])
    def _():
        for member in range(BATCH):
            group = step * BATCH + member
            leaf = leaf_ref[group]
            count = count_ref[group]
            slots = [slot_ref[group * GROUP + e] for e in range(GROUP)]
            target = target_ref[leaf]
            z_parts = []
            for half in range(GROUP // 2):
                left = packed[slots[2 * half]]
                right = packed[slots[2 * half + 1]]
                both = jnp.where(first, left, right)
                values = kernel_half(both[rank : rank + 3], target, lane, (count - 2 * half) * LEAF)
                high, low = halves(values)
                high_ref[member, :, half * LANES : (half + 1) * LANES] = high
                low_ref[member, :, half * LANES : (half + 1) * LANES] = low
                z_parts.append(both[:rank])
            z_high, z_low = halves(jnp.concatenate(z_parts, axis=1))
            k_high = high_ref[member]
            k_low = low_ref[member]
            update = dot_nt(z_high, k_high) + (dot_nt(z_low, k_high) + dot_nt(z_high, k_low))
            sketched_ref[leaf] += update

    @pl.when(step == pl.num_programs(0) - 1)
    def _():
        for leaf in range(gram_ref.shape[0]):
            block = sketched_ref[leaf]
            gram_ref[leaf] = dot_exact_nt(block, block)


def kernel_blocks(total, group_leaf, group_count, group_slots, place, own, other, coords, targets, rank, cap):
    leaves = targets.shape[0]
    groups = group_leaf.shape[0]
    slots = coords.shape[0] // 2
    steps = groups // BATCH

    def block_index(step, total_ref, *unused):
        last = (total_ref[0] - 1) // BATCH
        return (jnp.minimum(step, last), 0, 0)

    flat = lambda *unused: (0, 0)
    whole = lambda *unused: (0, 0, 0)
    once = pl.Buffered(1)
    return pl.pallas_call(
        functools.partial(blocks_body, rank=rank, cap=cap),
        grid_spec=pltpu.PrefetchScalarGridSpec(
            num_scalar_prefetch=5,
            grid=(steps,),
            in_specs=[
                pl.BlockSpec(own.shape, flat, pipeline_mode=once),
                pl.BlockSpec(other.shape, flat, pipeline_mode=once),
                pl.BlockSpec(coords.shape, flat, pipeline_mode=once),
                pl.BlockSpec(targets.shape, whole, pipeline_mode=once),
            ],
            out_specs=[
                pl.BlockSpec((BATCH, LEAF, GROUP * LEAF), block_index),
                pl.BlockSpec((BATCH, LEAF, GROUP * LEAF), block_index),
                pl.BlockSpec((leaves, rank, LEAF), whole),
                pl.BlockSpec((leaves, rank, rank), whole),
            ],
            scratch_shapes=[pltpu.VMEM((slots, rank + SUB, LANES), jnp.float32)],
        ),
        out_shape=[
            jax.ShapeDtypeStruct((groups, LEAF, GROUP * LEAF), jnp.bfloat16),
            jax.ShapeDtypeStruct((groups, LEAF, GROUP * LEAF), jnp.bfloat16),
            jax.ShapeDtypeStruct((leaves, rank, LEAF), jnp.float32),
            jax.ShapeDtypeStruct((leaves, rank, rank), jnp.float32),
        ],
        compiler_params=pltpu.CompilerParams(vmem_limit_bytes=vmem_bytes),
        name="kernel_blocks",
        cost_estimate=pl.CostEstimate(
            flops=2 * 10**10, bytes_accessed=2 * 10**7, transcendentals=0
        ),
    )(total, group_leaf, group_count, group_slots, place, own, other, coords, targets)


def far_body(
    total_ref, leaf_ref, slot_ref,
    own_ref, partner_ref, high_ref, low_ref, weights_ref,
    out_ref, projected_ref, copies_ref,
    s_high, s_low, acc,
):
    step = pl.program_id(0)
    samp_dev = own_ref.shape[2]
    part = own_ref.shape[0]

    @pl.when(step == 0)
    def _():
        acc[...] = jnp.zeros_like(acc)

        def split(slot, carry):
            s_high[slot], s_low[slot] = halves(own_ref[slot])
            s_high[part + slot], s_low[part + slot] = halves(partner_ref[slot])
            return carry

        lax.fori_loop(0, part, split, 0, unroll=4)

    @pl.when(step * BATCH < total_ref[0])
    def _():
        for member in range(BATCH):
            group = step * BATCH + member
            leaf = leaf_ref[group]
            slots = [slot_ref[group * GROUP + e] for e in range(GROUP)]
            rows_high = jnp.concatenate([s_high[slot] for slot in slots], axis=0)
            rows_low = jnp.concatenate([s_low[slot] for slot in slots], axis=0)
            k_high = high_ref[member]
            k_low = low_ref[member]
            acc[leaf] += dot(k_high, rows_high) + (dot(k_high, rows_low) + dot(k_low, rows_high))

    @pl.when(step == pl.num_programs(0) - 1)
    def _():
        leaves = acc.shape[0]
        rows = acc[...].reshape(leaves * LEAF, samp_dev)
        projected = dot_exact(weights_ref[...], rows)
        projected_ref[...] = projected
        for branch in range(copies_ref.shape[0]):
            copies_ref[branch] = projected
        for pair in range(leaves // 2):
            block = acc[2 * pair : 2 * pair + 2].reshape(2 * LEAF, samp_dev)
            out_ref[:, 2 * pair * LEAF : 2 * (pair + 1) * LEAF] = block.T


def far_products(total, group_leaf, group_slots, own, partner, high, low, weights, branches):
    part, unused, samp_dev = own.shape
    slots = 2 * part
    groups = group_leaf.shape[0]
    points_dev = weights.shape[1]
    leaves = points_dev // LEAF
    steps = groups // BATCH

    def block_index(step, total_ref, *unused):
        last = (total_ref[0] - 1) // BATCH
        return (jnp.minimum(step, last), 0, 0)

    return pl.pallas_call(
        far_body,
        grid_spec=pltpu.PrefetchScalarGridSpec(
            num_scalar_prefetch=3,
            grid=(steps,),
            in_specs=[
                pl.BlockSpec(own.shape, lambda *unused: (0, 0, 0), pipeline_mode=pl.Buffered(1)),
                pl.BlockSpec(partner.shape, lambda *unused: (0, 0, 0), pipeline_mode=pl.Buffered(1)),
                pl.BlockSpec((BATCH, LEAF, GROUP * LEAF), block_index),
                pl.BlockSpec((BATCH, LEAF, GROUP * LEAF), block_index),
                pl.BlockSpec(weights.shape, lambda *unused: (0, 0), pipeline_mode=pl.Buffered(1)),
            ],
            out_specs=[
                pl.BlockSpec((samp_dev, points_dev), lambda *unused: (0, 0)),
                pl.BlockSpec((weights.shape[0], samp_dev), lambda *unused: (0, 0)),
                pl.BlockSpec((branches, weights.shape[0], samp_dev), lambda *unused: (0, 0, 0)),
            ],
            scratch_shapes=[
                pltpu.VMEM((slots, LEAF, samp_dev), jnp.bfloat16),
                pltpu.VMEM((slots, LEAF, samp_dev), jnp.bfloat16),
                pltpu.VMEM((leaves, LEAF, samp_dev), jnp.float32),
            ],
        ),
        out_shape=[
            jax.ShapeDtypeStruct((samp_dev, points_dev), jnp.float32),
            jax.ShapeDtypeStruct((weights.shape[0], samp_dev), jnp.float32),
            jax.ShapeDtypeStruct((branches, weights.shape[0], samp_dev), jnp.float32),
        ],
        compiler_params=pltpu.CompilerParams(vmem_limit_bytes=vmem_bytes),
        name="far_products",
        cost_estimate=pl.CostEstimate(
            flops=10**10, bytes_accessed=2 * 10**7, transcendentals=0
        ),
    )(total, group_leaf, group_slots, own, partner, high, low, weights)


NEAR_LEAVES = 8


def near_body(mask_ref, rows_ref, coords_ref, target_ref, out_ref):
    step = pl.program_id(0)
    samp_dev = rows_ref.shape[2]
    lane = lax.broadcasted_iota(jnp.int32, (1, LANES), 1)
    first = lane < LEAF
    for pair in range(NEAR_LEAVES // 2):
        results = []
        for member in range(2):
            leaf = step * NEAR_LEAVES + 2 * pair + member
            target = target_ref[leaf]
            k_high = []
            k_low = []
            for half in range(2):
                both = jnp.where(first, coords_ref[leaf + 2 * half], coords_ref[leaf + 2 * half + 1])
                values = kernel_half(both, target, lane, LANES)
                left = mask_ref[leaf * 3 + 2 * half].astype(jnp.float32)
                if half == 0:
                    right = mask_ref[leaf * 3 + 1].astype(jnp.float32)
                else:
                    right = jnp.float32(0.0)
                high, low = halves(values * jnp.where(first, left, right))
                k_high.append(high)
                k_low.append(low)
            k_high = jnp.concatenate(k_high, axis=1)
            k_low = jnp.concatenate(k_low, axis=1)
            rows = rows_ref[pl.ds(leaf, 4)].reshape(4 * LEAF, samp_dev)
            rows_high, rows_low = halves(rows)
            results.append(
                dot(k_high, rows_high) + (dot(k_high, rows_low) + dot(k_low, rows_high))
            )
        block = jnp.concatenate(results, axis=0)
        out_ref[:, 2 * pair * LEAF : 2 * (pair + 1) * LEAF] = block.T


def near_products(mask, rows, coords, targets):
    leaves = targets.shape[0]
    samp_dev = rows.shape[2]
    whole = lambda *unused: (0, 0, 0)
    return pl.pallas_call(
        near_body,
        grid_spec=pltpu.PrefetchScalarGridSpec(
            num_scalar_prefetch=1,
            grid=(leaves // NEAR_LEAVES,),
            in_specs=[
                pl.BlockSpec(rows.shape, whole),
                pl.BlockSpec(coords.shape, whole),
                pl.BlockSpec(targets.shape, whole),
            ],
            out_specs=pl.BlockSpec((samp_dev, NEAR_LEAVES * LEAF), lambda step, *unused: (0, step)),
        ),
        out_shape=jax.ShapeDtypeStruct((samp_dev, leaves * LEAF), jnp.float32),
        compiler_params=pltpu.CompilerParams(vmem_limit_bytes=vmem_bytes),
        name="near_products",
        cost_estimate=pl.CostEstimate(
            flops=4 * 10**9, bytes_accessed=10**7, transcendentals=0
        ),
    )(mask, rows, coords, targets)


def to_lanes(source, target, rank):
    nodes = source.shape[0] // rank
    target[...] = jnp.zeros_like(target)
    for r in range(rank):
        target[r, :, 0:nodes] = source[pl.ds(r, nodes, stride=rank), :].T


def from_lanes(columns, target, r, nodes, rank):
    target[pl.ds(r, nodes, stride=rank), :] = columns.T[0:nodes]


def eliminate(current, left, inverse, level, rank):
    tiles = rank // SUB
    row = lax.broadcasted_iota(jnp.int32, (SUB, LANES), 0)
    diagonal = [current[j, j : j + 1, :] for j in range(rank)]
    while len(diagonal) > 1:
        diagonal = [diagonal[i] + diagonal[i + 1] for i in range(0, len(diagonal), 2)]
    share = shift_share * diagonal[0] / rank
    shift = share + 1e-06
    a = [
        {t: current[j, SUB * t : SUB * (t + 1), :] for t in range(j // SUB, tiles)}
        for j in range(rank)
    ]
    for j in range(rank):
        a[j][j // SUB] = a[j][j // SUB] + jnp.where(row == j % SUB, shift, 0.0)
    m = []
    scales = []
    for k in range(rank):
        tk, rk = k // SUB, k % SUB
        root = lax.rsqrt(a[k][tk][rk : rk + 1, :])
        scales.append(root)
        reciprocal = root * root
        column = {t: a[k][t] * reciprocal for t in range(tk, tiles)}
        column[tk] = jnp.where(row > rk, column[tk], 0.0)
        for j in range(k + 1, rank):
            factor = a[k][j // SUB][j % SUB : j % SUB + 1, :]
            for t in range(j // SUB, tiles):
                a[j][t] = a[j][t] - column[t] * factor
        for c in range(k):
            factor = m[c][tk][rk : rk + 1, :]
            for t in range(tk, tiles):
                m[c][t] = m[c][t] - column[t] * factor
        fresh = {t: -column[t] for t in range(tk, tiles)}
        fresh[tk] = jnp.where(row == rk, 1.0, fresh[tk])
        m.append(fresh)
        if left is not None:
            for t in range(tiles):
                if t < tk:
                    value = jnp.zeros((SUB, LANES), jnp.float32)
                else:
                    value = a[k][t] * root
                if t == tk:
                    value = jnp.where(row >= rk, value, 0.0)
                left[k, SUB * t : SUB * (t + 1), :] = value
    for t in range(tiles):
        scale = jnp.concatenate(scales[SUB * t : SUB * (t + 1)], axis=0)
        for c in range(rank):
            value = m[c][t] * scale if t >= c // SUB else jnp.zeros((SUB, LANES), jnp.float32)
            inverse[c * rank + SUB * t : c * rank + SUB * (t + 1), :] = value
    return shift, share


def inverse_row(inverse, r, t, rank):
    return inverse[pl.ds(SUB * t * rank + r, SUB, stride=rank), :]


def pair_up(value, level):
    return value + pltpu.roll(value, LANES - lax.shift_left(1, level), 1)


def level_fast(level, levels, current, left, inverse, squared, ratio, child, lowest, rank, child_at):
    tiles = rank // SUB
    row = lax.broadcasted_iota(jnp.int32, (SUB, LANES), 0)
    shift, share = eliminate(current, left, inverse, level, rank)
    lowest[...] = jnp.minimum(lowest[...], share)

    for block in range(tiles):
        sums = [[None] * tiles for _ in range(SUB)]
        for r in range(SUB * block, rank):
            parts = [inverse_row(inverse, r, t, rank) for t in range(block, r // SUB + 1)]
            for q in range(SUB):
                if SUB * block + q > r:
                    continue
                factor = parts[0][q : q + 1, :]
                for t in range(block, r // SUB + 1):
                    term = parts[t - block] * factor
                    sums[q][t] = term if sums[q][t] is None else sums[q][t] + term
        for q in range(SUB):
            at = (SUB * block + q) * rank
            for t in range(block, tiles):
                squared[at + SUB * t : at + SUB * (t + 1), :] = sums[q][t]

    if child is not None:
        @pl.when(child_at(level))
        def _():
            for r in range(rank):
                for t in range(tiles):
                    value = left[r, SUB * t : SUB * (t + 1), :]
                    if t <= r // SUB:
                        value = value - shift * inverse_row(inverse, r, t, rank)
                    child[r, SUB * t : SUB * (t + 1), :] = value

    for q in range(rank):
        for t in range(tiles):
            if t >= q // SUB:
                value = squared[q * rank + SUB * t : q * rank + SUB * (t + 1), :]
            else:
                value = squared[pl.ds(SUB * t * rank + q, SUB, stride=rank), :]
            value = -shift * value
            if t == q // SUB:
                value = value + jnp.where(row == q % SUB, 1.0, 0.0)
            if ratio is not None:
                ratio[level, q, SUB * t : SUB * (t + 1), :] = value
            here = current[q, SUB * t : SUB * (t + 1), :] - shift * value
            current[q, SUB * t : SUB * (t + 1), :] = pair_up(here, level)


def level_plain(level, levels, current, left, inverse, squared, ratio, child, lowest, rank, child_at):
    tiles = rank // SUB
    eliminate(current, left, inverse, level, rank)

    def products(out, count, left_of, right_of):
        def block_step(block, carry):
            offset = pl.multiple_of(block * SUB, SUB)
            sums = [[None] * tiles for _ in range(SUB)]
            for r in range(count):
                parts = [left_of(r, t) for t in range(tiles)]
                heads = right_of(r, offset)
                for q in range(SUB):
                    for t in range(tiles):
                        term = parts[t] * heads[q : q + 1, :]
                        sums[q][t] = term if sums[q][t] is None else sums[q][t] + term
            for q in range(SUB):
                for t in range(tiles):
                    out(offset + q, t, sums[q][t])
            return carry

        lax.fori_loop(0, tiles, block_step, 0)

    def tile(t):
        return slice(SUB * t, SUB * (t + 1))

    def put_child(r, t, value):
        squared[pl.ds(pl.multiple_of(r * rank + SUB * t, SUB), SUB), :] = value

    products(
        put_child, rank,
        lambda k, t: current[k, tile(t), :],
        lambda k, offset: inverse[pl.ds(pl.multiple_of(k * rank + offset, SUB), SUB), :],
    )
    if child is not None:
        @pl.when(child_at(level))
        def _():
            for r in range(rank):
                for t in range(tiles):
                    child[r, tile(t), :] = squared[r * rank + SUB * t : r * rank + SUB * (t + 1), :]

    def child_part(r, t):
        return squared[r * rank + SUB * t : r * rank + SUB * (t + 1), :]

    def put_current(q, t, value):
        current[q, tile(t), :] = pair_up(value, level)

    if ratio is not None:
        def put_ratio(c, t, value):
            ratio[level, c, tile(t), :] = value

        def inverse_head(r, offset):
            return inverse[pl.ds(offset * rank + r, SUB, stride=rank), :]

        products(put_ratio, rank, child_part, inverse_head)
    products(
        put_current, rank, child_part,
        lambda r, offset: squared[pl.ds(pl.multiple_of(r * rank + offset, SUB), SUB), :],
    )


def run_levels(source, levels, nodes, current, left, inverse, squared, ratio, child, lowest, rank, child_at, finish):
    lowest[...] = jnp.full((1, LANES), 1.0, jnp.float32)

    def sweep(level_step):
        to_lanes(source, current, rank)

        def body(level, carry):
            level_step(level, levels, current, left, inverse, squared, ratio, child, lowest, rank, child_at)
            finish(level)
            return carry

        lax.fori_loop(0, levels, body, 0)

    sweep(level_fast)
    lane = lax.broadcasted_iota(jnp.int32, (1, LANES), 1)
    least = jnp.min(jnp.where(lane < nodes, lowest[...], 1.0))

    @pl.when(least < 2e-06)
    def _():
        sweep(level_plain)


def branch_body(gram_ref, inverse_ref, ratio_ref, top_ref, child_ref, current, left, inverse, squared, child, lowest, *, rank, levels):
    nodes = gram_ref.shape[0] // rank

    def finish(level):
        @pl.when(level == 0)
        def _():
            for c in range(rank):
                inverse_ref[c] = inverse[c * rank : (c + 1) * rank, :]

        @pl.when(level == levels - 1)
        def _():
            for r in range(rank):
                child_ref[r : r + 1, :] = child[r].T[0:1, :]
                top_ref[r : r + 1, :] = jnp.concatenate(
                    [inverse_row(inverse, r, t, rank) for t in range(rank // SUB)], axis=0
                ).T[0:1, :]

    run_levels(
        gram_ref, levels, nodes, current, left, inverse, squared, ratio_ref, child, lowest, rank,
        lambda level: level == levels - 1, finish,
    )


vmem_spec = pl.BlockSpec(memory_space=pltpu.VMEM)


def tree_scratch(rank):
    return [
        pltpu.VMEM((rank, rank, LANES), jnp.float32),
        pltpu.VMEM((rank, rank, LANES), jnp.float32),
        pltpu.VMEM((rank * rank, LANES), jnp.float32),
        pltpu.VMEM((rank * rank, LANES), jnp.float32),
        pltpu.VMEM((rank, rank, LANES), jnp.float32),
        pltpu.VMEM((1, LANES), jnp.float32),
    ]


def branch_factors(gram, levels):
    leaves, rank, unused = gram.shape
    return pl.pallas_call(
        functools.partial(branch_body, rank=rank, levels=levels),
        in_specs=[vmem_spec],
        out_specs=[vmem_spec] * 4,
        out_shape=[
            jax.ShapeDtypeStruct((rank, rank, LANES), jnp.float32),
            jax.ShapeDtypeStruct((levels, rank, rank, LANES), jnp.float32),
            jax.ShapeDtypeStruct((rank, rank), jnp.float32),
            jax.ShapeDtypeStruct((rank, rank), jnp.float32),
        ],
        scratch_shapes=tree_scratch(rank),
        compiler_params=pltpu.CompilerParams(vmem_limit_bytes=vmem_bytes),
        name="branch_factors",
        cost_estimate=pl.CostEstimate(flops=10**10, bytes_accessed=10**7, transcendentals=0),
    )(gram.reshape(leaves * rank, rank))


def basis_body(inverse_ref, ratio_ref, top_ref, sketched_ref, weights_ref, basis_ref, natural, *, rank, levels):
    leaves = sketched_ref.shape[0]
    upper = [top_ref[...]]
    for level in range(levels - 2, -1, -1):
        stride = 2**level
        for c in range(rank):
            from_lanes(ratio_ref[level, c], natural, c, leaves, rank)
        fresh = []
        for node in range(leaves // stride):
            block = natural[node * stride * rank : (node * stride + 1) * rank, :]
            fresh.append(dot_exact(upper[node // 2], block))
        upper = fresh
    for r in range(rank):
        from_lanes(inverse_ref[r], natural, r, leaves, rank)
    for pair in range(leaves // 2):
        results = []
        for leaf in (2 * pair, 2 * pair + 1):
            block = sketched_ref[leaf]
            own = lax.dot_general(
                natural[leaf * rank : (leaf + 1) * rank, :], block, tn_dims,
                precision=highest, preferred_element_type=jnp.float32,
            )
            results.append(jnp.concatenate([dot_exact(upper[leaf], block), own], axis=0))
        both = jnp.concatenate(results, axis=1)
        weights_ref[:, pair * 2 * LEAF : (pair + 1) * 2 * LEAF] = both[:rank]
        basis_ref[:, pair * 2 * LEAF : (pair + 1) * 2 * LEAF] = both[rank:]


def bases(inverse, ratio, top, sketched):
    leaves, rank, unused = sketched.shape
    levels = ratio.shape[0]
    shape = jax.ShapeDtypeStruct((rank, leaves * LEAF), jnp.float32)
    return pl.pallas_call(
        functools.partial(basis_body, rank=rank, levels=levels),
        in_specs=[vmem_spec] * 4,
        out_specs=[vmem_spec] * 2,
        out_shape=[shape, shape],
        scratch_shapes=[pltpu.VMEM((leaves * rank, rank), jnp.float32)],
        compiler_params=pltpu.CompilerParams(vmem_limit_bytes=vmem_bytes),
        name="bases",
        cost_estimate=pl.CostEstimate(flops=5 * 10**9, bytes_accessed=10**7, transcendentals=0),
    )(inverse, ratio, top, sketched)


def top_body(children_ref, transfer_ref, paths_ref, source, current, left, inverse, squared, child, lowest, nat_inverse, nat_child, *, rank, levels):
    nodes = children_ref.shape[0] // 2
    for node in range(nodes):
        both = children_ref[2 * node : 2 * node + 2].reshape(2 * rank, rank)
        source[node * rank : (node + 1) * rank, :] = lax.dot_general(
            both, both, tn_dims, precision=highest, preferred_element_type=jnp.float32
        )

    def finish(level):
        for r in range(rank):
            from_lanes(child[r], nat_child.at[level], r, nodes, rank)
            from_lanes(inverse[r * rank : (r + 1) * rank, :], nat_inverse.at[level], r, nodes, rank)

    run_levels(
        source, levels, nodes, current, left, inverse, squared, None, child, lowest, rank,
        lambda level: level >= 0, finish,
    )
    offset = 0
    for level in range(levels):
        for node in range(nodes >> level):
            if level == 0:
                stacked = children_ref[2 * node : 2 * node + 2].reshape(2 * rank, rank)
            else:
                first = 2 * node << level - 1
                second = 2 * node + 1 << level - 1
                stacked = jnp.concatenate(
                    [
                        nat_child[level - 1, first * rank : (first + 1) * rank, :],
                        nat_child[level - 1, second * rank : (second + 1) * rank, :],
                    ],
                    axis=0,
                )
            at = (node << level) * rank
            transfer_ref[offset + node] = dot_exact(stacked, nat_inverse[level, at : at + rank, :])
        offset += nodes >> level
    above = [None]
    for level in range(levels - 1, -1, -1):
        offset -= nodes >> level
        fresh = []
        for node in range(nodes >> level):
            both = transfer_ref[offset + node]
            if above[0] is not None:
                both = dot_exact(both, above[node])
            fresh += [both[:rank], both[rank:]]
        above = fresh
    for branch in range(2 * nodes):
        paths_ref[branch * rank : (branch + 1) * rank, :] = above[branch]


def top_factors(children):
    branches, rank, unused = children.shape
    levels = branches.bit_length() - 1
    nodes = branches // 2
    natural = pltpu.VMEM((levels, nodes * rank, rank), jnp.float32)
    return pl.pallas_call(
        functools.partial(top_body, rank=rank, levels=levels),
        in_specs=[vmem_spec],
        out_specs=[vmem_spec] * 2,
        out_shape=[
            jax.ShapeDtypeStruct((branches - 1, 2 * rank, rank), jnp.float32),
            jax.ShapeDtypeStruct((branches * rank, rank), jnp.float32),
        ],
        scratch_shapes=[pltpu.VMEM((nodes * rank, rank), jnp.float32)]
        + tree_scratch(rank)
        + [natural, natural],
        compiler_params=pltpu.CompilerParams(vmem_limit_bytes=vmem_bytes),
        name="top_factors",
        cost_estimate=pl.CostEstimate(flops=10**10, bytes_accessed=10**7, transcendentals=0),
    )(children)


def exchange_sum(pieces, axis):
    count = pieces.shape[0]
    me = lax.axis_index(axis)
    mine = lax.dynamic_index_in_dim(pieces, me, 0, keepdims=False)
    for step in range(1, count):
        outgoing = lax.dynamic_index_in_dim(pieces, (me + step) % count, 0, keepdims=False)
        mine = mine + lax.ppermute(
            outgoing, axis, [(i, (i + step) % count) for i in range(count)]
        )
    return mine


def exchange_all(piece, axis):
    count = lax.axis_size(axis)
    me = lax.axis_index(axis)
    if count == 2:
        other = lax.ppermute(piece, axis, [(0, 1), (1, 0)])
        return jnp.stack([jnp.where(me == 0, piece, other), jnp.where(me == 0, other, piece)])
    result = jnp.zeros((count,) + piece.shape, piece.dtype)
    result = lax.dynamic_update_index_in_dim(result, piece, me, 0)
    for step in range(1, count):
        arrived = lax.ppermute(piece, axis, [(i, (i + step) % count) for i in range(count)])
        result = lax.dynamic_update_index_in_dim(result, arrived, (me - step) % count, 0)
    return result


def group_tables(far_slots, far_count, side, part):
    leaves = far_slots.shape[0]
    far_slots = far_slots % part + jnp.where(far_slots // part == side, 0, part)
    groups = leaves * FAR // GROUP
    per_leaf = (far_count + GROUP - 1) // GROUP
    before = jnp.arange(leaves)[:, None] >= jnp.arange(leaves)[None, :]
    ends = jnp.sum(jnp.where(before, per_leaf[None, :], 0), axis=1)
    total = ends[leaves - 1 :]
    ids = jnp.arange(groups, dtype=jnp.int32)
    leaf = jnp.minimum(jnp.sum((ends[None, :] <= ids[:, None]).astype(jnp.int32), axis=1), leaves - 1)
    hit = leaf[:, None] == jnp.arange(leaves)[None, :]
    start = jnp.sum(jnp.where(hit, (ends - per_leaf)[None, :], 0), axis=1)
    length = jnp.sum(jnp.where(hit, far_count[None, :], 0), axis=1)
    sub = ids - start
    count = jnp.where(ids < total, jnp.clip(length - GROUP * sub, 0, GROUP), 0)
    first = jnp.minimum(sub, FAR // GROUP - 1)
    slots = far_slots.reshape(leaves * FAR // GROUP, GROUP)[leaf * (FAR // GROUP) + first]
    return (
        total.astype(jnp.int32),
        leaf.astype(jnp.int32),
        count.astype(jnp.int32),
        slots.reshape(-1).astype(jnp.int32),
    )


def sketch_body(place_ref, sketch_ref, samples_ref, points_ref, mine_ref, other_ref):
    product = dot_exact(sketch_ref[...], samples_ref[...])
    rank, points_dev = product.shape
    quarter = rank // 4
    first = lax.broadcasted_iota(jnp.int32, (1, LANES), 1) < LEAF
    swap = place_ref[0] == 1
    leaves = points_dev // LEAF

    def interleave(low, high):
        even = jnp.where(first, low, pltpu.roll(high, LEAF, 1))
        odd = jnp.where(first, pltpu.roll(low, LEAF, 1), high)
        return even, odd

    for pair in range(leaves // 2):
        lanes = slice(pair * LANES, (pair + 1) * LANES)
        shares = []
        for share in range(2):
            base = 2 * quarter * share
            shares.append(
                interleave(product[base : base + quarter, lanes], product[base + quarter : base + 2 * quarter, lanes])
            )
        for member in range(2):
            at = (2 * pair + member) * quarter
            mine_ref[at : at + quarter, :] = jnp.where(swap, shares[1][member], shares[0][member])
            other_ref[at : at + quarter, :] = jnp.where(swap, shares[0][member], shares[1][member])
        x = points_ref[0:1, lanes]
        y = points_ref[1:2, lanes]
        z = points_ref[2:3, lanes]
        xy = interleave(x, y)
        zs = interleave(z, jnp.zeros_like(z))
        for member in range(2):
            at = leaves * quarter + (2 * pair + member) * 2
            mine_ref[at : at + 1, :] = xy[member]
            mine_ref[at + 1 : at + 2, :] = zs[member]


def sketched_shares(place, sketch, samples, points):
    rank = sketch.shape[0]
    leaves = samples.shape[1] // LEAF
    return pl.pallas_call(
        sketch_body,
        in_specs=[pl.BlockSpec(memory_space=pltpu.SMEM)] + [vmem_spec] * 3,
        out_specs=[vmem_spec] * 2,
        out_shape=[
            jax.ShapeDtypeStruct((leaves * (rank // 4 + 2), LANES), jnp.float32),
            jax.ShapeDtypeStruct((leaves * rank // 4, LANES), jnp.float32),
        ],
        compiler_params=pltpu.CompilerParams(vmem_limit_bytes=vmem_bytes),
        name="sketched_shares",
    )(place, sketch, samples, points)


def pack_body(asked_ref, mine_ref, arrived_ref, partner_ref, crossed_ref, out_ref, *, cap, leaves):
    z_rows = arrived_ref.shape[0] // leaves

    def one(peer, carry):
        for entry in range(2 * cap):
            leaf = asked_ref[peer, entry]
            first_ref, second_ref = (mine_ref, arrived_ref) if entry < cap else (partner_ref, crossed_ref)
            at = pl.ds(leaf * z_rows, z_rows)
            out_ref[peer, z_rows * entry : z_rows * (entry + 1), :] = first_ref[at, :] + second_ref[at, :]
            base = z_rows * 2 * cap + 2 * entry
            out_ref[peer, base : base + 2, :] = first_ref[pl.ds(leaves * z_rows + leaf * 2, 2), :]
        return carry

    lax.fori_loop(0, out_ref.shape[0], one, 0)


def packed_rows(asked, mine, arrived, partner, crossed, cap, leaves):
    z_rows = arrived.shape[0] // leaves
    return pl.pallas_call(
        functools.partial(pack_body, cap=cap, leaves=leaves),
        in_specs=[pl.BlockSpec(memory_space=pltpu.SMEM)] + [vmem_spec] * 4,
        out_specs=vmem_spec,
        out_shape=jax.ShapeDtypeStruct((asked.shape[0], 2 * cap * (z_rows + 2), LANES), jnp.float32),
        compiler_params=pltpu.CompilerParams(vmem_limit_bytes=vmem_bytes),
        name="packed_rows",
    )(asked, mine, arrived, partner, crossed)


def two_rows(values, rows):
    leaves = values.shape[1]
    split = jnp.transpose(values.reshape(2, rows, leaves, LEAF), (2, 1, 0, 3))
    return split.reshape(leaves, rows, 2 * LEAF)


def on_device(points, samples, sketch, far_requests, far_slots, far_count, near_mask):
    samp_dev = samples.shape[0]
    leaves = samples.shape[1] // LEAF
    rank = sketch.shape[0]
    branches = lax.axis_size("leaf")
    columns = lax.axis_size("cols")
    cap = far_requests.shape[2]
    share = rank // columns
    me = lax.axis_index("leaf")
    column = lax.axis_index("cols")

    half = branches // 2
    side = me // half
    groups = [list(range(half)), list(range(half, branches))]
    mirror = [(i, (i + half) % branches) for i in range(branches)]
    wanted = far_requests.reshape(2, half, cap)
    wanted = jnp.where(side == 0, wanted, wanted[::-1])
    wanted = jnp.transpose(wanted, (1, 0, 2)).reshape(half, 2 * cap)
    asked = lax.all_to_all(
        wanted, "leaf", split_axis=0, concat_axis=0, axis_index_groups=groups, tiled=True
    )

    if columns == 2:
        place = column.astype(jnp.int32).reshape(1)
        mine, other = sketched_shares(place, sketch, samples, points)
        arrived = lax.ppermute(other, "cols", [(0, 1), (1, 0)])
        partner = lax.ppermute(mine, "leaf", mirror)
        crossed = lax.ppermute(
            other,
            ("leaf", "cols"),
            [(2 * i + c, 2 * ((i + half) % branches) + 1 - c) for i in range(branches) for c in range(2)],
        )
    else:
        z_part = jnp.dot(sketch, samples, precision=highest)
        z_mine = exchange_sum(z_part.reshape(columns, share, leaves * LEAF), "cols")
        z_rows = two_rows(z_mine.reshape(share, leaves, LEAF), share // 2)
        planes = points.reshape(3, leaves, LEAF)
        c_rows = two_rows(
            jnp.concatenate([planes[0:1], planes[2:3], planes[1:2], jnp.zeros_like(planes[0:1])], axis=0), 2
        )
        mine = jnp.concatenate([z_rows.reshape(-1, LANES), c_rows.reshape(-1, LANES)], axis=0)
        partner = lax.ppermute(mine, "leaf", mirror)
        arrived = jnp.zeros((leaves * share // 2, LANES), jnp.float32)
        crossed = arrived

    coords = jnp.transpose(points.reshape(3, leaves, LEAF), (1, 0, 2))
    rows = jnp.transpose(samples.reshape(samp_dev, leaves, LEAF), (1, 2, 0))
    small_sent = packed_rows(asked, mine, arrived, partner, crossed, cap, leaves)
    small_got = lax.all_to_all(
        small_sent, "leaf", split_axis=0, concat_axis=0, axis_index_groups=groups, tiled=True
    )
    tables = group_tables(far_slots, far_count, side, half * cap)
    total, group_leaf, group_count, group_slots = tables

    forward = [(i, i + 1) for i in range(branches - 1)]
    backward = [(target, source) for source, target in forward]
    edges = jnp.concatenate([rows[:1], rows[leaves - 1 :]], axis=0)
    edge_coords = jnp.concatenate([coords[:1], coords[leaves - 1 :]], axis=0)
    width = max(samp_dev, LEAF)
    edges = jnp.concatenate(
        [
            jnp.pad(edges, ((0, 0), (0, 0), (0, width - samp_dev))),
            jnp.pad(edge_coords, ((0, 0), (0, 5), (0, width - LEAF))),
        ],
        axis=1,
    )
    edges, unused = lax.optimization_barrier((edges, small_sent))
    low_edge = lax.ppermute(edges[1], "leaf", forward)
    high_edge = lax.ppermute(edges[0], "leaf", backward)

    rows_out, low_edge, high_edge = lax.optimization_barrier((rows, low_edge, high_edge))
    partner_rows = lax.ppermute(rows_out, "leaf", mirror)

    own_sent = rows[asked[:, :cap].reshape(-1)].reshape(half, cap, LEAF, samp_dev)
    own_got = lax.all_to_all(
        own_sent, "leaf", split_axis=0, concat_axis=0, axis_index_groups=groups, tiled=True
    )
    own_got = own_got.reshape(half * cap, LEAF, samp_dev)

    z_count = 2 * cap * share // 2
    z_own = small_got[:, :z_count].reshape(half * z_count, LANES)
    c_got = small_got[:, z_count:].reshape(half * 4 * cap, LANES)
    if columns == 2:
        z_other = lax.ppermute(z_own, "cols", [(0, 1), (1, 0)])
    else:
        slots = branches * cap
        z_all = exchange_all(z_own, "cols").reshape(columns, slots, share // 2, 2, LEAF)
        z_all = jnp.transpose(z_all, (1, 0, 3, 2, 4)).reshape(slots, 2, 2, rank // 4, LEAF)
        z_all = jnp.transpose(z_all, (1, 0, 3, 2, 4)).reshape(2, slots * rank // 4, LANES)
        z_own, z_other = z_all[0], z_all[1]
        place = jnp.zeros((1,), jnp.int32)

    targets = jnp.transpose(coords, (0, 2, 1))
    high, low, sketched, gram = kernel_blocks(
        total, group_leaf, group_count, group_slots, place, z_own, z_other, c_got, targets, rank, cap
    )

    levels = leaves.bit_length()
    inverse, ratio, top_inverse, own_child = branch_factors(gram, levels)
    own_child = own_child.reshape(rank * rank // LANES, LANES)
    partner_child = lax.ppermute(own_child, "leaf", mirror)
    both_children = jnp.where(
        side == 0,
        jnp.concatenate([own_child, partner_child], axis=0),
        jnp.concatenate([partner_child, own_child], axis=0),
    )
    child_rows = both_children.shape[0]

    partner_sent = partner_rows[asked[:, cap:].reshape(-1)].reshape(half, cap * LEAF, samp_dev)
    if samp_dev == LANES:
        both = jnp.concatenate(
            [partner_sent, jnp.broadcast_to(both_children[None], (half,) + both_children.shape)], axis=1
        )
        partner_sent = both
        both = lax.all_to_all(
            both, "leaf", split_axis=0, concat_axis=0, axis_index_groups=groups, tiled=True
        )
        partner_got = both[:, : cap * LEAF]
        children = both[:, cap * LEAF :]
    else:
        partner_got = lax.all_to_all(
            partner_sent, "leaf", split_axis=0, concat_axis=0, axis_index_groups=groups, tiled=True
        )
        children = lax.all_to_all(
            jnp.broadcast_to(both_children[None], (half,) + both_children.shape),
            "leaf", split_axis=0, concat_axis=0, axis_index_groups=groups, tiled=True,
        )
    partner_got = partner_got.reshape(half * cap, LEAF, samp_dev)
    children = jnp.transpose(children.reshape(half, 2, child_rows // 2, LANES), (1, 0, 2, 3))
    children = children.reshape(branches, rank, rank)
    ratio, rows_low, rows_high, unused = lax.optimization_barrier(
        (ratio, low_edge[:LEAF, :samp_dev], high_edge[:LEAF, :samp_dev], partner_sent)
    )
    weights, leaf_basis = bases(inverse, ratio, top_inverse, sketched)

    coords_low, coords_high = low_edge[LEAF : LEAF + 3, :LEAF], high_edge[LEAF : LEAF + 3, :LEAF]
    near_rows = jnp.concatenate(
        [rows_low[None], rows, rows_high[None], jnp.zeros_like(rows_low)[None]], axis=0
    )
    near_coords = jnp.concatenate(
        [coords_low[None], coords, coords_high[None], jnp.zeros_like(coords_low)[None]], axis=0
    )
    near_coords = jnp.pad(near_coords, ((0, 0), (0, 5), (0, 0)))
    near_coords = jnp.concatenate([near_coords, near_coords], axis=2)
    near_sample = near_products(near_mask.reshape(-1), near_rows, near_coords, targets)

    far_sample, branch_samples, copies = far_products(
        total, group_leaf, group_slots, own_got, partner_got, high, low, weights, branches
    )
    everyone = lax.all_to_all(copies, "leaf", split_axis=0, concat_axis=0, tiled=True)
    children, unused = lax.optimization_barrier((children, branch_samples))
    top_transfer, paths = top_factors(children)
    root_sample = lax.dot_general(
        paths, everyone.reshape(branches * rank, samp_dev), tn_dims, precision=highest
    )
    return (far_sample, near_sample, leaf_basis, branch_samples, top_transfer, root_sample)


def solution(mesh):
    return jax.shard_map(
        on_device,
        mesh=mesh,
        in_specs=(
            P(None, "leaf"),
            P("cols", "leaf"),
            P(None, "cols"),
            P("leaf", None, None),
            P("leaf", None),
            P("leaf"),
            P("leaf", None),
        ),
        out_specs=(
            P("cols", "leaf"),
            P("cols", "leaf"),
            P(None, "leaf"),
            P("leaf", "cols"),
            P(),
            P(None, "cols"),
        ),
        check_vma=False,
    )
```

```python
import functools
import math

import jax
import jax.numpy as jnp
import numpy as np
from jax import lax
from jax.experimental import pallas as pl
from jax.experimental.pallas import tpu as pltpu
from jax.sharding import PartitionSpec as P

LEAF = 64
FAR = 16
GROUP = 4
BATCH = 16
LANES = 128
SUB = 8

length_scale = 0.3
shift_share = 0.05
highest = lax.Precision.HIGHEST
exponent_scale = -math.log2(math.e) / length_scale
vmem_bytes = 56 * 1024 * 1024

nt_dims = (((1,), (1,)), ((), ()))
tn_dims = (((0,), (0,)), ((), ()))


def halves(value):
    high = value.astype(jnp.bfloat16)
    low = (value - high.astype(jnp.float32)).astype(jnp.bfloat16)
    return high, low


def dot(a, b):
    return jnp.dot(a, b, preferred_element_type=jnp.float32)


def dot_exact(a, b):
    return jnp.dot(a, b, precision=highest, preferred_element_type=jnp.float32)


def dot_exact_nt(a, b):
    return lax.dot_general(a, b, nt_dims, precision=highest, preferred_element_type=jnp.float32)


def dot_nt(a, b):
    return lax.dot_general(a, b, nt_dims, preferred_element_type=jnp.float32)


def kernel_half(source_rows, target, lane, valid):
    total = None
    for axis in range(3):
        difference = source_rows[axis : axis + 1, :] - target[:, axis : axis + 1]
        square = difference * difference
        total = square if total is None else total + square
    distance = total * lax.rsqrt(jnp.maximum(total, 1e-30))
    values = jnp.exp2(distance * exponent_scale)
    return jnp.where(lane < valid, values, 0.0)


def blocks_body(
    total_ref, leaf_ref, count_ref, slot_ref, place_ref,
    own_ref, other_ref, coords_ref, target_ref,
    high_ref, low_ref, sketched_ref, gram_ref,
    packed,
    *, rank, cap,
):
    step = pl.program_id(0)
    lane = lax.broadcasted_iota(jnp.int32, (1, LANES), 1)
    first = lane < LEAF

    @pl.when(step == 0)
    def _():
        sketched_ref[...] = jnp.zeros_like(sketched_ref)
        quarter = rank // 4
        slots = packed.shape[0]
        own_at = pl.multiple_of(place_ref[0] * 2 * quarter, quarter)
        other_at = pl.multiple_of((1 - place_ref[0]) * 2 * quarter, quarter)

        def unpack(peer, carry):
            for entry in range(2 * cap):
                slot = (entry // cap) * (slots // 2) + peer * cap + entry % cap
                at = pl.multiple_of((peer * 2 * cap + entry) * quarter, quarter)
                for ref, base in ((own_ref, own_at), (other_ref, other_at)):
                    value = ref[pl.ds(at, quarter), :]
                    turned = pltpu.roll(value, LEAF, 1)
                    packed[slot, pl.ds(base, quarter), :] = jnp.where(first, value, turned)
                    packed[slot, pl.ds(base + quarter, quarter), :] = jnp.where(first, turned, value)
                value = coords_ref[pl.ds((peer * 2 * cap + entry) * 2, 2), :]
                turned = pltpu.roll(value, LEAF, 1)
                packed[slot, rank : rank + 1, :] = jnp.where(first, value, turned)[0:1]
                packed[slot, rank + 1 : rank + 2, :] = jnp.where(first, turned, value)[0:1]
                packed[slot, rank + 2 : rank + 3, :] = jnp.where(first, value, turned)[1:2]
            return carry

        lax.fori_loop(0, slots // (2 * cap), unpack, 0)

    @pl.when(step * BATCH < total_ref[0])
    def _():
        for member in range(BATCH):
            group = step * BATCH + member
            leaf = leaf_ref[group]
            count = count_ref[group]
            slots = [slot_ref[group * GROUP + e] for e in range(GROUP)]
            target = target_ref[leaf]
            z_parts = []
            for half in range(GROUP // 2):
                left = packed[slots[2 * half]]
                right = packed[slots[2 * half + 1]]
                both = jnp.where(first, left, right)
                values = kernel_half(both[rank : rank + 3], target, lane, (count - 2 * half) * LEAF)
                high, low = halves(values)
                high_ref[member, :, half * LANES : (half + 1) * LANES] = high
                low_ref[member, :, half * LANES : (half + 1) * LANES] = low
                z_parts.append(both[:rank])
            z_high, z_low = halves(jnp.concatenate(z_parts, axis=1))
            k_high = high_ref[member]
            k_low = low_ref[member]
            update = dot_nt(z_high, k_high) + (dot_nt(z_low, k_high) + dot_nt(z_high, k_low))
            sketched_ref[leaf] += update

    @pl.when(step == pl.num_programs(0) - 1)
    def _():
        for leaf in range(gram_ref.shape[0]):
            block = sketched_ref[leaf]
            gram_ref[leaf] = dot_exact_nt(block, block)


def kernel_blocks(total, group_leaf, group_count, group_slots, place, own, other, coords, targets, rank, cap):
    leaves = targets.shape[0]
    groups = group_leaf.shape[0]
    slots = coords.shape[0] // 2
    steps = groups // BATCH

    def block_index(step, total_ref, *unused):
        last = (total_ref[0] - 1) // BATCH
        return (jnp.minimum(step, last), 0, 0)

    flat = lambda *unused: (0, 0)
    whole = lambda *unused: (0, 0, 0)
    once = pl.Buffered(1)
    return pl.pallas_call(
        functools.partial(blocks_body, rank=rank, cap=cap),
        grid_spec=pltpu.PrefetchScalarGridSpec(
            num_scalar_prefetch=5,
            grid=(steps,),
            in_specs=[
                pl.BlockSpec(own.shape, flat, pipeline_mode=once),
                pl.BlockSpec(other.shape, flat, pipeline_mode=once),
                pl.BlockSpec(coords.shape, flat, pipeline_mode=once),
                pl.BlockSpec(targets.shape, whole, pipeline_mode=once),
            ],
            out_specs=[
                pl.BlockSpec((BATCH, LEAF, GROUP * LEAF), block_index),
                pl.BlockSpec((BATCH, LEAF, GROUP * LEAF), block_index),
                pl.BlockSpec((leaves, rank, LEAF), whole),
                pl.BlockSpec((leaves, rank, rank), whole),
            ],
            scratch_shapes=[pltpu.VMEM((slots, rank + SUB, LANES), jnp.float32)],
        ),
        out_shape=[
            jax.ShapeDtypeStruct((groups, LEAF, GROUP * LEAF), jnp.bfloat16),
            jax.ShapeDtypeStruct((groups, LEAF, GROUP * LEAF), jnp.bfloat16),
            jax.ShapeDtypeStruct((leaves, rank, LEAF), jnp.float32),
            jax.ShapeDtypeStruct((leaves, rank, rank), jnp.float32),
        ],
        compiler_params=pltpu.CompilerParams(vmem_limit_bytes=vmem_bytes),
        name="kernel_blocks",
        cost_estimate=pl.CostEstimate(
            flops=10**6, bytes_accessed=10**4, transcendentals=0
        ),
    )(total, group_leaf, group_count, group_slots, place, own, other, coords, targets)


def far_body(
    total_ref, leaf_ref, slot_ref, side_ref,
    own_ref, partner_ref, high_ref, low_ref, weights_ref,
    out_ref, projected_ref, copies_ref,
    s_high, s_low, acc,
):
    step = pl.program_id(0)
    samp_dev = own_ref.shape[2]
    part = own_ref.shape[0]

    @pl.when(step == 0)
    def _():
        acc[...] = jnp.zeros_like(acc)

        def split(slot, carry):
            here = side_ref[0] * part + slot
            there = (1 - side_ref[0]) * part + slot
            s_high[here], s_low[here] = halves(own_ref[slot])
            s_high[there], s_low[there] = halves(partner_ref[slot])
            return carry

        lax.fori_loop(0, part, split, 0, unroll=4)

    @pl.when(step * BATCH < total_ref[0])
    def _():
        for member in range(BATCH):
            group = step * BATCH + member
            leaf = leaf_ref[group]
            slots = [slot_ref[group * GROUP + e] for e in range(GROUP)]
            rows_high = jnp.concatenate([s_high[slot] for slot in slots], axis=0)
            rows_low = jnp.concatenate([s_low[slot] for slot in slots], axis=0)
            k_high = high_ref[member]
            k_low = low_ref[member]
            acc[leaf] += dot(k_high, rows_high) + (dot(k_high, rows_low) + dot(k_low, rows_high))

    @pl.when(step == pl.num_programs(0) - 1)
    def _():
        leaves = acc.shape[0]
        rows = acc[...].reshape(leaves * LEAF, samp_dev)
        projected = dot_exact(weights_ref[...], rows)
        projected_ref[...] = projected
        for branch in range(copies_ref.shape[0]):
            copies_ref[branch] = projected
        for pair in range(leaves // 2):
            block = acc[2 * pair : 2 * pair + 2].reshape(2 * LEAF, samp_dev)
            out_ref[:, 2 * pair * LEAF : 2 * (pair + 1) * LEAF] = block.T


def far_products(total, group_leaf, group_slots, side, own, partner, high, low, weights, branches):
    part, unused, samp_dev = own.shape
    slots = 2 * part
    groups = group_leaf.shape[0]
    points_dev = weights.shape[1]
    leaves = points_dev // LEAF
    steps = groups // BATCH

    def block_index(step, total_ref, *unused):
        last = (total_ref[0] - 1) // BATCH
        return (jnp.minimum(step, last), 0, 0)

    return pl.pallas_call(
        far_body,
        grid_spec=pltpu.PrefetchScalarGridSpec(
            num_scalar_prefetch=4,
            grid=(steps,),
            in_specs=[
                pl.BlockSpec(own.shape, lambda *unused: (0, 0, 0), pipeline_mode=pl.Buffered(1)),
                pl.BlockSpec(partner.shape, lambda *unused: (0, 0, 0), pipeline_mode=pl.Buffered(1)),
                pl.BlockSpec((BATCH, LEAF, GROUP * LEAF), block_index),
                pl.BlockSpec((BATCH, LEAF, GROUP * LEAF), block_index),
                pl.BlockSpec(weights.shape, lambda *unused: (0, 0), pipeline_mode=pl.Buffered(1)),
            ],
            out_specs=[
                pl.BlockSpec((samp_dev, points_dev), lambda *unused: (0, 0)),
                pl.BlockSpec((weights.shape[0], samp_dev), lambda *unused: (0, 0)),
                pl.BlockSpec((branches, weights.shape[0], samp_dev), lambda *unused: (0, 0, 0)),
            ],
            scratch_shapes=[
                pltpu.VMEM((slots, LEAF, samp_dev), jnp.bfloat16),
                pltpu.VMEM((slots, LEAF, samp_dev), jnp.bfloat16),
                pltpu.VMEM((leaves, LEAF, samp_dev), jnp.float32),
            ],
        ),
        out_shape=[
            jax.ShapeDtypeStruct((samp_dev, points_dev), jnp.float32),
            jax.ShapeDtypeStruct((weights.shape[0], samp_dev), jnp.float32),
            jax.ShapeDtypeStruct((branches, weights.shape[0], samp_dev), jnp.float32),
        ],
        compiler_params=pltpu.CompilerParams(vmem_limit_bytes=vmem_bytes),
        name="far_products",
        cost_estimate=pl.CostEstimate(
            flops=10**6, bytes_accessed=10**4, transcendentals=0
        ),
    )(total, group_leaf, group_slots, side, own, partner, high, low, weights)


NEAR_LEAVES = 8


def near_body(mask_ref, rows_ref, coords_ref, target_ref, out_ref):
    step = pl.program_id(0)
    samp_dev = rows_ref.shape[2]
    lane = lax.broadcasted_iota(jnp.int32, (1, LANES), 1)
    first = lane < LEAF
    for pair in range(NEAR_LEAVES // 2):
        results = []
        for member in range(2):
            leaf = step * NEAR_LEAVES + 2 * pair + member
            target = target_ref[leaf]
            k_high = []
            k_low = []
            for half in range(2):
                both = jnp.where(first, coords_ref[leaf + 2 * half], coords_ref[leaf + 2 * half + 1])
                values = kernel_half(both, target, lane, LANES)
                left = mask_ref[leaf * 3 + 2 * half].astype(jnp.float32)
                if half == 0:
                    right = mask_ref[leaf * 3 + 1].astype(jnp.float32)
                else:
                    right = jnp.float32(0.0)
                high, low = halves(values * jnp.where(first, left, right))
                k_high.append(high)
                k_low.append(low)
            k_high = jnp.concatenate(k_high, axis=1)
            k_low = jnp.concatenate(k_low, axis=1)
            rows = rows_ref[pl.ds(leaf, 4)].reshape(4 * LEAF, samp_dev)
            rows_high, rows_low = halves(rows)
            results.append(
                dot(k_high, rows_high) + (dot(k_high, rows_low) + dot(k_low, rows_high))
            )
        block = jnp.concatenate(results, axis=0)
        out_ref[:, 2 * pair * LEAF : 2 * (pair + 1) * LEAF] = block.T


def near_products(mask, rows, coords, targets):
    leaves = targets.shape[0]
    samp_dev = rows.shape[2]
    whole = lambda *unused: (0, 0, 0)
    return pl.pallas_call(
        near_body,
        grid_spec=pltpu.PrefetchScalarGridSpec(
            num_scalar_prefetch=1,
            grid=(leaves // NEAR_LEAVES,),
            in_specs=[
                pl.BlockSpec(rows.shape, whole),
                pl.BlockSpec(coords.shape, whole),
                pl.BlockSpec(targets.shape, whole),
            ],
            out_specs=pl.BlockSpec((samp_dev, NEAR_LEAVES * LEAF), lambda step, *unused: (0, step)),
        ),
        out_shape=jax.ShapeDtypeStruct((samp_dev, leaves * LEAF), jnp.float32),
        compiler_params=pltpu.CompilerParams(vmem_limit_bytes=vmem_bytes),
        name="near_products",
        cost_estimate=pl.CostEstimate(
            flops=10**6, bytes_accessed=10**4, transcendentals=0
        ),
    )(mask, rows, coords, targets)


def to_lanes(source, target, rank):
    nodes = source.shape[0] // rank
    target[...] = jnp.zeros_like(target)
    for r in range(rank):
        target[r, :, 0:nodes] = source[pl.ds(r, nodes, stride=rank), :].T


def from_lanes(columns, target, r, nodes, rank):
    target[pl.ds(r, nodes, stride=rank), :] = columns.T[0:nodes]


def eliminate(current, left, inverse, level, rank):
    tiles = rank // SUB
    row = lax.broadcasted_iota(jnp.int32, (SUB, LANES), 0)
    diagonal = [current[j, j : j + 1, :] for j in range(rank)]
    while len(diagonal) > 1:
        diagonal = [diagonal[i] + diagonal[i + 1] for i in range(0, len(diagonal), 2)]
    share = shift_share * diagonal[0] / rank
    shift = share + 1e-06
    a = [
        {t: current[j, SUB * t : SUB * (t + 1), :] for t in range(j // SUB, tiles)}
        for j in range(rank)
    ]
    for j in range(rank):
        a[j][j // SUB] = a[j][j // SUB] + jnp.where(row == j % SUB, shift, 0.0)
    m = []
    scales = []
    for k in range(rank):
        tk, rk = k // SUB, k % SUB
        root = lax.rsqrt(a[k][tk][rk : rk + 1, :])
        scales.append(root)
        reciprocal = root * root
        column = {t: a[k][t] * reciprocal for t in range(tk, tiles)}
        column[tk] = jnp.where(row > rk, column[tk], 0.0)
        for j in range(k + 1, rank):
            factor = a[k][j // SUB][j % SUB : j % SUB + 1, :]
            for t in range(j // SUB, tiles):
                a[j][t] = a[j][t] - column[t] * factor
        for c in range(k):
            factor = m[c][tk][rk : rk + 1, :]
            for t in range(tk, tiles):
                m[c][t] = m[c][t] - column[t] * factor
        fresh = {t: -column[t] for t in range(tk, tiles)}
        fresh[tk] = jnp.where(row == rk, 1.0, fresh[tk])
        m.append(fresh)
        if left is not None:
            for t in range(tiles):
                if t < tk:
                    value = jnp.zeros((SUB, LANES), jnp.float32)
                else:
                    value = a[k][t] * root
                if t == tk:
                    value = jnp.where(row >= rk, value, 0.0)
                left[k, SUB * t : SUB * (t + 1), :] = value
    for t in range(tiles):
        scale = jnp.concatenate(scales[SUB * t : SUB * (t + 1)], axis=0)
        for c in range(rank):
            value = m[c][t] * scale if t >= c // SUB else jnp.zeros((SUB, LANES), jnp.float32)
            inverse[c * rank + SUB * t : c * rank + SUB * (t + 1), :] = value
    return shift, share


def inverse_row(inverse, r, t, rank):
    return inverse[pl.ds(SUB * t * rank + r, SUB, stride=rank), :]


def pair_up(value, level):
    return value + pltpu.roll(value, LANES - lax.shift_left(1, level), 1)


def level_fast(level, levels, current, left, inverse, squared, ratio, child, lowest, rank, child_at):
    tiles = rank // SUB
    row = lax.broadcasted_iota(jnp.int32, (SUB, LANES), 0)
    shift, share = eliminate(current, left, inverse, level, rank)
    lowest[...] = jnp.minimum(lowest[...], share)

    for block in range(tiles):
        sums = [[None] * tiles for _ in range(SUB)]
        for r in range(SUB * block, rank):
            parts = [inverse_row(inverse, r, t, rank) for t in range(block, r // SUB + 1)]
            for q in range(SUB):
                if SUB * block + q > r:
                    continue
                factor = parts[0][q : q + 1, :]
                for t in range(block, r // SUB + 1):
                    term = parts[t - block] * factor
                    sums[q][t] = term if sums[q][t] is None else sums[q][t] + term
        for q in range(SUB):
            at = (SUB * block + q) * rank
            for t in range(block, tiles):
                squared[at + SUB * t : at + SUB * (t + 1), :] = sums[q][t]

    if child is not None:
        @pl.when(child_at(level))
        def _():
            for r in range(rank):
                for t in range(tiles):
                    value = left[r, SUB * t : SUB * (t + 1), :]
                    if t <= r // SUB:
                        value = value - shift * inverse_row(inverse, r, t, rank)
                    child[r, SUB * t : SUB * (t + 1), :] = value

    for q in range(rank):
        for t in range(tiles):
            if t >= q // SUB:
                value = squared[q * rank + SUB * t : q * rank + SUB * (t + 1), :]
            else:
                value = squared[pl.ds(SUB * t * rank + q, SUB, stride=rank), :]
            value = -shift * value
            if t == q // SUB:
                value = value + jnp.where(row == q % SUB, 1.0, 0.0)
            if ratio is not None:
                ratio[level, q, SUB * t : SUB * (t + 1), :] = value
            here = current[q, SUB * t : SUB * (t + 1), :] - shift * value
            current[q, SUB * t : SUB * (t + 1), :] = pair_up(here, level)


def level_plain(level, levels, current, left, inverse, squared, ratio, child, lowest, rank, child_at):
    tiles = rank // SUB
    eliminate(current, left, inverse, level, rank)

    def products(out, count, left_of, right_of):
        def block_step(block, carry):
            offset = pl.multiple_of(block * SUB, SUB)
            sums = [[None] * tiles for _ in range(SUB)]
            for r in range(count):
                parts = [left_of(r, t) for t in range(tiles)]
                heads = right_of(r, offset)
                for q in range(SUB):
                    for t in range(tiles):
                        term = parts[t] * heads[q : q + 1, :]
                        sums[q][t] = term if sums[q][t] is None else sums[q][t] + term
            for q in range(SUB):
                for t in range(tiles):
                    out(offset + q, t, sums[q][t])
            return carry

        lax.fori_loop(0, tiles, block_step, 0)

    def tile(t):
        return slice(SUB * t, SUB * (t + 1))

    def put_child(r, t, value):
        squared[pl.ds(pl.multiple_of(r * rank + SUB * t, SUB), SUB), :] = value

    products(
        put_child, rank,
        lambda k, t: current[k, tile(t), :],
        lambda k, offset: inverse[pl.ds(pl.multiple_of(k * rank + offset, SUB), SUB), :],
    )
    if child is not None:
        @pl.when(child_at(level))
        def _():
            for r in range(rank):
                for t in range(tiles):
                    child[r, tile(t), :] = squared[r * rank + SUB * t : r * rank + SUB * (t + 1), :]

    def child_part(r, t):
        return squared[r * rank + SUB * t : r * rank + SUB * (t + 1), :]

    def put_current(q, t, value):
        current[q, tile(t), :] = pair_up(value, level)

    if ratio is not None:
        def put_ratio(c, t, value):
            ratio[level, c, tile(t), :] = value

        def inverse_head(r, offset):
            return inverse[pl.ds(offset * rank + r, SUB, stride=rank), :]

        products(put_ratio, rank, child_part, inverse_head)
    products(
        put_current, rank, child_part,
        lambda r, offset: squared[pl.ds(pl.multiple_of(r * rank + offset, SUB), SUB), :],
    )


def run_levels(source, levels, nodes, current, left, inverse, squared, ratio, child, lowest, rank, child_at, finish):
    lowest[...] = jnp.full((1, LANES), 1.0, jnp.float32)

    def sweep(level_step):
        to_lanes(source, current, rank)

        def body(level, carry):
            level_step(level, levels, current, left, inverse, squared, ratio, child, lowest, rank, child_at)
            finish(level)
            return carry

        lax.fori_loop(0, levels, body, 0)

    sweep(level_fast)
    lane = lax.broadcasted_iota(jnp.int32, (1, LANES), 1)
    least = jnp.min(jnp.where(lane < nodes, lowest[...], 1.0))

    @pl.when(least < 2e-06)
    def _():
        sweep(level_plain)


def branch_body(gram_ref, inverse_ref, ratio_ref, top_ref, child_ref, current, left, inverse, squared, child, lowest, *, rank, levels):
    nodes = gram_ref.shape[0] // rank

    def finish(level):
        @pl.when(level == 0)
        def _():
            for c in range(rank):
                inverse_ref[c] = inverse[c * rank : (c + 1) * rank, :]

        @pl.when(level == levels - 1)
        def _():
            for r in range(rank):
                child_ref[r : r + 1, :] = child[r].T[0:1, :]
                top_ref[r : r + 1, :] = jnp.concatenate(
                    [inverse_row(inverse, r, t, rank) for t in range(rank // SUB)], axis=0
                ).T[0:1, :]

    run_levels(
        gram_ref, levels, nodes, current, left, inverse, squared, ratio_ref, child, lowest, rank,
        lambda level: level == levels - 1, finish,
    )


vmem_spec = pl.BlockSpec(memory_space=pltpu.VMEM)


def tree_scratch(rank):
    return [
        pltpu.VMEM((rank, rank, LANES), jnp.float32),
        pltpu.VMEM((rank, rank, LANES), jnp.float32),
        pltpu.VMEM((rank * rank, LANES), jnp.float32),
        pltpu.VMEM((rank * rank, LANES), jnp.float32),
        pltpu.VMEM((rank, rank, LANES), jnp.float32),
        pltpu.VMEM((1, LANES), jnp.float32),
    ]


def branch_factors(gram, levels):
    leaves, rank, unused = gram.shape
    return pl.pallas_call(
        functools.partial(branch_body, rank=rank, levels=levels),
        in_specs=[vmem_spec],
        out_specs=[vmem_spec] * 4,
        out_shape=[
            jax.ShapeDtypeStruct((rank, rank, LANES), jnp.float32),
            jax.ShapeDtypeStruct((levels, rank, rank, LANES), jnp.float32),
            jax.ShapeDtypeStruct((rank, rank), jnp.float32),
            jax.ShapeDtypeStruct((rank, rank), jnp.float32),
        ],
        scratch_shapes=tree_scratch(rank),
        compiler_params=pltpu.CompilerParams(vmem_limit_bytes=vmem_bytes),
        name="branch_factors",
        cost_estimate=pl.CostEstimate(flops=10**6, bytes_accessed=10**4, transcendentals=0),
    )(gram.reshape(leaves * rank, rank))


def basis_body(inverse_ref, ratio_ref, top_ref, sketched_ref, weights_ref, basis_ref, natural, *, rank, levels):
    leaves = sketched_ref.shape[0]
    upper = [top_ref[...]]
    for level in range(levels - 2, -1, -1):
        stride = 2**level
        for c in range(rank):
            from_lanes(ratio_ref[level, c], natural, c, leaves, rank)
        fresh = []
        for node in range(leaves // stride):
            block = natural[node * stride * rank : (node * stride + 1) * rank, :]
            fresh.append(dot_exact(upper[node // 2], block))
        upper = fresh
    for r in range(rank):
        from_lanes(inverse_ref[r], natural, r, leaves, rank)
    for pair in range(leaves // 2):
        results = []
        for leaf in (2 * pair, 2 * pair + 1):
            block = sketched_ref[leaf]
            own = lax.dot_general(
                natural[leaf * rank : (leaf + 1) * rank, :], block, tn_dims,
                precision=highest, preferred_element_type=jnp.float32,
            )
            results.append(jnp.concatenate([dot_exact(upper[leaf], block), own], axis=0))
        both = jnp.concatenate(results, axis=1)
        weights_ref[:, pair * 2 * LEAF : (pair + 1) * 2 * LEAF] = both[:rank]
        basis_ref[:, pair * 2 * LEAF : (pair + 1) * 2 * LEAF] = both[rank:]


def bases(inverse, ratio, top, sketched):
    leaves, rank, unused = sketched.shape
    levels = ratio.shape[0]
    shape = jax.ShapeDtypeStruct((rank, leaves * LEAF), jnp.float32)
    return pl.pallas_call(
        functools.partial(basis_body, rank=rank, levels=levels),
        in_specs=[vmem_spec] * 4,
        out_specs=[vmem_spec] * 2,
        out_shape=[shape, shape],
        scratch_shapes=[pltpu.VMEM((leaves * rank, rank), jnp.float32)],
        compiler_params=pltpu.CompilerParams(vmem_limit_bytes=vmem_bytes),
        name="bases",
        cost_estimate=pl.CostEstimate(flops=10**6, bytes_accessed=10**4, transcendentals=0),
    )(inverse, ratio, top, sketched)


def top_body(children_ref, transfer_ref, paths_ref, source, current, left, inverse, squared, child, lowest, nat_inverse, nat_child, *, rank, levels):
    nodes = children_ref.shape[0] // 2
    for node in range(nodes):
        both = children_ref[2 * node : 2 * node + 2].reshape(2 * rank, rank)
        source[node * rank : (node + 1) * rank, :] = lax.dot_general(
            both, both, tn_dims, precision=highest, preferred_element_type=jnp.float32
        )

    def finish(level):
        for r in range(rank):
            from_lanes(child[r], nat_child.at[level], r, nodes, rank)
            from_lanes(inverse[r * rank : (r + 1) * rank, :], nat_inverse.at[level], r, nodes, rank)

    run_levels(
        source, levels, nodes, current, left, inverse, squared, None, child, lowest, rank,
        lambda level: level >= 0, finish,
    )
    offset = 0
    for level in range(levels):
        for node in range(nodes >> level):
            if level == 0:
                stacked = children_ref[2 * node : 2 * node + 2].reshape(2 * rank, rank)
            else:
                first = 2 * node << level - 1
                second = 2 * node + 1 << level - 1
                stacked = jnp.concatenate(
                    [
                        nat_child[level - 1, first * rank : (first + 1) * rank, :],
                        nat_child[level - 1, second * rank : (second + 1) * rank, :],
                    ],
                    axis=0,
                )
            at = (node << level) * rank
            transfer_ref[offset + node] = lax.dot_general(
                nat_inverse[level, at : at + rank, :], stacked, (((0,), (1,)), ((), ())),
                precision=highest, preferred_element_type=jnp.float32,
            )
        offset += nodes >> level
    above = [None]
    for level in range(levels - 1, -1, -1):
        offset -= nodes >> level
        fresh = []
        for node in range(nodes >> level):
            both = transfer_ref[offset + node]
            if above[0] is None:
                both = both.T
            else:
                both = lax.dot_general(
                    both, above[node], tn_dims, precision=highest, preferred_element_type=jnp.float32
                )
            fresh += [both[:rank], both[rank:]]
        above = fresh
    for branch in range(2 * nodes):
        paths_ref[branch * rank : (branch + 1) * rank, :] = above[branch]


def top_factors(children):
    branches, rank, unused = children.shape
    levels = branches.bit_length() - 1
    nodes = branches // 2
    natural = pltpu.VMEM((levels, nodes * rank, rank), jnp.float32)
    return pl.pallas_call(
        functools.partial(top_body, rank=rank, levels=levels),
        in_specs=[vmem_spec],
        out_specs=[vmem_spec] * 2,
        out_shape=[
            jax.ShapeDtypeStruct((branches - 1, rank, 2 * rank), jnp.float32),
            jax.ShapeDtypeStruct((branches * rank, rank), jnp.float32),
        ],
        scratch_shapes=[pltpu.VMEM((nodes * rank, rank), jnp.float32)]
        + tree_scratch(rank)
        + [natural, natural],
        compiler_params=pltpu.CompilerParams(vmem_limit_bytes=vmem_bytes),
        name="top_factors",
        cost_estimate=pl.CostEstimate(flops=10**10, bytes_accessed=10**7, transcendentals=0),
    )(children)


def exchange_sum(pieces, axis):
    count = pieces.shape[0]
    me = lax.axis_index(axis)
    mine = lax.dynamic_index_in_dim(pieces, me, 0, keepdims=False)
    for step in range(1, count):
        outgoing = lax.dynamic_index_in_dim(pieces, (me + step) % count, 0, keepdims=False)
        mine = mine + lax.ppermute(
            outgoing, axis, [(i, (i + step) % count) for i in range(count)]
        )
    return mine


def exchange_all(piece, axis):
    count = lax.axis_size(axis)
    me = lax.axis_index(axis)
    if count == 2:
        other = lax.ppermute(piece, axis, [(0, 1), (1, 0)])
        return jnp.stack([jnp.where(me == 0, piece, other), jnp.where(me == 0, other, piece)])
    result = jnp.zeros((count,) + piece.shape, piece.dtype)
    result = lax.dynamic_update_index_in_dim(result, piece, me, 0)
    for step in range(1, count):
        arrived = lax.ppermute(piece, axis, [(i, (i + step) % count) for i in range(count)])
        result = lax.dynamic_update_index_in_dim(result, arrived, (me - step) % count, 0)
    return result


def group_tables(far_slots, far_count):
    leaves = far_slots.shape[0]
    groups = leaves * FAR // GROUP
    per_leaf = (far_count + GROUP - 1) // GROUP
    before = jnp.arange(leaves)[:, None] >= jnp.arange(leaves)[None, :]
    ends = jnp.sum(jnp.where(before, per_leaf[None, :], 0), axis=1)
    total = ends[leaves - 1 :]
    ids = jnp.arange(groups, dtype=jnp.int32)
    leaf = jnp.minimum(jnp.sum((ends[None, :] <= ids[:, None]).astype(jnp.int32), axis=1), leaves - 1)
    hit = leaf[:, None] == jnp.arange(leaves)[None, :]
    start = jnp.sum(jnp.where(hit, (ends - per_leaf)[None, :], 0), axis=1)
    length = jnp.sum(jnp.where(hit, far_count[None, :], 0), axis=1)
    sub = ids - start
    count = jnp.where(ids < total, jnp.clip(length - GROUP * sub, 0, GROUP), 0)
    first = jnp.minimum(sub, FAR // GROUP - 1)
    slots = far_slots.reshape(leaves * FAR // GROUP, GROUP)[leaf * (FAR // GROUP) + first]
    return (
        total.astype(jnp.int32),
        leaf.astype(jnp.int32),
        count.astype(jnp.int32),
        slots.reshape(-1).astype(jnp.int32),
    )


def sketch_body(place_ref, sketch_ref, samples_ref, points_ref, mine_ref, other_ref):
    product = dot_exact(sketch_ref[...], samples_ref[...])
    rank, points_dev = product.shape
    quarter = rank // 4
    first = lax.broadcasted_iota(jnp.int32, (1, LANES), 1) < LEAF
    swap = place_ref[0] == 1
    leaves = points_dev // LEAF

    def interleave(low, high):
        even = jnp.where(first, low, pltpu.roll(high, LEAF, 1))
        odd = jnp.where(first, pltpu.roll(low, LEAF, 1), high)
        return even, odd

    for pair in range(leaves // 2):
        lanes = slice(pair * LANES, (pair + 1) * LANES)
        shares = []
        for share in range(2):
            base = 2 * quarter * share
            shares.append(
                interleave(product[base : base + quarter, lanes], product[base + quarter : base + 2 * quarter, lanes])
            )
        for member in range(2):
            at = (2 * pair + member) * quarter
            mine_ref[at : at + quarter, :] = jnp.where(swap, shares[1][member], shares[0][member])
            other_ref[at : at + quarter, :] = jnp.where(swap, shares[0][member], shares[1][member])
        x = points_ref[0:1, lanes]
        y = points_ref[1:2, lanes]
        z = points_ref[2:3, lanes]
        xy = interleave(x, y)
        zs = interleave(z, jnp.zeros_like(z))
        for member in range(2):
            at = leaves * quarter + (2 * pair + member) * 2
            mine_ref[at : at + 1, :] = xy[member]
            mine_ref[at + 1 : at + 2, :] = zs[member]


def sketched_shares(place, sketch, samples, points):
    rank = sketch.shape[0]
    leaves = samples.shape[1] // LEAF
    return pl.pallas_call(
        sketch_body,
        in_specs=[pl.BlockSpec(memory_space=pltpu.SMEM)] + [vmem_spec] * 3,
        out_specs=[vmem_spec] * 2,
        out_shape=[
            jax.ShapeDtypeStruct((leaves * (rank // 4 + 2), LANES), jnp.float32),
            jax.ShapeDtypeStruct((leaves * rank // 4, LANES), jnp.float32),
        ],
        compiler_params=pltpu.CompilerParams(vmem_limit_bytes=vmem_bytes),
        name="sketched_shares",
        cost_estimate=pl.CostEstimate(flops=10**6, bytes_accessed=10**4, transcendentals=0),
    )(place, sketch, samples, points)


def pack_body(asked_ref, side_ref, mine_ref, arrived_ref, partner_ref, crossed_ref, out_ref, *, cap, leaves):
    z_rows = arrived_ref.shape[0] // leaves
    side = side_ref[0]

    def one(peer, carry):
        for entry in range(2 * cap):
            leaf = asked_ref[peer, entry]
            here = side == entry // cap
            at = pl.ds(leaf * z_rows, z_rows)
            out_ref[peer, z_rows * entry : z_rows * (entry + 1), :] = jnp.where(
                here, mine_ref[at, :] + arrived_ref[at, :], partner_ref[at, :] + crossed_ref[at, :]
            )
            base = z_rows * 2 * cap + 2 * entry
            at = pl.ds(leaves * z_rows + leaf * 2, 2)
            out_ref[peer, base : base + 2, :] = jnp.where(here, mine_ref[at, :], partner_ref[at, :])
        return carry

    lax.fori_loop(0, out_ref.shape[0], one, 0)


def packed_rows(asked, side, mine, arrived, partner, crossed, cap, leaves):
    z_rows = arrived.shape[0] // leaves
    return pl.pallas_call(
        functools.partial(pack_body, cap=cap, leaves=leaves),
        in_specs=[pl.BlockSpec(memory_space=pltpu.SMEM)] * 2 + [vmem_spec] * 4,
        out_specs=vmem_spec,
        out_shape=jax.ShapeDtypeStruct((asked.shape[0], 2 * cap * (z_rows + 2), LANES), jnp.float32),
        compiler_params=pltpu.CompilerParams(vmem_limit_bytes=vmem_bytes),
        name="packed_rows",
    )(asked, side, mine, arrived, partner, crossed)


def payload_body(asked_ref, rows_ref, child_ref, out_ref, *, cap):
    def one(peer, carry):
        for entry in range(cap):
            out_ref[peer, LEAF * entry : LEAF * (entry + 1), :] = rows_ref[asked_ref[peer, entry]]
        out_ref[peer, LEAF * cap :, :] = child_ref[...]
        return carry

    lax.fori_loop(0, out_ref.shape[0], one, 0)


def payload_rows(asked, rows, child):
    half, cap = asked.shape
    return pl.pallas_call(
        functools.partial(payload_body, cap=cap),
        in_specs=[pl.BlockSpec(memory_space=pltpu.SMEM)] + [vmem_spec] * 2,
        out_specs=vmem_spec,
        out_shape=jax.ShapeDtypeStruct((half, cap * LEAF + child.shape[0], rows.shape[2]), jnp.float32),
        compiler_params=pltpu.CompilerParams(vmem_limit_bytes=vmem_bytes),
        name="payload_rows",
    )(asked, rows, child)


def two_rows(values, rows):
    leaves = values.shape[1]
    split = jnp.transpose(values.reshape(2, rows, leaves, LEAF), (2, 1, 0, 3))
    return split.reshape(leaves, rows, 2 * LEAF)


def on_device(points, samples, sketch, far_requests, far_slots, far_count, near_mask):
    samp_dev = samples.shape[0]
    leaves = samples.shape[1] // LEAF
    rank = sketch.shape[0]
    branches = lax.axis_size("leaf")
    columns = lax.axis_size("cols")
    cap = far_requests.shape[2]
    share = rank // columns
    me = lax.axis_index("leaf")
    column = lax.axis_index("cols")

    half = branches // 2
    side = me // half
    groups = [list(range(half)), list(range(half, branches))]
    mirror = [(i, (i + half) % branches) for i in range(branches)]
    side_ref = side.astype(jnp.int32).reshape(1)
    wanted = jnp.transpose(far_requests.reshape(2, half, cap), (1, 0, 2)).reshape(half, 2 * cap)
    asked = lax.all_to_all(
        wanted, "leaf", split_axis=0, concat_axis=0, axis_index_groups=groups, tiled=True
    )

    if columns == 2:
        place = column.astype(jnp.int32).reshape(1)
        mine, other = sketched_shares(place, sketch, samples, points)
        arrived = lax.ppermute(other, "cols", [(0, 1), (1, 0)])
        partner = lax.ppermute(mine, "leaf", mirror)
        crossed = lax.ppermute(
            other,
            ("leaf", "cols"),
            [(2 * i + c, 2 * ((i + half) % branches) + 1 - c) for i in range(branches) for c in range(2)],
        )
    else:
        z_part = jnp.dot(sketch, samples, precision=highest)
        z_mine = exchange_sum(z_part.reshape(columns, share, leaves * LEAF), "cols")
        z_rows = two_rows(z_mine.reshape(share, leaves, LEAF), share // 2)
        planes = points.reshape(3, leaves, LEAF)
        c_rows = two_rows(
            jnp.concatenate([planes[0:1], planes[2:3], planes[1:2], jnp.zeros_like(planes[0:1])], axis=0), 2
        )
        mine = jnp.concatenate([z_rows.reshape(-1, LANES), c_rows.reshape(-1, LANES)], axis=0)
        partner = lax.ppermute(mine, "leaf", mirror)
        arrived = jnp.zeros((leaves * share // 2, LANES), jnp.float32)
        crossed = arrived

    coords = jnp.transpose(points.reshape(3, leaves, LEAF), (1, 0, 2))
    rows = jnp.transpose(samples.reshape(samp_dev, leaves, LEAF), (1, 2, 0))

    forward = [(i, i + 1) for i in range(branches - 1)]
    backward = [(target, source) for source, target in forward]
    width = max(samp_dev, LEAF)

    def edge(first):
        samples_edge = jnp.transpose(lax.slice_in_dim(samples, first, first + LEAF, axis=1))
        points_edge = lax.slice_in_dim(points, first, first + LEAF, axis=1)
        return jnp.concatenate(
            [
                jnp.pad(samples_edge, ((0, 0), (0, width - samp_dev))),
                jnp.pad(points_edge, ((0, 5), (0, width - LEAF))),
            ],
            axis=0,
        )

    low_edge = lax.ppermute(edge((leaves - 1) * LEAF), "leaf", forward)
    high_edge = lax.ppermute(edge(0), "leaf", backward)
    asked, low_edge, high_edge = lax.optimization_barrier((asked, low_edge, high_edge))

    small_sent = packed_rows(asked, side_ref, mine, arrived, partner, crossed, cap, leaves)
    small_got = lax.all_to_all(
        small_sent, "leaf", split_axis=0, concat_axis=0, axis_index_groups=groups, tiled=True
    )
    total, group_leaf, group_count, group_slots = group_tables(far_slots, far_count)

    rows_out, unused = lax.optimization_barrier((rows, small_sent))
    partner_rows = lax.ppermute(rows_out, "leaf", mirror)

    own_asked = lax.dynamic_slice_in_dim(asked, side * cap, cap, axis=1)
    partner_asked = lax.dynamic_slice_in_dim(asked, (1 - side) * cap, cap, axis=1)
    own_sent = rows_out[own_asked.reshape(-1)].reshape(half, cap, LEAF, samp_dev)
    own_got = lax.all_to_all(
        own_sent, "leaf", split_axis=0, concat_axis=0, axis_index_groups=groups, tiled=True
    )
    own_got = own_got.reshape(half * cap, LEAF, samp_dev)

    z_count = 2 * cap * share // 2
    z_own = small_got[:, :z_count].reshape(half * z_count, LANES)
    c_got = small_got[:, z_count:].reshape(half * 4 * cap, LANES)
    if columns == 2:
        z_other = lax.ppermute(z_own, "cols", [(0, 1), (1, 0)])
    else:
        slots = branches * cap
        z_all = exchange_all(z_own, "cols").reshape(columns, slots, share // 2, 2, LEAF)
        z_all = jnp.transpose(z_all, (1, 0, 3, 2, 4)).reshape(slots, 2, 2, rank // 4, LEAF)
        z_all = jnp.transpose(z_all, (1, 0, 3, 2, 4)).reshape(2, slots * rank // 4, LANES)
        z_own, z_other = z_all[0], z_all[1]
        place = jnp.zeros((1,), jnp.int32)

    targets = jnp.transpose(coords, (0, 2, 1))
    high, low, sketched, gram = kernel_blocks(
        total, group_leaf, group_count, group_slots, place, z_own, z_other, c_got, targets, rank, cap
    )

    levels = leaves.bit_length()
    inverse, ratio, top_inverse, own_child = branch_factors(gram, levels)
    own_child = own_child.reshape(-1, min(samp_dev, LANES))
    weights, leaf_basis = bases(inverse, ratio, top_inverse, sketched)

    low_edge, high_edge, unused = lax.optimization_barrier((low_edge, high_edge, own_child))
    rows_low, rows_high = low_edge[:LEAF, :samp_dev], high_edge[:LEAF, :samp_dev]
    coords_low, coords_high = low_edge[LEAF : LEAF + 3, :LEAF], high_edge[LEAF : LEAF + 3, :LEAF]
    near_rows = jnp.concatenate(
        [rows_low[None], rows, rows_high[None], jnp.zeros_like(rows_low)[None]], axis=0
    )
    near_coords = jnp.concatenate(
        [coords_low[None], coords, coords_high[None], jnp.zeros_like(coords_low)[None]], axis=0
    )
    near_coords = jnp.pad(near_coords, ((0, 0), (0, 5), (0, 0)))
    near_coords = jnp.concatenate([near_coords, near_coords], axis=2)
    near_sample = near_products(near_mask.reshape(-1), near_rows, near_coords, targets)


    own_child, own_got, partner_rows, weights, near_sample = lax.optimization_barrier(
        (own_child, own_got, partner_rows, weights, near_sample)
    )
    payload = payload_rows(partner_asked, partner_rows, own_child)
    arrived = lax.all_to_all(
        payload, "leaf", split_axis=0, concat_axis=0, axis_index_groups=groups, tiled=True
    )
    partner_got = arrived[:, : cap * LEAF].reshape(half * cap, LEAF, samp_dev)
    children = arrived[:, cap * LEAF :]
    mirrored = lax.ppermute(children, "leaf", mirror)
    children = jnp.concatenate(
        [jnp.where(side == 0, children, mirrored), jnp.where(side == 0, mirrored, children)], axis=0
    )
    children = children.reshape(branches, rank, rank)

    far_sample, branch_samples, copies = far_products(
        total, group_leaf, group_slots, side_ref, own_got, partner_got, high, low, weights, branches
    )
    everyone = lax.all_to_all(copies, "leaf", split_axis=0, concat_axis=0, tiled=True)
    children, unused = lax.optimization_barrier((children, branch_samples))
    transfer_t, paths = top_factors(children)
    top_transfer = jnp.swapaxes(transfer_t, 1, 2)
    root_sample = lax.dot_general(
        paths, everyone.reshape(branches * rank, samp_dev), tn_dims, precision=highest
    )
    return (far_sample, near_sample, leaf_basis, branch_samples, top_transfer, root_sample)


def solution(mesh):
    return jax.shard_map(
        on_device,
        mesh=mesh,
        in_specs=(
            P(None, "leaf"),
            P("cols", "leaf"),
            P(None, "cols"),
            P("leaf", None, None),
            P("leaf", None),
            P("leaf"),
            P("leaf", None),
        ),
        out_specs=(
            P("cols", "leaf"),
            P("cols", "leaf"),
            P(None, "leaf"),
            P("leaf", "cols"),
            P(),
            P(None, "cols"),
        ),
        check_vma=False,
    )
```

```python
import functools
import math

import jax
import jax.numpy as jnp
import numpy as np
from jax import lax
from jax.experimental import pallas as pl
from jax.experimental.pallas import tpu as pltpu
from jax.sharding import PartitionSpec as P

LEAF = 64
FAR = 16
GROUP = 4
BATCH = 16
LANES = 128
SUB = 8

length_scale = 0.3
shift_share = 0.05
highest = lax.Precision.HIGHEST
exponent_scale = -math.log2(math.e) / length_scale
vmem_bytes = 56 * 1024 * 1024

nt_dims = (((1,), (1,)), ((), ()))
tn_dims = (((0,), (0,)), ((), ()))


def halves(value):
    high = value.astype(jnp.bfloat16)
    low = (value - high.astype(jnp.float32)).astype(jnp.bfloat16)
    return high, low


def dot(a, b):
    return jnp.dot(a, b, preferred_element_type=jnp.float32)


def dot_exact(a, b):
    return jnp.dot(a, b, precision=highest, preferred_element_type=jnp.float32)


def dot_exact_nt(a, b):
    return lax.dot_general(a, b, nt_dims, precision=highest, preferred_element_type=jnp.float32)


def dot_nt(a, b):
    return lax.dot_general(a, b, nt_dims, preferred_element_type=jnp.float32)


def kernel_half(source_rows, target, lane, valid):
    total = None
    for axis in range(3):
        difference = source_rows[axis : axis + 1, :] - target[:, axis : axis + 1]
        square = difference * difference
        total = square if total is None else total + square
    distance = total * lax.rsqrt(jnp.maximum(total, 1e-30))
    values = jnp.exp2(distance * exponent_scale)
    return jnp.where(lane < valid, values, 0.0)


def blocks_body(
    total_ref, leaf_ref, count_ref, slot_ref, place_ref,
    own_ref, other_ref, coords_ref, target_ref,
    high_ref, low_ref, sketched_ref, gram_ref,
    packed,
    *, rank, cap,
):
    step = pl.program_id(0)
    lane = lax.broadcasted_iota(jnp.int32, (1, LANES), 1)
    first = lane < LEAF

    @pl.when(step == 0)
    def _():
        sketched_ref[...] = jnp.zeros_like(sketched_ref)
        quarter = rank // 4
        slots = packed.shape[0]
        own_at = pl.multiple_of(place_ref[0] * 2 * quarter, quarter)
        other_at = pl.multiple_of((1 - place_ref[0]) * 2 * quarter, quarter)

        def unpack(peer, carry):
            for entry in range(2 * cap):
                slot = (entry // cap) * (slots // 2) + peer * cap + entry % cap
                at = pl.multiple_of((peer * 2 * cap + entry) * quarter, quarter)
                for ref, base in ((own_ref, own_at), (other_ref, other_at)):
                    value = ref[pl.ds(at, quarter), :]
                    turned = pltpu.roll(value, LEAF, 1)
                    packed[slot, pl.ds(base, quarter), :] = jnp.where(first, value, turned)
                    packed[slot, pl.ds(base + quarter, quarter), :] = jnp.where(first, turned, value)
                value = coords_ref[pl.ds((peer * 2 * cap + entry) * 2, 2), :]
                turned = pltpu.roll(value, LEAF, 1)
                packed[slot, rank : rank + 1, :] = jnp.where(first, value, turned)[0:1]
                packed[slot, rank + 1 : rank + 2, :] = jnp.where(first, turned, value)[0:1]
                packed[slot, rank + 2 : rank + 3, :] = jnp.where(first, value, turned)[1:2]
            return carry

        lax.fori_loop(0, slots // (2 * cap), unpack, 0)

    @pl.when(step * BATCH < total_ref[0])
    def _():
        for member in range(BATCH):
            group = step * BATCH + member
            leaf = leaf_ref[group]
            count = count_ref[group]
            slots = [slot_ref[group * GROUP + e] for e in range(GROUP)]
            target = target_ref[leaf]
            z_parts = []
            for half in range(GROUP // 2):
                left = packed[slots[2 * half]]
                right = packed[slots[2 * half + 1]]
                both = jnp.where(first, left, right)
                values = kernel_half(both[rank : rank + 3], target, lane, (count - 2 * half) * LEAF)
                high, low = halves(values)
                high_ref[member, :, half * LANES : (half + 1) * LANES] = high
                low_ref[member, :, half * LANES : (half + 1) * LANES] = low
                z_parts.append(both[:rank])
            z_high, z_low = halves(jnp.concatenate(z_parts, axis=1))
            k_high = high_ref[member]
            k_low = low_ref[member]
            update = dot_nt(z_high, k_high) + (dot_nt(z_low, k_high) + dot_nt(z_high, k_low))
            sketched_ref[leaf] += update

    @pl.when(step == pl.num_programs(0) - 1)
    def _():
        for leaf in range(gram_ref.shape[0]):
            block = sketched_ref[leaf]
            gram_ref[leaf] = dot_exact_nt(block, block)


def kernel_blocks(total, group_leaf, group_count, group_slots, place, own, other, coords, targets, rank, cap):
    leaves = targets.shape[0]
    groups = group_leaf.shape[0]
    slots = coords.shape[0] // 2
    steps = groups // BATCH

    def block_index(step, total_ref, *unused):
        last = (total_ref[0] - 1) // BATCH
        return (jnp.minimum(step, last), 0, 0)

    flat = lambda *unused: (0, 0)
    whole = lambda *unused: (0, 0, 0)
    once = pl.Buffered(1)
    return pl.pallas_call(
        functools.partial(blocks_body, rank=rank, cap=cap),
        grid_spec=pltpu.PrefetchScalarGridSpec(
            num_scalar_prefetch=5,
            grid=(steps,),
            in_specs=[
                pl.BlockSpec(own.shape, flat, pipeline_mode=once),
                pl.BlockSpec(other.shape, flat, pipeline_mode=once),
                pl.BlockSpec(coords.shape, flat, pipeline_mode=once),
                pl.BlockSpec(targets.shape, whole, pipeline_mode=once),
            ],
            out_specs=[
                pl.BlockSpec((BATCH, LEAF, GROUP * LEAF), block_index),
                pl.BlockSpec((BATCH, LEAF, GROUP * LEAF), block_index),
                pl.BlockSpec((leaves, rank, LEAF), whole),
                pl.BlockSpec((leaves, rank, rank), whole),
            ],
            scratch_shapes=[pltpu.VMEM((slots, rank + SUB, LANES), jnp.float32)],
        ),
        out_shape=[
            jax.ShapeDtypeStruct((groups, LEAF, GROUP * LEAF), jnp.bfloat16),
            jax.ShapeDtypeStruct((groups, LEAF, GROUP * LEAF), jnp.bfloat16),
            jax.ShapeDtypeStruct((leaves, rank, LEAF), jnp.float32),
            jax.ShapeDtypeStruct((leaves, rank, rank), jnp.float32),
        ],
        compiler_params=pltpu.CompilerParams(vmem_limit_bytes=vmem_bytes),
        name="kernel_blocks",
        cost_estimate=pl.CostEstimate(
            flops=10**6, bytes_accessed=10**4, transcendentals=0
        ),
    )(total, group_leaf, group_count, group_slots, place, own, other, coords, targets)


def far_body(
    total_ref, leaf_ref, slot_ref, side_ref,
    own_ref, partner_ref, high_ref, low_ref, weights_ref,
    out_ref, projected_ref, copies_ref,
    s_high, s_low, acc,
    *, cap,
):
    step = pl.program_id(0)
    samp_dev = own_ref.shape[2]
    part = own_ref.shape[0]

    @pl.when(step == 0)
    def _():
        acc[...] = jnp.zeros_like(acc)

        def split(slot, carry):
            here = side_ref[0] * part + slot
            there = (1 - side_ref[0]) * part + slot
            s_high[here], s_low[here] = halves(own_ref[slot])
            at = pl.multiple_of((slot % cap) * LEAF, LEAF)
            s_high[there], s_low[there] = halves(partner_ref[slot // cap, pl.ds(at, LEAF), :])
            return carry

        lax.fori_loop(0, part, split, 0, unroll=4)

    @pl.when(step * BATCH < total_ref[0])
    def _():
        for member in range(BATCH):
            group = step * BATCH + member
            leaf = leaf_ref[group]
            slots = [slot_ref[group * GROUP + e] for e in range(GROUP)]
            rows_high = jnp.concatenate([s_high[slot] for slot in slots], axis=0)
            rows_low = jnp.concatenate([s_low[slot] for slot in slots], axis=0)
            k_high = high_ref[member]
            k_low = low_ref[member]
            acc[leaf] += dot(k_high, rows_high) + (dot(k_high, rows_low) + dot(k_low, rows_high))

    @pl.when(step == pl.num_programs(0) - 1)
    def _():
        leaves = acc.shape[0]
        rows = acc[...].reshape(leaves * LEAF, samp_dev)
        projected = dot_exact(weights_ref[...], rows)
        projected_ref[...] = projected
        for branch in range(copies_ref.shape[0]):
            copies_ref[branch] = projected
        for pair in range(leaves // 2):
            block = acc[2 * pair : 2 * pair + 2].reshape(2 * LEAF, samp_dev)
            out_ref[:, 2 * pair * LEAF : 2 * (pair + 1) * LEAF] = block.T


def far_products(total, group_leaf, group_slots, side, own, partner, high, low, weights, branches):
    part, unused, samp_dev = own.shape
    slots = 2 * part
    groups = group_leaf.shape[0]
    points_dev = weights.shape[1]
    leaves = points_dev // LEAF
    steps = groups // BATCH

    def block_index(step, total_ref, *unused):
        last = (total_ref[0] - 1) // BATCH
        return (jnp.minimum(step, last), 0, 0)

    return pl.pallas_call(
        functools.partial(far_body, cap=part // partner.shape[0]),
        grid_spec=pltpu.PrefetchScalarGridSpec(
            num_scalar_prefetch=4,
            grid=(steps,),
            in_specs=[
                pl.BlockSpec(own.shape, lambda *unused: (0, 0, 0), pipeline_mode=pl.Buffered(1)),
                pl.BlockSpec(partner.shape, lambda *unused: (0, 0, 0), pipeline_mode=pl.Buffered(1)),
                pl.BlockSpec((BATCH, LEAF, GROUP * LEAF), block_index),
                pl.BlockSpec((BATCH, LEAF, GROUP * LEAF), block_index),
                pl.BlockSpec(weights.shape, lambda *unused: (0, 0), pipeline_mode=pl.Buffered(1)),
            ],
            out_specs=[
                pl.BlockSpec((samp_dev, points_dev), lambda *unused: (0, 0)),
                pl.BlockSpec((weights.shape[0], samp_dev), lambda *unused: (0, 0)),
                pl.BlockSpec((branches, weights.shape[0], samp_dev), lambda *unused: (0, 0, 0)),
            ],
            scratch_shapes=[
                pltpu.VMEM((slots, LEAF, samp_dev), jnp.bfloat16),
                pltpu.VMEM((slots, LEAF, samp_dev), jnp.bfloat16),
                pltpu.VMEM((leaves, LEAF, samp_dev), jnp.float32),
            ],
        ),
        out_shape=[
            jax.ShapeDtypeStruct((samp_dev, points_dev), jnp.float32),
            jax.ShapeDtypeStruct((weights.shape[0], samp_dev), jnp.float32),
            jax.ShapeDtypeStruct((branches, weights.shape[0], samp_dev), jnp.float32),
        ],
        compiler_params=pltpu.CompilerParams(vmem_limit_bytes=vmem_bytes),
        name="far_products",
        cost_estimate=pl.CostEstimate(
            flops=10**6, bytes_accessed=10**4, transcendentals=0
        ),
    )(total, group_leaf, group_slots, side, own, partner, high, low, weights)


NEAR_LEAVES = 8


def near_body(mask_ref, rows_ref, coords_ref, target_ref, out_ref):
    step = pl.program_id(0)
    samp_dev = rows_ref.shape[2]
    lane = lax.broadcasted_iota(jnp.int32, (1, LANES), 1)
    first = lane < LEAF
    for pair in range(NEAR_LEAVES // 2):
        results = []
        for member in range(2):
            leaf = step * NEAR_LEAVES + 2 * pair + member
            target = target_ref[leaf]
            k_high = []
            k_low = []
            for half in range(2):
                both = jnp.where(first, coords_ref[leaf + 2 * half], coords_ref[leaf + 2 * half + 1])
                values = kernel_half(both, target, lane, LANES)
                left = mask_ref[leaf * 3 + 2 * half].astype(jnp.float32)
                if half == 0:
                    right = mask_ref[leaf * 3 + 1].astype(jnp.float32)
                else:
                    right = jnp.float32(0.0)
                high, low = halves(values * jnp.where(first, left, right))
                k_high.append(high)
                k_low.append(low)
            k_high = jnp.concatenate(k_high, axis=1)
            k_low = jnp.concatenate(k_low, axis=1)
            rows = rows_ref[pl.ds(leaf, 4)].reshape(4 * LEAF, samp_dev)
            rows_high, rows_low = halves(rows)
            results.append(
                dot(k_high, rows_high) + (dot(k_high, rows_low) + dot(k_low, rows_high))
            )
        block = jnp.concatenate(results, axis=0)
        out_ref[:, 2 * pair * LEAF : 2 * (pair + 1) * LEAF] = block.T


def near_products(mask, rows, coords, targets):
    leaves = targets.shape[0]
    samp_dev = rows.shape[2]
    whole = lambda *unused: (0, 0, 0)
    return pl.pallas_call(
        near_body,
        grid_spec=pltpu.PrefetchScalarGridSpec(
            num_scalar_prefetch=1,
            grid=(leaves // NEAR_LEAVES,),
            in_specs=[
                pl.BlockSpec(rows.shape, whole),
                pl.BlockSpec(coords.shape, whole),
                pl.BlockSpec(targets.shape, whole),
            ],
            out_specs=pl.BlockSpec((samp_dev, NEAR_LEAVES * LEAF), lambda step, *unused: (0, step)),
        ),
        out_shape=jax.ShapeDtypeStruct((samp_dev, leaves * LEAF), jnp.float32),
        compiler_params=pltpu.CompilerParams(vmem_limit_bytes=vmem_bytes),
        name="near_products",
        cost_estimate=pl.CostEstimate(
            flops=10**6, bytes_accessed=10**4, transcendentals=0
        ),
    )(mask, rows, coords, targets)


def to_lanes(source, target, rank):
    nodes = source.shape[0] // rank
    target[...] = jnp.zeros_like(target)
    for r in range(rank):
        target[r, :, 0:nodes] = source[pl.ds(r, nodes, stride=rank), :].T


def from_lanes(columns, target, r, nodes, rank):
    target[pl.ds(r, nodes, stride=rank), :] = columns.T[0:nodes]


def eliminate(current, left, inverse, level, rank):
    tiles = rank // SUB
    row = lax.broadcasted_iota(jnp.int32, (SUB, LANES), 0)
    diagonal = [current[j, j : j + 1, :] for j in range(rank)]
    while len(diagonal) > 1:
        diagonal = [diagonal[i] + diagonal[i + 1] for i in range(0, len(diagonal), 2)]
    share = shift_share * diagonal[0] / rank
    shift = share + 1e-06
    a = [
        {t: current[j, SUB * t : SUB * (t + 1), :] for t in range(j // SUB, tiles)}
        for j in range(rank)
    ]
    for j in range(rank):
        a[j][j // SUB] = a[j][j // SUB] + jnp.where(row == j % SUB, shift, 0.0)
    m = []
    scales = []
    for k in range(rank):
        tk, rk = k // SUB, k % SUB
        root = lax.rsqrt(a[k][tk][rk : rk + 1, :])
        scales.append(root)
        reciprocal = root * root
        column = {t: a[k][t] * reciprocal for t in range(tk, tiles)}
        column[tk] = jnp.where(row > rk, column[tk], 0.0)
        for j in range(k + 1, rank):
            factor = a[k][j // SUB][j % SUB : j % SUB + 1, :]
            for t in range(j // SUB, tiles):
                a[j][t] = a[j][t] - column[t] * factor
        for c in range(k):
            factor = m[c][tk][rk : rk + 1, :]
            for t in range(tk, tiles):
                m[c][t] = m[c][t] - column[t] * factor
        fresh = {t: -column[t] for t in range(tk, tiles)}
        fresh[tk] = jnp.where(row == rk, 1.0, fresh[tk])
        m.append(fresh)
        if left is not None:
            for t in range(tiles):
                if t < tk:
                    value = jnp.zeros((SUB, LANES), jnp.float32)
                else:
                    value = a[k][t] * root
                if t == tk:
                    value = jnp.where(row >= rk, value, 0.0)
                left[k, SUB * t : SUB * (t + 1), :] = value
    for t in range(tiles):
        scale = jnp.concatenate(scales[SUB * t : SUB * (t + 1)], axis=0)
        for c in range(rank):
            value = m[c][t] * scale if t >= c // SUB else jnp.zeros((SUB, LANES), jnp.float32)
            inverse[c * rank + SUB * t : c * rank + SUB * (t + 1), :] = value
    return shift, share


def inverse_row(inverse, r, t, rank):
    return inverse[pl.ds(SUB * t * rank + r, SUB, stride=rank), :]


def pair_up(value, level):
    return value + pltpu.roll(value, LANES - lax.shift_left(1, level), 1)


def level_fast(level, levels, current, left, inverse, squared, ratio, child, lowest, rank, child_at):
    tiles = rank // SUB
    row = lax.broadcasted_iota(jnp.int32, (SUB, LANES), 0)
    shift, share = eliminate(current, left, inverse, level, rank)
    lowest[...] = jnp.minimum(lowest[...], share)

    for block in range(tiles):
        sums = [[None] * tiles for _ in range(SUB)]
        for r in range(SUB * block, rank):
            parts = [inverse_row(inverse, r, t, rank) for t in range(block, r // SUB + 1)]
            for q in range(SUB):
                if SUB * block + q > r:
                    continue
                factor = parts[0][q : q + 1, :]
                for t in range(block, r // SUB + 1):
                    term = parts[t - block] * factor
                    sums[q][t] = term if sums[q][t] is None else sums[q][t] + term
        for q in range(SUB):
            at = (SUB * block + q) * rank
            for t in range(block, tiles):
                squared[at + SUB * t : at + SUB * (t + 1), :] = sums[q][t]

    if child is not None:
        @pl.when(child_at(level))
        def _():
            for r in range(rank):
                for t in range(tiles):
                    value = left[r, SUB * t : SUB * (t + 1), :]
                    if t <= r // SUB:
                        value = value - shift * inverse_row(inverse, r, t, rank)
                    child[r, SUB * t : SUB * (t + 1), :] = value

    for q in range(rank):
        for t in range(tiles):
            if t >= q // SUB:
                value = squared[q * rank + SUB * t : q * rank + SUB * (t + 1), :]
            else:
                value = squared[pl.ds(SUB * t * rank + q, SUB, stride=rank), :]
            value = -shift * value
            if t == q // SUB:
                value = value + jnp.where(row == q % SUB, 1.0, 0.0)
            if ratio is not None:
                ratio[level, q, SUB * t : SUB * (t + 1), :] = value
            here = current[q, SUB * t : SUB * (t + 1), :] - shift * value
            current[q, SUB * t : SUB * (t + 1), :] = pair_up(here, level)


def level_plain(level, levels, current, left, inverse, squared, ratio, child, lowest, rank, child_at):
    tiles = rank // SUB
    eliminate(current, left, inverse, level, rank)

    def products(out, count, left_of, right_of):
        def block_step(block, carry):
            offset = pl.multiple_of(block * SUB, SUB)
            sums = [[None] * tiles for _ in range(SUB)]
            for r in range(count):
                parts = [left_of(r, t) for t in range(tiles)]
                heads = right_of(r, offset)
                for q in range(SUB):
                    for t in range(tiles):
                        term = parts[t] * heads[q : q + 1, :]
                        sums[q][t] = term if sums[q][t] is None else sums[q][t] + term
            for q in range(SUB):
                for t in range(tiles):
                    out(offset + q, t, sums[q][t])
            return carry

        lax.fori_loop(0, tiles, block_step, 0)

    def tile(t):
        return slice(SUB * t, SUB * (t + 1))

    def put_child(r, t, value):
        squared[pl.ds(pl.multiple_of(r * rank + SUB * t, SUB), SUB), :] = value

    products(
        put_child, rank,
        lambda k, t: current[k, tile(t), :],
        lambda k, offset: inverse[pl.ds(pl.multiple_of(k * rank + offset, SUB), SUB), :],
    )
    if child is not None:
        @pl.when(child_at(level))
        def _():
            for r in range(rank):
                for t in range(tiles):
                    child[r, tile(t), :] = squared[r * rank + SUB * t : r * rank + SUB * (t + 1), :]

    def child_part(r, t):
        return squared[r * rank + SUB * t : r * rank + SUB * (t + 1), :]

    def put_current(q, t, value):
        current[q, tile(t), :] = pair_up(value, level)

    if ratio is not None:
        def put_ratio(c, t, value):
            ratio[level, c, tile(t), :] = value

        def inverse_head(r, offset):
            return inverse[pl.ds(offset * rank + r, SUB, stride=rank), :]

        products(put_ratio, rank, child_part, inverse_head)
    products(
        put_current, rank, child_part,
        lambda r, offset: squared[pl.ds(pl.multiple_of(r * rank + offset, SUB), SUB), :],
    )


def run_levels(source, levels, nodes, current, left, inverse, squared, ratio, child, lowest, rank, child_at, finish):
    lowest[...] = jnp.full((1, LANES), 1.0, jnp.float32)

    def sweep(level_step):
        to_lanes(source, current, rank)

        def body(level, carry):
            level_step(level, levels, current, left, inverse, squared, ratio, child, lowest, rank, child_at)
            finish(level)
            return carry

        lax.fori_loop(0, levels, body, 0)

    sweep(level_fast)
    lane = lax.broadcasted_iota(jnp.int32, (1, LANES), 1)
    least = jnp.min(jnp.where(lane < nodes, lowest[...], 1.0))

    @pl.when(least < 2e-06)
    def _():
        sweep(level_plain)


def branch_body(gram_ref, inverse_ref, ratio_ref, top_ref, child_ref, current, left, inverse, squared, child, lowest, *, rank, levels):
    nodes = gram_ref.shape[0] // rank

    def finish(level):
        @pl.when(level == 0)
        def _():
            for c in range(rank):
                inverse_ref[c] = inverse[c * rank : (c + 1) * rank, :]

        @pl.when(level == levels - 1)
        def _():
            for r in range(rank):
                child_ref[r : r + 1, :] = child[r].T[0:1, :]
                top_ref[r : r + 1, :] = jnp.concatenate(
                    [inverse_row(inverse, r, t, rank) for t in range(rank // SUB)], axis=0
                ).T[0:1, :]

    run_levels(
        gram_ref, levels, nodes, current, left, inverse, squared, ratio_ref, child, lowest, rank,
        lambda level: level == levels - 1, finish,
    )


vmem_spec = pl.BlockSpec(memory_space=pltpu.VMEM)


def tree_scratch(rank):
    return [
        pltpu.VMEM((rank, rank, LANES), jnp.float32),
        pltpu.VMEM((rank, rank, LANES), jnp.float32),
        pltpu.VMEM((rank * rank, LANES), jnp.float32),
        pltpu.VMEM((rank * rank, LANES), jnp.float32),
        pltpu.VMEM((rank, rank, LANES), jnp.float32),
        pltpu.VMEM((1, LANES), jnp.float32),
    ]


def branch_factors(gram, levels):
    leaves, rank, unused = gram.shape
    return pl.pallas_call(
        functools.partial(branch_body, rank=rank, levels=levels),
        in_specs=[vmem_spec],
        out_specs=[vmem_spec] * 4,
        out_shape=[
            jax.ShapeDtypeStruct((rank, rank, LANES), jnp.float32),
            jax.ShapeDtypeStruct((levels, rank, rank, LANES), jnp.float32),
            jax.ShapeDtypeStruct((rank, rank), jnp.float32),
            jax.ShapeDtypeStruct((rank, rank), jnp.float32),
        ],
        scratch_shapes=tree_scratch(rank),
        compiler_params=pltpu.CompilerParams(vmem_limit_bytes=vmem_bytes),
        name="branch_factors",
        cost_estimate=pl.CostEstimate(flops=10**6, bytes_accessed=10**4, transcendentals=0),
    )(gram.reshape(leaves * rank, rank))


def basis_body(inverse_ref, ratio_ref, top_ref, sketched_ref, weights_ref, basis_ref, natural, *, rank, levels):
    leaves = sketched_ref.shape[0]
    upper = [top_ref[...]]
    for level in range(levels - 2, -1, -1):
        stride = 2**level
        for c in range(rank):
            from_lanes(ratio_ref[level, c], natural, c, leaves, rank)
        fresh = []
        for node in range(leaves // stride):
            block = natural[node * stride * rank : (node * stride + 1) * rank, :]
            fresh.append(dot_exact(upper[node // 2], block))
        upper = fresh
    for r in range(rank):
        from_lanes(inverse_ref[r], natural, r, leaves, rank)
    for pair in range(leaves // 2):
        results = []
        for leaf in (2 * pair, 2 * pair + 1):
            block = sketched_ref[leaf]
            own = lax.dot_general(
                natural[leaf * rank : (leaf + 1) * rank, :], block, tn_dims,
                precision=highest, preferred_element_type=jnp.float32,
            )
            results.append(jnp.concatenate([dot_exact(upper[leaf], block), own], axis=0))
        both = jnp.concatenate(results, axis=1)
        weights_ref[:, pair * 2 * LEAF : (pair + 1) * 2 * LEAF] = both[:rank]
        basis_ref[:, pair * 2 * LEAF : (pair + 1) * 2 * LEAF] = both[rank:]


def bases(inverse, ratio, top, sketched):
    leaves, rank, unused = sketched.shape
    levels = ratio.shape[0]
    shape = jax.ShapeDtypeStruct((rank, leaves * LEAF), jnp.float32)
    return pl.pallas_call(
        functools.partial(basis_body, rank=rank, levels=levels),
        in_specs=[vmem_spec] * 4,
        out_specs=[vmem_spec] * 2,
        out_shape=[shape, shape],
        scratch_shapes=[pltpu.VMEM((leaves * rank, rank), jnp.float32)],
        compiler_params=pltpu.CompilerParams(vmem_limit_bytes=vmem_bytes),
        name="bases",
        cost_estimate=pl.CostEstimate(flops=10**6, bytes_accessed=10**4, transcendentals=0),
    )(inverse, ratio, top, sketched)


def top_body(children_ref, transfer_ref, paths_ref, source, current, left, inverse, squared, child, lowest, nat_inverse, nat_child, *, rank, levels):
    nodes = children_ref.shape[0] // 2
    for node in range(nodes):
        both = children_ref[2 * node : 2 * node + 2].reshape(2 * rank, rank)
        source[node * rank : (node + 1) * rank, :] = lax.dot_general(
            both, both, tn_dims, precision=highest, preferred_element_type=jnp.float32
        )

    def finish(level):
        for r in range(rank):
            from_lanes(child[r], nat_child.at[level], r, nodes, rank)
            from_lanes(inverse[r * rank : (r + 1) * rank, :], nat_inverse.at[level], r, nodes, rank)

    run_levels(
        source, levels, nodes, current, left, inverse, squared, None, child, lowest, rank,
        lambda level: level >= 0, finish,
    )
    offset = 0
    for level in range(levels):
        for node in range(nodes >> level):
            if level == 0:
                stacked = children_ref[2 * node : 2 * node + 2].reshape(2 * rank, rank)
            else:
                first = 2 * node << level - 1
                second = 2 * node + 1 << level - 1
                stacked = jnp.concatenate(
                    [
                        nat_child[level - 1, first * rank : (first + 1) * rank, :],
                        nat_child[level - 1, second * rank : (second + 1) * rank, :],
                    ],
                    axis=0,
                )
            at = (node << level) * rank
            transfer_ref[offset + node] = lax.dot_general(
                nat_inverse[level, at : at + rank, :], stacked, (((0,), (1,)), ((), ())),
                precision=highest, preferred_element_type=jnp.float32,
            )
        offset += nodes >> level
    above = [None]
    for level in range(levels - 1, -1, -1):
        offset -= nodes >> level
        fresh = []
        for node in range(nodes >> level):
            both = transfer_ref[offset + node]
            if above[0] is None:
                both = both.T
            else:
                both = lax.dot_general(
                    both, above[node], tn_dims, precision=highest, preferred_element_type=jnp.float32
                )
            fresh += [both[:rank], both[rank:]]
        above = fresh
    for branch in range(2 * nodes):
        paths_ref[branch * rank : (branch + 1) * rank, :] = above[branch]


def top_factors(children):
    branches, rank, unused = children.shape
    levels = branches.bit_length() - 1
    nodes = branches // 2
    natural = pltpu.VMEM((levels, nodes * rank, rank), jnp.float32)
    return pl.pallas_call(
        functools.partial(top_body, rank=rank, levels=levels),
        in_specs=[vmem_spec],
        out_specs=[vmem_spec] * 2,
        out_shape=[
            jax.ShapeDtypeStruct((branches - 1, rank, 2 * rank), jnp.float32),
            jax.ShapeDtypeStruct((branches * rank, rank), jnp.float32),
        ],
        scratch_shapes=[pltpu.VMEM((nodes * rank, rank), jnp.float32)]
        + tree_scratch(rank)
        + [natural, natural],
        compiler_params=pltpu.CompilerParams(vmem_limit_bytes=vmem_bytes),
        name="top_factors",
        cost_estimate=pl.CostEstimate(flops=10**10, bytes_accessed=10**7, transcendentals=0),
    )(children)


def exchange_sum(pieces, axis):
    count = pieces.shape[0]
    me = lax.axis_index(axis)
    mine = lax.dynamic_index_in_dim(pieces, me, 0, keepdims=False)
    for step in range(1, count):
        outgoing = lax.dynamic_index_in_dim(pieces, (me + step) % count, 0, keepdims=False)
        mine = mine + lax.ppermute(
            outgoing, axis, [(i, (i + step) % count) for i in range(count)]
        )
    return mine


def exchange_all(piece, axis):
    count = lax.axis_size(axis)
    me = lax.axis_index(axis)
    if count == 2:
        other = lax.ppermute(piece, axis, [(0, 1), (1, 0)])
        return jnp.stack([jnp.where(me == 0, piece, other), jnp.where(me == 0, other, piece)])
    result = jnp.zeros((count,) + piece.shape, piece.dtype)
    result = lax.dynamic_update_index_in_dim(result, piece, me, 0)
    for step in range(1, count):
        arrived = lax.ppermute(piece, axis, [(i, (i + step) % count) for i in range(count)])
        result = lax.dynamic_update_index_in_dim(result, arrived, (me - step) % count, 0)
    return result


def group_tables(far_slots, far_count):
    leaves = far_slots.shape[0]
    groups = leaves * FAR // GROUP
    per_leaf = (far_count + GROUP - 1) // GROUP
    before = jnp.arange(leaves)[:, None] >= jnp.arange(leaves)[None, :]
    ends = jnp.sum(jnp.where(before, per_leaf[None, :], 0), axis=1)
    total = ends[leaves - 1 :]
    ids = jnp.arange(groups, dtype=jnp.int32)
    leaf = jnp.minimum(jnp.sum((ends[None, :] <= ids[:, None]).astype(jnp.int32), axis=1), leaves - 1)
    hit = leaf[:, None] == jnp.arange(leaves)[None, :]
    start = jnp.sum(jnp.where(hit, (ends - per_leaf)[None, :], 0), axis=1)
    length = jnp.sum(jnp.where(hit, far_count[None, :], 0), axis=1)
    sub = ids - start
    count = jnp.where(ids < total, jnp.clip(length - GROUP * sub, 0, GROUP), 0)
    first = jnp.minimum(sub, FAR // GROUP - 1)
    slots = far_slots.reshape(leaves * FAR // GROUP, GROUP)[leaf * (FAR // GROUP) + first]
    return (
        total.astype(jnp.int32),
        leaf.astype(jnp.int32),
        count.astype(jnp.int32),
        slots.reshape(-1).astype(jnp.int32),
    )


def sketch_body(place_ref, sketch_ref, samples_ref, points_ref, mine_ref, other_ref):
    product = dot_exact(sketch_ref[...], samples_ref[...])
    rank, points_dev = product.shape
    quarter = rank // 4
    first = lax.broadcasted_iota(jnp.int32, (1, LANES), 1) < LEAF
    swap = place_ref[0] == 1
    leaves = points_dev // LEAF

    def interleave(low, high):
        even = jnp.where(first, low, pltpu.roll(high, LEAF, 1))
        odd = jnp.where(first, pltpu.roll(low, LEAF, 1), high)
        return even, odd

    for pair in range(leaves // 2):
        lanes = slice(pair * LANES, (pair + 1) * LANES)
        shares = []
        for share in range(2):
            base = 2 * quarter * share
            shares.append(
                interleave(product[base : base + quarter, lanes], product[base + quarter : base + 2 * quarter, lanes])
            )
        for member in range(2):
            at = (2 * pair + member) * quarter
            mine_ref[at : at + quarter, :] = jnp.where(swap, shares[1][member], shares[0][member])
            other_ref[at : at + quarter, :] = jnp.where(swap, shares[0][member], shares[1][member])
        x = points_ref[0:1, lanes]
        y = points_ref[1:2, lanes]
        z = points_ref[2:3, lanes]
        xy = interleave(x, y)
        zs = interleave(z, jnp.zeros_like(z))
        for member in range(2):
            at = leaves * quarter + (2 * pair + member) * 2
            mine_ref[at : at + 1, :] = xy[member]
            mine_ref[at + 1 : at + 2, :] = zs[member]


def sketched_shares(place, sketch, samples, points):
    rank = sketch.shape[0]
    leaves = samples.shape[1] // LEAF
    return pl.pallas_call(
        sketch_body,
        in_specs=[pl.BlockSpec(memory_space=pltpu.SMEM)] + [vmem_spec] * 3,
        out_specs=[vmem_spec] * 2,
        out_shape=[
            jax.ShapeDtypeStruct((leaves * (rank // 4 + 2), LANES), jnp.float32),
            jax.ShapeDtypeStruct((leaves * rank // 4, LANES), jnp.float32),
        ],
        compiler_params=pltpu.CompilerParams(vmem_limit_bytes=vmem_bytes),
        name="sketched_shares",
        cost_estimate=pl.CostEstimate(flops=10**6, bytes_accessed=10**4, transcendentals=0),
    )(place, sketch, samples, points)


def pack_body(asked_ref, side_ref, mine_ref, arrived_ref, partner_ref, crossed_ref, out_ref, *, cap, leaves):
    z_rows = arrived_ref.shape[0] // leaves
    side = side_ref[0]

    def one(peer, carry):
        for entry in range(2 * cap):
            leaf = asked_ref[peer, entry]
            here = side == entry // cap
            at = pl.ds(leaf * z_rows, z_rows)
            out_ref[peer, z_rows * entry : z_rows * (entry + 1), :] = jnp.where(
                here, mine_ref[at, :] + arrived_ref[at, :], partner_ref[at, :] + crossed_ref[at, :]
            )
            base = z_rows * 2 * cap + 2 * entry
            at = pl.ds(leaves * z_rows + leaf * 2, 2)
            out_ref[peer, base : base + 2, :] = jnp.where(here, mine_ref[at, :], partner_ref[at, :])
        return carry

    lax.fori_loop(0, out_ref.shape[0], one, 0)


def packed_rows(asked, side, mine, arrived, partner, crossed, cap, leaves):
    z_rows = arrived.shape[0] // leaves
    return pl.pallas_call(
        functools.partial(pack_body, cap=cap, leaves=leaves),
        in_specs=[pl.BlockSpec(memory_space=pltpu.SMEM)] * 2 + [vmem_spec] * 4,
        out_specs=vmem_spec,
        out_shape=jax.ShapeDtypeStruct((asked.shape[0], 2 * cap * (z_rows + 2), LANES), jnp.float32),
        compiler_params=pltpu.CompilerParams(vmem_limit_bytes=vmem_bytes),
        name="packed_rows",
    )(asked, side, mine, arrived, partner, crossed)


def payload_body(asked_ref, early_ref, late_ref, child_ref, out_ref, *, cap):
    early = early_ref.shape[0]

    def one(peer, carry):
        for entry in range(cap):
            leaf = asked_ref[peer, entry]
            first = early_ref[jnp.minimum(leaf, early - 1)]
            second = late_ref[jnp.maximum(leaf - early, 0)]
            out_ref[peer, LEAF * entry : LEAF * (entry + 1), :] = jnp.where(leaf < early, first, second)
        out_ref[peer, LEAF * cap :, :] = child_ref[...]
        return carry

    lax.fori_loop(0, out_ref.shape[0], one, 0)


def payload_rows(asked, early, late, child):
    half, cap = asked.shape
    return pl.pallas_call(
        functools.partial(payload_body, cap=cap),
        in_specs=[pl.BlockSpec(memory_space=pltpu.SMEM)] + [vmem_spec] * 3,
        out_specs=vmem_spec,
        out_shape=jax.ShapeDtypeStruct((half, cap * LEAF + child.shape[0], late.shape[2]), jnp.float32),
        compiler_params=pltpu.CompilerParams(vmem_limit_bytes=vmem_bytes),
        name="payload_rows",
    )(asked, early, late, child)


def two_rows(values, rows):
    leaves = values.shape[1]
    split = jnp.transpose(values.reshape(2, rows, leaves, LEAF), (2, 1, 0, 3))
    return split.reshape(leaves, rows, 2 * LEAF)


def on_device(points, samples, sketch, far_requests, far_slots, far_count, near_mask):
    samp_dev = samples.shape[0]
    leaves = samples.shape[1] // LEAF
    rank = sketch.shape[0]
    branches = lax.axis_size("leaf")
    columns = lax.axis_size("cols")
    cap = far_requests.shape[2]
    share = rank // columns
    me = lax.axis_index("leaf")
    column = lax.axis_index("cols")

    half = branches // 2
    side = me // half
    groups = [list(range(half)), list(range(half, branches))]
    mirror = [(i, (i + half) % branches) for i in range(branches)]
    side_ref = side.astype(jnp.int32).reshape(1)
    wanted = jnp.transpose(far_requests.reshape(2, half, cap), (1, 0, 2)).reshape(half, 2 * cap)
    asked = lax.all_to_all(
        wanted, "leaf", split_axis=0, concat_axis=0, axis_index_groups=groups, tiled=True
    )

    if columns == 2:
        place = column.astype(jnp.int32).reshape(1)
        mine, other = sketched_shares(place, sketch, samples, points)
        arrived = lax.ppermute(other, "cols", [(0, 1), (1, 0)])
        partner = lax.ppermute(mine, "leaf", mirror)
        crossed = lax.ppermute(
            other,
            ("leaf", "cols"),
            [(2 * i + c, 2 * ((i + half) % branches) + 1 - c) for i in range(branches) for c in range(2)],
        )
    else:
        z_part = jnp.dot(sketch, samples, precision=highest)
        z_mine = exchange_sum(z_part.reshape(columns, share, leaves * LEAF), "cols")
        z_rows = two_rows(z_mine.reshape(share, leaves, LEAF), share // 2)
        planes = points.reshape(3, leaves, LEAF)
        c_rows = two_rows(
            jnp.concatenate([planes[0:1], planes[2:3], planes[1:2], jnp.zeros_like(planes[0:1])], axis=0), 2
        )
        mine = jnp.concatenate([z_rows.reshape(-1, LANES), c_rows.reshape(-1, LANES)], axis=0)
        partner = lax.ppermute(mine, "leaf", mirror)
        arrived = jnp.zeros((leaves * share // 2, LANES), jnp.float32)
        crossed = arrived

    coords = jnp.transpose(points.reshape(3, leaves, LEAF), (1, 0, 2))
    rows = jnp.transpose(samples.reshape(samp_dev, leaves, LEAF), (1, 2, 0))

    small_sent = packed_rows(asked, side_ref, mine, arrived, partner, crossed, cap, leaves)
    small_got = lax.all_to_all(
        small_sent, "leaf", split_axis=0, concat_axis=0, axis_index_groups=groups, tiled=True
    )
    total, group_leaf, group_count, group_slots = group_tables(far_slots, far_count)

    early = leaves // 8
    rows_out, unused = lax.optimization_barrier((rows, small_sent))
    partner_early = lax.ppermute(rows_out[:early], "leaf", mirror)
    partner_late = lax.ppermute(rows_out[early:], "leaf", mirror)

    forward = [(i, i + 1) for i in range(branches - 1)]
    backward = [(target, source) for source, target in forward]
    width = max(samp_dev, LEAF)

    def edge(first):
        samples_edge = jnp.transpose(lax.slice_in_dim(samples, first, first + LEAF, axis=1))
        points_edge = lax.slice_in_dim(points, first, first + LEAF, axis=1)
        return jnp.concatenate(
            [
                jnp.pad(samples_edge, ((0, 0), (0, width - samp_dev))),
                jnp.pad(points_edge, ((0, 5), (0, width - LEAF))),
            ],
            axis=0,
        )

    last, first, unused = lax.optimization_barrier((edge((leaves - 1) * LEAF), edge(0), small_sent))
    low_edge = lax.ppermute(last, "leaf", forward)
    high_edge = lax.ppermute(first, "leaf", backward)

    own_asked = lax.dynamic_slice_in_dim(asked, side * cap, cap, axis=1)
    partner_asked = lax.dynamic_slice_in_dim(asked, (1 - side) * cap, cap, axis=1)
    own_sent = rows_out[own_asked.reshape(-1)].reshape(half, cap, LEAF, samp_dev)
    own_sent, partner_early, total, group_leaf, group_count, group_slots = lax.optimization_barrier(
        (own_sent, partner_early, total, group_leaf, group_count, group_slots)
    )
    own_got = lax.all_to_all(
        own_sent, "leaf", split_axis=0, concat_axis=0, axis_index_groups=groups, tiled=True
    )
    own_got = own_got.reshape(half * cap, LEAF, samp_dev)

    z_count = 2 * cap * share // 2
    z_own = small_got[:, :z_count].reshape(half * z_count, LANES)
    c_got = small_got[:, z_count:].reshape(half * 4 * cap, LANES)
    if columns == 2:
        z_other = lax.ppermute(z_own, "cols", [(0, 1), (1, 0)])
    else:
        slots = branches * cap
        z_all = exchange_all(z_own, "cols").reshape(columns, slots, share // 2, 2, LEAF)
        z_all = jnp.transpose(z_all, (1, 0, 3, 2, 4)).reshape(slots, 2, 2, rank // 4, LEAF)
        z_all = jnp.transpose(z_all, (1, 0, 3, 2, 4)).reshape(2, slots * rank // 4, LANES)
        z_own, z_other = z_all[0], z_all[1]
        place = jnp.zeros((1,), jnp.int32)

    targets = jnp.transpose(coords, (0, 2, 1))
    high, low, sketched, gram = kernel_blocks(
        total, group_leaf, group_count, group_slots, place, z_own, z_other, c_got, targets, rank, cap
    )

    levels = leaves.bit_length()
    inverse, ratio, top_inverse, own_child = branch_factors(gram, levels)
    own_child = own_child.reshape(-1, min(samp_dev, LANES))
    own_child, own_got, partner_late = lax.optimization_barrier((own_child, own_got, partner_late))
    payload = payload_rows(partner_asked, partner_early, partner_late, own_child)
    arrived = lax.all_to_all(
        payload, "leaf", split_axis=0, concat_axis=0, axis_index_groups=groups, tiled=True
    )
    ratio, low_edge, high_edge, unused = lax.optimization_barrier((ratio, low_edge, high_edge, payload))
    weights, leaf_basis = bases(inverse, ratio, top_inverse, sketched)

    rows_low, rows_high = low_edge[:LEAF, :samp_dev], high_edge[:LEAF, :samp_dev]
    coords_low, coords_high = low_edge[LEAF : LEAF + 3, :LEAF], high_edge[LEAF : LEAF + 3, :LEAF]
    near_rows = jnp.concatenate(
        [rows_low[None], rows, rows_high[None], jnp.zeros_like(rows_low)[None]], axis=0
    )
    near_coords = jnp.concatenate(
        [coords_low[None], coords, coords_high[None], jnp.zeros_like(coords_low)[None]], axis=0
    )
    near_coords = jnp.pad(near_coords, ((0, 0), (0, 5), (0, 0)))
    near_coords = jnp.concatenate([near_coords, near_coords], axis=2)
    near_sample = near_products(near_mask.reshape(-1), near_rows, near_coords, targets)


    children = arrived[:, cap * LEAF :]
    mirrored = lax.ppermute(children, "leaf", mirror)
    children = jnp.concatenate(
        [jnp.where(side == 0, children, mirrored), jnp.where(side == 0, mirrored, children)], axis=0
    )
    children = children.reshape(branches, rank, rank)

    weights, near_sample = lax.optimization_barrier((weights, near_sample))
    far_sample, branch_samples, copies = far_products(
        total, group_leaf, group_slots, side_ref, own_got, arrived, high, low, weights, branches
    )
    everyone = lax.all_to_all(copies, "leaf", split_axis=0, concat_axis=0, tiled=True)
    children, unused = lax.optimization_barrier((children, branch_samples))
    transfer_t, paths = top_factors(children)
    top_transfer = jnp.swapaxes(transfer_t, 1, 2)
    root_sample = lax.dot_general(
        paths, everyone.reshape(branches * rank, samp_dev), tn_dims, precision=highest
    )
    return (far_sample, near_sample, leaf_basis, branch_samples, top_transfer, root_sample)


def solution(mesh):
    return jax.shard_map(
        on_device,
        mesh=mesh,
        in_specs=(
            P(None, "leaf"),
            P("cols", "leaf"),
            P(None, "cols"),
            P("leaf", None, None),
            P("leaf", None),
            P("leaf"),
            P("leaf", None),
        ),
        out_specs=(
            P("cols", "leaf"),
            P("cols", "leaf"),
            P(None, "leaf"),
            P("leaf", "cols"),
            P(),
            P(None, "cols"),
        ),
        check_vma=False,
    )
```

```python
import functools
import math

import jax
import jax.numpy as jnp
import numpy as np
from jax import lax
from jax.experimental import pallas as pl
from jax.experimental.pallas import tpu as pltpu
from jax.sharding import PartitionSpec as P

LEAF = 64
FAR = 16
GROUP = 4
BATCH = 16
LANES = 128
SUB = 8

length_scale = 0.3
shift_share = 0.05
highest = lax.Precision.HIGHEST
exponent_scale = -math.log2(math.e) / length_scale
vmem_bytes = 56 * 1024 * 1024

nt_dims = (((1,), (1,)), ((), ()))
tn_dims = (((0,), (0,)), ((), ()))


def halves(value):
    high = value.astype(jnp.bfloat16)
    low = (value - high.astype(jnp.float32)).astype(jnp.bfloat16)
    return high, low


def dot(a, b):
    return jnp.dot(a, b, preferred_element_type=jnp.float32)


def dot_exact(a, b):
    return jnp.dot(a, b, precision=highest, preferred_element_type=jnp.float32)


def dot_exact_nt(a, b):
    return lax.dot_general(a, b, nt_dims, precision=highest, preferred_element_type=jnp.float32)


def dot_nt(a, b):
    return lax.dot_general(a, b, nt_dims, preferred_element_type=jnp.float32)


def kernel_half(source_rows, target, lane, valid):
    total = None
    for axis in range(3):
        difference = source_rows[axis : axis + 1, :] - target[:, axis : axis + 1]
        square = difference * difference
        total = square if total is None else total + square
    distance = total * lax.rsqrt(jnp.maximum(total, 1e-30))
    values = jnp.exp2(distance * exponent_scale)
    return jnp.where(lane < valid, values, 0.0)


def blocks_body(
    total_ref, leaf_ref, count_ref, slot_ref, place_ref,
    own_ref, other_ref, target_ref,
    high_ref, low_ref, sketched_ref, gram_ref,
    packed,
    *, rank, cap,
):
    step = pl.program_id(0)
    lane = lax.broadcasted_iota(jnp.int32, (1, LANES), 1)
    first = lane < LEAF

    @pl.when(step == 0)
    def _():
        sketched_ref[...] = jnp.zeros_like(sketched_ref)
        quarter = rank // 4
        slots = packed.shape[0]
        own_at = pl.multiple_of(place_ref[0] * 2 * quarter, quarter)
        other_at = pl.multiple_of((1 - place_ref[0]) * 2 * quarter, quarter)

        def unpack(peer, carry):
            for entry in range(2 * cap):
                slot = (entry // cap) * (slots // 2) + peer * cap + entry % cap
                at = entry * quarter
                for ref, base in ((own_ref, own_at), (other_ref, other_at)):
                    value = ref[peer, at : at + quarter, :]
                    turned = pltpu.roll(value, LEAF, 1)
                    packed[slot, pl.ds(base, quarter), :] = jnp.where(first, value, turned)
                    packed[slot, pl.ds(base + quarter, quarter), :] = jnp.where(first, turned, value)
                at = 2 * cap * quarter + 2 * entry
                value = own_ref[peer, at : at + 2, :]
                turned = pltpu.roll(value, LEAF, 1)
                packed[slot, rank : rank + 1, :] = jnp.where(first, value, turned)[0:1]
                packed[slot, rank + 1 : rank + 2, :] = jnp.where(first, turned, value)[0:1]
                packed[slot, rank + 2 : rank + 3, :] = jnp.where(first, value, turned)[1:2]
            return carry

        lax.fori_loop(0, slots // (2 * cap), unpack, 0)

    @pl.when(step * BATCH < total_ref[0])
    def _():
        for member in range(BATCH):
            group = step * BATCH + member
            leaf = leaf_ref[group]
            count = count_ref[group]
            slots = [slot_ref[group * GROUP + e] for e in range(GROUP)]
            target = target_ref[leaf]
            z_parts = []
            for half in range(GROUP // 2):
                left = packed[slots[2 * half]]
                right = packed[slots[2 * half + 1]]
                both = jnp.where(first, left, right)
                values = kernel_half(both[rank : rank + 3], target, lane, (count - 2 * half) * LEAF)
                high, low = halves(values)
                high_ref[member, :, half * LANES : (half + 1) * LANES] = high
                low_ref[member, :, half * LANES : (half + 1) * LANES] = low
                z_parts.append(both[:rank])
            z_high, z_low = halves(jnp.concatenate(z_parts, axis=1))
            k_high = high_ref[member]
            k_low = low_ref[member]
            both = dot_nt(jnp.concatenate([z_high, z_low], axis=0), k_high)
            update = both[:rank] + (both[rank:] + dot_nt(z_high, k_low))
            sketched_ref[leaf] += update

    @pl.when(step == pl.num_programs(0) - 1)
    def _():
        for leaf in range(gram_ref.shape[0]):
            block = sketched_ref[leaf]
            gram_ref[leaf] = dot_exact_nt(block, block)


def kernel_blocks(total, group_leaf, group_count, group_slots, place, own, other, targets, rank, cap):
    leaves = targets.shape[0]
    groups = group_leaf.shape[0]
    slots = own.shape[0] * 2 * cap
    steps = groups // BATCH

    def block_index(step, total_ref, *unused):
        last = (total_ref[0] - 1) // BATCH
        return (jnp.minimum(step, last), 0, 0)

    whole = lambda *unused: (0, 0, 0)
    once = pl.Buffered(1)
    return pl.pallas_call(
        functools.partial(blocks_body, rank=rank, cap=cap),
        grid_spec=pltpu.PrefetchScalarGridSpec(
            num_scalar_prefetch=5,
            grid=(steps,),
            in_specs=[
                pl.BlockSpec(own.shape, whole, pipeline_mode=once),
                pl.BlockSpec(other.shape, whole, pipeline_mode=once),
                pl.BlockSpec(targets.shape, whole, pipeline_mode=once),
            ],
            out_specs=[
                pl.BlockSpec((BATCH, LEAF, GROUP * LEAF), block_index),
                pl.BlockSpec((BATCH, LEAF, GROUP * LEAF), block_index),
                pl.BlockSpec((leaves, rank, LEAF), whole),
                pl.BlockSpec((leaves, rank, rank), whole),
            ],
            scratch_shapes=[pltpu.VMEM((slots, rank + SUB, LANES), jnp.float32)],
        ),
        out_shape=[
            jax.ShapeDtypeStruct((groups, LEAF, GROUP * LEAF), jnp.bfloat16),
            jax.ShapeDtypeStruct((groups, LEAF, GROUP * LEAF), jnp.bfloat16),
            jax.ShapeDtypeStruct((leaves, rank, LEAF), jnp.float32),
            jax.ShapeDtypeStruct((leaves, rank, rank), jnp.float32),
        ],
        compiler_params=pltpu.CompilerParams(vmem_limit_bytes=vmem_bytes),
        name="kernel_blocks",
        cost_estimate=pl.CostEstimate(
            flops=10**6, bytes_accessed=10**4, transcendentals=0
        ),
    )(total, group_leaf, group_count, group_slots, place, own, other, targets)


def far_body(
    total_ref, leaf_ref, slot_ref, side_ref,
    own_ref, partner_ref, high_ref, low_ref, weights_ref,
    out_ref, projected_ref, copies_ref,
    s_high, s_low, acc,
    *, cap,
):
    step = pl.program_id(0)
    samp_dev = own_ref.shape[2]
    part = own_ref.shape[0]

    @pl.when(step == 0)
    def _():
        acc[...] = jnp.zeros_like(acc)

        def split(slot, carry):
            here = side_ref[0] * part + slot
            there = (1 - side_ref[0]) * part + slot
            s_high[here], s_low[here] = halves(own_ref[slot])
            at = pl.multiple_of((slot % cap) * LEAF, LEAF)
            s_high[there], s_low[there] = halves(partner_ref[slot // cap, pl.ds(at, LEAF), :])
            return carry

        lax.fori_loop(0, part, split, 0, unroll=4)

    @pl.when(step * BATCH < total_ref[0])
    def _():
        for member in range(BATCH):
            group = step * BATCH + member
            leaf = leaf_ref[group]
            slots = [slot_ref[group * GROUP + e] for e in range(GROUP)]
            rows_high = jnp.concatenate([s_high[slot] for slot in slots], axis=0)
            rows_low = jnp.concatenate([s_low[slot] for slot in slots], axis=0)
            k_high = high_ref[member]
            k_low = low_ref[member]
            acc[leaf] += dot(k_high, rows_high) + (dot(k_high, rows_low) + dot(k_low, rows_high))

    @pl.when(step == pl.num_programs(0) - 1)
    def _():
        leaves = acc.shape[0]
        rows = acc[...].reshape(leaves * LEAF, samp_dev)
        projected = dot_exact(weights_ref[...], rows)
        projected_ref[...] = projected
        for branch in range(copies_ref.shape[0]):
            copies_ref[branch] = projected
        for pair in range(leaves // 2):
            block = acc[2 * pair : 2 * pair + 2].reshape(2 * LEAF, samp_dev)
            out_ref[:, 2 * pair * LEAF : 2 * (pair + 1) * LEAF] = block.T


def far_products(total, group_leaf, group_slots, side, own, partner, high, low, weights, branches):
    part, unused, samp_dev = own.shape
    slots = 2 * part
    groups = group_leaf.shape[0]
    points_dev = weights.shape[1]
    leaves = points_dev // LEAF
    steps = groups // BATCH

    def block_index(step, total_ref, *unused):
        last = (total_ref[0] - 1) // BATCH
        return (jnp.minimum(step, last), 0, 0)

    return pl.pallas_call(
        functools.partial(far_body, cap=part // partner.shape[0]),
        grid_spec=pltpu.PrefetchScalarGridSpec(
            num_scalar_prefetch=4,
            grid=(steps,),
            in_specs=[
                pl.BlockSpec(own.shape, lambda *unused: (0, 0, 0), pipeline_mode=pl.Buffered(1)),
                pl.BlockSpec(partner.shape, lambda *unused: (0, 0, 0), pipeline_mode=pl.Buffered(1)),
                pl.BlockSpec((BATCH, LEAF, GROUP * LEAF), block_index),
                pl.BlockSpec((BATCH, LEAF, GROUP * LEAF), block_index),
                pl.BlockSpec(weights.shape, lambda *unused: (0, 0), pipeline_mode=pl.Buffered(1)),
            ],
            out_specs=[
                pl.BlockSpec((samp_dev, points_dev), lambda *unused: (0, 0)),
                pl.BlockSpec((weights.shape[0], samp_dev), lambda *unused: (0, 0)),
                pl.BlockSpec((branches, weights.shape[0], samp_dev), lambda *unused: (0, 0, 0)),
            ],
            scratch_shapes=[
                pltpu.VMEM((slots, LEAF, samp_dev), jnp.bfloat16),
                pltpu.VMEM((slots, LEAF, samp_dev), jnp.bfloat16),
                pltpu.VMEM((leaves, LEAF, samp_dev), jnp.float32),
            ],
        ),
        out_shape=[
            jax.ShapeDtypeStruct((samp_dev, points_dev), jnp.float32),
            jax.ShapeDtypeStruct((weights.shape[0], samp_dev), jnp.float32),
            jax.ShapeDtypeStruct((branches, weights.shape[0], samp_dev), jnp.float32),
        ],
        compiler_params=pltpu.CompilerParams(vmem_limit_bytes=vmem_bytes),
        name="far_products",
        cost_estimate=pl.CostEstimate(
            flops=10**6, bytes_accessed=10**4, transcendentals=0
        ),
    )(total, group_leaf, group_slots, side, own, partner, high, low, weights)


NEAR_LEAVES = 8


def near_body(mask_ref, rows_ref, coords_ref, target_ref, out_ref):
    step = pl.program_id(0)
    samp_dev = rows_ref.shape[2]
    lane = lax.broadcasted_iota(jnp.int32, (1, LANES), 1)
    first = lane < LEAF
    for pair in range(NEAR_LEAVES // 2):
        results = []
        for member in range(2):
            leaf = step * NEAR_LEAVES + 2 * pair + member
            target = target_ref[leaf]
            k_high = []
            k_low = []
            for half in range(2):
                both = jnp.where(first, coords_ref[leaf + 2 * half], coords_ref[leaf + 2 * half + 1])
                values = kernel_half(both, target, lane, LANES)
                left = mask_ref[leaf * 3 + 2 * half].astype(jnp.float32)
                if half == 0:
                    right = mask_ref[leaf * 3 + 1].astype(jnp.float32)
                else:
                    right = jnp.float32(0.0)
                high, low = halves(values * jnp.where(first, left, right))
                k_high.append(high)
                k_low.append(low)
            k_high = jnp.concatenate(k_high, axis=1)
            k_low = jnp.concatenate(k_low, axis=1)
            rows = rows_ref[pl.ds(leaf, 4)].reshape(4 * LEAF, samp_dev)
            rows_high, rows_low = halves(rows)
            results.append(
                dot(k_high, rows_high) + (dot(k_high, rows_low) + dot(k_low, rows_high))
            )
        block = jnp.concatenate(results, axis=0)
        out_ref[:, 2 * pair * LEAF : 2 * (pair + 1) * LEAF] = block.T


def near_products(mask, rows, coords, targets):
    leaves = targets.shape[0]
    samp_dev = rows.shape[2]
    whole = lambda *unused: (0, 0, 0)
    return pl.pallas_call(
        near_body,
        grid_spec=pltpu.PrefetchScalarGridSpec(
            num_scalar_prefetch=1,
            grid=(leaves // NEAR_LEAVES,),
            in_specs=[
                pl.BlockSpec(rows.shape, whole),
                pl.BlockSpec(coords.shape, whole),
                pl.BlockSpec(targets.shape, whole),
            ],
            out_specs=pl.BlockSpec((samp_dev, NEAR_LEAVES * LEAF), lambda step, *unused: (0, step)),
        ),
        out_shape=jax.ShapeDtypeStruct((samp_dev, leaves * LEAF), jnp.float32),
        compiler_params=pltpu.CompilerParams(vmem_limit_bytes=vmem_bytes),
        name="near_products",
        cost_estimate=pl.CostEstimate(
            flops=10**6, bytes_accessed=10**4, transcendentals=0
        ),
    )(mask, rows, coords, targets)


def to_lanes(source, target, rank):
    nodes = source.shape[0] // rank
    target[...] = jnp.zeros_like(target)
    for r in range(rank):
        target[r, :, 0:nodes] = source[pl.ds(r, nodes, stride=rank), :].T


def from_lanes(columns, target, r, nodes, rank):
    target[pl.ds(r, nodes, stride=rank), :] = columns.T[0:nodes]


def eliminate(current, left, inverse, level, rank):
    tiles = rank // SUB
    row = lax.broadcasted_iota(jnp.int32, (SUB, LANES), 0)
    diagonal = [current[j, j : j + 1, :] for j in range(rank)]
    while len(diagonal) > 1:
        diagonal = [diagonal[i] + diagonal[i + 1] for i in range(0, len(diagonal), 2)]
    share = shift_share * diagonal[0] / rank
    shift = share + 1e-06
    a = [
        {t: current[j, SUB * t : SUB * (t + 1), :] for t in range(j // SUB, tiles)}
        for j in range(rank)
    ]
    for j in range(rank):
        a[j][j // SUB] = a[j][j // SUB] + jnp.where(row == j % SUB, shift, 0.0)
    m = []
    scales = []
    for k in range(rank):
        tk, rk = k // SUB, k % SUB
        root = lax.rsqrt(a[k][tk][rk : rk + 1, :])
        scales.append(root)
        reciprocal = root * root
        column = {t: a[k][t] * reciprocal for t in range(tk, tiles)}
        column[tk] = jnp.where(row > rk, column[tk], 0.0)
        for j in range(k + 1, rank):
            factor = a[k][j // SUB][j % SUB : j % SUB + 1, :]
            for t in range(j // SUB, tiles):
                a[j][t] = a[j][t] - column[t] * factor
        for c in range(k):
            factor = m[c][tk][rk : rk + 1, :]
            for t in range(tk, tiles):
                m[c][t] = m[c][t] - column[t] * factor
        fresh = {t: -column[t] for t in range(tk, tiles)}
        fresh[tk] = jnp.where(row == rk, 1.0, fresh[tk])
        m.append(fresh)
        if left is not None:
            for t in range(tiles):
                if t < tk:
                    value = jnp.zeros((SUB, LANES), jnp.float32)
                else:
                    value = a[k][t] * root
                if t == tk:
                    value = jnp.where(row >= rk, value, 0.0)
                left[k, SUB * t : SUB * (t + 1), :] = value
    for t in range(tiles):
        scale = jnp.concatenate(scales[SUB * t : SUB * (t + 1)], axis=0)
        for c in range(rank):
            value = m[c][t] * scale if t >= c // SUB else jnp.zeros((SUB, LANES), jnp.float32)
            inverse[c * rank + SUB * t : c * rank + SUB * (t + 1), :] = value
    return shift, share


def inverse_row(inverse, r, t, rank):
    return inverse[pl.ds(SUB * t * rank + r, SUB, stride=rank), :]


def pair_up(value, level):
    reach = LANES - (1 << level if isinstance(level, int) else lax.shift_left(1, level))
    return value + pltpu.roll(value, reach, 1)


def when(condition):
    if isinstance(condition, bool):
        return lambda body: body() if condition else None
    return pl.when(condition)


def level_fast(level, levels, current, left, inverse, squared, ratio, child, lowest, rank, child_at):
    tiles = rank // SUB
    row = lax.broadcasted_iota(jnp.int32, (SUB, LANES), 0)
    shift, share = eliminate(current, left, inverse, level, rank)
    lowest[...] = jnp.minimum(lowest[...], share)

    for block in range(tiles):
        sums = [[None] * tiles for _ in range(SUB)]
        for r in range(SUB * block, rank):
            parts = [inverse_row(inverse, r, t, rank) for t in range(block, r // SUB + 1)]
            for q in range(SUB):
                if SUB * block + q > r:
                    continue
                factor = parts[0][q : q + 1, :]
                for t in range(block, r // SUB + 1):
                    term = parts[t - block] * factor
                    sums[q][t] = term if sums[q][t] is None else sums[q][t] + term
        for q in range(SUB):
            at = (SUB * block + q) * rank
            for t in range(block, tiles):
                squared[at + SUB * t : at + SUB * (t + 1), :] = sums[q][t]

    if child is not None:
        @when(child_at(level))
        def _():
            for r in range(rank):
                for t in range(tiles):
                    value = left[r, SUB * t : SUB * (t + 1), :]
                    if t <= r // SUB:
                        value = value - shift * inverse_row(inverse, r, t, rank)
                    child[r, SUB * t : SUB * (t + 1), :] = value

    for q in range(rank):
        for t in range(tiles):
            if t >= q // SUB:
                value = squared[q * rank + SUB * t : q * rank + SUB * (t + 1), :]
            else:
                value = squared[pl.ds(SUB * t * rank + q, SUB, stride=rank), :]
            value = -shift * value
            if t == q // SUB:
                value = value + jnp.where(row == q % SUB, 1.0, 0.0)
            if ratio is not None:
                ratio[level, q, SUB * t : SUB * (t + 1), :] = value
            here = current[q, SUB * t : SUB * (t + 1), :] - shift * value
            current[q, SUB * t : SUB * (t + 1), :] = pair_up(here, level)


def level_plain(level, levels, current, left, inverse, squared, ratio, child, lowest, rank, child_at):
    tiles = rank // SUB
    eliminate(current, left, inverse, level, rank)

    def products(out, count, left_of, right_of):
        def block_step(block, carry):
            offset = pl.multiple_of(block * SUB, SUB)
            sums = [[None] * tiles for _ in range(SUB)]
            for r in range(count):
                parts = [left_of(r, t) for t in range(tiles)]
                heads = right_of(r, offset)
                for q in range(SUB):
                    for t in range(tiles):
                        term = parts[t] * heads[q : q + 1, :]
                        sums[q][t] = term if sums[q][t] is None else sums[q][t] + term
            for q in range(SUB):
                for t in range(tiles):
                    out(offset + q, t, sums[q][t])
            return carry

        lax.fori_loop(0, tiles, block_step, 0)

    def tile(t):
        return slice(SUB * t, SUB * (t + 1))

    def put_child(r, t, value):
        squared[pl.ds(pl.multiple_of(r * rank + SUB * t, SUB), SUB), :] = value

    products(
        put_child, rank,
        lambda k, t: current[k, tile(t), :],
        lambda k, offset: inverse[pl.ds(pl.multiple_of(k * rank + offset, SUB), SUB), :],
    )
    if child is not None:
        @when(child_at(level))
        def _():
            for r in range(rank):
                for t in range(tiles):
                    child[r, tile(t), :] = squared[r * rank + SUB * t : r * rank + SUB * (t + 1), :]

    def child_part(r, t):
        return squared[r * rank + SUB * t : r * rank + SUB * (t + 1), :]

    def put_current(q, t, value):
        current[q, tile(t), :] = pair_up(value, level)

    if ratio is not None:
        def put_ratio(c, t, value):
            ratio[level, c, tile(t), :] = value

        def inverse_head(r, offset):
            return inverse[pl.ds(offset * rank + r, SUB, stride=rank), :]

        products(put_ratio, rank, child_part, inverse_head)
    products(
        put_current, rank, child_part,
        lambda r, offset: squared[pl.ds(pl.multiple_of(r * rank + offset, SUB), SUB), :],
    )


def run_levels(source, levels, nodes, current, left, inverse, squared, ratio, child, lowest, rank, child_at, finish, unrolled=False):
    lowest[...] = jnp.full((1, LANES), 1.0, jnp.float32)

    def sweep(level_step):
        to_lanes(source, current, rank)

        def body(level, carry):
            level_step(level, levels, current, left, inverse, squared, ratio, child, lowest, rank, child_at)
            finish(level)
            return carry

        if unrolled and level_step is level_fast:
            for level in range(levels):
                body(level, 0)
        else:
            lax.fori_loop(0, levels, body, 0)

    sweep(level_fast)
    lane = lax.broadcasted_iota(jnp.int32, (1, LANES), 1)
    least = jnp.min(jnp.where(lane < nodes, lowest[...], 1.0))

    @pl.when(least < 2e-06)
    def _():
        sweep(level_plain)


def branch_body(gram_ref, inverse_ref, ratio_ref, top_ref, child_ref, current, left, inverse, squared, child, lowest, *, rank, levels):
    nodes = gram_ref.shape[0] // rank

    def finish(level):
        @pl.when(level == 0)
        def _():
            for c in range(rank):
                inverse_ref[c] = inverse[c * rank : (c + 1) * rank, :]

        @pl.when(level == levels - 1)
        def _():
            for r in range(rank):
                width = child_ref.shape[1]
                at = r * rank
                child_ref[at // width : at // width + 1, at % width : at % width + rank] = child[r].T[0:1, :]
                top_ref[r : r + 1, :] = jnp.concatenate(
                    [inverse_row(inverse, r, t, rank) for t in range(rank // SUB)], axis=0
                ).T[0:1, :]

    run_levels(
        gram_ref, levels, nodes, current, left, inverse, squared, ratio_ref, child, lowest, rank,
        lambda level: level == levels - 1, finish,
    )


vmem_spec = pl.BlockSpec(memory_space=pltpu.VMEM)


def tree_scratch(rank):
    return [
        pltpu.VMEM((rank, rank, LANES), jnp.float32),
        pltpu.VMEM((rank, rank, LANES), jnp.float32),
        pltpu.VMEM((rank * rank, LANES), jnp.float32),
        pltpu.VMEM((rank * rank, LANES), jnp.float32),
        pltpu.VMEM((rank, rank, LANES), jnp.float32),
        pltpu.VMEM((1, LANES), jnp.float32),
    ]


def branch_factors(gram, levels, width):
    leaves, rank, unused = gram.shape
    return pl.pallas_call(
        functools.partial(branch_body, rank=rank, levels=levels),
        in_specs=[vmem_spec],
        out_specs=[vmem_spec] * 4,
        out_shape=[
            jax.ShapeDtypeStruct((rank, rank, LANES), jnp.float32),
            jax.ShapeDtypeStruct((levels, rank, rank, LANES), jnp.float32),
            jax.ShapeDtypeStruct((rank, rank), jnp.float32),
            jax.ShapeDtypeStruct((rank * rank // width, width), jnp.float32),
        ],
        scratch_shapes=tree_scratch(rank),
        compiler_params=pltpu.CompilerParams(vmem_limit_bytes=vmem_bytes),
        name="branch_factors",
        cost_estimate=pl.CostEstimate(flops=10**6, bytes_accessed=10**4, transcendentals=0),
    )(gram.reshape(leaves * rank, rank))


def basis_body(inverse_ref, ratio_ref, top_ref, sketched_ref, weights_ref, basis_ref, natural, *, rank, levels):
    leaves = sketched_ref.shape[0]
    upper = [top_ref[...]]
    for level in range(levels - 2, -1, -1):
        stride = 2**level
        for c in range(rank):
            from_lanes(ratio_ref[level, c], natural, c, leaves, rank)
        fresh = []
        for node in range(leaves // stride):
            block = natural[node * stride * rank : (node * stride + 1) * rank, :]
            fresh.append(dot_exact(upper[node // 2], block))
        upper = fresh
    for r in range(rank):
        from_lanes(inverse_ref[r], natural, r, leaves, rank)
    for pair in range(leaves // 2):
        results = []
        for leaf in (2 * pair, 2 * pair + 1):
            block = sketched_ref[leaf]
            own = lax.dot_general(
                natural[leaf * rank : (leaf + 1) * rank, :], block, tn_dims,
                precision=highest, preferred_element_type=jnp.float32,
            )
            results.append(jnp.concatenate([dot_exact(upper[leaf], block), own], axis=0))
        both = jnp.concatenate(results, axis=1)
        weights_ref[:, pair * 2 * LEAF : (pair + 1) * 2 * LEAF] = both[:rank]
        basis_ref[:, pair * 2 * LEAF : (pair + 1) * 2 * LEAF] = both[rank:]


def bases(inverse, ratio, top, sketched):
    leaves, rank, unused = sketched.shape
    levels = ratio.shape[0]
    shape = jax.ShapeDtypeStruct((rank, leaves * LEAF), jnp.float32)
    return pl.pallas_call(
        functools.partial(basis_body, rank=rank, levels=levels),
        in_specs=[vmem_spec] * 4,
        out_specs=[vmem_spec] * 2,
        out_shape=[shape, shape],
        scratch_shapes=[pltpu.VMEM((leaves * rank, rank), jnp.float32)],
        compiler_params=pltpu.CompilerParams(vmem_limit_bytes=vmem_bytes),
        name="bases",
        cost_estimate=pl.CostEstimate(flops=10**6, bytes_accessed=10**4, transcendentals=0),
    )(inverse, ratio, top, sketched)


def top_body(packed_ref, transfer_ref, paths_ref, children_ref, source, current, left, inverse, squared, child, lowest, nat_inverse, nat_child, *, rank, levels):
    branches, packed_rows_each, width = packed_ref.shape
    nodes = branches // 2
    every = width // rank
    flat = packed_ref[...].reshape(branches * packed_rows_each, width)
    for part in range(every):
        children_ref[pl.ds(part, branches * packed_rows_each, stride=every), :] = flat[
            :, part * rank : (part + 1) * rank
        ]
    for node in range(nodes):
        both = children_ref[2 * node * rank : (2 * node + 2) * rank, :]
        source[node * rank : (node + 1) * rank, :] = lax.dot_general(
            both, both, tn_dims, precision=highest, preferred_element_type=jnp.float32
        )

    def finish(level):
        for r in range(rank):
            from_lanes(child[r], nat_child.at[level], r, nodes, rank)
            from_lanes(inverse[r * rank : (r + 1) * rank, :], nat_inverse.at[level], r, nodes, rank)

    run_levels(
        source, levels, nodes, current, left, inverse, squared, None, child, lowest, rank,
        lambda level: True, finish, unrolled=True,
    )
    offset = 0
    for level in range(levels):
        for node in range(nodes >> level):
            if level == 0:
                stacked = children_ref[2 * node * rank : (2 * node + 2) * rank, :]
            else:
                first = 2 * node << level - 1
                second = 2 * node + 1 << level - 1
                stacked = jnp.concatenate(
                    [
                        nat_child[level - 1, first * rank : (first + 1) * rank, :],
                        nat_child[level - 1, second * rank : (second + 1) * rank, :],
                    ],
                    axis=0,
                )
            at = (node << level) * rank
            transfer_ref[offset + node] = lax.dot_general(
                nat_inverse[level, at : at + rank, :], stacked, (((0,), (1,)), ((), ())),
                precision=highest, preferred_element_type=jnp.float32,
            )
        offset += nodes >> level
    above = [None]
    for level in range(levels - 1, -1, -1):
        offset -= nodes >> level
        fresh = []
        for node in range(nodes >> level):
            both = transfer_ref[offset + node]
            if above[0] is None:
                both = both.T
            else:
                both = lax.dot_general(
                    both, above[node], tn_dims, precision=highest, preferred_element_type=jnp.float32
                )
            fresh += [both[:rank], both[rank:]]
        above = fresh
    for branch in range(2 * nodes):
        paths_ref[branch * rank : (branch + 1) * rank, :] = above[branch]


def top_factors(children, rank):
    branches = children.shape[0]
    levels = branches.bit_length() - 1
    nodes = branches // 2
    natural = pltpu.VMEM((levels, nodes * rank, rank), jnp.float32)
    return pl.pallas_call(
        functools.partial(top_body, rank=rank, levels=levels),
        in_specs=[vmem_spec],
        out_specs=[vmem_spec] * 2,
        out_shape=[
            jax.ShapeDtypeStruct((branches - 1, rank, 2 * rank), jnp.float32),
            jax.ShapeDtypeStruct((branches * rank, rank), jnp.float32),
        ],
        scratch_shapes=[
            pltpu.VMEM((branches * rank, rank), jnp.float32),
            pltpu.VMEM((nodes * rank, rank), jnp.float32),
        ]
        + tree_scratch(rank)
        + [natural, natural],
        compiler_params=pltpu.CompilerParams(vmem_limit_bytes=vmem_bytes),
        name="top_factors",
        cost_estimate=pl.CostEstimate(flops=10**10, bytes_accessed=10**7, transcendentals=0),
    )(children)


def exchange_sum(pieces, axis):
    count = pieces.shape[0]
    me = lax.axis_index(axis)
    mine = lax.dynamic_index_in_dim(pieces, me, 0, keepdims=False)
    for step in range(1, count):
        outgoing = lax.dynamic_index_in_dim(pieces, (me + step) % count, 0, keepdims=False)
        mine = mine + lax.ppermute(
            outgoing, axis, [(i, (i + step) % count) for i in range(count)]
        )
    return mine


def exchange_all(piece, axis):
    count = lax.axis_size(axis)
    me = lax.axis_index(axis)
    if count == 2:
        other = lax.ppermute(piece, axis, [(0, 1), (1, 0)])
        return jnp.stack([jnp.where(me == 0, piece, other), jnp.where(me == 0, other, piece)])
    result = jnp.zeros((count,) + piece.shape, piece.dtype)
    result = lax.dynamic_update_index_in_dim(result, piece, me, 0)
    for step in range(1, count):
        arrived = lax.ppermute(piece, axis, [(i, (i + step) % count) for i in range(count)])
        result = lax.dynamic_update_index_in_dim(result, arrived, (me - step) % count, 0)
    return result


def group_tables(far_slots, far_count):
    leaves = far_slots.shape[0]
    groups = leaves * FAR // GROUP
    per_leaf = (far_count + GROUP - 1) // GROUP
    before = jnp.arange(leaves)[:, None] >= jnp.arange(leaves)[None, :]
    ends = jnp.sum(jnp.where(before, per_leaf[None, :], 0), axis=1)
    total = ends[leaves - 1 :]
    ids = jnp.arange(groups, dtype=jnp.int32)
    leaf = jnp.minimum(jnp.sum((ends[None, :] <= ids[:, None]).astype(jnp.int32), axis=1), leaves - 1)
    hit = leaf[:, None] == jnp.arange(leaves)[None, :]
    start = jnp.sum(jnp.where(hit, (ends - per_leaf)[None, :], 0), axis=1)
    length = jnp.sum(jnp.where(hit, far_count[None, :], 0), axis=1)
    sub = ids - start
    count = jnp.where(ids < total, jnp.clip(length - GROUP * sub, 0, GROUP), 0)
    first = jnp.minimum(sub, FAR // GROUP - 1)
    slots = far_slots.reshape(leaves * FAR // GROUP, GROUP)[leaf * (FAR // GROUP) + first]
    return (
        total.astype(jnp.int32),
        leaf.astype(jnp.int32),
        count.astype(jnp.int32),
        slots.reshape(-1).astype(jnp.int32),
    )


def sketch_body(place_ref, sketch_ref, samples_ref, points_ref, mine_ref, other_ref):
    product = dot_exact(sketch_ref[...], samples_ref[...])
    rank, points_dev = product.shape
    quarter = rank // 4
    first = lax.broadcasted_iota(jnp.int32, (1, LANES), 1) < LEAF
    swap = place_ref[0] == 1
    leaves = points_dev // LEAF

    def interleave(low, high):
        even = jnp.where(first, low, pltpu.roll(high, LEAF, 1))
        odd = jnp.where(first, pltpu.roll(low, LEAF, 1), high)
        return even, odd

    for pair in range(leaves // 2):
        lanes = slice(pair * LANES, (pair + 1) * LANES)
        shares = []
        for share in range(2):
            base = 2 * quarter * share
            shares.append(
                interleave(product[base : base + quarter, lanes], product[base + quarter : base + 2 * quarter, lanes])
            )
        for member in range(2):
            at = (2 * pair + member) * quarter
            mine_ref[at : at + quarter, :] = jnp.where(swap, shares[1][member], shares[0][member])
            other_ref[at : at + quarter, :] = jnp.where(swap, shares[0][member], shares[1][member])
        x = points_ref[0:1, lanes]
        y = points_ref[1:2, lanes]
        z = points_ref[2:3, lanes]
        xy = interleave(x, y)
        zs = interleave(z, jnp.zeros_like(z))
        for member in range(2):
            at = leaves * quarter + (2 * pair + member) * 2
            mine_ref[at : at + 1, :] = xy[member]
            mine_ref[at + 1 : at + 2, :] = zs[member]
    other_ref[leaves * quarter :, :] = jnp.zeros((2 * leaves, LANES), jnp.float32)


def sketched_shares(place, sketch, samples, points):
    rank = sketch.shape[0]
    leaves = samples.shape[1] // LEAF
    return pl.pallas_call(
        sketch_body,
        in_specs=[pl.BlockSpec(memory_space=pltpu.SMEM)] + [vmem_spec] * 3,
        out_specs=[vmem_spec] * 2,
        out_shape=[
            jax.ShapeDtypeStruct((leaves * (rank // 4 + 2), LANES), jnp.float32),
            jax.ShapeDtypeStruct((leaves * (rank // 4 + 2), LANES), jnp.float32),
        ],
        compiler_params=pltpu.CompilerParams(vmem_limit_bytes=vmem_bytes),
        name="sketched_shares",
        cost_estimate=pl.CostEstimate(flops=10**6, bytes_accessed=10**4, transcendentals=0),
    )(place, sketch, samples, points)


def pack_body(asked_ref, side_ref, mine_ref, partner_ref, out_ref, *, cap, leaves):
    z_rows = mine_ref.shape[0] // leaves - 2
    side = side_ref[0]

    def one(peer, carry):
        for entry in range(2 * cap):
            leaf = asked_ref[peer, entry]
            here = side == entry // cap
            at = pl.ds(leaf * z_rows, z_rows)
            out_ref[peer, z_rows * entry : z_rows * (entry + 1), :] = jnp.where(
                here, mine_ref[at, :], partner_ref[at, :]
            )
            base = z_rows * 2 * cap + 2 * entry
            at = pl.ds(leaves * z_rows + leaf * 2, 2)
            out_ref[peer, base : base + 2, :] = jnp.where(here, mine_ref[at, :], partner_ref[at, :])
        return carry

    lax.fori_loop(0, out_ref.shape[0], one, 0)


def packed_rows(asked, side, mine, partner, cap, leaves):
    z_rows = mine.shape[0] // leaves - 2
    return pl.pallas_call(
        functools.partial(pack_body, cap=cap, leaves=leaves),
        in_specs=[pl.BlockSpec(memory_space=pltpu.SMEM)] * 2 + [vmem_spec] * 2,
        out_specs=vmem_spec,
        out_shape=jax.ShapeDtypeStruct((asked.shape[0], 2 * cap * (z_rows + 2), LANES), jnp.float32),
        compiler_params=pltpu.CompilerParams(vmem_limit_bytes=vmem_bytes),
        name="packed_rows",
    )(asked, side, mine, partner)


def payload_body(asked_ref, side_ref, early_ref, late_ref, child_ref, out_ref, sems, *, cap):
    early = early_ref.shape[0]
    peers = out_ref.shape[0]
    rows = child_ref.shape[0]
    base = (1 - side_ref[0]) * cap

    def place(peer, entry):
        return out_ref.at[peer, pl.ds(LEAF * entry, LEAF)], sems.at[peer, entry]

    def child_place(peer):
        return out_ref.at[peer, pl.ds(LEAF * cap, rows)], sems.at[peer, cap]

    for peer in range(peers):
        for entry in range(cap):
            leaf = asked_ref[peer, base + entry]
            target, sem = place(peer, entry)

            @pl.when(leaf < early)
            def _():
                pltpu.make_async_copy(early_ref.at[leaf], target, sem).start()

            @pl.when(leaf >= early)
            def _():
                pltpu.make_async_copy(late_ref.at[leaf - early], target, sem).start()

        target, sem = child_place(peer)
        pltpu.make_async_copy(child_ref, target, sem).start()
    for peer in range(peers):
        for entry in range(cap):
            target, sem = place(peer, entry)
            pltpu.make_async_copy(late_ref.at[0], target, sem).wait()
        target, sem = child_place(peer)
        pltpu.make_async_copy(child_ref, target, sem).wait()


def payload_rows(asked, side, early, late, child):
    half = asked.shape[0]
    cap = asked.shape[1] // 2
    smem = pl.BlockSpec(memory_space=pltpu.SMEM)
    anywhere = pl.BlockSpec(memory_space=pl.ANY)
    return pl.pallas_call(
        functools.partial(payload_body, cap=cap),
        in_specs=[smem, smem, anywhere, anywhere, anywhere],
        out_specs=anywhere,
        out_shape=jax.ShapeDtypeStruct((half, cap * LEAF + child.shape[0], late.shape[2]), jnp.float32),
        scratch_shapes=[pltpu.SemaphoreType.DMA((half, cap + 1))],
        compiler_params=pltpu.CompilerParams(vmem_limit_bytes=vmem_bytes),
        name="payload_rows",
    )(asked, side, early, late, child)


def two_rows(values, rows):
    leaves = values.shape[1]
    split = jnp.transpose(values.reshape(2, rows, leaves, LEAF), (2, 1, 0, 3))
    return split.reshape(leaves, rows, 2 * LEAF)


def on_device(points, samples, sketch, far_requests, far_slots, far_count, near_mask):
    samp_dev = samples.shape[0]
    leaves = samples.shape[1] // LEAF
    rank = sketch.shape[0]
    branches = lax.axis_size("leaf")
    columns = lax.axis_size("cols")
    cap = far_requests.shape[2]
    share = rank // columns
    me = lax.axis_index("leaf")
    column = lax.axis_index("cols")

    half = branches // 2
    side = me // half
    groups = [list(range(half)), list(range(half, branches))]
    mirror = [(i, (i + half) % branches) for i in range(branches)]
    side_ref = side.astype(jnp.int32).reshape(1)
    wanted = jnp.transpose(far_requests.reshape(2, half, cap), (1, 0, 2)).reshape(half, 2 * cap)
    asked = lax.all_to_all(
        wanted, "leaf", split_axis=0, concat_axis=0, axis_index_groups=groups, tiled=True
    )

    if columns == 2:
        place = column.astype(jnp.int32).reshape(1)
        mine, other = sketched_shares(place, sketch, samples, points)
        mine = mine + lax.ppermute(other, "cols", [(0, 1), (1, 0)])
    else:
        z_part = jnp.dot(sketch, samples, precision=highest)
        z_mine = exchange_sum(z_part.reshape(columns, share, leaves * LEAF), "cols")
        z_rows = two_rows(z_mine.reshape(share, leaves, LEAF), share // 2)
        planes = points.reshape(3, leaves, LEAF)
        c_rows = two_rows(
            jnp.concatenate([planes[0:1], planes[2:3], planes[1:2], jnp.zeros_like(planes[0:1])], axis=0), 2
        )
        mine = jnp.concatenate([z_rows.reshape(-1, LANES), c_rows.reshape(-1, LANES)], axis=0)

    partner = lax.ppermute(mine, "leaf", mirror)
    coords = jnp.transpose(points.reshape(3, leaves, LEAF), (1, 0, 2))
    targets = jnp.transpose(coords, (0, 2, 1))
    rows = jnp.transpose(samples.reshape(samp_dev, leaves, LEAF), (1, 2, 0))

    small_sent = packed_rows(asked, side_ref, mine, partner, cap, leaves)
    small_got = lax.all_to_all(
        small_sent, "leaf", split_axis=0, concat_axis=0, axis_index_groups=groups, tiled=True
    )
    total, group_leaf, group_count, group_slots = group_tables(far_slots, far_count)

    early = leaves // 8
    rows_out, unused = lax.optimization_barrier((rows, small_sent))
    partner_early = lax.ppermute(rows_out[:early], "leaf", mirror)
    rows_late = rows_out[early:]

    forward = [(i, i + 1) for i in range(branches - 1)]
    backward = [(target, source) for source, target in forward]
    width = max(samp_dev, LEAF)

    def edge(first):
        samples_edge = jnp.transpose(lax.slice_in_dim(samples, first, first + LEAF, axis=1))
        points_edge = lax.slice_in_dim(points, first, first + LEAF, axis=1)
        return jnp.concatenate(
            [
                jnp.pad(samples_edge, ((0, 0), (0, width - samp_dev))),
                jnp.pad(points_edge, ((0, 5), (0, width - LEAF))),
            ],
            axis=0,
        )

    last, first, unused = lax.optimization_barrier((edge((leaves - 1) * LEAF), edge(0), small_sent))
    low_edge = lax.ppermute(last, "leaf", forward)
    high_edge = lax.ppermute(first, "leaf", backward)

    own_asked = lax.dynamic_slice_in_dim(asked, side * cap, cap, axis=1)
    own_sent = rows_out[own_asked.reshape(-1)].reshape(half, cap, LEAF, samp_dev)
    (
        own_sent, rows_late, partner_early, low_edge, high_edge, targets, total, group_leaf, group_count, group_slots,
    ) = lax.optimization_barrier(
        (
            own_sent, rows_late, partner_early, low_edge, high_edge, targets,
            total, group_leaf, group_count, group_slots,
        )
    )
    partner_late = lax.ppermute(rows_late, "leaf", mirror)
    own_got = lax.all_to_all(
        own_sent, "leaf", split_axis=0, concat_axis=0, axis_index_groups=groups, tiled=True
    )
    own_got = own_got.reshape(half * cap, LEAF, samp_dev)

    if columns == 2:
        small_other = lax.ppermute(small_got, "cols", [(0, 1), (1, 0)])
    else:
        z_count = cap * share
        z_all = exchange_all(small_got[:, :z_count], "cols")
        z_all = z_all.reshape(columns, half, 2 * cap, share // 2, 2, LEAF)
        z_all = jnp.transpose(z_all, (1, 2, 0, 4, 3, 5)).reshape(half, 2 * cap, 2, 2, rank // 4, LEAF)
        z_all = jnp.transpose(z_all, (2, 0, 1, 4, 3, 5)).reshape(2, half, cap * rank // 2, LANES)
        c_got = small_got[:, z_count:]
        small_got = jnp.concatenate([z_all[0], c_got], axis=1)
        small_other = jnp.concatenate([z_all[1], c_got], axis=1)
        place = jnp.zeros((1,), jnp.int32)

    high, low, sketched, gram = kernel_blocks(
        total, group_leaf, group_count, group_slots, place, small_got, small_other, targets, rank, cap
    )

    levels = leaves.bit_length()
    inverse, ratio, top_inverse, own_child = branch_factors(gram, levels, min(samp_dev, LANES))
    own_child, own_got, partner_late = lax.optimization_barrier((own_child, own_got, partner_late))
    payload = payload_rows(asked, side_ref, partner_early, partner_late, own_child)
    arrived = lax.all_to_all(
        payload, "leaf", split_axis=0, concat_axis=0, axis_index_groups=groups, tiled=True
    )
    ratio, low_edge, high_edge, unused = lax.optimization_barrier((ratio, low_edge, high_edge, payload))
    weights, leaf_basis = bases(inverse, ratio, top_inverse, sketched)

    rows_low, rows_high = low_edge[:LEAF, :samp_dev], high_edge[:LEAF, :samp_dev]
    coords_low, coords_high = low_edge[LEAF : LEAF + 3, :LEAF], high_edge[LEAF : LEAF + 3, :LEAF]
    near_rows = jnp.concatenate(
        [rows_low[None], rows, rows_high[None], jnp.zeros_like(rows_low)[None]], axis=0
    )
    near_coords = jnp.concatenate(
        [coords_low[None], coords, coords_high[None], jnp.zeros_like(coords_low)[None]], axis=0
    )
    near_coords = jnp.pad(near_coords, ((0, 0), (0, 5), (0, 0)))
    near_coords = jnp.concatenate([near_coords, near_coords], axis=2)
    near_sample = near_products(near_mask.reshape(-1), near_rows, near_coords, targets)


    children = arrived[:, cap * LEAF :]
    mirrored = lax.ppermute(children, "leaf", mirror)
    children = jnp.concatenate(
        [jnp.where(side == 0, children, mirrored), jnp.where(side == 0, mirrored, children)], axis=0
    )

    weights, near_sample = lax.optimization_barrier((weights, near_sample))
    far_sample, branch_samples, copies = far_products(
        total, group_leaf, group_slots, side_ref, own_got, arrived, high, low, weights, branches
    )
    everyone = lax.all_to_all(copies, "leaf", split_axis=0, concat_axis=0, tiled=True)
    children, unused = lax.optimization_barrier((children, branch_samples))
    transfer_t, paths = top_factors(children, rank)
    top_transfer = jnp.swapaxes(transfer_t, 1, 2)
    root_sample = lax.dot_general(
        paths, everyone.reshape(branches * rank, samp_dev), tn_dims, precision=highest
    )
    return (far_sample, near_sample, leaf_basis, branch_samples, top_transfer, root_sample)


def solution(mesh):
    return jax.shard_map(
        on_device,
        mesh=mesh,
        in_specs=(
            P(None, "leaf"),
            P("cols", "leaf"),
            P(None, "cols"),
            P("leaf", None, None),
            P("leaf", None),
            P("leaf"),
            P("leaf", None),
        ),
        out_specs=(
            P("cols", "leaf"),
            P("cols", "leaf"),
            P(None, "leaf"),
            P("leaf", "cols"),
            P(),
            P(None, "cols"),
        ),
        check_vma=False,
    )
```

```python
import functools
import math

import jax
import jax.numpy as jnp
import numpy as np
from jax import lax
from jax.experimental import pallas as pl
from jax.experimental.pallas import tpu as pltpu
from jax.sharding import PartitionSpec as P

LEAF = 64
FAR = 16
GROUP = 4
BATCH = 16
LANES = 128
SUB = 8

length_scale = 0.3
shift_share = 0.05
highest = lax.Precision.HIGHEST
exponent_scale = -math.log2(math.e) / length_scale
vmem_bytes = 56 * 1024 * 1024

nt_dims = (((1,), (1,)), ((), ()))
tn_dims = (((0,), (0,)), ((), ()))


def halves(value):
    high = value.astype(jnp.bfloat16)
    low = (value - high.astype(jnp.float32)).astype(jnp.bfloat16)
    return high, low


def dot(a, b):
    return jnp.dot(a, b, preferred_element_type=jnp.float32)


def dot_exact(a, b):
    return jnp.dot(a, b, precision=highest, preferred_element_type=jnp.float32)


def dot_exact_nt(a, b):
    return lax.dot_general(a, b, nt_dims, precision=highest, preferred_element_type=jnp.float32)


def dot_nt(a, b):
    return lax.dot_general(a, b, nt_dims, preferred_element_type=jnp.float32)


def kernel_half(source_rows, target, lane, valid):
    total = None
    for axis in range(3):
        difference = source_rows[axis : axis + 1, :] - target[:, axis : axis + 1]
        square = difference * difference
        total = square if total is None else total + square
    distance = total * lax.rsqrt(jnp.maximum(total, 1e-30))
    values = jnp.exp2(distance * exponent_scale)
    return jnp.where(lane < valid, values, 0.0)


def blocks_body(
    total_ref, leaf_ref, count_ref, slot_ref, place_ref,
    own_ref, other_ref, target_ref,
    high_ref, low_ref, sketched_ref, gram_ref,
    packed,
    *, rank, cap,
):
    step = pl.program_id(0)
    lane = lax.broadcasted_iota(jnp.int32, (1, LANES), 1)
    first = lane < LEAF

    @pl.when(step == 0)
    def _():
        sketched_ref[...] = jnp.zeros_like(sketched_ref)
        quarter = rank // 4
        slots = packed.shape[0]
        own_at = pl.multiple_of(place_ref[0] * 2 * quarter, quarter)
        other_at = pl.multiple_of((1 - place_ref[0]) * 2 * quarter, quarter)

        def unpack(peer, carry):
            for entry in range(2 * cap):
                slot = (entry // cap) * (slots // 2) + peer * cap + entry % cap
                at = entry * quarter
                for ref, base in ((own_ref, own_at), (other_ref, other_at)):
                    value = ref[peer, at : at + quarter, :]
                    turned = pltpu.roll(value, LEAF, 1)
                    packed[slot, pl.ds(base, quarter), :] = jnp.where(first, value, turned)
                    packed[slot, pl.ds(base + quarter, quarter), :] = jnp.where(first, turned, value)
                at = 2 * cap * quarter + 2 * entry
                value = own_ref[peer, at : at + 2, :]
                turned = pltpu.roll(value, LEAF, 1)
                packed[slot, rank : rank + 1, :] = jnp.where(first, value, turned)[0:1]
                packed[slot, rank + 1 : rank + 2, :] = jnp.where(first, turned, value)[0:1]
                packed[slot, rank + 2 : rank + 3, :] = jnp.where(first, value, turned)[1:2]
            return carry

        lax.fori_loop(0, slots // (2 * cap), unpack, 0)

    @pl.when(step * BATCH < total_ref[0])
    def _():
        for member in range(BATCH):
            group = step * BATCH + member
            leaf = leaf_ref[group]
            count = count_ref[group]
            slots = [slot_ref[group * GROUP + e] for e in range(GROUP)]
            target = target_ref[leaf]
            z_parts = []
            for half in range(GROUP // 2):
                left = packed[slots[2 * half]]
                right = packed[slots[2 * half + 1]]
                both = jnp.where(first, left, right)
                values = kernel_half(both[rank : rank + 3], target, lane, (count - 2 * half) * LEAF)
                high, low = halves(values)
                high_ref[member, :, half * LANES : (half + 1) * LANES] = high
                low_ref[member, :, half * LANES : (half + 1) * LANES] = low
                z_parts.append(both[:rank])
            z_high, z_low = halves(jnp.concatenate(z_parts, axis=1))
            k_high = high_ref[member]
            k_low = low_ref[member]
            both = dot_nt(jnp.concatenate([z_high, z_low], axis=0), k_high)
            update = both[:rank] + (both[rank:] + dot_nt(z_high, k_low))
            sketched_ref[leaf] += update

    @pl.when(step == pl.num_programs(0) - 1)
    def _():
        for leaf in range(gram_ref.shape[0]):
            block = sketched_ref[leaf]
            gram_ref[leaf] = dot_exact_nt(block, block)


def kernel_blocks(total, group_leaf, group_count, group_slots, place, own, other, targets, rank, cap):
    leaves = targets.shape[0]
    groups = group_leaf.shape[0]
    slots = own.shape[0] * 2 * cap
    steps = groups // BATCH

    def block_index(step, total_ref, *unused):
        last = (total_ref[0] - 1) // BATCH
        return (jnp.minimum(step, last), 0, 0)

    whole = lambda *unused: (0, 0, 0)
    once = pl.Buffered(1)
    return pl.pallas_call(
        functools.partial(blocks_body, rank=rank, cap=cap),
        grid_spec=pltpu.PrefetchScalarGridSpec(
            num_scalar_prefetch=5,
            grid=(steps,),
            in_specs=[
                pl.BlockSpec(own.shape, whole, pipeline_mode=once),
                pl.BlockSpec(other.shape, whole, pipeline_mode=once),
                pl.BlockSpec(targets.shape, whole, pipeline_mode=once),
            ],
            out_specs=[
                pl.BlockSpec((BATCH, LEAF, GROUP * LEAF), block_index),
                pl.BlockSpec((BATCH, LEAF, GROUP * LEAF), block_index),
                pl.BlockSpec((leaves, rank, LEAF), whole),
                pl.BlockSpec((leaves, rank, rank), whole),
            ],
            scratch_shapes=[pltpu.VMEM((slots, rank + SUB, LANES), jnp.float32)],
        ),
        out_shape=[
            jax.ShapeDtypeStruct((groups, LEAF, GROUP * LEAF), jnp.bfloat16),
            jax.ShapeDtypeStruct((groups, LEAF, GROUP * LEAF), jnp.bfloat16),
            jax.ShapeDtypeStruct((leaves, rank, LEAF), jnp.float32),
            jax.ShapeDtypeStruct((leaves, rank, rank), jnp.float32),
        ],
        compiler_params=pltpu.CompilerParams(vmem_limit_bytes=vmem_bytes),
        name="kernel_blocks",
        cost_estimate=pl.CostEstimate(
            flops=10**6, bytes_accessed=10**4, transcendentals=0
        ),
    )(total, group_leaf, group_count, group_slots, place, own, other, targets)


def far_body(
    total_ref, leaf_ref, slot_ref, side_ref,
    own_ref, partner_ref, high_ref, low_ref, weights_ref,
    out_ref, projected_ref, copies_ref,
    s_high, s_low, acc,
    *, cap,
):
    step = pl.program_id(0)
    samp_dev = own_ref.shape[2]
    part = own_ref.shape[0]

    @pl.when(step == 0)
    def _():
        acc[...] = jnp.zeros_like(acc)

        def split(slot, carry):
            here = side_ref[0] * part + slot
            there = (1 - side_ref[0]) * part + slot
            s_high[here], s_low[here] = halves(own_ref[slot])
            at = pl.multiple_of((slot % cap) * LEAF, LEAF)
            s_high[there], s_low[there] = halves(partner_ref[slot // cap, pl.ds(at, LEAF), :])
            return carry

        lax.fori_loop(0, part, split, 0, unroll=4)

    @pl.when(step * BATCH < total_ref[0])
    def _():
        for member in range(BATCH):
            group = step * BATCH + member
            leaf = leaf_ref[group]
            slots = [slot_ref[group * GROUP + e] for e in range(GROUP)]
            rows_high = jnp.concatenate([s_high[slot] for slot in slots], axis=0)
            rows_low = jnp.concatenate([s_low[slot] for slot in slots], axis=0)
            k_high = high_ref[member]
            k_low = low_ref[member]
            acc[leaf] += dot(k_high, rows_high) + (dot(k_high, rows_low) + dot(k_low, rows_high))

    @pl.when(step == pl.num_programs(0) - 1)
    def _():
        leaves = acc.shape[0]
        rows = acc[...].reshape(leaves * LEAF, samp_dev)
        projected = dot_exact(weights_ref[...], rows)
        projected_ref[...] = projected
        for branch in range(copies_ref.shape[0]):
            copies_ref[branch] = projected
        for pair in range(leaves // 2):
            block = acc[2 * pair : 2 * pair + 2].reshape(2 * LEAF, samp_dev)
            out_ref[:, 2 * pair * LEAF : 2 * (pair + 1) * LEAF] = block.T


def far_products(total, group_leaf, group_slots, side, own, partner, high, low, weights, branches):
    part, unused, samp_dev = own.shape
    slots = 2 * part
    groups = group_leaf.shape[0]
    points_dev = weights.shape[1]
    leaves = points_dev // LEAF
    steps = groups // BATCH

    def block_index(step, total_ref, *unused):
        last = (total_ref[0] - 1) // BATCH
        return (jnp.minimum(step, last), 0, 0)

    return pl.pallas_call(
        functools.partial(far_body, cap=part // partner.shape[0]),
        grid_spec=pltpu.PrefetchScalarGridSpec(
            num_scalar_prefetch=4,
            grid=(steps,),
            in_specs=[
                pl.BlockSpec(own.shape, lambda *unused: (0, 0, 0), pipeline_mode=pl.Buffered(1)),
                pl.BlockSpec(partner.shape, lambda *unused: (0, 0, 0), pipeline_mode=pl.Buffered(1)),
                pl.BlockSpec((BATCH, LEAF, GROUP * LEAF), block_index),
                pl.BlockSpec((BATCH, LEAF, GROUP * LEAF), block_index),
                pl.BlockSpec(weights.shape, lambda *unused: (0, 0), pipeline_mode=pl.Buffered(1)),
            ],
            out_specs=[
                pl.BlockSpec((samp_dev, points_dev), lambda *unused: (0, 0)),
                pl.BlockSpec((weights.shape[0], samp_dev), lambda *unused: (0, 0)),
                pl.BlockSpec((branches, weights.shape[0], samp_dev), lambda *unused: (0, 0, 0)),
            ],
            scratch_shapes=[
                pltpu.VMEM((slots, LEAF, samp_dev), jnp.bfloat16),
                pltpu.VMEM((slots, LEAF, samp_dev), jnp.bfloat16),
                pltpu.VMEM((leaves, LEAF, samp_dev), jnp.float32),
            ],
        ),
        out_shape=[
            jax.ShapeDtypeStruct((samp_dev, points_dev), jnp.float32),
            jax.ShapeDtypeStruct((weights.shape[0], samp_dev), jnp.float32),
            jax.ShapeDtypeStruct((branches, weights.shape[0], samp_dev), jnp.float32),
        ],
        compiler_params=pltpu.CompilerParams(vmem_limit_bytes=vmem_bytes),
        name="far_products",
        cost_estimate=pl.CostEstimate(
            flops=10**6, bytes_accessed=10**4, transcendentals=0
        ),
    )(total, group_leaf, group_slots, side, own, partner, high, low, weights)


NEAR_LEAVES = 8


def near_body(mask_ref, rows_ref, coords_ref, target_ref, out_ref):
    step = pl.program_id(0)
    samp_dev = rows_ref.shape[2]
    lane = lax.broadcasted_iota(jnp.int32, (1, LANES), 1)
    first = lane < LEAF
    for pair in range(NEAR_LEAVES // 2):
        results = []
        for member in range(2):
            leaf = step * NEAR_LEAVES + 2 * pair + member
            target = target_ref[leaf]
            k_high = []
            k_low = []
            for half in range(2):
                both = jnp.where(first, coords_ref[leaf + 2 * half], coords_ref[leaf + 2 * half + 1])
                values = kernel_half(both, target, lane, LANES)
                left = mask_ref[leaf * 3 + 2 * half].astype(jnp.float32)
                if half == 0:
                    right = mask_ref[leaf * 3 + 1].astype(jnp.float32)
                else:
                    right = jnp.float32(0.0)
                high, low = halves(values * jnp.where(first, left, right))
                k_high.append(high)
                k_low.append(low)
            k_high = jnp.concatenate(k_high, axis=1)
            k_low = jnp.concatenate(k_low, axis=1)
            rows = rows_ref[pl.ds(leaf, 4)].reshape(4 * LEAF, samp_dev)
            rows_high, rows_low = halves(rows)
            results.append(
                dot(k_high, rows_high) + (dot(k_high, rows_low) + dot(k_low, rows_high))
            )
        block = jnp.concatenate(results, axis=0)
        out_ref[:, 2 * pair * LEAF : 2 * (pair + 1) * LEAF] = block.T


def near_products(mask, rows, coords, targets):
    leaves = targets.shape[0]
    samp_dev = rows.shape[2]
    whole = lambda *unused: (0, 0, 0)
    return pl.pallas_call(
        near_body,
        grid_spec=pltpu.PrefetchScalarGridSpec(
            num_scalar_prefetch=1,
            grid=(leaves // NEAR_LEAVES,),
            in_specs=[
                pl.BlockSpec(rows.shape, whole),
                pl.BlockSpec(coords.shape, whole),
                pl.BlockSpec(targets.shape, whole),
            ],
            out_specs=pl.BlockSpec((samp_dev, NEAR_LEAVES * LEAF), lambda step, *unused: (0, step)),
        ),
        out_shape=jax.ShapeDtypeStruct((samp_dev, leaves * LEAF), jnp.float32),
        compiler_params=pltpu.CompilerParams(vmem_limit_bytes=vmem_bytes),
        name="near_products",
        cost_estimate=pl.CostEstimate(
            flops=10**10, bytes_accessed=10**7, transcendentals=0
        ),
    )(mask, rows, coords, targets)


def to_lanes(source, target, rank):
    nodes = source.shape[0] // rank
    target[...] = jnp.zeros_like(target)
    for r in range(rank):
        target[r, :, 0:nodes] = source[pl.ds(r, nodes, stride=rank), :].T


def from_lanes(columns, target, r, nodes, rank):
    target[pl.ds(r, nodes, stride=rank), :] = columns.T[0:nodes]


def eliminate(current, left, inverse, level, rank):
    tiles = rank // SUB
    row = lax.broadcasted_iota(jnp.int32, (SUB, LANES), 0)
    diagonal = [current[j, j : j + 1, :] for j in range(rank)]
    while len(diagonal) > 1:
        diagonal = [diagonal[i] + diagonal[i + 1] for i in range(0, len(diagonal), 2)]
    share = shift_share * diagonal[0] / rank
    shift = share + 1e-06
    a = [
        {t: current[j, SUB * t : SUB * (t + 1), :] for t in range(j // SUB, tiles)}
        for j in range(rank)
    ]
    for j in range(rank):
        a[j][j // SUB] = a[j][j // SUB] + jnp.where(row == j % SUB, shift, 0.0)
    m = []
    scales = []
    for k in range(rank):
        tk, rk = k // SUB, k % SUB
        root = lax.rsqrt(a[k][tk][rk : rk + 1, :])
        scales.append(root)
        reciprocal = root * root
        column = {t: a[k][t] * reciprocal for t in range(tk, tiles)}
        column[tk] = jnp.where(row > rk, column[tk], 0.0)
        for j in range(k + 1, rank):
            factor = a[k][j // SUB][j % SUB : j % SUB + 1, :]
            for t in range(j // SUB, tiles):
                a[j][t] = a[j][t] - column[t] * factor
        for c in range(k):
            factor = m[c][tk][rk : rk + 1, :]
            for t in range(tk, tiles):
                m[c][t] = m[c][t] - column[t] * factor
        fresh = {t: -column[t] for t in range(tk, tiles)}
        fresh[tk] = jnp.where(row == rk, 1.0, fresh[tk])
        m.append(fresh)
        if left is not None:
            for t in range(tiles):
                if t < tk:
                    value = jnp.zeros((SUB, LANES), jnp.float32)
                else:
                    value = a[k][t] * root
                if t == tk:
                    value = jnp.where(row >= rk, value, 0.0)
                left[k, SUB * t : SUB * (t + 1), :] = value
    for t in range(tiles):
        scale = jnp.concatenate(scales[SUB * t : SUB * (t + 1)], axis=0)
        for c in range(rank):
            value = m[c][t] * scale if t >= c // SUB else jnp.zeros((SUB, LANES), jnp.float32)
            inverse[c * rank + SUB * t : c * rank + SUB * (t + 1), :] = value
    return shift, share


def inverse_row(inverse, r, t, rank):
    return inverse[pl.ds(SUB * t * rank + r, SUB, stride=rank), :]


def pair_up(value, level):
    reach = LANES - (1 << level if isinstance(level, int) else lax.shift_left(1, level))
    return value + pltpu.roll(value, reach, 1)


def when(condition):
    if isinstance(condition, bool):
        return lambda body: body() if condition else None
    return pl.when(condition)


def level_fast(level, levels, current, left, inverse, squared, ratio, child, lowest, rank, child_at):
    tiles = rank // SUB
    row = lax.broadcasted_iota(jnp.int32, (SUB, LANES), 0)
    shift, share = eliminate(current, left, inverse, level, rank)
    lowest[...] = jnp.minimum(lowest[...], share)

    for block in range(tiles):
        sums = [[None] * tiles for _ in range(SUB)]
        for r in range(SUB * block, rank):
            parts = [inverse_row(inverse, r, t, rank) for t in range(block, r // SUB + 1)]
            for q in range(SUB):
                if SUB * block + q > r:
                    continue
                factor = parts[0][q : q + 1, :]
                for t in range(block, r // SUB + 1):
                    term = parts[t - block] * factor
                    sums[q][t] = term if sums[q][t] is None else sums[q][t] + term
        for q in range(SUB):
            at = (SUB * block + q) * rank
            for t in range(block, tiles):
                squared[at + SUB * t : at + SUB * (t + 1), :] = sums[q][t]

    if child is not None:
        @when(child_at(level))
        def _():
            for r in range(rank):
                for t in range(tiles):
                    value = left[r, SUB * t : SUB * (t + 1), :]
                    if t <= r // SUB:
                        value = value - shift * inverse_row(inverse, r, t, rank)
                    child[r, SUB * t : SUB * (t + 1), :] = value

    for q in range(rank):
        for t in range(tiles):
            if t >= q // SUB:
                value = squared[q * rank + SUB * t : q * rank + SUB * (t + 1), :]
            else:
                value = squared[pl.ds(SUB * t * rank + q, SUB, stride=rank), :]
            value = -shift * value
            if t == q // SUB:
                value = value + jnp.where(row == q % SUB, 1.0, 0.0)
            if ratio is not None:
                ratio[level, q, SUB * t : SUB * (t + 1), :] = value
            here = current[q, SUB * t : SUB * (t + 1), :] - shift * value
            current[q, SUB * t : SUB * (t + 1), :] = pair_up(here, level)


def level_plain(level, levels, current, left, inverse, squared, ratio, child, lowest, rank, child_at):
    tiles = rank // SUB
    eliminate(current, left, inverse, level, rank)

    def products(out, count, left_of, right_of):
        def block_step(block, carry):
            offset = pl.multiple_of(block * SUB, SUB)
            sums = [[None] * tiles for _ in range(SUB)]
            for r in range(count):
                parts = [left_of(r, t) for t in range(tiles)]
                heads = right_of(r, offset)
                for q in range(SUB):
                    for t in range(tiles):
                        term = parts[t] * heads[q : q + 1, :]
                        sums[q][t] = term if sums[q][t] is None else sums[q][t] + term
            for q in range(SUB):
                for t in range(tiles):
                    out(offset + q, t, sums[q][t])
            return carry

        lax.fori_loop(0, tiles, block_step, 0)

    def tile(t):
        return slice(SUB * t, SUB * (t + 1))

    def put_child(r, t, value):
        squared[pl.ds(pl.multiple_of(r * rank + SUB * t, SUB), SUB), :] = value

    products(
        put_child, rank,
        lambda k, t: current[k, tile(t), :],
        lambda k, offset: inverse[pl.ds(pl.multiple_of(k * rank + offset, SUB), SUB), :],
    )
    if child is not None:
        @when(child_at(level))
        def _():
            for r in range(rank):
                for t in range(tiles):
                    child[r, tile(t), :] = squared[r * rank + SUB * t : r * rank + SUB * (t + 1), :]

    def child_part(r, t):
        return squared[r * rank + SUB * t : r * rank + SUB * (t + 1), :]

    def put_current(q, t, value):
        current[q, tile(t), :] = pair_up(value, level)

    if ratio is not None:
        def put_ratio(c, t, value):
            ratio[level, c, tile(t), :] = value

        def inverse_head(r, offset):
            return inverse[pl.ds(offset * rank + r, SUB, stride=rank), :]

        products(put_ratio, rank, child_part, inverse_head)
    products(
        put_current, rank, child_part,
        lambda r, offset: squared[pl.ds(pl.multiple_of(r * rank + offset, SUB), SUB), :],
    )


def run_levels(source, levels, nodes, current, left, inverse, squared, ratio, child, lowest, rank, child_at, finish, unrolled=False):
    lowest[...] = jnp.full((1, LANES), 1.0, jnp.float32)

    def sweep(level_step):
        to_lanes(source, current, rank)

        def body(level, carry):
            level_step(level, levels, current, left, inverse, squared, ratio, child, lowest, rank, child_at)
            finish(level)
            return carry

        if unrolled and level_step is level_fast:
            for level in range(levels):
                body(level, 0)
        else:
            lax.fori_loop(0, levels, body, 0)

    sweep(level_fast)
    lane = lax.broadcasted_iota(jnp.int32, (1, LANES), 1)
    least = jnp.min(jnp.where(lane < nodes, lowest[...], 1.0))

    @pl.when(least < 2e-06)
    def _():
        sweep(level_plain)


def branch_body(gram_ref, inverse_ref, ratio_ref, top_ref, child_ref, current, left, inverse, squared, child, lowest, *, rank, levels):
    nodes = gram_ref.shape[0] // rank

    def finish(level):
        @pl.when(level == 0)
        def _():
            for c in range(rank):
                inverse_ref[c] = inverse[c * rank : (c + 1) * rank, :]

        @pl.when(level == levels - 1)
        def _():
            for r in range(rank):
                width = child_ref.shape[1]
                at = r * rank
                child_ref[at // width : at // width + 1, at % width : at % width + rank] = child[r].T[0:1, :]
                top_ref[r : r + 1, :] = jnp.concatenate(
                    [inverse_row(inverse, r, t, rank) for t in range(rank // SUB)], axis=0
                ).T[0:1, :]

    run_levels(
        gram_ref, levels, nodes, current, left, inverse, squared, ratio_ref, child, lowest, rank,
        lambda level: level == levels - 1, finish,
    )


vmem_spec = pl.BlockSpec(memory_space=pltpu.VMEM)


def tree_scratch(rank):
    return [
        pltpu.VMEM((rank, rank, LANES), jnp.float32),
        pltpu.VMEM((rank, rank, LANES), jnp.float32),
        pltpu.VMEM((rank * rank, LANES), jnp.float32),
        pltpu.VMEM((rank * rank, LANES), jnp.float32),
        pltpu.VMEM((rank, rank, LANES), jnp.float32),
        pltpu.VMEM((1, LANES), jnp.float32),
    ]


def branch_factors(gram, levels, width):
    leaves, rank, unused = gram.shape
    return pl.pallas_call(
        functools.partial(branch_body, rank=rank, levels=levels),
        in_specs=[vmem_spec],
        out_specs=[vmem_spec] * 4,
        out_shape=[
            jax.ShapeDtypeStruct((rank, rank, LANES), jnp.float32),
            jax.ShapeDtypeStruct((levels, rank, rank, LANES), jnp.float32),
            jax.ShapeDtypeStruct((rank, rank), jnp.float32),
            jax.ShapeDtypeStruct((rank * rank // width, width), jnp.float32),
        ],
        scratch_shapes=tree_scratch(rank),
        compiler_params=pltpu.CompilerParams(vmem_limit_bytes=vmem_bytes),
        name="branch_factors",
        cost_estimate=pl.CostEstimate(flops=10**6, bytes_accessed=10**4, transcendentals=0),
    )(gram.reshape(leaves * rank, rank))


def basis_body(inverse_ref, ratio_ref, top_ref, sketched_ref, weights_ref, basis_ref, natural, *, rank, levels):
    leaves = sketched_ref.shape[0]
    upper = [top_ref[...]]
    for level in range(levels - 2, -1, -1):
        stride = 2**level
        for c in range(rank):
            from_lanes(ratio_ref[level, c], natural, c, leaves, rank)
        fresh = []
        for node in range(leaves // stride):
            block = natural[node * stride * rank : (node * stride + 1) * rank, :]
            fresh.append(dot_exact(upper[node // 2], block))
        upper = fresh
    for r in range(rank):
        from_lanes(inverse_ref[r], natural, r, leaves, rank)
    for pair in range(leaves // 2):
        results = []
        for leaf in (2 * pair, 2 * pair + 1):
            block = sketched_ref[leaf]
            own = lax.dot_general(
                natural[leaf * rank : (leaf + 1) * rank, :], block, tn_dims,
                precision=highest, preferred_element_type=jnp.float32,
            )
            results.append(jnp.concatenate([dot_exact(upper[leaf], block), own], axis=0))
        both = jnp.concatenate(results, axis=1)
        weights_ref[:, pair * 2 * LEAF : (pair + 1) * 2 * LEAF] = both[:rank]
        basis_ref[:, pair * 2 * LEAF : (pair + 1) * 2 * LEAF] = both[rank:]


def bases(inverse, ratio, top, sketched):
    leaves, rank, unused = sketched.shape
    levels = ratio.shape[0]
    shape = jax.ShapeDtypeStruct((rank, leaves * LEAF), jnp.float32)
    return pl.pallas_call(
        functools.partial(basis_body, rank=rank, levels=levels),
        in_specs=[vmem_spec] * 4,
        out_specs=[vmem_spec] * 2,
        out_shape=[shape, shape],
        scratch_shapes=[pltpu.VMEM((leaves * rank, rank), jnp.float32)],
        compiler_params=pltpu.CompilerParams(vmem_limit_bytes=vmem_bytes),
        name="bases",
        cost_estimate=pl.CostEstimate(flops=10**10, bytes_accessed=10**7, transcendentals=0),
    )(inverse, ratio, top, sketched)


def top_body(side_ref, mine_ref, mirrored_ref, transfer_ref, paths_ref, children_ref, source, current, left, inverse, squared, child, lowest, nat_inverse, nat_child, *, rank, levels):
    half, packed_rows_each, width = mine_ref.shape
    nodes = half
    every = width // rank
    count = half * packed_rows_each
    for ref, side in ((mine_ref, side_ref[0]), (mirrored_ref, 1 - side_ref[0])):
        flat = ref[...].reshape(count, width)
        base = pl.multiple_of(side * (half * rank), half * rank)
        for part in range(every):
            children_ref[pl.ds(base + part, count, stride=every), :] = flat[:, part * rank : (part + 1) * rank]
    for node in range(nodes):
        both = children_ref[2 * node * rank : (2 * node + 2) * rank, :]
        source[node * rank : (node + 1) * rank, :] = lax.dot_general(
            both, both, tn_dims, precision=highest, preferred_element_type=jnp.float32
        )

    def finish(level):
        for r in range(rank):
            from_lanes(child[r], nat_child.at[level], r, nodes, rank)
            from_lanes(inverse[r * rank : (r + 1) * rank, :], nat_inverse.at[level], r, nodes, rank)

    run_levels(
        source, levels, nodes, current, left, inverse, squared, None, child, lowest, rank,
        lambda level: True, finish, unrolled=True,
    )
    offset = 0
    for level in range(levels):
        for node in range(nodes >> level):
            if level == 0:
                stacked = children_ref[2 * node * rank : (2 * node + 2) * rank, :]
            else:
                first = 2 * node << level - 1
                second = 2 * node + 1 << level - 1
                stacked = jnp.concatenate(
                    [
                        nat_child[level - 1, first * rank : (first + 1) * rank, :],
                        nat_child[level - 1, second * rank : (second + 1) * rank, :],
                    ],
                    axis=0,
                )
            at = (node << level) * rank
            transfer_ref[offset + node] = lax.dot_general(
                nat_inverse[level, at : at + rank, :], stacked, (((0,), (1,)), ((), ())),
                precision=highest, preferred_element_type=jnp.float32,
            )
        offset += nodes >> level
    above = [None]
    for level in range(levels - 1, -1, -1):
        offset -= nodes >> level
        fresh = []
        for node in range(nodes >> level):
            both = transfer_ref[offset + node]
            if above[0] is None:
                both = both.T
            else:
                both = lax.dot_general(
                    both, above[node], tn_dims, precision=highest, preferred_element_type=jnp.float32
                )
            fresh += [both[:rank], both[rank:]]
        above = fresh
    for branch in range(2 * nodes):
        paths_ref[branch * rank : (branch + 1) * rank, :] = above[branch]


def top_factors(side, mine, mirrored, rank):
    branches = 2 * mine.shape[0]
    levels = branches.bit_length() - 1
    nodes = branches // 2
    natural = pltpu.VMEM((levels, nodes * rank, rank), jnp.float32)
    return pl.pallas_call(
        functools.partial(top_body, rank=rank, levels=levels),
        in_specs=[pl.BlockSpec(memory_space=pltpu.SMEM), vmem_spec, vmem_spec],
        out_specs=[vmem_spec] * 2,
        out_shape=[
            jax.ShapeDtypeStruct((branches - 1, rank, 2 * rank), jnp.float32),
            jax.ShapeDtypeStruct((branches * rank, rank), jnp.float32),
        ],
        scratch_shapes=[
            pltpu.VMEM((branches * rank, rank), jnp.float32),
            pltpu.VMEM((nodes * rank, rank), jnp.float32),
        ]
        + tree_scratch(rank)
        + [natural, natural],
        compiler_params=pltpu.CompilerParams(vmem_limit_bytes=vmem_bytes),
        name="top_factors",
        cost_estimate=pl.CostEstimate(flops=10**10, bytes_accessed=10**7, transcendentals=0),
    )(side, mine, mirrored)


def exchange_sum(pieces, axis):
    count = pieces.shape[0]
    me = lax.axis_index(axis)
    mine = lax.dynamic_index_in_dim(pieces, me, 0, keepdims=False)
    for step in range(1, count):
        outgoing = lax.dynamic_index_in_dim(pieces, (me + step) % count, 0, keepdims=False)
        mine = mine + lax.ppermute(
            outgoing, axis, [(i, (i + step) % count) for i in range(count)]
        )
    return mine


def exchange_all(piece, axis):
    count = lax.axis_size(axis)
    me = lax.axis_index(axis)
    if count == 2:
        other = lax.ppermute(piece, axis, [(0, 1), (1, 0)])
        return jnp.stack([jnp.where(me == 0, piece, other), jnp.where(me == 0, other, piece)])
    result = jnp.zeros((count,) + piece.shape, piece.dtype)
    result = lax.dynamic_update_index_in_dim(result, piece, me, 0)
    for step in range(1, count):
        arrived = lax.ppermute(piece, axis, [(i, (i + step) % count) for i in range(count)])
        result = lax.dynamic_update_index_in_dim(result, arrived, (me - step) % count, 0)
    return result


def group_tables(far_slots, far_count):
    leaves = far_slots.shape[0]
    groups = leaves * FAR // GROUP
    per_leaf = (far_count + GROUP - 1) // GROUP
    before = jnp.arange(leaves)[:, None] >= jnp.arange(leaves)[None, :]
    ends = jnp.sum(jnp.where(before, per_leaf[None, :], 0), axis=1)
    total = ends[leaves - 1 :]
    ids = jnp.arange(groups, dtype=jnp.int32)
    leaf = jnp.minimum(jnp.sum((ends[None, :] <= ids[:, None]).astype(jnp.int32), axis=1), leaves - 1)
    hit = leaf[:, None] == jnp.arange(leaves)[None, :]
    start = jnp.sum(jnp.where(hit, (ends - per_leaf)[None, :], 0), axis=1)
    length = jnp.sum(jnp.where(hit, far_count[None, :], 0), axis=1)
    sub = ids - start
    count = jnp.where(ids < total, jnp.clip(length - GROUP * sub, 0, GROUP), 0)
    first = jnp.minimum(sub, FAR // GROUP - 1)
    slots = far_slots.reshape(leaves * FAR // GROUP, GROUP)[leaf * (FAR // GROUP) + first]
    return (
        total.astype(jnp.int32),
        leaf.astype(jnp.int32),
        count.astype(jnp.int32),
        slots.reshape(-1).astype(jnp.int32),
    )


def sketch_body(place_ref, sketch_ref, samples_ref, points_ref, mine_ref, other_ref):
    product = dot_exact(sketch_ref[...], samples_ref[...])
    rank, points_dev = product.shape
    quarter = rank // 4
    first = lax.broadcasted_iota(jnp.int32, (1, LANES), 1) < LEAF
    swap = place_ref[0] == 1
    leaves = points_dev // LEAF

    def interleave(low, high):
        even = jnp.where(first, low, pltpu.roll(high, LEAF, 1))
        odd = jnp.where(first, pltpu.roll(low, LEAF, 1), high)
        return even, odd

    for pair in range(leaves // 2):
        lanes = slice(pair * LANES, (pair + 1) * LANES)
        shares = []
        for share in range(2):
            base = 2 * quarter * share
            shares.append(
                interleave(product[base : base + quarter, lanes], product[base + quarter : base + 2 * quarter, lanes])
            )
        for member in range(2):
            at = (2 * pair + member) * quarter
            mine_ref[at : at + quarter, :] = jnp.where(swap, shares[1][member], shares[0][member])
            other_ref[at : at + quarter, :] = jnp.where(swap, shares[0][member], shares[1][member])
        x = points_ref[0:1, lanes]
        y = points_ref[1:2, lanes]
        z = points_ref[2:3, lanes]
        xy = interleave(x, y)
        zs = interleave(z, jnp.zeros_like(z))
        for member in range(2):
            at = leaves * quarter + (2 * pair + member) * 2
            mine_ref[at : at + 1, :] = xy[member]
            mine_ref[at + 1 : at + 2, :] = zs[member]
    other_ref[leaves * quarter :, :] = jnp.zeros((2 * leaves, LANES), jnp.float32)


def sketched_shares(place, sketch, samples, points):
    rank = sketch.shape[0]
    leaves = samples.shape[1] // LEAF
    return pl.pallas_call(
        sketch_body,
        in_specs=[pl.BlockSpec(memory_space=pltpu.SMEM)] + [vmem_spec] * 3,
        out_specs=[vmem_spec] * 2,
        out_shape=[
            jax.ShapeDtypeStruct((leaves * (rank // 4 + 2), LANES), jnp.float32),
            jax.ShapeDtypeStruct((leaves * (rank // 4 + 2), LANES), jnp.float32),
        ],
        compiler_params=pltpu.CompilerParams(vmem_limit_bytes=vmem_bytes),
        name="sketched_shares",
        cost_estimate=pl.CostEstimate(flops=10**6, bytes_accessed=10**4, transcendentals=0),
    )(place, sketch, samples, points)


def pack_body(asked_ref, side_ref, mine_ref, partner_ref, out_ref, *, cap, leaves):
    z_rows = mine_ref.shape[0] // leaves - 2
    side = side_ref[0]

    def one(peer, carry):
        for entry in range(2 * cap):
            leaf = asked_ref[peer, entry]
            here = side == entry // cap
            at = pl.ds(leaf * z_rows, z_rows)
            out_ref[peer, z_rows * entry : z_rows * (entry + 1), :] = jnp.where(
                here, mine_ref[at, :], partner_ref[at, :]
            )
            base = z_rows * 2 * cap + 2 * entry
            at = pl.ds(leaves * z_rows + leaf * 2, 2)
            out_ref[peer, base : base + 2, :] = jnp.where(here, mine_ref[at, :], partner_ref[at, :])
        return carry

    lax.fori_loop(0, out_ref.shape[0], one, 0)


def packed_rows(asked, side, mine, partner, cap, leaves):
    z_rows = mine.shape[0] // leaves - 2
    return pl.pallas_call(
        functools.partial(pack_body, cap=cap, leaves=leaves),
        in_specs=[pl.BlockSpec(memory_space=pltpu.SMEM)] * 2 + [vmem_spec] * 2,
        out_specs=vmem_spec,
        out_shape=jax.ShapeDtypeStruct((asked.shape[0], 2 * cap * (z_rows + 2), LANES), jnp.float32),
        compiler_params=pltpu.CompilerParams(vmem_limit_bytes=vmem_bytes),
        name="packed_rows",
    )(asked, side, mine, partner)


def payload_body(asked_ref, side_ref, rows_ref, child_ref, out_ref, *, cap):
    base = (1 - side_ref[0]) * cap

    def one(peer, carry):
        for entry in range(cap):
            out_ref[peer, LEAF * entry : LEAF * (entry + 1), :] = rows_ref[asked_ref[peer, base + entry]]
        out_ref[peer, LEAF * cap :, :] = child_ref[...]
        return carry

    lax.fori_loop(0, out_ref.shape[0], one, 0)


def payload_rows(asked, side, rows, child):
    half = asked.shape[0]
    cap = asked.shape[1] // 2
    return pl.pallas_call(
        functools.partial(payload_body, cap=cap),
        in_specs=[pl.BlockSpec(memory_space=pltpu.SMEM)] * 2 + [vmem_spec] * 2,
        out_specs=vmem_spec,
        out_shape=jax.ShapeDtypeStruct((half, cap * LEAF + child.shape[0], rows.shape[2]), jnp.float32),
        compiler_params=pltpu.CompilerParams(vmem_limit_bytes=vmem_bytes),
        name="payload_rows",
    )(asked, side, rows, child)


def root_body(paths_ref, parts_ref, root_ref):
    root_ref[...] = lax.dot_general(
        paths_ref[...], parts_ref[...], tn_dims, precision=highest, preferred_element_type=jnp.float32
    )


def root_product(paths, parts):
    return pl.pallas_call(
        root_body,
        in_specs=[vmem_spec] * 2,
        out_specs=vmem_spec,
        out_shape=jax.ShapeDtypeStruct((paths.shape[1], parts.shape[1]), jnp.float32),
        compiler_params=pltpu.CompilerParams(vmem_limit_bytes=vmem_bytes),
        name="root_product",
    )(paths, parts)


def two_rows(values, rows):
    leaves = values.shape[1]
    split = jnp.transpose(values.reshape(2, rows, leaves, LEAF), (2, 1, 0, 3))
    return split.reshape(leaves, rows, 2 * LEAF)


def on_device(points, samples, sketch, far_requests, far_slots, far_count, near_mask):
    samp_dev = samples.shape[0]
    leaves = samples.shape[1] // LEAF
    rank = sketch.shape[0]
    branches = lax.axis_size("leaf")
    columns = lax.axis_size("cols")
    cap = far_requests.shape[2]
    share = rank // columns
    me = lax.axis_index("leaf")
    column = lax.axis_index("cols")

    half = branches // 2
    side = me // half
    groups = [list(range(half)), list(range(half, branches))]
    mirror = [(i, (i + half) % branches) for i in range(branches)]
    side_ref = side.astype(jnp.int32).reshape(1)
    wanted = jnp.transpose(far_requests.reshape(2, half, cap), (1, 0, 2)).reshape(half, 2 * cap)
    asked = lax.all_to_all(
        wanted, "leaf", split_axis=0, concat_axis=0, axis_index_groups=groups, tiled=True
    )

    if columns == 2:
        place = column.astype(jnp.int32).reshape(1)
        mine, other = sketched_shares(place, sketch, samples, points)
        mine = mine + lax.ppermute(other, "cols", [(0, 1), (1, 0)])
    else:
        z_part = jnp.dot(sketch, samples, precision=highest)
        z_mine = exchange_sum(z_part.reshape(columns, share, leaves * LEAF), "cols")
        z_rows = two_rows(z_mine.reshape(share, leaves, LEAF), share // 2)
        planes = points.reshape(3, leaves, LEAF)
        c_rows = two_rows(
            jnp.concatenate([planes[0:1], planes[2:3], planes[1:2], jnp.zeros_like(planes[0:1])], axis=0), 2
        )
        mine = jnp.concatenate([z_rows.reshape(-1, LANES), c_rows.reshape(-1, LANES)], axis=0)

    partner = lax.ppermute(mine, "leaf", mirror)
    coords = jnp.transpose(points.reshape(3, leaves, LEAF), (1, 0, 2))
    targets = jnp.transpose(coords, (0, 2, 1))
    rows = jnp.transpose(samples.reshape(samp_dev, leaves, LEAF), (1, 2, 0))

    forward = [(i, i + 1) for i in range(branches - 1)]
    backward = [(target, source) for source, target in forward]
    width = max(samp_dev, LEAF)

    def edge(first):
        samples_edge = jnp.transpose(lax.slice_in_dim(samples, first, first + LEAF, axis=1))
        points_edge = lax.slice_in_dim(points, first, first + LEAF, axis=1)
        return jnp.concatenate(
            [
                jnp.pad(samples_edge, ((0, 0), (0, width - samp_dev))),
                jnp.pad(points_edge, ((0, 5), (0, width - LEAF))),
            ],
            axis=0,
        )

    low_edge = lax.ppermute(edge((leaves - 1) * LEAF), "leaf", forward)
    high_edge = lax.ppermute(edge(0), "leaf", backward)

    tables = group_tables(far_slots, far_count)
    asked, low_edge, high_edge, rows, targets, tables = lax.optimization_barrier(
        (asked, low_edge, high_edge, rows, targets, tables)
    )
    total, group_leaf, group_count, group_slots = tables
    small_sent = packed_rows(asked, side_ref, mine, partner, cap, leaves)
    small_got = lax.all_to_all(
        small_sent, "leaf", split_axis=0, concat_axis=0, axis_index_groups=groups, tiled=True
    )

    rows_out, unused = lax.optimization_barrier((rows, small_sent))
    partner_rows = lax.ppermute(rows_out, "leaf", mirror)

    own_asked = lax.dynamic_slice_in_dim(asked, side * cap, cap, axis=1)
    own_sent = rows_out[own_asked.reshape(-1)].reshape(half, cap, LEAF, samp_dev)
    own_got = lax.all_to_all(
        own_sent, "leaf", split_axis=0, concat_axis=0, axis_index_groups=groups, tiled=True
    )
    own_got = own_got.reshape(half * cap, LEAF, samp_dev)

    if columns == 2:
        small_other = lax.ppermute(small_got, "cols", [(0, 1), (1, 0)])
    else:
        z_count = cap * share
        z_all = exchange_all(small_got[:, :z_count], "cols")
        z_all = z_all.reshape(columns, half, 2 * cap, share // 2, 2, LEAF)
        z_all = jnp.transpose(z_all, (1, 2, 0, 4, 3, 5)).reshape(half, 2 * cap, 2, 2, rank // 4, LEAF)
        z_all = jnp.transpose(z_all, (2, 0, 1, 4, 3, 5)).reshape(2, half, cap * rank // 2, LANES)
        c_got = small_got[:, z_count:]
        small_got = jnp.concatenate([z_all[0], c_got], axis=1)
        small_other = jnp.concatenate([z_all[1], c_got], axis=1)
        place = jnp.zeros((1,), jnp.int32)

    high, low, sketched, gram = kernel_blocks(
        total, group_leaf, group_count, group_slots, place, small_got, small_other, targets, rank, cap
    )

    levels = leaves.bit_length()
    inverse, ratio, top_inverse, own_child = branch_factors(gram, levels, min(samp_dev, LANES))
    own_child, own_got, partner_rows = lax.optimization_barrier((own_child, own_got, partner_rows))
    payload = payload_rows(asked, side_ref, partner_rows, own_child)
    arrived = lax.all_to_all(
        payload, "leaf", split_axis=0, concat_axis=0, axis_index_groups=groups, tiled=True
    )
    ratio, low_edge, high_edge, unused = lax.optimization_barrier((ratio, low_edge, high_edge, payload))
    weights, leaf_basis = bases(inverse, ratio, top_inverse, sketched)

    rows_low, rows_high = low_edge[:LEAF, :samp_dev], high_edge[:LEAF, :samp_dev]
    coords_low, coords_high = low_edge[LEAF : LEAF + 3, :LEAF], high_edge[LEAF : LEAF + 3, :LEAF]
    near_rows = jnp.concatenate(
        [rows_low[None], rows, rows_high[None], jnp.zeros_like(rows_low)[None]], axis=0
    )
    near_coords = jnp.concatenate(
        [coords_low[None], coords, coords_high[None], jnp.zeros_like(coords_low)[None]], axis=0
    )
    near_coords = jnp.pad(near_coords, ((0, 0), (0, 5), (0, 0)))
    near_coords = jnp.concatenate([near_coords, near_coords], axis=2)
    near_sample = near_products(near_mask.reshape(-1), near_rows, near_coords, targets)


    children = arrived[:, cap * LEAF :]
    mirrored = lax.ppermute(children, "leaf", mirror)
    weights, near_sample = lax.optimization_barrier((weights, near_sample))
    far_sample, branch_samples, copies = far_products(
        total, group_leaf, group_slots, side_ref, own_got, arrived, high, low, weights, branches
    )
    everyone = lax.all_to_all(copies, "leaf", split_axis=0, concat_axis=0, tiled=True)
    children, mirrored, unused = lax.optimization_barrier((children, mirrored, branch_samples))
    transfer_t, paths = top_factors(side_ref, children, mirrored, rank)
    top_transfer = jnp.swapaxes(transfer_t, 1, 2)
    root_sample = root_product(paths, everyone.reshape(branches * rank, samp_dev))
    return (far_sample, near_sample, leaf_basis, branch_samples, top_transfer, root_sample)


def solution(mesh):
    return jax.shard_map(
        on_device,
        mesh=mesh,
        in_specs=(
            P(None, "leaf"),
            P("cols", "leaf"),
            P(None, "cols"),
            P("leaf", None, None),
            P("leaf", None),
            P("leaf"),
            P("leaf", None),
        ),
        out_specs=(
            P("cols", "leaf"),
            P("cols", "leaf"),
            P(None, "leaf"),
            P("leaf", "cols"),
            P(),
            P(None, "cols"),
        ),
        check_vma=False,
    )
```

```python
import functools
import math

import jax
import jax.numpy as jnp
import numpy as np
from jax import lax
from jax.experimental import pallas as pl
from jax.experimental.pallas import tpu as pltpu
from jax.sharding import PartitionSpec as P

LEAF = 64
FAR = 16
GROUP = 4
BATCH = 16
LANES = 128
SUB = 8

length_scale = 0.3
shift_share = 0.05
highest = lax.Precision.HIGHEST
exponent_scale = -math.log2(math.e) / length_scale
vmem_bytes = 56 * 1024 * 1024

nt_dims = (((1,), (1,)), ((), ()))
tn_dims = (((0,), (0,)), ((), ()))


def halves(value):
    high = value.astype(jnp.bfloat16)
    low = (value - high.astype(jnp.float32)).astype(jnp.bfloat16)
    return high, low


def dot(a, b):
    return jnp.dot(a, b, preferred_element_type=jnp.float32)


def dot_exact(a, b):
    return jnp.dot(a, b, precision=highest, preferred_element_type=jnp.float32)


def dot_exact_nt(a, b):
    return lax.dot_general(a, b, nt_dims, precision=highest, preferred_element_type=jnp.float32)


def dot_nt(a, b):
    return lax.dot_general(a, b, nt_dims, preferred_element_type=jnp.float32)


def kernel_half(source_rows, target, lane, valid):
    total = None
    for axis in range(3):
        difference = source_rows[axis : axis + 1, :] - target[:, axis : axis + 1]
        square = difference * difference
        total = square if total is None else total + square
    distance = total * lax.rsqrt(jnp.maximum(total, 1e-30))
    values = jnp.exp2(distance * exponent_scale)
    return jnp.where(lane < valid, values, 0.0)


def blocks_body(
    total_ref, leaf_ref, count_ref, slot_ref, place_ref,
    own_ref, other_ref, target_ref,
    high_ref, low_ref, sketched_ref, gram_ref,
    packed,
    *, rank, cap,
):
    step = pl.program_id(0)
    lane = lax.broadcasted_iota(jnp.int32, (1, LANES), 1)
    first = lane < LEAF

    @pl.when(step == 0)
    def _():
        sketched_ref[...] = jnp.zeros_like(sketched_ref)
        quarter = rank // 4
        slots = packed.shape[0]
        own_at = pl.multiple_of(place_ref[0] * 2 * quarter, quarter)
        other_at = pl.multiple_of((1 - place_ref[0]) * 2 * quarter, quarter)

        def unpack(peer, carry):
            for entry in range(2 * cap):
                slot = (entry // cap) * (slots // 2) + peer * cap + entry % cap
                at = entry * quarter
                for ref, base in ((own_ref, own_at), (other_ref, other_at)):
                    value = ref[peer, at : at + quarter, :]
                    turned = pltpu.roll(value, LEAF, 1)
                    packed[slot, pl.ds(base, quarter), :] = jnp.where(first, value, turned)
                    packed[slot, pl.ds(base + quarter, quarter), :] = jnp.where(first, turned, value)
                at = 2 * cap * quarter + 2 * entry
                value = own_ref[peer, at : at + 2, :]
                turned = pltpu.roll(value, LEAF, 1)
                packed[slot, rank : rank + 1, :] = jnp.where(first, value, turned)[0:1]
                packed[slot, rank + 1 : rank + 2, :] = jnp.where(first, turned, value)[0:1]
                packed[slot, rank + 2 : rank + 3, :] = jnp.where(first, value, turned)[1:2]
            return carry

        lax.fori_loop(0, slots // (2 * cap), unpack, 0)

    @pl.when(step * BATCH < total_ref[0])
    def _():
        for member in range(BATCH):
            group = step * BATCH + member
            leaf = leaf_ref[group]
            count = count_ref[group]
            slots = [slot_ref[group * GROUP + e] for e in range(GROUP)]
            target = target_ref[leaf]
            z_parts = []
            for half in range(GROUP // 2):
                left = packed[slots[2 * half]]
                right = packed[slots[2 * half + 1]]
                both = jnp.where(first, left, right)
                values = kernel_half(both[rank : rank + 3], target, lane, (count - 2 * half) * LEAF)
                high, low = halves(values)
                high_ref[member, :, half * LANES : (half + 1) * LANES] = high
                low_ref[member, :, half * LANES : (half + 1) * LANES] = low
                z_parts.append(both[:rank])
            z_high, z_low = halves(jnp.concatenate(z_parts, axis=1))
            k_high = high_ref[member]
            k_low = low_ref[member]
            both = dot_nt(jnp.concatenate([z_high, z_low], axis=0), k_high)
            update = both[:rank] + (both[rank:] + dot_nt(z_high, k_low))
            sketched_ref[leaf] += update

    @pl.when(step == pl.num_programs(0) - 1)
    def _():
        for leaf in range(gram_ref.shape[0]):
            block = sketched_ref[leaf]
            gram_ref[leaf] = dot_exact_nt(block, block)


def kernel_blocks(total, group_leaf, group_count, group_slots, place, own, other, targets, rank, cap):
    leaves = targets.shape[0]
    groups = group_leaf.shape[0]
    slots = own.shape[0] * 2 * cap
    steps = groups // BATCH

    def block_index(step, total_ref, *unused):
        last = (total_ref[0] - 1) // BATCH
        return (jnp.minimum(step, last), 0, 0)

    whole = lambda *unused: (0, 0, 0)
    once = pl.Buffered(1)
    return pl.pallas_call(
        functools.partial(blocks_body, rank=rank, cap=cap),
        grid_spec=pltpu.PrefetchScalarGridSpec(
            num_scalar_prefetch=5,
            grid=(steps,),
            in_specs=[
                pl.BlockSpec(own.shape, whole, pipeline_mode=once),
                pl.BlockSpec(other.shape, whole, pipeline_mode=once),
                pl.BlockSpec(targets.shape, whole, pipeline_mode=once),
            ],
            out_specs=[
                pl.BlockSpec((BATCH, LEAF, GROUP * LEAF), block_index),
                pl.BlockSpec((BATCH, LEAF, GROUP * LEAF), block_index),
                pl.BlockSpec((leaves, rank, LEAF), whole),
                pl.BlockSpec((leaves, rank, rank), whole),
            ],
            scratch_shapes=[pltpu.VMEM((slots, rank + SUB, LANES), jnp.float32)],
        ),
        out_shape=[
            jax.ShapeDtypeStruct((groups, LEAF, GROUP * LEAF), jnp.bfloat16),
            jax.ShapeDtypeStruct((groups, LEAF, GROUP * LEAF), jnp.bfloat16),
            jax.ShapeDtypeStruct((leaves, rank, LEAF), jnp.float32),
            jax.ShapeDtypeStruct((leaves, rank, rank), jnp.float32),
        ],
        compiler_params=pltpu.CompilerParams(vmem_limit_bytes=vmem_bytes),
        name="kernel_blocks",
        cost_estimate=pl.CostEstimate(
            flops=10**6, bytes_accessed=10**4, transcendentals=0
        ),
    )(total, group_leaf, group_count, group_slots, place, own, other, targets)


def far_body(
    total_ref, leaf_ref, slot_ref, side_ref,
    own_ref, partner_ref, high_ref, low_ref, weights_ref,
    out_ref, projected_ref, copies_ref,
    s_high, s_low, acc,
    *, cap,
):
    step = pl.program_id(0)
    samp_dev = own_ref.shape[2]
    part = own_ref.shape[0]

    @pl.when(step == 0)
    def _():
        acc[...] = jnp.zeros_like(acc)

        def split(slot, carry):
            here = side_ref[0] * part + slot
            there = (1 - side_ref[0]) * part + slot
            s_high[here], s_low[here] = halves(own_ref[slot])
            at = pl.multiple_of((slot % cap) * LEAF, LEAF)
            s_high[there], s_low[there] = halves(partner_ref[slot // cap, pl.ds(at, LEAF), :])
            return carry

        lax.fori_loop(0, part, split, 0, unroll=4)

    @pl.when(step * BATCH < total_ref[0])
    def _():
        for member in range(BATCH):
            group = step * BATCH + member
            leaf = leaf_ref[group]
            slots = [slot_ref[group * GROUP + e] for e in range(GROUP)]
            rows_high = jnp.concatenate([s_high[slot] for slot in slots], axis=0)
            rows_low = jnp.concatenate([s_low[slot] for slot in slots], axis=0)
            k_high = high_ref[member]
            k_low = low_ref[member]
            acc[leaf] += dot(k_high, rows_high) + (dot(k_high, rows_low) + dot(k_low, rows_high))

    @pl.when(step == pl.num_programs(0) - 1)
    def _():
        leaves = acc.shape[0]
        rows = acc[...].reshape(leaves * LEAF, samp_dev)
        projected = dot_exact(weights_ref[...], rows)
        projected_ref[...] = projected
        for branch in range(copies_ref.shape[0]):
            copies_ref[branch] = projected
        for pair in range(leaves // 2):
            block = acc[2 * pair : 2 * pair + 2].reshape(2 * LEAF, samp_dev)
            out_ref[:, 2 * pair * LEAF : 2 * (pair + 1) * LEAF] = block.T


def far_products(total, group_leaf, group_slots, side, own, partner, high, low, weights, branches):
    part, unused, samp_dev = own.shape
    slots = 2 * part
    groups = group_leaf.shape[0]
    points_dev = weights.shape[1]
    leaves = points_dev // LEAF
    steps = groups // BATCH

    def block_index(step, total_ref, *unused):
        last = (total_ref[0] - 1) // BATCH
        return (jnp.minimum(step, last), 0, 0)

    return pl.pallas_call(
        functools.partial(far_body, cap=part // partner.shape[0]),
        grid_spec=pltpu.PrefetchScalarGridSpec(
            num_scalar_prefetch=4,
            grid=(steps,),
            in_specs=[
                pl.BlockSpec(own.shape, lambda *unused: (0, 0, 0), pipeline_mode=pl.Buffered(1)),
                pl.BlockSpec(partner.shape, lambda *unused: (0, 0, 0), pipeline_mode=pl.Buffered(1)),
                pl.BlockSpec((BATCH, LEAF, GROUP * LEAF), block_index),
                pl.BlockSpec((BATCH, LEAF, GROUP * LEAF), block_index),
                pl.BlockSpec(weights.shape, lambda *unused: (0, 0), pipeline_mode=pl.Buffered(1)),
            ],
            out_specs=[
                pl.BlockSpec((samp_dev, points_dev), lambda *unused: (0, 0)),
                pl.BlockSpec((weights.shape[0], samp_dev), lambda *unused: (0, 0)),
                pl.BlockSpec((branches, weights.shape[0], samp_dev), lambda *unused: (0, 0, 0)),
            ],
            scratch_shapes=[
                pltpu.VMEM((slots, LEAF, samp_dev), jnp.bfloat16),
                pltpu.VMEM((slots, LEAF, samp_dev), jnp.bfloat16),
                pltpu.VMEM((leaves, LEAF, samp_dev), jnp.float32),
            ],
        ),
        out_shape=[
            jax.ShapeDtypeStruct((samp_dev, points_dev), jnp.float32),
            jax.ShapeDtypeStruct((weights.shape[0], samp_dev), jnp.float32),
            jax.ShapeDtypeStruct((branches, weights.shape[0], samp_dev), jnp.float32),
        ],
        compiler_params=pltpu.CompilerParams(vmem_limit_bytes=vmem_bytes),
        name="far_products",
        cost_estimate=pl.CostEstimate(
            flops=10**6, bytes_accessed=10**4, transcendentals=0
        ),
    )(total, group_leaf, group_slots, side, own, partner, high, low, weights)


NEAR_LEAVES = 8


def near_body(mask_ref, rows_ref, coords_ref, target_ref, out_ref):
    step = pl.program_id(0)
    samp_dev = rows_ref.shape[2]
    lane = lax.broadcasted_iota(jnp.int32, (1, LANES), 1)
    first = lane < LEAF
    for pair in range(NEAR_LEAVES // 2):
        results = []
        for member in range(2):
            leaf = step * NEAR_LEAVES + 2 * pair + member
            target = target_ref[leaf]
            k_high = []
            k_low = []
            for half in range(2):
                both = jnp.where(first, coords_ref[leaf + 2 * half], coords_ref[leaf + 2 * half + 1])
                values = kernel_half(both, target, lane, LANES)
                left = mask_ref[leaf * 3 + 2 * half].astype(jnp.float32)
                if half == 0:
                    right = mask_ref[leaf * 3 + 1].astype(jnp.float32)
                else:
                    right = jnp.float32(0.0)
                high, low = halves(values * jnp.where(first, left, right))
                k_high.append(high)
                k_low.append(low)
            k_high = jnp.concatenate(k_high, axis=1)
            k_low = jnp.concatenate(k_low, axis=1)
            rows = rows_ref[pl.ds(leaf, 4)].reshape(4 * LEAF, samp_dev)
            rows_high, rows_low = halves(rows)
            results.append(
                dot(k_high, rows_high) + (dot(k_high, rows_low) + dot(k_low, rows_high))
            )
        block = jnp.concatenate(results, axis=0)
        out_ref[:, 2 * pair * LEAF : 2 * (pair + 1) * LEAF] = block.T


def near_products(mask, rows, coords, targets):
    leaves = targets.shape[0]
    samp_dev = rows.shape[2]
    whole = lambda *unused: (0, 0, 0)
    return pl.pallas_call(
        near_body,
        grid_spec=pltpu.PrefetchScalarGridSpec(
            num_scalar_prefetch=1,
            grid=(leaves // NEAR_LEAVES,),
            in_specs=[
                pl.BlockSpec(rows.shape, whole),
                pl.BlockSpec(coords.shape, whole),
                pl.BlockSpec(targets.shape, whole),
            ],
            out_specs=pl.BlockSpec((samp_dev, NEAR_LEAVES * LEAF), lambda step, *unused: (0, step)),
        ),
        out_shape=jax.ShapeDtypeStruct((samp_dev, leaves * LEAF), jnp.float32),
        compiler_params=pltpu.CompilerParams(vmem_limit_bytes=vmem_bytes),
        name="near_products",
        cost_estimate=pl.CostEstimate(
            flops=10**9, bytes_accessed=10**6, transcendentals=0
        ),
    )(mask, rows, coords, targets)


def to_lanes(source, target, rank):
    nodes = source.shape[0] // rank
    target[...] = jnp.zeros_like(target)
    for r in range(rank):
        target[r, :, 0:nodes] = source[pl.ds(r, nodes, stride=rank), :].T


def from_lanes(columns, target, r, nodes, rank):
    target[pl.ds(r, nodes, stride=rank), :] = columns.T[0:nodes]


def eliminate(current, left, inverse, level, rank):
    tiles = rank // SUB
    row = lax.broadcasted_iota(jnp.int32, (SUB, LANES), 0)
    diagonal = [current[j, j : j + 1, :] for j in range(rank)]
    while len(diagonal) > 1:
        diagonal = [diagonal[i] + diagonal[i + 1] for i in range(0, len(diagonal), 2)]
    share = shift_share * diagonal[0] / rank
    shift = share + 1e-06
    a = [
        {t: current[j, SUB * t : SUB * (t + 1), :] for t in range(j // SUB, tiles)}
        for j in range(rank)
    ]
    for j in range(rank):
        a[j][j // SUB] = a[j][j // SUB] + jnp.where(row == j % SUB, shift, 0.0)
    m = []
    scales = []
    for k in range(rank):
        tk, rk = k // SUB, k % SUB
        root = lax.rsqrt(a[k][tk][rk : rk + 1, :])
        scales.append(root)
        reciprocal = root * root
        column = {t: a[k][t] * reciprocal for t in range(tk, tiles)}
        column[tk] = jnp.where(row > rk, column[tk], 0.0)
        for j in range(k + 1, rank):
            factor = a[k][j // SUB][j % SUB : j % SUB + 1, :]
            for t in range(j // SUB, tiles):
                a[j][t] = a[j][t] - column[t] * factor
        for c in range(k):
            factor = m[c][tk][rk : rk + 1, :]
            for t in range(tk, tiles):
                m[c][t] = m[c][t] - column[t] * factor
        fresh = {t: -column[t] for t in range(tk, tiles)}
        fresh[tk] = jnp.where(row == rk, 1.0, fresh[tk])
        m.append(fresh)
        if left is not None:
            for t in range(tiles):
                if t < tk:
                    value = jnp.zeros((SUB, LANES), jnp.float32)
                else:
                    value = a[k][t] * root
                if t == tk:
                    value = jnp.where(row >= rk, value, 0.0)
                left[k, SUB * t : SUB * (t + 1), :] = value
    for t in range(tiles):
        scale = jnp.concatenate(scales[SUB * t : SUB * (t + 1)], axis=0)
        for c in range(rank):
            value = m[c][t] * scale if t >= c // SUB else jnp.zeros((SUB, LANES), jnp.float32)
            inverse[c * rank + SUB * t : c * rank + SUB * (t + 1), :] = value
    return shift, share


def inverse_row(inverse, r, t, rank):
    return inverse[pl.ds(SUB * t * rank + r, SUB, stride=rank), :]


def pair_up(value, level):
    reach = LANES - (1 << level if isinstance(level, int) else lax.shift_left(1, level))
    return value + pltpu.roll(value, reach, 1)


def when(condition):
    if isinstance(condition, bool):
        return lambda body: body() if condition else None
    return pl.when(condition)


def level_fast(level, levels, current, left, inverse, squared, ratio, child, lowest, rank, child_at):
    tiles = rank // SUB
    row = lax.broadcasted_iota(jnp.int32, (SUB, LANES), 0)
    shift, share = eliminate(current, left, inverse, level, rank)
    lowest[...] = jnp.minimum(lowest[...], share)

    for block in range(tiles):
        sums = [[None] * tiles for _ in range(SUB)]
        for r in range(SUB * block, rank):
            parts = [inverse_row(inverse, r, t, rank) for t in range(block, r // SUB + 1)]
            for q in range(SUB):
                if SUB * block + q > r:
                    continue
                factor = parts[0][q : q + 1, :]
                for t in range(block, r // SUB + 1):
                    term = parts[t - block] * factor
                    sums[q][t] = term if sums[q][t] is None else sums[q][t] + term
        for q in range(SUB):
            at = (SUB * block + q) * rank
            for t in range(block, tiles):
                squared[at + SUB * t : at + SUB * (t + 1), :] = sums[q][t]

    if child is not None:
        @when(child_at(level))
        def _():
            for r in range(rank):
                for t in range(tiles):
                    value = left[r, SUB * t : SUB * (t + 1), :]
                    if t <= r // SUB:
                        value = value - shift * inverse_row(inverse, r, t, rank)
                    child[r, SUB * t : SUB * (t + 1), :] = value

    for q in range(rank):
        for t in range(tiles):
            if t >= q // SUB:
                value = squared[q * rank + SUB * t : q * rank + SUB * (t + 1), :]
            else:
                value = squared[pl.ds(SUB * t * rank + q, SUB, stride=rank), :]
            value = -shift * value
            if t == q // SUB:
                value = value + jnp.where(row == q % SUB, 1.0, 0.0)
            if ratio is not None:
                ratio[level, q, SUB * t : SUB * (t + 1), :] = value
            here = current[q, SUB * t : SUB * (t + 1), :] - shift * value
            current[q, SUB * t : SUB * (t + 1), :] = pair_up(here, level)


def level_plain(level, levels, current, left, inverse, squared, ratio, child, lowest, rank, child_at):
    tiles = rank // SUB
    eliminate(current, left, inverse, level, rank)

    def products(out, count, left_of, right_of):
        def block_step(block, carry):
            offset = pl.multiple_of(block * SUB, SUB)
            sums = [[None] * tiles for _ in range(SUB)]
            for r in range(count):
                parts = [left_of(r, t) for t in range(tiles)]
                heads = right_of(r, offset)
                for q in range(SUB):
                    for t in range(tiles):
                        term = parts[t] * heads[q : q + 1, :]
                        sums[q][t] = term if sums[q][t] is None else sums[q][t] + term
            for q in range(SUB):
                for t in range(tiles):
                    out(offset + q, t, sums[q][t])
            return carry

        lax.fori_loop(0, tiles, block_step, 0)

    def tile(t):
        return slice(SUB * t, SUB * (t + 1))

    def put_child(r, t, value):
        squared[pl.ds(pl.multiple_of(r * rank + SUB * t, SUB), SUB), :] = value

    products(
        put_child, rank,
        lambda k, t: current[k, tile(t), :],
        lambda k, offset: inverse[pl.ds(pl.multiple_of(k * rank + offset, SUB), SUB), :],
    )
    if child is not None:
        @when(child_at(level))
        def _():
            for r in range(rank):
                for t in range(tiles):
                    child[r, tile(t), :] = squared[r * rank + SUB * t : r * rank + SUB * (t + 1), :]

    def child_part(r, t):
        return squared[r * rank + SUB * t : r * rank + SUB * (t + 1), :]

    def put_current(q, t, value):
        current[q, tile(t), :] = pair_up(value, level)

    if ratio is not None:
        def put_ratio(c, t, value):
            ratio[level, c, tile(t), :] = value

        def inverse_head(r, offset):
            return inverse[pl.ds(offset * rank + r, SUB, stride=rank), :]

        products(put_ratio, rank, child_part, inverse_head)
    products(
        put_current, rank, child_part,
        lambda r, offset: squared[pl.ds(pl.multiple_of(r * rank + offset, SUB), SUB), :],
    )


def run_levels(source, levels, nodes, current, left, inverse, squared, ratio, child, lowest, rank, child_at, finish, unrolled=False):
    lowest[...] = jnp.full((1, LANES), 1.0, jnp.float32)

    def sweep(level_step):
        to_lanes(source, current, rank)

        def body(level, carry):
            level_step(level, levels, current, left, inverse, squared, ratio, child, lowest, rank, child_at)
            finish(level)
            return carry

        if unrolled and level_step is level_fast:
            for level in range(levels):
                body(level, 0)
        else:
            lax.fori_loop(0, levels, body, 0)

    sweep(level_fast)
    lane = lax.broadcasted_iota(jnp.int32, (1, LANES), 1)
    least = jnp.min(jnp.where(lane < nodes, lowest[...], 1.0))

    @pl.when(least < 2e-06)
    def _():
        sweep(level_plain)


def branch_body(gram_ref, inverse_ref, ratio_ref, top_ref, child_ref, current, left, inverse, squared, child, lowest, *, rank, levels):
    nodes = gram_ref.shape[0] // rank

    def finish(level):
        @pl.when(level == 0)
        def _():
            for c in range(rank):
                inverse_ref[c] = inverse[c * rank : (c + 1) * rank, :]

        @pl.when(level == levels - 1)
        def _():
            for r in range(rank):
                width = child_ref.shape[1]
                at = r * rank
                child_ref[at // width : at // width + 1, at % width : at % width + rank] = child[r].T[0:1, :]
                top_ref[r : r + 1, :] = jnp.concatenate(
                    [inverse_row(inverse, r, t, rank) for t in range(rank // SUB)], axis=0
                ).T[0:1, :]

    run_levels(
        gram_ref, levels, nodes, current, left, inverse, squared, ratio_ref, child, lowest, rank,
        lambda level: level == levels - 1, finish,
    )


vmem_spec = pl.BlockSpec(memory_space=pltpu.VMEM)


def tree_scratch(rank):
    return [
        pltpu.VMEM((rank, rank, LANES), jnp.float32),
        pltpu.VMEM((rank, rank, LANES), jnp.float32),
        pltpu.VMEM((rank * rank, LANES), jnp.float32),
        pltpu.VMEM((rank * rank, LANES), jnp.float32),
        pltpu.VMEM((rank, rank, LANES), jnp.float32),
        pltpu.VMEM((1, LANES), jnp.float32),
    ]


def branch_factors(gram, levels, width):
    leaves, rank, unused = gram.shape
    return pl.pallas_call(
        functools.partial(branch_body, rank=rank, levels=levels),
        in_specs=[vmem_spec],
        out_specs=[vmem_spec] * 4,
        out_shape=[
            jax.ShapeDtypeStruct((rank, rank, LANES), jnp.float32),
            jax.ShapeDtypeStruct((levels, rank, rank, LANES), jnp.float32),
            jax.ShapeDtypeStruct((rank, rank), jnp.float32),
            jax.ShapeDtypeStruct((rank * rank // width, width), jnp.float32),
        ],
        scratch_shapes=tree_scratch(rank),
        compiler_params=pltpu.CompilerParams(vmem_limit_bytes=vmem_bytes),
        name="branch_factors",
        cost_estimate=pl.CostEstimate(flops=10**6, bytes_accessed=10**4, transcendentals=0),
    )(gram.reshape(leaves * rank, rank))


def basis_body(inverse_ref, ratio_ref, top_ref, sketched_ref, weights_ref, basis_ref, natural, *, rank, levels):
    leaves = sketched_ref.shape[0]
    upper = [top_ref[...]]
    for level in range(levels - 2, -1, -1):
        stride = 2**level
        for c in range(rank):
            from_lanes(ratio_ref[level, c], natural, c, leaves, rank)
        fresh = []
        for node in range(leaves // stride):
            block = natural[node * stride * rank : (node * stride + 1) * rank, :]
            fresh.append(dot_exact(upper[node // 2], block))
        upper = fresh
    for r in range(rank):
        from_lanes(inverse_ref[r], natural, r, leaves, rank)
    for pair in range(leaves // 2):
        results = []
        for leaf in (2 * pair, 2 * pair + 1):
            block = sketched_ref[leaf]
            own = lax.dot_general(
                natural[leaf * rank : (leaf + 1) * rank, :], block, tn_dims,
                precision=highest, preferred_element_type=jnp.float32,
            )
            results.append(jnp.concatenate([dot_exact(upper[leaf], block), own], axis=0))
        both = jnp.concatenate(results, axis=1)
        weights_ref[:, pair * 2 * LEAF : (pair + 1) * 2 * LEAF] = both[:rank]
        basis_ref[:, pair * 2 * LEAF : (pair + 1) * 2 * LEAF] = both[rank:]


def bases(inverse, ratio, top, sketched):
    leaves, rank, unused = sketched.shape
    levels = ratio.shape[0]
    shape = jax.ShapeDtypeStruct((rank, leaves * LEAF), jnp.float32)
    return pl.pallas_call(
        functools.partial(basis_body, rank=rank, levels=levels),
        in_specs=[vmem_spec] * 4,
        out_specs=[vmem_spec] * 2,
        out_shape=[shape, shape],
        scratch_shapes=[pltpu.VMEM((leaves * rank, rank), jnp.float32)],
        compiler_params=pltpu.CompilerParams(vmem_limit_bytes=vmem_bytes),
        name="bases",
        cost_estimate=pl.CostEstimate(flops=10**9, bytes_accessed=10**6, transcendentals=0),
    )(inverse, ratio, top, sketched)


def top_body(side_ref, mine_ref, mirrored_ref, transfer_ref, paths_ref, children_ref, source, current, left, inverse, squared, child, lowest, nat_inverse, nat_child, *, rank, levels):
    half, packed_rows_each, width = mine_ref.shape
    nodes = half
    every = width // rank
    count = half * packed_rows_each
    for ref, side in ((mine_ref, side_ref[0]), (mirrored_ref, 1 - side_ref[0])):
        flat = ref[...].reshape(count, width)
        base = pl.multiple_of(side * (half * rank), half * rank)
        for part in range(every):
            children_ref[pl.ds(base + part, count, stride=every), :] = flat[:, part * rank : (part + 1) * rank]
    for node in range(nodes):
        both = children_ref[2 * node * rank : (2 * node + 2) * rank, :]
        source[node * rank : (node + 1) * rank, :] = lax.dot_general(
            both, both, tn_dims, precision=highest, preferred_element_type=jnp.float32
        )

    def finish(level):
        for r in range(rank):
            from_lanes(child[r], nat_child.at[level], r, nodes, rank)
            from_lanes(inverse[r * rank : (r + 1) * rank, :], nat_inverse.at[level], r, nodes, rank)

    run_levels(
        source, levels, nodes, current, left, inverse, squared, None, child, lowest, rank,
        lambda level: True, finish, unrolled=True,
    )
    offset = 0
    for level in range(levels):
        for node in range(nodes >> level):
            if level == 0:
                stacked = children_ref[2 * node * rank : (2 * node + 2) * rank, :]
            else:
                first = 2 * node << level - 1
                second = 2 * node + 1 << level - 1
                stacked = jnp.concatenate(
                    [
                        nat_child[level - 1, first * rank : (first + 1) * rank, :],
                        nat_child[level - 1, second * rank : (second + 1) * rank, :],
                    ],
                    axis=0,
                )
            at = (node << level) * rank
            transfer_ref[offset + node] = lax.dot_general(
                nat_inverse[level, at : at + rank, :], stacked, (((0,), (1,)), ((), ())),
                precision=highest, preferred_element_type=jnp.float32,
            )
        offset += nodes >> level
    above = [None]
    for level in range(levels - 1, -1, -1):
        offset -= nodes >> level
        fresh = []
        for node in range(nodes >> level):
            both = transfer_ref[offset + node]
            if above[0] is None:
                both = both.T
            else:
                both = lax.dot_general(
                    both, above[node], tn_dims, precision=highest, preferred_element_type=jnp.float32
                )
            fresh += [both[:rank], both[rank:]]
        above = fresh
    for branch in range(2 * nodes):
        paths_ref[branch * rank : (branch + 1) * rank, :] = above[branch]


def top_factors(side, mine, mirrored, rank):
    branches = 2 * mine.shape[0]
    levels = branches.bit_length() - 1
    nodes = branches // 2
    natural = pltpu.VMEM((levels, nodes * rank, rank), jnp.float32)
    return pl.pallas_call(
        functools.partial(top_body, rank=rank, levels=levels),
        in_specs=[pl.BlockSpec(memory_space=pltpu.SMEM), vmem_spec, vmem_spec],
        out_specs=[vmem_spec] * 2,
        out_shape=[
            jax.ShapeDtypeStruct((branches - 1, rank, 2 * rank), jnp.float32),
            jax.ShapeDtypeStruct((branches * rank, rank), jnp.float32),
        ],
        scratch_shapes=[
            pltpu.VMEM((branches * rank, rank), jnp.float32),
            pltpu.VMEM((nodes * rank, rank), jnp.float32),
        ]
        + tree_scratch(rank)
        + [natural, natural],
        compiler_params=pltpu.CompilerParams(vmem_limit_bytes=vmem_bytes),
        name="top_factors",
        cost_estimate=pl.CostEstimate(flops=10**10, bytes_accessed=10**7, transcendentals=0),
    )(side, mine, mirrored)


def exchange_sum(pieces, axis):
    count = pieces.shape[0]
    me = lax.axis_index(axis)
    mine = lax.dynamic_index_in_dim(pieces, me, 0, keepdims=False)
    for step in range(1, count):
        outgoing = lax.dynamic_index_in_dim(pieces, (me + step) % count, 0, keepdims=False)
        mine = mine + lax.ppermute(
            outgoing, axis, [(i, (i + step) % count) for i in range(count)]
        )
    return mine


def exchange_all(piece, axis):
    count = lax.axis_size(axis)
    me = lax.axis_index(axis)
    if count == 2:
        other = lax.ppermute(piece, axis, [(0, 1), (1, 0)])
        return jnp.stack([jnp.where(me == 0, piece, other), jnp.where(me == 0, other, piece)])
    result = jnp.zeros((count,) + piece.shape, piece.dtype)
    result = lax.dynamic_update_index_in_dim(result, piece, me, 0)
    for step in range(1, count):
        arrived = lax.ppermute(piece, axis, [(i, (i + step) % count) for i in range(count)])
        result = lax.dynamic_update_index_in_dim(result, arrived, (me - step) % count, 0)
    return result


def group_tables(far_slots, far_count):
    leaves = far_slots.shape[0]
    groups = leaves * FAR // GROUP
    per_leaf = (far_count + GROUP - 1) // GROUP
    before = jnp.arange(leaves)[:, None] >= jnp.arange(leaves)[None, :]
    ends = jnp.sum(jnp.where(before, per_leaf[None, :], 0), axis=1)
    total = ends[leaves - 1 :]
    ids = jnp.arange(groups, dtype=jnp.int32)
    leaf = jnp.minimum(jnp.sum((ends[None, :] <= ids[:, None]).astype(jnp.int32), axis=1), leaves - 1)
    hit = leaf[:, None] == jnp.arange(leaves)[None, :]
    start = jnp.sum(jnp.where(hit, (ends - per_leaf)[None, :], 0), axis=1)
    length = jnp.sum(jnp.where(hit, far_count[None, :], 0), axis=1)
    sub = ids - start
    count = jnp.where(ids < total, jnp.clip(length - GROUP * sub, 0, GROUP), 0)
    first = jnp.minimum(sub, FAR // GROUP - 1)
    slots = far_slots.reshape(leaves * FAR // GROUP, GROUP)[leaf * (FAR // GROUP) + first]
    return (
        total.astype(jnp.int32),
        leaf.astype(jnp.int32),
        count.astype(jnp.int32),
        slots.reshape(-1).astype(jnp.int32),
    )


def sketch_body(place_ref, sketch_ref, samples_ref, points_ref, mine_ref, other_ref):
    product = dot_exact(sketch_ref[...], samples_ref[...])
    rank, points_dev = product.shape
    quarter = rank // 4
    first = lax.broadcasted_iota(jnp.int32, (1, LANES), 1) < LEAF
    swap = place_ref[0] == 1
    leaves = points_dev // LEAF

    def interleave(low, high):
        even = jnp.where(first, low, pltpu.roll(high, LEAF, 1))
        odd = jnp.where(first, pltpu.roll(low, LEAF, 1), high)
        return even, odd

    for pair in range(leaves // 2):
        lanes = slice(pair * LANES, (pair + 1) * LANES)
        shares = []
        for share in range(2):
            base = 2 * quarter * share
            shares.append(
                interleave(product[base : base + quarter, lanes], product[base + quarter : base + 2 * quarter, lanes])
            )
        for member in range(2):
            at = (2 * pair + member) * quarter
            mine_ref[at : at + quarter, :] = jnp.where(swap, shares[1][member], shares[0][member])
            other_ref[at : at + quarter, :] = jnp.where(swap, shares[0][member], shares[1][member])
        x = points_ref[0:1, lanes]
        y = points_ref[1:2, lanes]
        z = points_ref[2:3, lanes]
        xy = interleave(x, y)
        zs = interleave(z, jnp.zeros_like(z))
        for member in range(2):
            at = leaves * quarter + (2 * pair + member) * 2
            mine_ref[at : at + 1, :] = xy[member]
            mine_ref[at + 1 : at + 2, :] = zs[member]
    other_ref[leaves * quarter :, :] = jnp.zeros((2 * leaves, LANES), jnp.float32)


def sketched_shares(place, sketch, samples, points):
    rank = sketch.shape[0]
    leaves = samples.shape[1] // LEAF
    return pl.pallas_call(
        sketch_body,
        in_specs=[pl.BlockSpec(memory_space=pltpu.SMEM)] + [vmem_spec] * 3,
        out_specs=[vmem_spec] * 2,
        out_shape=[
            jax.ShapeDtypeStruct((leaves * (rank // 4 + 2), LANES), jnp.float32),
            jax.ShapeDtypeStruct((leaves * (rank // 4 + 2), LANES), jnp.float32),
        ],
        compiler_params=pltpu.CompilerParams(vmem_limit_bytes=vmem_bytes),
        name="sketched_shares",
        cost_estimate=pl.CostEstimate(flops=10**6, bytes_accessed=10**4, transcendentals=0),
    )(place, sketch, samples, points)


def pack_body(asked_ref, side_ref, mine_ref, partner_ref, out_ref, *, cap, leaves):
    z_rows = mine_ref.shape[0] // leaves - 2
    side = side_ref[0]

    def one(peer, carry):
        for entry in range(2 * cap):
            leaf = asked_ref[peer, entry]
            here = side == entry // cap
            at = pl.ds(leaf * z_rows, z_rows)
            out_ref[peer, z_rows * entry : z_rows * (entry + 1), :] = jnp.where(
                here, mine_ref[at, :], partner_ref[at, :]
            )
            base = z_rows * 2 * cap + 2 * entry
            at = pl.ds(leaves * z_rows + leaf * 2, 2)
            out_ref[peer, base : base + 2, :] = jnp.where(here, mine_ref[at, :], partner_ref[at, :])
        return carry

    lax.fori_loop(0, out_ref.shape[0], one, 0)


def packed_rows(asked, side, mine, partner, cap, leaves):
    z_rows = mine.shape[0] // leaves - 2
    return pl.pallas_call(
        functools.partial(pack_body, cap=cap, leaves=leaves),
        in_specs=[pl.BlockSpec(memory_space=pltpu.SMEM)] * 2 + [vmem_spec] * 2,
        out_specs=vmem_spec,
        out_shape=jax.ShapeDtypeStruct((asked.shape[0], 2 * cap * (z_rows + 2), LANES), jnp.float32),
        compiler_params=pltpu.CompilerParams(vmem_limit_bytes=vmem_bytes),
        name="packed_rows",
    )(asked, side, mine, partner)


def payload_body(asked_ref, side_ref, early_ref, late_ref, child_ref, out_ref, *, cap):
    early = early_ref.shape[0]
    base = (1 - side_ref[0]) * cap

    def one(peer, carry):
        for entry in range(cap):
            leaf = asked_ref[peer, base + entry]
            first = early_ref[jnp.minimum(leaf, early - 1)]
            second = late_ref[jnp.maximum(leaf - early, 0)]
            out_ref[peer, LEAF * entry : LEAF * (entry + 1), :] = jnp.where(leaf < early, first, second)
        out_ref[peer, LEAF * cap :, :] = child_ref[...]
        return carry

    lax.fori_loop(0, out_ref.shape[0], one, 0)


def payload_rows(asked, side, early, late, child):
    half = asked.shape[0]
    cap = asked.shape[1] // 2
    return pl.pallas_call(
        functools.partial(payload_body, cap=cap),
        in_specs=[pl.BlockSpec(memory_space=pltpu.SMEM)] * 2 + [vmem_spec] * 3,
        out_specs=vmem_spec,
        out_shape=jax.ShapeDtypeStruct((half, cap * LEAF + child.shape[0], late.shape[2]), jnp.float32),
        compiler_params=pltpu.CompilerParams(vmem_limit_bytes=vmem_bytes),
        name="payload_rows",
    )(asked, side, early, late, child)


def two_rows(values, rows):
    leaves = values.shape[1]
    split = jnp.transpose(values.reshape(2, rows, leaves, LEAF), (2, 1, 0, 3))
    return split.reshape(leaves, rows, 2 * LEAF)


def on_device(points, samples, sketch, far_requests, far_slots, far_count, near_mask):
    samp_dev = samples.shape[0]
    leaves = samples.shape[1] // LEAF
    rank = sketch.shape[0]
    branches = lax.axis_size("leaf")
    columns = lax.axis_size("cols")
    cap = far_requests.shape[2]
    share = rank // columns
    me = lax.axis_index("leaf")
    column = lax.axis_index("cols")

    half = branches // 2
    side = me // half
    groups = [list(range(half)), list(range(half, branches))]
    mirror = [(i, (i + half) % branches) for i in range(branches)]
    side_ref = side.astype(jnp.int32).reshape(1)
    wanted = jnp.transpose(far_requests.reshape(2, half, cap), (1, 0, 2)).reshape(half, 2 * cap)
    if columns == 2:
        place = column.astype(jnp.int32).reshape(1)
        mine, other = sketched_shares(place, sketch, samples, points)
        wanted, other = lax.optimization_barrier((wanted, other))
        mine = mine + lax.ppermute(other, "cols", [(0, 1), (1, 0)])
    else:
        z_part = jnp.dot(sketch, samples, precision=highest)
        z_mine = exchange_sum(z_part.reshape(columns, share, leaves * LEAF), "cols")
        z_rows = two_rows(z_mine.reshape(share, leaves, LEAF), share // 2)
        planes = points.reshape(3, leaves, LEAF)
        c_rows = two_rows(
            jnp.concatenate([planes[0:1], planes[2:3], planes[1:2], jnp.zeros_like(planes[0:1])], axis=0), 2
        )
        mine = jnp.concatenate([z_rows.reshape(-1, LANES), c_rows.reshape(-1, LANES)], axis=0)

    partner = lax.ppermute(mine, "leaf", mirror)
    asked = lax.all_to_all(
        wanted, "leaf", split_axis=0, concat_axis=0, axis_index_groups=groups, tiled=True
    )
    coords = jnp.transpose(points.reshape(3, leaves, LEAF), (1, 0, 2))
    targets = jnp.transpose(coords, (0, 2, 1))
    rows = jnp.transpose(samples.reshape(samp_dev, leaves, LEAF), (1, 2, 0))

    tables = group_tables(far_slots, far_count)
    asked, rows, targets, tables = lax.optimization_barrier((asked, rows, targets, tables))
    total, group_leaf, group_count, group_slots = tables
    small_sent = packed_rows(asked, side_ref, mine, partner, cap, leaves)
    small_got = lax.all_to_all(
        small_sent, "leaf", split_axis=0, concat_axis=0, axis_index_groups=groups, tiled=True
    )

    early = leaves // 8
    rows_out, unused = lax.optimization_barrier((rows, small_sent))
    partner_early = lax.ppermute(rows_out[:early], "leaf", mirror)
    rows_late = rows_out[early:]

    forward = [(i, i + 1) for i in range(branches - 1)]
    backward = [(target, source) for source, target in forward]
    width = max(samp_dev, LEAF)

    def edge(first):
        samples_edge = jnp.transpose(lax.slice_in_dim(samples, first, first + LEAF, axis=1))
        points_edge = lax.slice_in_dim(points, first, first + LEAF, axis=1)
        return jnp.concatenate(
            [
                jnp.pad(samples_edge, ((0, 0), (0, width - samp_dev))),
                jnp.pad(points_edge, ((0, 5), (0, width - LEAF))),
            ],
            axis=0,
        )

    last, first, unused = lax.optimization_barrier((edge((leaves - 1) * LEAF), edge(0), small_sent))
    low_edge = lax.ppermute(last, "leaf", forward)
    high_edge = lax.ppermute(first, "leaf", backward)

    own_asked = lax.dynamic_slice_in_dim(asked, side * cap, cap, axis=1)
    own_sent = rows_out[own_asked.reshape(-1)].reshape(half, cap, LEAF, samp_dev)
    own_sent, rows_late, partner_early, low_edge, high_edge = lax.optimization_barrier(
        (own_sent, rows_late, partner_early, low_edge, high_edge)
    )
    partner_late = lax.ppermute(rows_late, "leaf", mirror)
    own_got = lax.all_to_all(
        own_sent, "leaf", split_axis=0, concat_axis=0, axis_index_groups=groups, tiled=True
    )
    own_got = own_got.reshape(half * cap, LEAF, samp_dev)

    if columns == 2:
        small_other = lax.ppermute(small_got, "cols", [(0, 1), (1, 0)])
    else:
        z_count = cap * share
        z_all = exchange_all(small_got[:, :z_count], "cols")
        z_all = z_all.reshape(columns, half, 2 * cap, share // 2, 2, LEAF)
        z_all = jnp.transpose(z_all, (1, 2, 0, 4, 3, 5)).reshape(half, 2 * cap, 2, 2, rank // 4, LEAF)
        z_all = jnp.transpose(z_all, (2, 0, 1, 4, 3, 5)).reshape(2, half, cap * rank // 2, LANES)
        c_got = small_got[:, z_count:]
        small_got = jnp.concatenate([z_all[0], c_got], axis=1)
        small_other = jnp.concatenate([z_all[1], c_got], axis=1)
        place = jnp.zeros((1,), jnp.int32)

    high, low, sketched, gram = kernel_blocks(
        total, group_leaf, group_count, group_slots, place, small_got, small_other, targets, rank, cap
    )

    levels = leaves.bit_length()
    inverse, ratio, top_inverse, own_child = branch_factors(gram, levels, min(samp_dev, LANES))
    own_child, own_got, partner_late = lax.optimization_barrier((own_child, own_got, partner_late))
    payload = payload_rows(asked, side_ref, partner_early, partner_late, own_child)
    arrived = lax.all_to_all(
        payload, "leaf", split_axis=0, concat_axis=0, axis_index_groups=groups, tiled=True
    )
    ratio, low_edge, high_edge, unused = lax.optimization_barrier((ratio, low_edge, high_edge, payload))
    weights, leaf_basis = bases(inverse, ratio, top_inverse, sketched)

    rows_low, rows_high = low_edge[:LEAF, :samp_dev], high_edge[:LEAF, :samp_dev]
    coords_low, coords_high = low_edge[LEAF : LEAF + 3, :LEAF], high_edge[LEAF : LEAF + 3, :LEAF]
    near_rows = jnp.concatenate(
        [rows_low[None], rows, rows_high[None], jnp.zeros_like(rows_low)[None]], axis=0
    )
    near_coords = jnp.concatenate(
        [coords_low[None], coords, coords_high[None], jnp.zeros_like(coords_low)[None]], axis=0
    )
    near_coords = jnp.pad(near_coords, ((0, 0), (0, 5), (0, 0)))
    near_coords = jnp.concatenate([near_coords, near_coords], axis=2)
    near_sample = near_products(near_mask.reshape(-1), near_rows, near_coords, targets)


    children = arrived[:, cap * LEAF :]
    mirrored = lax.ppermute(children, "leaf", mirror)
    weights, near_sample = lax.optimization_barrier((weights, near_sample))
    far_sample, branch_samples, copies = far_products(
        total, group_leaf, group_slots, side_ref, own_got, arrived, high, low, weights, branches
    )
    everyone = lax.all_to_all(copies, "leaf", split_axis=0, concat_axis=0, tiled=True)
    children, mirrored, unused = lax.optimization_barrier((children, mirrored, branch_samples))
    transfer_t, paths = top_factors(side_ref, children, mirrored, rank)
    top_transfer = jnp.swapaxes(transfer_t, 1, 2)
    root_sample = lax.dot_general(
        paths, everyone.reshape(branches * rank, samp_dev), tn_dims, precision=highest
    )
    return (far_sample, near_sample, leaf_basis, branch_samples, top_transfer, root_sample)


def solution(mesh):
    return jax.shard_map(
        on_device,
        mesh=mesh,
        in_specs=(
            P(None, "leaf"),
            P("cols", "leaf"),
            P(None, "cols"),
            P("leaf", None, None),
            P("leaf", None),
            P("leaf"),
            P("leaf", None),
        ),
        out_specs=(
            P("cols", "leaf"),
            P("cols", "leaf"),
            P(None, "leaf"),
            P("leaf", "cols"),
            P(),
            P(None, "cols"),
        ),
        check_vma=False,
    )
```

```python
import functools
import math

import jax
import jax.numpy as jnp
import numpy as np
from jax import lax
from jax.experimental import pallas as pl
from jax.experimental.pallas import tpu as pltpu
from jax.sharding import PartitionSpec as P

LEAF = 64
FAR = 16
GROUP = 4
BATCH = 16
LANES = 128
SUB = 8

length_scale = 0.3
shift_share = 0.05
highest = lax.Precision.HIGHEST
exponent_scale = -math.log2(math.e) / length_scale
vmem_bytes = 56 * 1024 * 1024

nt_dims = (((1,), (1,)), ((), ()))
tn_dims = (((0,), (0,)), ((), ()))


def halves(value):
    high = value.astype(jnp.bfloat16)
    low = (value - high.astype(jnp.float32)).astype(jnp.bfloat16)
    return high, low


def dot(a, b):
    return jnp.dot(a, b, preferred_element_type=jnp.float32)


def dot_exact(a, b):
    return jnp.dot(a, b, precision=highest, preferred_element_type=jnp.float32)


def dot_exact_nt(a, b):
    return lax.dot_general(a, b, nt_dims, precision=highest, preferred_element_type=jnp.float32)


def stacked_halves(value, axis):
    return jnp.concatenate(halves(value), axis=axis)


def quadrants(product):
    rows, columns = product.shape[0] // 2, product.shape[1] // 2
    top = product[:rows, :columns] + product[:rows, columns:]
    return top + (product[rows:, :columns] + product[rows:, columns:])


def dot_nt(a, b):
    return lax.dot_general(a, b, nt_dims, preferred_element_type=jnp.float32)


def kernel_half(source_rows, target, lane, valid):
    total = None
    for axis in range(3):
        difference = source_rows[axis : axis + 1, :] - target[:, axis : axis + 1]
        square = difference * difference
        total = square if total is None else total + square
    distance = total * lax.rsqrt(jnp.maximum(total, 1e-30))
    values = jnp.exp2(distance * exponent_scale)
    return jnp.where(lane < valid, values, 0.0)


def blocks_body(
    total_ref, leaf_ref, count_ref, slot_ref, place_ref,
    own_ref, other_ref, target_ref,
    both_ref, sketched_ref, gram_ref,
    packed,
    *, rank, cap,
):
    step = pl.program_id(0)
    lane = lax.broadcasted_iota(jnp.int32, (1, LANES), 1)
    first = lane < LEAF

    @pl.when(step == 0)
    def _():
        sketched_ref[...] = jnp.zeros_like(sketched_ref)
        quarter = rank // 4
        slots = packed.shape[0]
        own_at = pl.multiple_of(place_ref[0] * 2 * quarter, quarter)
        other_at = pl.multiple_of((1 - place_ref[0]) * 2 * quarter, quarter)

        def unpack(peer, carry):
            for entry in range(2 * cap):
                slot = (entry // cap) * (slots // 2) + peer * cap + entry % cap
                at = entry * quarter
                for ref, base in ((own_ref, own_at), (other_ref, other_at)):
                    value = ref[peer, at : at + quarter, :]
                    turned = pltpu.roll(value, LEAF, 1)
                    packed[slot, pl.ds(base, quarter), :] = jnp.where(first, value, turned)
                    packed[slot, pl.ds(base + quarter, quarter), :] = jnp.where(first, turned, value)
                at = 2 * cap * quarter + 2 * entry
                value = own_ref[peer, at : at + 2, :]
                turned = pltpu.roll(value, LEAF, 1)
                packed[slot, rank : rank + 1, :] = jnp.where(first, value, turned)[0:1]
                packed[slot, rank + 1 : rank + 2, :] = jnp.where(first, turned, value)[0:1]
                packed[slot, rank + 2 : rank + 3, :] = jnp.where(first, value, turned)[1:2]
            return carry

        lax.fori_loop(0, slots // (2 * cap), unpack, 0)

    @pl.when(step * BATCH < total_ref[0])
    def _():
        for member in range(BATCH):
            group = step * BATCH + member
            leaf = leaf_ref[group]
            count = count_ref[group]
            slots = [slot_ref[group * GROUP + e] for e in range(GROUP)]
            target = target_ref[leaf]
            z_parts = []
            for half in range(GROUP // 2):
                left = packed[slots[2 * half]]
                right = packed[slots[2 * half + 1]]
                both = jnp.where(first, left, right)
                values = kernel_half(both[rank : rank + 3], target, lane, (count - 2 * half) * LEAF)
                both_ref[member, :, half * LANES : (half + 1) * LANES] = stacked_halves(values, 0)
                z_parts.append(both[:rank])
            z_both = stacked_halves(jnp.concatenate(z_parts, axis=1), 0)
            sketched_ref[leaf] += quadrants(dot_nt(z_both, both_ref[member]))

    @pl.when(step == pl.num_programs(0) - 1)
    def _():
        for leaf in range(gram_ref.shape[0]):
            block = sketched_ref[leaf]
            gram_ref[leaf] = dot_exact_nt(block, block)


def kernel_blocks(total, group_leaf, group_count, group_slots, place, own, other, targets, rank, cap):
    leaves = targets.shape[0]
    groups = group_leaf.shape[0]
    slots = own.shape[0] * 2 * cap
    steps = groups // BATCH

    def block_index(step, total_ref, *unused):
        last = (total_ref[0] - 1) // BATCH
        return (jnp.minimum(step, last), 0, 0)

    whole = lambda *unused: (0, 0, 0)
    once = pl.Buffered(1)
    return pl.pallas_call(
        functools.partial(blocks_body, rank=rank, cap=cap),
        grid_spec=pltpu.PrefetchScalarGridSpec(
            num_scalar_prefetch=5,
            grid=(steps,),
            in_specs=[
                pl.BlockSpec(own.shape, whole, pipeline_mode=once),
                pl.BlockSpec(other.shape, whole, pipeline_mode=once),
                pl.BlockSpec(targets.shape, whole, pipeline_mode=once),
            ],
            out_specs=[
                pl.BlockSpec((BATCH, 2 * LEAF, GROUP * LEAF), block_index),
                pl.BlockSpec((leaves, rank, LEAF), whole),
                pl.BlockSpec((leaves, rank, rank), whole),
            ],
            scratch_shapes=[pltpu.VMEM((slots, rank + SUB, LANES), jnp.float32)],
        ),
        out_shape=[
            jax.ShapeDtypeStruct((groups, 2 * LEAF, GROUP * LEAF), jnp.bfloat16),
            jax.ShapeDtypeStruct((leaves, rank, LEAF), jnp.float32),
            jax.ShapeDtypeStruct((leaves, rank, rank), jnp.float32),
        ],
        compiler_params=pltpu.CompilerParams(vmem_limit_bytes=vmem_bytes),
        name="kernel_blocks",
        cost_estimate=pl.CostEstimate(
            flops=10**6, bytes_accessed=10**4, transcendentals=0
        ),
    )(total, group_leaf, group_count, group_slots, place, own, other, targets)


def far_body(
    total_ref, leaf_ref, slot_ref, side_ref,
    own_ref, partner_ref, blocks_ref, weights_ref,
    out_ref, projected_ref, copies_ref,
    s_both, acc,
    *, cap,
):
    step = pl.program_id(0)
    samp_dev = own_ref.shape[2]
    part = own_ref.shape[0]

    @pl.when(step == 0)
    def _():
        acc[...] = jnp.zeros_like(acc)

        def split(slot, carry):
            here = side_ref[0] * part + slot
            there = (1 - side_ref[0]) * part + slot
            s_both[here] = stacked_halves(own_ref[slot], 1)
            at = pl.multiple_of((slot % cap) * LEAF, LEAF)
            s_both[there] = stacked_halves(partner_ref[slot // cap, pl.ds(at, LEAF), :], 1)
            return carry

        lax.fori_loop(0, part, split, 0, unroll=4)

    @pl.when(step * BATCH < total_ref[0])
    def _():
        for member in range(BATCH):
            group = step * BATCH + member
            leaf = leaf_ref[group]
            slots = [slot_ref[group * GROUP + e] for e in range(GROUP)]
            rows = jnp.concatenate([s_both[slot] for slot in slots], axis=0)
            acc[leaf] += quadrants(dot(blocks_ref[member], rows))

    @pl.when(step == pl.num_programs(0) - 1)
    def _():
        leaves = acc.shape[0]
        rows = acc[...].reshape(leaves * LEAF, samp_dev)
        projected = dot_exact(weights_ref[...], rows)
        projected_ref[...] = projected
        for branch in range(copies_ref.shape[0]):
            copies_ref[branch] = projected
        for pair in range(leaves // 2):
            block = acc[2 * pair : 2 * pair + 2].reshape(2 * LEAF, samp_dev)
            out_ref[:, 2 * pair * LEAF : 2 * (pair + 1) * LEAF] = block.T


def far_products(total, group_leaf, group_slots, side, own, partner, blocks, weights, branches):
    part, unused, samp_dev = own.shape
    slots = 2 * part
    groups = group_leaf.shape[0]
    points_dev = weights.shape[1]
    leaves = points_dev // LEAF
    steps = groups // BATCH

    def block_index(step, total_ref, *unused):
        last = (total_ref[0] - 1) // BATCH
        return (jnp.minimum(step, last), 0, 0)

    return pl.pallas_call(
        functools.partial(far_body, cap=part // partner.shape[0]),
        grid_spec=pltpu.PrefetchScalarGridSpec(
            num_scalar_prefetch=4,
            grid=(steps,),
            in_specs=[
                pl.BlockSpec(own.shape, lambda *unused: (0, 0, 0), pipeline_mode=pl.Buffered(1)),
                pl.BlockSpec(partner.shape, lambda *unused: (0, 0, 0), pipeline_mode=pl.Buffered(1)),
                pl.BlockSpec((BATCH, 2 * LEAF, GROUP * LEAF), block_index),
                pl.BlockSpec(weights.shape, lambda *unused: (0, 0), pipeline_mode=pl.Buffered(1)),
            ],
            out_specs=[
                pl.BlockSpec((samp_dev, points_dev), lambda *unused: (0, 0)),
                pl.BlockSpec((weights.shape[0], samp_dev), lambda *unused: (0, 0)),
                pl.BlockSpec((branches, weights.shape[0], samp_dev), lambda *unused: (0, 0, 0)),
            ],
            scratch_shapes=[
                pltpu.VMEM((slots, LEAF, 2 * samp_dev), jnp.bfloat16),
                pltpu.VMEM((leaves, LEAF, samp_dev), jnp.float32),
            ],
        ),
        out_shape=[
            jax.ShapeDtypeStruct((samp_dev, points_dev), jnp.float32),
            jax.ShapeDtypeStruct((weights.shape[0], samp_dev), jnp.float32),
            jax.ShapeDtypeStruct((branches, weights.shape[0], samp_dev), jnp.float32),
        ],
        compiler_params=pltpu.CompilerParams(vmem_limit_bytes=vmem_bytes),
        name="far_products",
        cost_estimate=pl.CostEstimate(
            flops=10**10, bytes_accessed=10**7, transcendentals=0
        ),
    )(total, group_leaf, group_slots, side, own, partner, blocks, weights)


NEAR_LEAVES = 8


def near_body(mask_ref, rows_ref, coords_ref, target_ref, out_ref):
    step = pl.program_id(0)
    samp_dev = rows_ref.shape[2]
    lane = lax.broadcasted_iota(jnp.int32, (1, LANES), 1)
    first = lane < LEAF
    for pair in range(NEAR_LEAVES // 2):
        results = []
        for member in range(2):
            leaf = step * NEAR_LEAVES + 2 * pair + member
            target = target_ref[leaf]
            k_parts = []
            for half in range(2):
                both = jnp.where(first, coords_ref[leaf + 2 * half], coords_ref[leaf + 2 * half + 1])
                values = kernel_half(both, target, lane, LANES)
                left = mask_ref[leaf * 3 + 2 * half].astype(jnp.float32)
                if half == 0:
                    right = mask_ref[leaf * 3 + 1].astype(jnp.float32)
                else:
                    right = jnp.float32(0.0)
                k_parts.append(stacked_halves(values * jnp.where(first, left, right), 0))
            rows = rows_ref[pl.ds(leaf, 4)].reshape(4 * LEAF, samp_dev)
            product = dot(jnp.concatenate(k_parts, axis=1), stacked_halves(rows, 1))
            results.append(quadrants(product))
        block = jnp.concatenate(results, axis=0)
        out_ref[:, 2 * pair * LEAF : 2 * (pair + 1) * LEAF] = block.T


def near_products(mask, rows, coords, targets):
    leaves = targets.shape[0]
    samp_dev = rows.shape[2]
    whole = lambda *unused: (0, 0, 0)
    return pl.pallas_call(
        near_body,
        grid_spec=pltpu.PrefetchScalarGridSpec(
            num_scalar_prefetch=1,
            grid=(leaves // NEAR_LEAVES,),
            in_specs=[
                pl.BlockSpec(rows.shape, whole),
                pl.BlockSpec(coords.shape, whole),
                pl.BlockSpec(targets.shape, whole),
            ],
            out_specs=pl.BlockSpec((samp_dev, NEAR_LEAVES * LEAF), lambda step, *unused: (0, step)),
        ),
        out_shape=jax.ShapeDtypeStruct((samp_dev, leaves * LEAF), jnp.float32),
        compiler_params=pltpu.CompilerParams(vmem_limit_bytes=vmem_bytes),
        name="near_products",
        cost_estimate=pl.CostEstimate(
            flops=10**9, bytes_accessed=10**6, transcendentals=0
        ),
    )(mask, rows, coords, targets)


def to_lanes(source, target, rank):
    nodes = source.shape[0] // rank
    target[...] = jnp.zeros_like(target)
    for r in range(rank):
        target[r, :, 0:nodes] = source[pl.ds(r, nodes, stride=rank), :].T


def from_lanes(columns, target, r, nodes, rank):
    target[pl.ds(r, nodes, stride=rank), :] = columns.T[0:nodes]


def eliminate(current, left, inverse, level, rank):
    tiles = rank // SUB
    row = lax.broadcasted_iota(jnp.int32, (SUB, LANES), 0)
    diagonal = [current[j, j : j + 1, :] for j in range(rank)]
    while len(diagonal) > 1:
        diagonal = [diagonal[i] + diagonal[i + 1] for i in range(0, len(diagonal), 2)]
    share = shift_share * diagonal[0] / rank
    shift = share + 1e-06
    a = [
        {t: current[j, SUB * t : SUB * (t + 1), :] for t in range(j // SUB, tiles)}
        for j in range(rank)
    ]
    for j in range(rank):
        a[j][j // SUB] = a[j][j // SUB] + jnp.where(row == j % SUB, shift, 0.0)
    m = []
    scales = []
    for k in range(rank):
        tk, rk = k // SUB, k % SUB
        root = lax.rsqrt(a[k][tk][rk : rk + 1, :])
        scales.append(root)
        reciprocal = root * root
        column = {t: a[k][t] * reciprocal for t in range(tk, tiles)}
        column[tk] = jnp.where(row > rk, column[tk], 0.0)
        for j in range(k + 1, rank):
            factor = a[k][j // SUB][j % SUB : j % SUB + 1, :]
            for t in range(j // SUB, tiles):
                a[j][t] = a[j][t] - column[t] * factor
        for c in range(k):
            factor = m[c][tk][rk : rk + 1, :]
            for t in range(tk, tiles):
                m[c][t] = m[c][t] - column[t] * factor
        fresh = {t: -column[t] for t in range(tk, tiles)}
        fresh[tk] = jnp.where(row == rk, 1.0, fresh[tk])
        m.append(fresh)
        if left is not None:
            for t in range(tiles):
                if t < tk:
                    value = jnp.zeros((SUB, LANES), jnp.float32)
                else:
                    value = a[k][t] * root
                if t == tk:
                    value = jnp.where(row >= rk, value, 0.0)
                left[k, SUB * t : SUB * (t + 1), :] = value
    for t in range(tiles):
        scale = jnp.concatenate(scales[SUB * t : SUB * (t + 1)], axis=0)
        for c in range(rank):
            value = m[c][t] * scale if t >= c // SUB else jnp.zeros((SUB, LANES), jnp.float32)
            inverse[c * rank + SUB * t : c * rank + SUB * (t + 1), :] = value
    return shift, share


def inverse_row(inverse, r, t, rank):
    return inverse[pl.ds(SUB * t * rank + r, SUB, stride=rank), :]


def pair_up(value, level):
    reach = LANES - (1 << level if isinstance(level, int) else lax.shift_left(1, level))
    return value + pltpu.roll(value, reach, 1)


def when(condition):
    if isinstance(condition, bool):
        return lambda body: body() if condition else None
    return pl.when(condition)


def level_fast(level, levels, current, left, inverse, squared, ratio, child, lowest, rank, child_at):
    tiles = rank // SUB
    row = lax.broadcasted_iota(jnp.int32, (SUB, LANES), 0)
    shift, share = eliminate(current, left, inverse, level, rank)
    lowest[...] = jnp.minimum(lowest[...], share)

    for block in range(tiles):
        sums = [[None] * tiles for _ in range(SUB)]
        for r in range(SUB * block, rank):
            parts = [inverse_row(inverse, r, t, rank) for t in range(block, r // SUB + 1)]
            for q in range(SUB):
                if SUB * block + q > r:
                    continue
                factor = parts[0][q : q + 1, :]
                for t in range(block, r // SUB + 1):
                    term = parts[t - block] * factor
                    sums[q][t] = term if sums[q][t] is None else sums[q][t] + term
        for q in range(SUB):
            at = (SUB * block + q) * rank
            for t in range(block, tiles):
                squared[at + SUB * t : at + SUB * (t + 1), :] = sums[q][t]

    if child is not None:
        @when(child_at(level))
        def _():
            for r in range(rank):
                for t in range(tiles):
                    value = left[r, SUB * t : SUB * (t + 1), :]
                    if t <= r // SUB:
                        value = value - shift * inverse_row(inverse, r, t, rank)
                    child[r, SUB * t : SUB * (t + 1), :] = value

    for q in range(rank):
        for t in range(tiles):
            if t >= q // SUB:
                value = squared[q * rank + SUB * t : q * rank + SUB * (t + 1), :]
            else:
                value = squared[pl.ds(SUB * t * rank + q, SUB, stride=rank), :]
            value = -shift * value
            if t == q // SUB:
                value = value + jnp.where(row == q % SUB, 1.0, 0.0)
            if ratio is not None:
                ratio[level, q, SUB * t : SUB * (t + 1), :] = value
            here = current[q, SUB * t : SUB * (t + 1), :] - shift * value
            current[q, SUB * t : SUB * (t + 1), :] = pair_up(here, level)


def level_plain(level, levels, current, left, inverse, squared, ratio, child, lowest, rank, child_at):
    tiles = rank // SUB
    eliminate(current, left, inverse, level, rank)

    def products(out, count, left_of, right_of):
        def block_step(block, carry):
            offset = pl.multiple_of(block * SUB, SUB)
            sums = [[None] * tiles for _ in range(SUB)]
            for r in range(count):
                parts = [left_of(r, t) for t in range(tiles)]
                heads = right_of(r, offset)
                for q in range(SUB):
                    for t in range(tiles):
                        term = parts[t] * heads[q : q + 1, :]
                        sums[q][t] = term if sums[q][t] is None else sums[q][t] + term
            for q in range(SUB):
                for t in range(tiles):
                    out(offset + q, t, sums[q][t])
            return carry

        lax.fori_loop(0, tiles, block_step, 0)

    def tile(t):
        return slice(SUB * t, SUB * (t + 1))

    def put_child(r, t, value):
        squared[pl.ds(pl.multiple_of(r * rank + SUB * t, SUB), SUB), :] = value

    products(
        put_child, rank,
        lambda k, t: current[k, tile(t), :],
        lambda k, offset: inverse[pl.ds(pl.multiple_of(k * rank + offset, SUB), SUB), :],
    )
    if child is not None:
        @when(child_at(level))
        def _():
            for r in range(rank):
                for t in range(tiles):
                    child[r, tile(t), :] = squared[r * rank + SUB * t : r * rank + SUB * (t + 1), :]

    def child_part(r, t):
        return squared[r * rank + SUB * t : r * rank + SUB * (t + 1), :]

    def put_current(q, t, value):
        current[q, tile(t), :] = pair_up(value, level)

    if ratio is not None:
        def put_ratio(c, t, value):
            ratio[level, c, tile(t), :] = value

        def inverse_head(r, offset):
            return inverse[pl.ds(offset * rank + r, SUB, stride=rank), :]

        products(put_ratio, rank, child_part, inverse_head)
    products(
        put_current, rank, child_part,
        lambda r, offset: squared[pl.ds(pl.multiple_of(r * rank + offset, SUB), SUB), :],
    )


def run_levels(source, levels, nodes, current, left, inverse, squared, ratio, child, lowest, rank, child_at, finish, unrolled=False):
    lowest[...] = jnp.full((1, LANES), 1.0, jnp.float32)

    def sweep(level_step):
        to_lanes(source, current, rank)

        def body(level, carry):
            level_step(level, levels, current, left, inverse, squared, ratio, child, lowest, rank, child_at)
            finish(level)
            return carry

        if unrolled and level_step is level_fast:
            for level in range(levels):
                body(level, 0)
        else:
            lax.fori_loop(0, levels, body, 0)

    sweep(level_fast)
    lane = lax.broadcasted_iota(jnp.int32, (1, LANES), 1)
    least = jnp.min(jnp.where(lane < nodes, lowest[...], 1.0))

    @pl.when(least < 2e-06)
    def _():
        sweep(level_plain)


def branch_body(gram_ref, inverse_ref, ratio_ref, top_ref, child_ref, current, left, inverse, squared, child, lowest, *, rank, levels):
    nodes = gram_ref.shape[0] // rank

    def finish(level):
        @pl.when(level == 0)
        def _():
            for c in range(rank):
                inverse_ref[c] = inverse[c * rank : (c + 1) * rank, :]

        @pl.when(level == levels - 1)
        def _():
            for r in range(rank):
                width = child_ref.shape[1]
                at = r * rank
                child_ref[at // width : at // width + 1, at % width : at % width + rank] = child[r].T[0:1, :]
                top_ref[r : r + 1, :] = jnp.concatenate(
                    [inverse_row(inverse, r, t, rank) for t in range(rank // SUB)], axis=0
                ).T[0:1, :]

    run_levels(
        gram_ref, levels, nodes, current, left, inverse, squared, ratio_ref, child, lowest, rank,
        lambda level: level == levels - 1, finish,
    )


vmem_spec = pl.BlockSpec(memory_space=pltpu.VMEM)


def tree_scratch(rank):
    return [
        pltpu.VMEM((rank, rank, LANES), jnp.float32),
        pltpu.VMEM((rank, rank, LANES), jnp.float32),
        pltpu.VMEM((rank * rank, LANES), jnp.float32),
        pltpu.VMEM((rank * rank, LANES), jnp.float32),
        pltpu.VMEM((rank, rank, LANES), jnp.float32),
        pltpu.VMEM((1, LANES), jnp.float32),
    ]


def branch_factors(gram, levels, width):
    leaves, rank, unused = gram.shape
    return pl.pallas_call(
        functools.partial(branch_body, rank=rank, levels=levels),
        in_specs=[vmem_spec],
        out_specs=[vmem_spec] * 4,
        out_shape=[
            jax.ShapeDtypeStruct((rank, rank, LANES), jnp.float32),
            jax.ShapeDtypeStruct((levels, rank, rank, LANES), jnp.float32),
            jax.ShapeDtypeStruct((rank, rank), jnp.float32),
            jax.ShapeDtypeStruct((rank * rank // width, width), jnp.float32),
        ],
        scratch_shapes=tree_scratch(rank),
        compiler_params=pltpu.CompilerParams(vmem_limit_bytes=vmem_bytes),
        name="branch_factors",
        cost_estimate=pl.CostEstimate(flops=10**6, bytes_accessed=10**4, transcendentals=0),
    )(gram.reshape(leaves * rank, rank))


def basis_body(inverse_ref, ratio_ref, top_ref, sketched_ref, weights_ref, basis_ref, natural, *, rank, levels):
    leaves = sketched_ref.shape[0]
    upper = [top_ref[...]]
    for level in range(levels - 2, -1, -1):
        stride = 2**level
        for c in range(rank):
            from_lanes(ratio_ref[level, c], natural, c, leaves, rank)
        fresh = []
        for node in range(leaves // stride):
            block = natural[node * stride * rank : (node * stride + 1) * rank, :]
            fresh.append(dot_exact(upper[node // 2], block))
        upper = fresh
    for r in range(rank):
        from_lanes(inverse_ref[r], natural, r, leaves, rank)
    for pair in range(leaves // 2):
        results = []
        for leaf in (2 * pair, 2 * pair + 1):
            block = sketched_ref[leaf]
            own = lax.dot_general(
                natural[leaf * rank : (leaf + 1) * rank, :], block, tn_dims,
                precision=highest, preferred_element_type=jnp.float32,
            )
            results.append(jnp.concatenate([dot_exact(upper[leaf], block), own], axis=0))
        both = jnp.concatenate(results, axis=1)
        weights_ref[:, pair * 2 * LEAF : (pair + 1) * 2 * LEAF] = both[:rank]
        basis_ref[:, pair * 2 * LEAF : (pair + 1) * 2 * LEAF] = both[rank:]


def bases(inverse, ratio, top, sketched):
    leaves, rank, unused = sketched.shape
    levels = ratio.shape[0]
    shape = jax.ShapeDtypeStruct((rank, leaves * LEAF), jnp.float32)
    return pl.pallas_call(
        functools.partial(basis_body, rank=rank, levels=levels),
        in_specs=[vmem_spec] * 4,
        out_specs=[vmem_spec] * 2,
        out_shape=[shape, shape],
        scratch_shapes=[pltpu.VMEM((leaves * rank, rank), jnp.float32)],
        compiler_params=pltpu.CompilerParams(vmem_limit_bytes=vmem_bytes),
        name="bases",
        cost_estimate=pl.CostEstimate(flops=10**9, bytes_accessed=10**6, transcendentals=0),
    )(inverse, ratio, top, sketched)


def top_body(side_ref, mine_ref, mirrored_ref, transfer_ref, paths_ref, children_ref, source, current, left, inverse, squared, child, lowest, nat_inverse, nat_child, *, rank, levels):
    half, packed_rows_each, width = mine_ref.shape
    nodes = half
    every = width // rank
    count = half * packed_rows_each
    for ref, side in ((mine_ref, side_ref[0]), (mirrored_ref, 1 - side_ref[0])):
        flat = ref[...].reshape(count, width)
        base = pl.multiple_of(side * (half * rank), half * rank)
        for part in range(every):
            children_ref[pl.ds(base + part, count, stride=every), :] = flat[:, part * rank : (part + 1) * rank]
    for node in range(nodes):
        both = children_ref[2 * node * rank : (2 * node + 2) * rank, :]
        source[node * rank : (node + 1) * rank, :] = lax.dot_general(
            both, both, tn_dims, precision=highest, preferred_element_type=jnp.float32
        )

    def finish(level):
        for r in range(rank):
            from_lanes(child[r], nat_child.at[level], r, nodes, rank)
            from_lanes(inverse[r * rank : (r + 1) * rank, :], nat_inverse.at[level], r, nodes, rank)

    run_levels(
        source, levels, nodes, current, left, inverse, squared, None, child, lowest, rank,
        lambda level: True, finish, unrolled=True,
    )
    offset = 0
    for level in range(levels):
        for node in range(nodes >> level):
            if level == 0:
                stacked = children_ref[2 * node * rank : (2 * node + 2) * rank, :]
            else:
                first = 2 * node << level - 1
                second = 2 * node + 1 << level - 1
                stacked = jnp.concatenate(
                    [
                        nat_child[level - 1, first * rank : (first + 1) * rank, :],
                        nat_child[level - 1, second * rank : (second + 1) * rank, :],
                    ],
                    axis=0,
                )
            at = (node << level) * rank
            transfer_ref[offset + node] = lax.dot_general(
                nat_inverse[level, at : at + rank, :], stacked, (((0,), (1,)), ((), ())),
                precision=highest, preferred_element_type=jnp.float32,
            )
        offset += nodes >> level
    above = [None]
    for level in range(levels - 1, -1, -1):
        offset -= nodes >> level
        fresh = []
        for node in range(nodes >> level):
            both = transfer_ref[offset + node]
            if above[0] is None:
                both = both.T
            else:
                both = lax.dot_general(
                    both, above[node], tn_dims, precision=highest, preferred_element_type=jnp.float32
                )
            fresh += [both[:rank], both[rank:]]
        above = fresh
    for branch in range(2 * nodes):
        paths_ref[branch * rank : (branch + 1) * rank, :] = above[branch]


def top_factors(side, mine, mirrored, rank):
    branches = 2 * mine.shape[0]
    levels = branches.bit_length() - 1
    nodes = branches // 2
    natural = pltpu.VMEM((levels, nodes * rank, rank), jnp.float32)
    return pl.pallas_call(
        functools.partial(top_body, rank=rank, levels=levels),
        in_specs=[pl.BlockSpec(memory_space=pltpu.SMEM), vmem_spec, vmem_spec],
        out_specs=[vmem_spec] * 2,
        out_shape=[
            jax.ShapeDtypeStruct((branches - 1, rank, 2 * rank), jnp.float32),
            jax.ShapeDtypeStruct((branches * rank, rank), jnp.float32),
        ],
        scratch_shapes=[
            pltpu.VMEM((branches * rank, rank), jnp.float32),
            pltpu.VMEM((nodes * rank, rank), jnp.float32),
        ]
        + tree_scratch(rank)
        + [natural, natural],
        compiler_params=pltpu.CompilerParams(vmem_limit_bytes=vmem_bytes),
        name="top_factors",
        cost_estimate=pl.CostEstimate(flops=10**10, bytes_accessed=10**7, transcendentals=0),
    )(side, mine, mirrored)


def exchange_sum(pieces, axis):
    count = pieces.shape[0]
    me = lax.axis_index(axis)
    mine = lax.dynamic_index_in_dim(pieces, me, 0, keepdims=False)
    for step in range(1, count):
        outgoing = lax.dynamic_index_in_dim(pieces, (me + step) % count, 0, keepdims=False)
        mine = mine + lax.ppermute(
            outgoing, axis, [(i, (i + step) % count) for i in range(count)]
        )
    return mine


def exchange_all(piece, axis):
    count = lax.axis_size(axis)
    me = lax.axis_index(axis)
    if count == 2:
        other = lax.ppermute(piece, axis, [(0, 1), (1, 0)])
        return jnp.stack([jnp.where(me == 0, piece, other), jnp.where(me == 0, other, piece)])
    result = jnp.zeros((count,) + piece.shape, piece.dtype)
    result = lax.dynamic_update_index_in_dim(result, piece, me, 0)
    for step in range(1, count):
        arrived = lax.ppermute(piece, axis, [(i, (i + step) % count) for i in range(count)])
        result = lax.dynamic_update_index_in_dim(result, arrived, (me - step) % count, 0)
    return result


def group_tables(far_slots, far_count):
    leaves = far_slots.shape[0]
    groups = leaves * FAR // GROUP
    per_leaf = (far_count + GROUP - 1) // GROUP
    before = jnp.arange(leaves)[:, None] >= jnp.arange(leaves)[None, :]
    ends = jnp.sum(jnp.where(before, per_leaf[None, :], 0), axis=1)
    total = ends[leaves - 1 :]
    ids = jnp.arange(groups, dtype=jnp.int32)
    leaf = jnp.minimum(jnp.sum((ends[None, :] <= ids[:, None]).astype(jnp.int32), axis=1), leaves - 1)
    hit = leaf[:, None] == jnp.arange(leaves)[None, :]
    start = jnp.sum(jnp.where(hit, (ends - per_leaf)[None, :], 0), axis=1)
    length = jnp.sum(jnp.where(hit, far_count[None, :], 0), axis=1)
    sub = ids - start
    count = jnp.where(ids < total, jnp.clip(length - GROUP * sub, 0, GROUP), 0)
    first = jnp.minimum(sub, FAR // GROUP - 1)
    slots = far_slots.reshape(leaves * FAR // GROUP, GROUP)[leaf * (FAR // GROUP) + first]
    return (
        total.astype(jnp.int32),
        leaf.astype(jnp.int32),
        count.astype(jnp.int32),
        slots.reshape(-1).astype(jnp.int32),
    )


def sketch_body(place_ref, sketch_ref, samples_ref, points_ref, mine_ref, other_ref):
    product = dot_exact(sketch_ref[...], samples_ref[...])
    rank, points_dev = product.shape
    quarter = rank // 4
    first = lax.broadcasted_iota(jnp.int32, (1, LANES), 1) < LEAF
    swap = place_ref[0] == 1
    leaves = points_dev // LEAF

    def interleave(low, high):
        even = jnp.where(first, low, pltpu.roll(high, LEAF, 1))
        odd = jnp.where(first, pltpu.roll(low, LEAF, 1), high)
        return even, odd

    for pair in range(leaves // 2):
        lanes = slice(pair * LANES, (pair + 1) * LANES)
        shares = []
        for share in range(2):
            base = 2 * quarter * share
            shares.append(
                interleave(product[base : base + quarter, lanes], product[base + quarter : base + 2 * quarter, lanes])
            )
        for member in range(2):
            at = (2 * pair + member) * quarter
            mine_ref[at : at + quarter, :] = jnp.where(swap, shares[1][member], shares[0][member])
            other_ref[at : at + quarter, :] = jnp.where(swap, shares[0][member], shares[1][member])
        x = points_ref[0:1, lanes]
        y = points_ref[1:2, lanes]
        z = points_ref[2:3, lanes]
        xy = interleave(x, y)
        zs = interleave(z, jnp.zeros_like(z))
        for member in range(2):
            at = leaves * quarter + (2 * pair + member) * 2
            mine_ref[at : at + 1, :] = xy[member]
            mine_ref[at + 1 : at + 2, :] = zs[member]
    other_ref[leaves * quarter :, :] = jnp.zeros((2 * leaves, LANES), jnp.float32)


def sketched_shares(place, sketch, samples, points):
    rank = sketch.shape[0]
    leaves = samples.shape[1] // LEAF
    return pl.pallas_call(
        sketch_body,
        in_specs=[pl.BlockSpec(memory_space=pltpu.SMEM)] + [vmem_spec] * 3,
        out_specs=[vmem_spec] * 2,
        out_shape=[
            jax.ShapeDtypeStruct((leaves * (rank // 4 + 2), LANES), jnp.float32),
            jax.ShapeDtypeStruct((leaves * (rank // 4 + 2), LANES), jnp.float32),
        ],
        compiler_params=pltpu.CompilerParams(vmem_limit_bytes=vmem_bytes),
        name="sketched_shares",
        cost_estimate=pl.CostEstimate(flops=10**6, bytes_accessed=10**4, transcendentals=0),
    )(place, sketch, samples, points)


def pack_body(asked_ref, side_ref, mine_ref, partner_ref, out_ref, *, cap, leaves):
    z_rows = mine_ref.shape[0] // leaves - 2
    side = side_ref[0]

    def one(peer, carry):
        for entry in range(2 * cap):
            leaf = asked_ref[peer, entry]
            here = side == entry // cap
            at = pl.ds(leaf * z_rows, z_rows)
            out_ref[peer, z_rows * entry : z_rows * (entry + 1), :] = jnp.where(
                here, mine_ref[at, :], partner_ref[at, :]
            )
            base = z_rows * 2 * cap + 2 * entry
            at = pl.ds(leaves * z_rows + leaf * 2, 2)
            out_ref[peer, base : base + 2, :] = jnp.where(here, mine_ref[at, :], partner_ref[at, :])
        return carry

    lax.fori_loop(0, out_ref.shape[0], one, 0)


def packed_rows(asked, side, mine, partner, cap, leaves):
    z_rows = mine.shape[0] // leaves - 2
    return pl.pallas_call(
        functools.partial(pack_body, cap=cap, leaves=leaves),
        in_specs=[pl.BlockSpec(memory_space=pltpu.SMEM)] * 2 + [vmem_spec] * 2,
        out_specs=vmem_spec,
        out_shape=jax.ShapeDtypeStruct((asked.shape[0], 2 * cap * (z_rows + 2), LANES), jnp.float32),
        compiler_params=pltpu.CompilerParams(vmem_limit_bytes=vmem_bytes),
        name="packed_rows",
    )(asked, side, mine, partner)


def payload_body(asked_ref, side_ref, rows_ref, child_ref, out_ref, *, cap):
    base = (1 - side_ref[0]) * cap

    def one(peer, carry):
        for entry in range(cap):
            out_ref[peer, LEAF * entry : LEAF * (entry + 1), :] = rows_ref[asked_ref[peer, base + entry]]
        out_ref[peer, LEAF * cap :, :] = child_ref[...]
        return carry

    lax.fori_loop(0, out_ref.shape[0], one, 0)


def payload_rows(asked, side, rows, child):
    half = asked.shape[0]
    cap = asked.shape[1] // 2
    return pl.pallas_call(
        functools.partial(payload_body, cap=cap),
        in_specs=[pl.BlockSpec(memory_space=pltpu.SMEM)] * 2 + [vmem_spec] * 2,
        out_specs=vmem_spec,
        out_shape=jax.ShapeDtypeStruct((half, cap * LEAF + child.shape[0], rows.shape[2]), jnp.float32),
        compiler_params=pltpu.CompilerParams(vmem_limit_bytes=vmem_bytes),
        name="payload_rows",
    )(asked, side, rows, child)


def two_rows(values, rows):
    leaves = values.shape[1]
    split = jnp.transpose(values.reshape(2, rows, leaves, LEAF), (2, 1, 0, 3))
    return split.reshape(leaves, rows, 2 * LEAF)


def on_device(points, samples, sketch, far_requests, far_slots, far_count, near_mask):
    samp_dev = samples.shape[0]
    leaves = samples.shape[1] // LEAF
    rank = sketch.shape[0]
    branches = lax.axis_size("leaf")
    columns = lax.axis_size("cols")
    cap = far_requests.shape[2]
    share = rank // columns
    me = lax.axis_index("leaf")
    column = lax.axis_index("cols")

    half = branches // 2
    side = me // half
    groups = [list(range(half)), list(range(half, branches))]
    mirror = [(i, (i + half) % branches) for i in range(branches)]
    side_ref = side.astype(jnp.int32).reshape(1)
    wanted = jnp.transpose(far_requests.reshape(2, half, cap), (1, 0, 2)).reshape(half, 2 * cap)
    if columns == 2:
        place = column.astype(jnp.int32).reshape(1)
        mine, other = sketched_shares(place, sketch, samples, points)
        mine = mine + lax.ppermute(other, "cols", [(0, 1), (1, 0)])
        wanted, mine = lax.optimization_barrier((wanted, mine))
    else:
        z_part = jnp.dot(sketch, samples, precision=highest)
        z_mine = exchange_sum(z_part.reshape(columns, share, leaves * LEAF), "cols")
        z_rows = two_rows(z_mine.reshape(share, leaves, LEAF), share // 2)
        planes = points.reshape(3, leaves, LEAF)
        c_rows = two_rows(
            jnp.concatenate([planes[0:1], planes[2:3], planes[1:2], jnp.zeros_like(planes[0:1])], axis=0), 2
        )
        mine = jnp.concatenate([z_rows.reshape(-1, LANES), c_rows.reshape(-1, LANES)], axis=0)

    partner = lax.ppermute(mine, "leaf", mirror)
    asked = lax.all_to_all(
        wanted, "leaf", split_axis=0, concat_axis=0, axis_index_groups=groups, tiled=True
    )
    coords = jnp.transpose(points.reshape(3, leaves, LEAF), (1, 0, 2))
    targets = jnp.transpose(coords, (0, 2, 1))
    rows = jnp.transpose(samples.reshape(samp_dev, leaves, LEAF), (1, 2, 0))

    tables = group_tables(far_slots, far_count)
    asked, rows, targets, tables = lax.optimization_barrier((asked, rows, targets, tables))
    total, group_leaf, group_count, group_slots = tables
    small_sent = packed_rows(asked, side_ref, mine, partner, cap, leaves)
    small_got = lax.all_to_all(
        small_sent, "leaf", split_axis=0, concat_axis=0, axis_index_groups=groups, tiled=True
    )

    rows_out, unused = lax.optimization_barrier((rows, small_sent))
    partner_rows = lax.ppermute(rows_out, "leaf", mirror)

    forward = [(i, i + 1) for i in range(branches - 1)]
    backward = [(target, source) for source, target in forward]
    width = max(samp_dev, LEAF)

    def edge(first):
        samples_edge = jnp.transpose(lax.slice_in_dim(samples, first, first + LEAF, axis=1))
        points_edge = lax.slice_in_dim(points, first, first + LEAF, axis=1)
        return jnp.concatenate(
            [
                jnp.pad(samples_edge, ((0, 0), (0, width - samp_dev))),
                jnp.pad(points_edge, ((0, 5), (0, width - LEAF))),
            ],
            axis=0,
        )

    last, first, unused = lax.optimization_barrier((edge((leaves - 1) * LEAF), edge(0), small_sent))
    low_edge = lax.ppermute(last, "leaf", forward)
    high_edge = lax.ppermute(first, "leaf", backward)

    own_asked = lax.dynamic_slice_in_dim(asked, side * cap, cap, axis=1)
    own_sent = rows_out[own_asked.reshape(-1)].reshape(half, cap, LEAF, samp_dev)
    own_sent, low_edge, high_edge = lax.optimization_barrier((own_sent, low_edge, high_edge))
    own_got = lax.all_to_all(
        own_sent, "leaf", split_axis=0, concat_axis=0, axis_index_groups=groups, tiled=True
    )
    own_got = own_got.reshape(half * cap, LEAF, samp_dev)

    if columns == 2:
        small_other = lax.ppermute(small_got, "cols", [(0, 1), (1, 0)])
    else:
        z_count = cap * share
        z_all = exchange_all(small_got[:, :z_count], "cols")
        z_all = z_all.reshape(columns, half, 2 * cap, share // 2, 2, LEAF)
        z_all = jnp.transpose(z_all, (1, 2, 0, 4, 3, 5)).reshape(half, 2 * cap, 2, 2, rank // 4, LEAF)
        z_all = jnp.transpose(z_all, (2, 0, 1, 4, 3, 5)).reshape(2, half, cap * rank // 2, LANES)
        c_got = small_got[:, z_count:]
        small_got = jnp.concatenate([z_all[0], c_got], axis=1)
        small_other = jnp.concatenate([z_all[1], c_got], axis=1)
        place = jnp.zeros((1,), jnp.int32)

    blocks, sketched, gram = kernel_blocks(
        total, group_leaf, group_count, group_slots, place, small_got, small_other, targets, rank, cap
    )

    levels = leaves.bit_length()
    inverse, ratio, top_inverse, own_child = branch_factors(gram, levels, min(samp_dev, LANES))
    own_child, own_got, partner_rows = lax.optimization_barrier((own_child, own_got, partner_rows))
    payload = payload_rows(asked, side_ref, partner_rows, own_child)
    arrived = lax.all_to_all(
        payload, "leaf", split_axis=0, concat_axis=0, axis_index_groups=groups, tiled=True
    )
    ratio, low_edge, high_edge, unused = lax.optimization_barrier((ratio, low_edge, high_edge, payload))
    weights, leaf_basis = bases(inverse, ratio, top_inverse, sketched)

    rows_low, rows_high = low_edge[:LEAF, :samp_dev], high_edge[:LEAF, :samp_dev]
    coords_low, coords_high = low_edge[LEAF : LEAF + 3, :LEAF], high_edge[LEAF : LEAF + 3, :LEAF]
    near_rows = jnp.concatenate(
        [rows_low[None], rows, rows_high[None], jnp.zeros_like(rows_low)[None]], axis=0
    )
    near_coords = jnp.concatenate(
        [coords_low[None], coords, coords_high[None], jnp.zeros_like(coords_low)[None]], axis=0
    )
    near_coords = jnp.pad(near_coords, ((0, 0), (0, 5), (0, 0)))
    near_coords = jnp.concatenate([near_coords, near_coords], axis=2)
    near_sample = near_products(near_mask.reshape(-1), near_rows, near_coords, targets)


    children = arrived[:, cap * LEAF :]
    mirrored = lax.ppermute(children, "leaf", mirror)
    weights, near_sample = lax.optimization_barrier((weights, near_sample))
    far_sample, branch_samples, copies = far_products(
        total, group_leaf, group_slots, side_ref, own_got, arrived, blocks, weights, branches
    )
    everyone = lax.all_to_all(copies, "leaf", split_axis=0, concat_axis=0, tiled=True)
    children, mirrored, unused = lax.optimization_barrier((children, mirrored, branch_samples))
    transfer_t, paths = top_factors(side_ref, children, mirrored, rank)
    top_transfer = jnp.swapaxes(transfer_t, 1, 2)
    root_sample = lax.dot_general(
        paths, everyone.reshape(branches * rank, samp_dev), tn_dims, precision=highest
    )
    return (far_sample, near_sample, leaf_basis, branch_samples, top_transfer, root_sample)


def solution(mesh):
    return jax.shard_map(
        on_device,
        mesh=mesh,
        in_specs=(
            P(None, "leaf"),
            P("cols", "leaf"),
            P(None, "cols"),
            P("leaf", None, None),
            P("leaf", None),
            P("leaf"),
            P("leaf", None),
        ),
        out_specs=(
            P("cols", "leaf"),
            P("cols", "leaf"),
            P(None, "leaf"),
            P("leaf", "cols"),
            P(),
            P(None, "cols"),
        ),
        check_vma=False,
    )
```

```python
import functools
import math

import jax
import jax.numpy as jnp
import numpy as np
from jax import lax
from jax.experimental import pallas as pl
from jax.experimental.pallas import tpu as pltpu
from jax.sharding import PartitionSpec as P

LEAF = 64
FAR = 16
GROUP = 4
BATCH = 16
LANES = 128
SUB = 8

length_scale = 0.3
shift_share = 0.05
highest = lax.Precision.HIGHEST
exponent_scale = -math.log2(math.e) / length_scale
vmem_bytes = 56 * 1024 * 1024

nt_dims = (((1,), (1,)), ((), ()))
tn_dims = (((0,), (0,)), ((), ()))


def halves(value):
    high = value.astype(jnp.bfloat16)
    low = (value - high.astype(jnp.float32)).astype(jnp.bfloat16)
    return high, low


def dot(a, b):
    return jnp.dot(a, b, preferred_element_type=jnp.float32)


def dot_exact(a, b):
    return jnp.dot(a, b, precision=highest, preferred_element_type=jnp.float32)


def dot_exact_nt(a, b):
    return lax.dot_general(a, b, nt_dims, precision=highest, preferred_element_type=jnp.float32)


def stacked_halves(value, axis):
    return jnp.concatenate(halves(value), axis=axis)


def quadrants(product):
    rows, columns = product.shape[0] // 2, product.shape[1] // 2
    top = product[:rows, :columns] + product[:rows, columns:]
    return top + (product[rows:, :columns] + product[rows:, columns:])


def dot_nt(a, b):
    return lax.dot_general(a, b, nt_dims, preferred_element_type=jnp.float32)


def kernel_half(source_rows, target, lane, valid):
    total = None
    for axis in range(3):
        difference = source_rows[axis : axis + 1, :] - target[:, axis : axis + 1]
        square = difference * difference
        total = square if total is None else total + square
    distance = total * lax.rsqrt(jnp.maximum(total, 1e-30))
    values = jnp.exp2(distance * exponent_scale)
    return jnp.where(lane < valid, values, 0.0)


def blocks_body(
    total_ref, leaf_ref, count_ref, slot_ref, place_ref,
    own_ref, other_ref, target_ref,
    both_ref, sketched_ref, gram_ref,
    packed,
    *, rank, cap,
):
    step = pl.program_id(0)
    lane = lax.broadcasted_iota(jnp.int32, (1, LANES), 1)
    first = lane < LEAF

    @pl.when(step == 0)
    def _():
        sketched_ref[...] = jnp.zeros_like(sketched_ref)
        quarter = rank // 4
        slots = packed.shape[0]
        own_at = pl.multiple_of(place_ref[0] * 2 * quarter, quarter)
        other_at = pl.multiple_of((1 - place_ref[0]) * 2 * quarter, quarter)

        def unpack(peer, carry):
            for entry in range(2 * cap):
                slot = (entry // cap) * (slots // 2) + peer * cap + entry % cap
                at = entry * quarter
                for ref, base in ((own_ref, own_at), (other_ref, other_at)):
                    value = ref[peer, at : at + quarter, :]
                    turned = pltpu.roll(value, LEAF, 1)
                    packed[slot, pl.ds(base, quarter), :] = jnp.where(first, value, turned)
                    packed[slot, pl.ds(base + quarter, quarter), :] = jnp.where(first, turned, value)
                at = 2 * cap * quarter + 2 * entry
                value = own_ref[peer, at : at + 2, :]
                turned = pltpu.roll(value, LEAF, 1)
                packed[slot, rank : rank + 1, :] = jnp.where(first, value, turned)[0:1]
                packed[slot, rank + 1 : rank + 2, :] = jnp.where(first, turned, value)[0:1]
                packed[slot, rank + 2 : rank + 3, :] = jnp.where(first, value, turned)[1:2]
            return carry

        lax.fori_loop(0, slots // (2 * cap), unpack, 0)

    @pl.when(step * BATCH < total_ref[0])
    def _():
        for member in range(BATCH):
            group = step * BATCH + member
            leaf = leaf_ref[group]
            count = count_ref[group]
            slots = [slot_ref[group * GROUP + e] for e in range(GROUP)]
            target = target_ref[leaf]
            z_parts = []
            for half in range(GROUP // 2):
                left = packed[slots[2 * half]]
                right = packed[slots[2 * half + 1]]
                both = jnp.where(first, left, right)
                values = kernel_half(both[rank : rank + 3], target, lane, (count - 2 * half) * LEAF)
                both_ref[member, :, half * LANES : (half + 1) * LANES] = stacked_halves(values, 0)
                z_parts.append(both[:rank])
            z_both = stacked_halves(jnp.concatenate(z_parts, axis=1), 0)
            sketched_ref[leaf] += quadrants(dot_nt(z_both, both_ref[member]))

    @pl.when(step == pl.num_programs(0) - 1)
    def _():
        for leaf in range(gram_ref.shape[0]):
            block = sketched_ref[leaf]
            gram_ref[leaf] = dot_exact_nt(block, block)


def kernel_blocks(total, group_leaf, group_count, group_slots, place, own, other, targets, rank, cap):
    leaves = targets.shape[0]
    groups = group_leaf.shape[0]
    slots = own.shape[0] * 2 * cap
    steps = groups // BATCH

    def block_index(step, total_ref, *unused):
        last = (total_ref[0] - 1) // BATCH
        return (jnp.minimum(step, last), 0, 0)

    whole = lambda *unused: (0, 0, 0)
    once = pl.Buffered(1)
    return pl.pallas_call(
        functools.partial(blocks_body, rank=rank, cap=cap),
        grid_spec=pltpu.PrefetchScalarGridSpec(
            num_scalar_prefetch=5,
            grid=(steps,),
            in_specs=[
                pl.BlockSpec(own.shape, whole, pipeline_mode=once),
                pl.BlockSpec(other.shape, whole, pipeline_mode=once),
                pl.BlockSpec(targets.shape, whole, pipeline_mode=once),
            ],
            out_specs=[
                pl.BlockSpec((BATCH, 2 * LEAF, GROUP * LEAF), block_index),
                pl.BlockSpec((leaves, rank, LEAF), whole),
                pl.BlockSpec((leaves, rank, rank), whole),
            ],
            scratch_shapes=[pltpu.VMEM((slots, rank + SUB, LANES), jnp.float32)],
        ),
        out_shape=[
            jax.ShapeDtypeStruct((groups, 2 * LEAF, GROUP * LEAF), jnp.bfloat16),
            jax.ShapeDtypeStruct((leaves, rank, LEAF), jnp.float32),
            jax.ShapeDtypeStruct((leaves, rank, rank), jnp.float32),
        ],
        compiler_params=pltpu.CompilerParams(vmem_limit_bytes=vmem_bytes),
        name="kernel_blocks",
        cost_estimate=pl.CostEstimate(
            flops=10**6, bytes_accessed=10**4, transcendentals=0
        ),
    )(total, group_leaf, group_count, group_slots, place, own, other, targets)


def far_groups(sizes_ref, leaf_ref, slot_ref, first_batch, live, blocks_ref, s_both, acc):
    step = pl.program_id(0)

    @pl.when(step * BATCH < live)
    def _():
        for member in range(BATCH):
            group = first_batch * BATCH + step * BATCH + member
            leaf = leaf_ref[group]
            slots = [slot_ref[group * GROUP + e] for e in range(GROUP)]
            rows = jnp.concatenate([s_both[slot] for slot in slots], axis=0)
            acc[leaf] += quadrants(dot(blocks_ref[member], rows))


def far_own_body(sizes_ref, leaf_ref, slot_ref, own_ref, blocks_ref, acc_ref, s_both):
    @pl.when(pl.program_id(0) == 0)
    def _():
        acc_ref[...] = jnp.zeros_like(acc_ref)

        def split(slot, carry):
            s_both[slot] = stacked_halves(own_ref[slot], 1)
            return carry

        lax.fori_loop(0, own_ref.shape[0], split, 0, unroll=8)

    far_groups(sizes_ref, leaf_ref, slot_ref, 0, sizes_ref[1], blocks_ref, s_both, acc_ref)


def far_partner_body(
    sizes_ref, leaf_ref, slot_ref,
    partner_ref, blocks_ref, start_ref, weights_ref,
    out_ref, projected_ref, copies_ref,
    s_both, acc,
    *, cap,
):
    step = pl.program_id(0)
    samp_dev = partner_ref.shape[2]

    @pl.when(step == 0)
    def _():
        acc[...] = start_ref[...]

        def split(peer, carry):
            for entry in range(cap):
                s_both[peer * cap + entry] = stacked_halves(
                    partner_ref[peer, LEAF * entry : LEAF * (entry + 1), :], 1
                )
            return carry

        lax.fori_loop(0, partner_ref.shape[0], split, 0)

    far_groups(
        sizes_ref, leaf_ref, slot_ref, sizes_ref[2] // BATCH, sizes_ref[3], blocks_ref, s_both, acc
    )

    @pl.when(step == pl.num_programs(0) - 1)
    def _():
        leaves = acc.shape[0]
        rows = acc[...].reshape(leaves * LEAF, samp_dev)
        projected = dot_exact(weights_ref[...], rows)
        projected_ref[...] = projected
        for branch in range(copies_ref.shape[0]):
            copies_ref[branch] = projected
        for pair in range(leaves // 2):
            block = acc[2 * pair : 2 * pair + 2].reshape(2 * LEAF, samp_dev)
            out_ref[:, 2 * pair * LEAF : 2 * (pair + 1) * LEAF] = block.T


def far_own(sizes, group_leaf, group_slots, own, blocks, leaves):
    part, unused, samp_dev = own.shape
    steps = leaves * FAR // GROUP // BATCH

    def block_index(step, sizes_ref, *unused):
        last = jnp.maximum(sizes_ref[1] - 1, 0) // BATCH
        return (jnp.minimum(step, last), 0, 0)

    whole = lambda *unused: (0, 0, 0)
    return pl.pallas_call(
        far_own_body,
        grid_spec=pltpu.PrefetchScalarGridSpec(
            num_scalar_prefetch=3,
            grid=(steps,),
            in_specs=[
                pl.BlockSpec(own.shape, whole, pipeline_mode=pl.Buffered(1)),
                pl.BlockSpec((BATCH, 2 * LEAF, GROUP * LEAF), block_index),
            ],
            out_specs=pl.BlockSpec((leaves, LEAF, samp_dev), whole),
            scratch_shapes=[pltpu.VMEM((part, LEAF, 2 * samp_dev), jnp.bfloat16)],
        ),
        out_shape=jax.ShapeDtypeStruct((leaves, LEAF, samp_dev), jnp.float32),
        compiler_params=pltpu.CompilerParams(vmem_limit_bytes=vmem_bytes),
        name="far_own",
        cost_estimate=pl.CostEstimate(flops=10**9, bytes_accessed=10**6, transcendentals=0),
    )(sizes, group_leaf, group_slots, own, blocks)


def far_partner(sizes, group_leaf, group_slots, partner, blocks, start, weights, cap, branches):
    leaves, unused, samp_dev = start.shape
    part = partner.shape[0] * cap
    points_dev = leaves * LEAF
    rank = weights.shape[0]
    steps = leaves * FAR // GROUP // BATCH

    def block_index(step, sizes_ref, *unused):
        last = jnp.maximum(sizes_ref[3] - 1, 0) // BATCH
        most = blocks.shape[0] // BATCH - 1
        return (jnp.minimum(sizes_ref[2] // BATCH + jnp.minimum(step, last), most), 0, 0)

    flat = lambda *unused: (0, 0)
    whole = lambda *unused: (0, 0, 0)
    once = pl.Buffered(1)
    return pl.pallas_call(
        functools.partial(far_partner_body, cap=cap),
        grid_spec=pltpu.PrefetchScalarGridSpec(
            num_scalar_prefetch=3,
            grid=(steps,),
            in_specs=[
                pl.BlockSpec(partner.shape, whole, pipeline_mode=once),
                pl.BlockSpec((BATCH, 2 * LEAF, GROUP * LEAF), block_index),
                pl.BlockSpec(start.shape, whole, pipeline_mode=once),
                pl.BlockSpec(weights.shape, flat, pipeline_mode=once),
            ],
            out_specs=[
                pl.BlockSpec((samp_dev, points_dev), flat),
                pl.BlockSpec((rank, samp_dev), flat),
                pl.BlockSpec((branches, rank, samp_dev), whole),
            ],
            scratch_shapes=[
                pltpu.VMEM((part, LEAF, 2 * samp_dev), jnp.bfloat16),
                pltpu.VMEM((leaves, LEAF, samp_dev), jnp.float32),
            ],
        ),
        out_shape=[
            jax.ShapeDtypeStruct((samp_dev, points_dev), jnp.float32),
            jax.ShapeDtypeStruct((rank, samp_dev), jnp.float32),
            jax.ShapeDtypeStruct((branches, rank, samp_dev), jnp.float32),
        ],
        compiler_params=pltpu.CompilerParams(vmem_limit_bytes=vmem_bytes),
        name="far_partner",
        cost_estimate=pl.CostEstimate(flops=10**10, bytes_accessed=10**7, transcendentals=0),
    )(sizes, group_leaf, group_slots, partner, blocks, start, weights)


NEAR_LEAVES = 8


def near_body(mask_ref, rows_ref, coords_ref, target_ref, out_ref):
    step = pl.program_id(0)
    samp_dev = rows_ref.shape[2]
    lane = lax.broadcasted_iota(jnp.int32, (1, LANES), 1)
    first = lane < LEAF
    for pair in range(NEAR_LEAVES // 2):
        results = []
        for member in range(2):
            leaf = step * NEAR_LEAVES + 2 * pair + member
            target = target_ref[leaf]
            k_parts = []
            for half in range(2):
                both = jnp.where(first, coords_ref[leaf + 2 * half], coords_ref[leaf + 2 * half + 1])
                values = kernel_half(both, target, lane, LANES)
                left = mask_ref[leaf * 3 + 2 * half].astype(jnp.float32)
                if half == 0:
                    right = mask_ref[leaf * 3 + 1].astype(jnp.float32)
                else:
                    right = jnp.float32(0.0)
                k_parts.append(stacked_halves(values * jnp.where(first, left, right), 0))
            rows = rows_ref[pl.ds(leaf, 4)].reshape(4 * LEAF, samp_dev)
            product = dot(jnp.concatenate(k_parts, axis=1), stacked_halves(rows, 1))
            results.append(quadrants(product))
        block = jnp.concatenate(results, axis=0)
        out_ref[:, 2 * pair * LEAF : 2 * (pair + 1) * LEAF] = block.T


def near_products(mask, rows, coords, targets):
    leaves = targets.shape[0]
    samp_dev = rows.shape[2]
    whole = lambda *unused: (0, 0, 0)
    return pl.pallas_call(
        near_body,
        grid_spec=pltpu.PrefetchScalarGridSpec(
            num_scalar_prefetch=1,
            grid=(leaves // NEAR_LEAVES,),
            in_specs=[
                pl.BlockSpec(rows.shape, whole),
                pl.BlockSpec(coords.shape, whole),
                pl.BlockSpec(targets.shape, whole),
            ],
            out_specs=pl.BlockSpec((samp_dev, NEAR_LEAVES * LEAF), lambda step, *unused: (0, step)),
        ),
        out_shape=jax.ShapeDtypeStruct((samp_dev, leaves * LEAF), jnp.float32),
        compiler_params=pltpu.CompilerParams(vmem_limit_bytes=vmem_bytes),
        name="near_products",
        cost_estimate=pl.CostEstimate(
            flops=10**9, bytes_accessed=10**6, transcendentals=0
        ),
    )(mask, rows, coords, targets)


def to_lanes(source, target, rank):
    nodes = source.shape[0] // rank
    target[...] = jnp.zeros_like(target)
    for r in range(rank):
        target[r, :, 0:nodes] = source[pl.ds(r, nodes, stride=rank), :].T


def from_lanes(columns, target, r, nodes, rank):
    target[pl.ds(r, nodes, stride=rank), :] = columns.T[0:nodes]


def eliminate(current, left, inverse, level, rank):
    tiles = rank // SUB
    row = lax.broadcasted_iota(jnp.int32, (SUB, LANES), 0)
    diagonal = [current[j, j : j + 1, :] for j in range(rank)]
    while len(diagonal) > 1:
        diagonal = [diagonal[i] + diagonal[i + 1] for i in range(0, len(diagonal), 2)]
    share = shift_share * diagonal[0] / rank
    shift = share + 1e-06
    a = [
        {t: current[j, SUB * t : SUB * (t + 1), :] for t in range(j // SUB, tiles)}
        for j in range(rank)
    ]
    for j in range(rank):
        a[j][j // SUB] = a[j][j // SUB] + jnp.where(row == j % SUB, shift, 0.0)
    m = []
    scales = []
    for k in range(rank):
        tk, rk = k // SUB, k % SUB
        root = lax.rsqrt(a[k][tk][rk : rk + 1, :])
        scales.append(root)
        reciprocal = root * root
        column = {t: a[k][t] * reciprocal for t in range(tk, tiles)}
        column[tk] = jnp.where(row > rk, column[tk], 0.0)
        for j in range(k + 1, rank):
            factor = a[k][j // SUB][j % SUB : j % SUB + 1, :]
            for t in range(j // SUB, tiles):
                a[j][t] = a[j][t] - column[t] * factor
        for c in range(k):
            factor = m[c][tk][rk : rk + 1, :]
            for t in range(tk, tiles):
                m[c][t] = m[c][t] - column[t] * factor
        fresh = {t: -column[t] for t in range(tk, tiles)}
        fresh[tk] = jnp.where(row == rk, 1.0, fresh[tk])
        m.append(fresh)
        if left is not None:
            for t in range(tiles):
                if t < tk:
                    value = jnp.zeros((SUB, LANES), jnp.float32)
                else:
                    value = a[k][t] * root
                if t == tk:
                    value = jnp.where(row >= rk, value, 0.0)
                left[k, SUB * t : SUB * (t + 1), :] = value
    for t in range(tiles):
        scale = jnp.concatenate(scales[SUB * t : SUB * (t + 1)], axis=0)
        for c in range(rank):
            value = m[c][t] * scale if t >= c // SUB else jnp.zeros((SUB, LANES), jnp.float32)
            inverse[c * rank + SUB * t : c * rank + SUB * (t + 1), :] = value
    return shift, share


def inverse_row(inverse, r, t, rank):
    return inverse[pl.ds(SUB * t * rank + r, SUB, stride=rank), :]


def pair_up(value, level):
    reach = LANES - (1 << level if isinstance(level, int) else lax.shift_left(1, level))
    return value + pltpu.roll(value, reach, 1)


def when(condition):
    if isinstance(condition, bool):
        return lambda body: body() if condition else None
    return pl.when(condition)


def level_fast(level, levels, current, left, inverse, squared, ratio, child, lowest, rank, child_at):
    tiles = rank // SUB
    row = lax.broadcasted_iota(jnp.int32, (SUB, LANES), 0)
    shift, share = eliminate(current, left, inverse, level, rank)
    lowest[...] = jnp.minimum(lowest[...], share)

    for block in range(tiles):
        sums = [[None] * tiles for _ in range(SUB)]
        for r in range(SUB * block, rank):
            parts = [inverse_row(inverse, r, t, rank) for t in range(block, r // SUB + 1)]
            for q in range(SUB):
                if SUB * block + q > r:
                    continue
                factor = parts[0][q : q + 1, :]
                for t in range(block, r // SUB + 1):
                    term = parts[t - block] * factor
                    sums[q][t] = term if sums[q][t] is None else sums[q][t] + term
        for q in range(SUB):
            at = (SUB * block + q) * rank
            for t in range(block, tiles):
                squared[at + SUB * t : at + SUB * (t + 1), :] = sums[q][t]

    if child is not None:
        @when(child_at(level))
        def _():
            for r in range(rank):
                for t in range(tiles):
                    value = left[r, SUB * t : SUB * (t + 1), :]
                    if t <= r // SUB:
                        value = value - shift * inverse_row(inverse, r, t, rank)
                    child[r, SUB * t : SUB * (t + 1), :] = value

    for q in range(rank):
        for t in range(tiles):
            if t >= q // SUB:
                value = squared[q * rank + SUB * t : q * rank + SUB * (t + 1), :]
            else:
                value = squared[pl.ds(SUB * t * rank + q, SUB, stride=rank), :]
            value = -shift * value
            if t == q // SUB:
                value = value + jnp.where(row == q % SUB, 1.0, 0.0)
            if ratio is not None:
                ratio[level, q, SUB * t : SUB * (t + 1), :] = value
            here = current[q, SUB * t : SUB * (t + 1), :] - shift * value
            current[q, SUB * t : SUB * (t + 1), :] = pair_up(here, level)


def level_plain(level, levels, current, left, inverse, squared, ratio, child, lowest, rank, child_at):
    tiles = rank // SUB
    eliminate(current, left, inverse, level, rank)

    def products(out, count, left_of, right_of):
        def block_step(block, carry):
            offset = pl.multiple_of(block * SUB, SUB)
            sums = [[None] * tiles for _ in range(SUB)]
            for r in range(count):
                parts = [left_of(r, t) for t in range(tiles)]
                heads = right_of(r, offset)
                for q in range(SUB):
                    for t in range(tiles):
                        term = parts[t] * heads[q : q + 1, :]
                        sums[q][t] = term if sums[q][t] is None else sums[q][t] + term
            for q in range(SUB):
                for t in range(tiles):
                    out(offset + q, t, sums[q][t])
            return carry

        lax.fori_loop(0, tiles, block_step, 0)

    def tile(t):
        return slice(SUB * t, SUB * (t + 1))

    def put_child(r, t, value):
        squared[pl.ds(pl.multiple_of(r * rank + SUB * t, SUB), SUB), :] = value

    products(
        put_child, rank,
        lambda k, t: current[k, tile(t), :],
        lambda k, offset: inverse[pl.ds(pl.multiple_of(k * rank + offset, SUB), SUB), :],
    )
    if child is not None:
        @when(child_at(level))
        def _():
            for r in range(rank):
                for t in range(tiles):
                    child[r, tile(t), :] = squared[r * rank + SUB * t : r * rank + SUB * (t + 1), :]

    def child_part(r, t):
        return squared[r * rank + SUB * t : r * rank + SUB * (t + 1), :]

    def put_current(q, t, value):
        current[q, tile(t), :] = pair_up(value, level)

    if ratio is not None:
        def put_ratio(c, t, value):
            ratio[level, c, tile(t), :] = value

        def inverse_head(r, offset):
            return inverse[pl.ds(offset * rank + r, SUB, stride=rank), :]

        products(put_ratio, rank, child_part, inverse_head)
    products(
        put_current, rank, child_part,
        lambda r, offset: squared[pl.ds(pl.multiple_of(r * rank + offset, SUB), SUB), :],
    )


def run_levels(source, levels, nodes, current, left, inverse, squared, ratio, child, lowest, rank, child_at, finish, unrolled=False):
    lowest[...] = jnp.full((1, LANES), 1.0, jnp.float32)

    def sweep(level_step):
        to_lanes(source, current, rank)

        def body(level, carry):
            level_step(level, levels, current, left, inverse, squared, ratio, child, lowest, rank, child_at)
            finish(level)
            return carry

        if unrolled and level_step is level_fast:
            for level in range(levels):
                body(level, 0)
        else:
            lax.fori_loop(0, levels, body, 0)

    sweep(level_fast)
    lane = lax.broadcasted_iota(jnp.int32, (1, LANES), 1)
    least = jnp.min(jnp.where(lane < nodes, lowest[...], 1.0))

    @pl.when(least < 2e-06)
    def _():
        sweep(level_plain)


def branch_body(gram_ref, inverse_ref, ratio_ref, top_ref, child_ref, current, left, inverse, squared, child, lowest, *, rank, levels):
    nodes = gram_ref.shape[0] // rank

    def finish(level):
        @pl.when(level == 0)
        def _():
            for c in range(rank):
                inverse_ref[c] = inverse[c * rank : (c + 1) * rank, :]

        @pl.when(level == levels - 1)
        def _():
            for r in range(rank):
                width = child_ref.shape[1]
                at = r * rank
                child_ref[at // width : at // width + 1, at % width : at % width + rank] = child[r].T[0:1, :]
                top_ref[r : r + 1, :] = jnp.concatenate(
                    [inverse_row(inverse, r, t, rank) for t in range(rank // SUB)], axis=0
                ).T[0:1, :]

    run_levels(
        gram_ref, levels, nodes, current, left, inverse, squared, ratio_ref, child, lowest, rank,
        lambda level: level == levels - 1, finish,
    )


vmem_spec = pl.BlockSpec(memory_space=pltpu.VMEM)


def tree_scratch(rank):
    return [
        pltpu.VMEM((rank, rank, LANES), jnp.float32),
        pltpu.VMEM((rank, rank, LANES), jnp.float32),
        pltpu.VMEM((rank * rank, LANES), jnp.float32),
        pltpu.VMEM((rank * rank, LANES), jnp.float32),
        pltpu.VMEM((rank, rank, LANES), jnp.float32),
        pltpu.VMEM((1, LANES), jnp.float32),
    ]


def branch_factors(gram, levels, width):
    leaves, rank, unused = gram.shape
    return pl.pallas_call(
        functools.partial(branch_body, rank=rank, levels=levels),
        in_specs=[vmem_spec],
        out_specs=[vmem_spec] * 4,
        out_shape=[
            jax.ShapeDtypeStruct((rank, rank, LANES), jnp.float32),
            jax.ShapeDtypeStruct((levels, rank, rank, LANES), jnp.float32),
            jax.ShapeDtypeStruct((rank, rank), jnp.float32),
            jax.ShapeDtypeStruct((rank * rank // width, width), jnp.float32),
        ],
        scratch_shapes=tree_scratch(rank),
        compiler_params=pltpu.CompilerParams(vmem_limit_bytes=vmem_bytes),
        name="branch_factors",
        cost_estimate=pl.CostEstimate(flops=10**6, bytes_accessed=10**4, transcendentals=0),
    )(gram.reshape(leaves * rank, rank))


def basis_body(inverse_ref, ratio_ref, top_ref, sketched_ref, weights_ref, basis_ref, natural, *, rank, levels):
    leaves = sketched_ref.shape[0]
    upper = [top_ref[...]]
    for level in range(levels - 2, -1, -1):
        stride = 2**level
        for c in range(rank):
            from_lanes(ratio_ref[level, c], natural, c, leaves, rank)
        fresh = []
        for node in range(leaves // stride):
            block = natural[node * stride * rank : (node * stride + 1) * rank, :]
            fresh.append(dot_exact(upper[node // 2], block))
        upper = fresh
    for r in range(rank):
        from_lanes(inverse_ref[r], natural, r, leaves, rank)
    for pair in range(leaves // 2):
        results = []
        for leaf in (2 * pair, 2 * pair + 1):
            block = sketched_ref[leaf]
            own = lax.dot_general(
                natural[leaf * rank : (leaf + 1) * rank, :], block, tn_dims,
                precision=highest, preferred_element_type=jnp.float32,
            )
            results.append(jnp.concatenate([dot_exact(upper[leaf], block), own], axis=0))
        both = jnp.concatenate(results, axis=1)
        weights_ref[:, pair * 2 * LEAF : (pair + 1) * 2 * LEAF] = both[:rank]
        basis_ref[:, pair * 2 * LEAF : (pair + 1) * 2 * LEAF] = both[rank:]


def bases(inverse, ratio, top, sketched):
    leaves, rank, unused = sketched.shape
    levels = ratio.shape[0]
    shape = jax.ShapeDtypeStruct((rank, leaves * LEAF), jnp.float32)
    return pl.pallas_call(
        functools.partial(basis_body, rank=rank, levels=levels),
        in_specs=[vmem_spec] * 4,
        out_specs=[vmem_spec] * 2,
        out_shape=[shape, shape],
        scratch_shapes=[pltpu.VMEM((leaves * rank, rank), jnp.float32)],
        compiler_params=pltpu.CompilerParams(vmem_limit_bytes=vmem_bytes),
        name="bases",
        cost_estimate=pl.CostEstimate(flops=10**9, bytes_accessed=10**6, transcendentals=0),
    )(inverse, ratio, top, sketched)


def top_body(side_ref, mine_ref, mirrored_ref, transfer_ref, paths_ref, children_ref, source, current, left, inverse, squared, child, lowest, nat_inverse, nat_child, *, rank, levels):
    half, packed_rows_each, width = mine_ref.shape
    nodes = half
    every = width // rank
    count = half * packed_rows_each
    for ref, side in ((mine_ref, side_ref[0]), (mirrored_ref, 1 - side_ref[0])):
        flat = ref[...].reshape(count, width)
        base = pl.multiple_of(side * (half * rank), half * rank)
        for part in range(every):
            children_ref[pl.ds(base + part, count, stride=every), :] = flat[:, part * rank : (part + 1) * rank]
    for node in range(nodes):
        both = children_ref[2 * node * rank : (2 * node + 2) * rank, :]
        source[node * rank : (node + 1) * rank, :] = lax.dot_general(
            both, both, tn_dims, precision=highest, preferred_element_type=jnp.float32
        )

    def finish(level):
        for r in range(rank):
            from_lanes(child[r], nat_child.at[level], r, nodes, rank)
            from_lanes(inverse[r * rank : (r + 1) * rank, :], nat_inverse.at[level], r, nodes, rank)

    run_levels(
        source, levels, nodes, current, left, inverse, squared, None, child, lowest, rank,
        lambda level: True, finish, unrolled=True,
    )
    offset = 0
    for level in range(levels):
        for node in range(nodes >> level):
            if level == 0:
                stacked = children_ref[2 * node * rank : (2 * node + 2) * rank, :]
            else:
                first = 2 * node << level - 1
                second = 2 * node + 1 << level - 1
                stacked = jnp.concatenate(
                    [
                        nat_child[level - 1, first * rank : (first + 1) * rank, :],
                        nat_child[level - 1, second * rank : (second + 1) * rank, :],
                    ],
                    axis=0,
                )
            at = (node << level) * rank
            transfer_ref[offset + node] = lax.dot_general(
                nat_inverse[level, at : at + rank, :], stacked, (((0,), (1,)), ((), ())),
                precision=highest, preferred_element_type=jnp.float32,
            )
        offset += nodes >> level
    above = [None]
    for level in range(levels - 1, -1, -1):
        offset -= nodes >> level
        fresh = []
        for node in range(nodes >> level):
            both = transfer_ref[offset + node]
            if above[0] is None:
                both = both.T
            else:
                both = lax.dot_general(
                    both, above[node], tn_dims, precision=highest, preferred_element_type=jnp.float32
                )
            fresh += [both[:rank], both[rank:]]
        above = fresh
    for branch in range(2 * nodes):
        paths_ref[branch * rank : (branch + 1) * rank, :] = above[branch]


def top_factors(side, mine, mirrored, rank):
    branches = 2 * mine.shape[0]
    levels = branches.bit_length() - 1
    nodes = branches // 2
    natural = pltpu.VMEM((levels, nodes * rank, rank), jnp.float32)
    return pl.pallas_call(
        functools.partial(top_body, rank=rank, levels=levels),
        in_specs=[pl.BlockSpec(memory_space=pltpu.SMEM), vmem_spec, vmem_spec],
        out_specs=[vmem_spec] * 2,
        out_shape=[
            jax.ShapeDtypeStruct((branches - 1, rank, 2 * rank), jnp.float32),
            jax.ShapeDtypeStruct((branches * rank, rank), jnp.float32),
        ],
        scratch_shapes=[
            pltpu.VMEM((branches * rank, rank), jnp.float32),
            pltpu.VMEM((nodes * rank, rank), jnp.float32),
        ]
        + tree_scratch(rank)
        + [natural, natural],
        compiler_params=pltpu.CompilerParams(vmem_limit_bytes=vmem_bytes),
        name="top_factors",
        cost_estimate=pl.CostEstimate(flops=10**10, bytes_accessed=10**7, transcendentals=0),
    )(side, mine, mirrored)


def exchange_sum(pieces, axis):
    count = pieces.shape[0]
    me = lax.axis_index(axis)
    mine = lax.dynamic_index_in_dim(pieces, me, 0, keepdims=False)
    for step in range(1, count):
        outgoing = lax.dynamic_index_in_dim(pieces, (me + step) % count, 0, keepdims=False)
        mine = mine + lax.ppermute(
            outgoing, axis, [(i, (i + step) % count) for i in range(count)]
        )
    return mine


def exchange_all(piece, axis):
    count = lax.axis_size(axis)
    me = lax.axis_index(axis)
    if count == 2:
        other = lax.ppermute(piece, axis, [(0, 1), (1, 0)])
        return jnp.stack([jnp.where(me == 0, piece, other), jnp.where(me == 0, other, piece)])
    result = jnp.zeros((count,) + piece.shape, piece.dtype)
    result = lax.dynamic_update_index_in_dim(result, piece, me, 0)
    for step in range(1, count):
        arrived = lax.ppermute(piece, axis, [(i, (i + step) % count) for i in range(count)])
        result = lax.dynamic_update_index_in_dim(result, arrived, (me - step) % count, 0)
    return result


def group_tables(far_slots, far_count, side, part):
    leaves = far_slots.shape[0]
    groups = -(-(leaves * (FAR // GROUP + 1) + BATCH - 1) // BATCH) * BATCH
    places = jnp.arange(FAR, dtype=jnp.int32)
    valid = places[None, :] < far_count[:, None]
    here = far_slots // part == side
    local = far_slots % part
    held = jnp.concatenate([valid & here, valid & ~here], axis=0)
    local = jnp.concatenate([local, local], axis=0)
    earlier = places[None, :] < places[:, None]
    rank = jnp.sum((held[:, None, :] & earlier[None]).astype(jnp.int32), axis=2)
    chosen = held[:, None, :] & (rank[:, None, :] == places[None, :, None])
    ordered = jnp.sum(jnp.where(chosen, local[:, None, :], 0), axis=2)
    lengths = jnp.sum(held.astype(jnp.int32), axis=1)
    lists = 2 * leaves
    per_list = (lengths + GROUP - 1) // GROUP
    before = jnp.arange(lists)[:, None] >= jnp.arange(lists)[None, :]
    ends = jnp.sum(jnp.where(before, per_list[None, :], 0), axis=1)
    own_total = ends[leaves - 1]
    total = ends[lists - 1]
    base = (own_total + BATCH - 1) // BATCH * BATCH
    ids = jnp.arange(groups, dtype=jnp.int32)
    at = jnp.where(ids < base, ids, ids - base + own_total)
    dead = ((ids < base) & (ids >= own_total)) | (at >= total)
    index = jnp.minimum(jnp.sum((ends[None, :] <= at[:, None]).astype(jnp.int32), axis=1), lists - 1)
    hit = index[:, None] == jnp.arange(lists)[None, :]
    start = jnp.sum(jnp.where(hit, (ends - per_list)[None, :], 0), axis=1)
    length = jnp.sum(jnp.where(hit, lengths[None, :], 0), axis=1)
    sub = at - start
    count = jnp.where(dead, 0, jnp.clip(length - GROUP * sub, 0, GROUP))
    first = jnp.clip(sub, 0, FAR // GROUP - 1)
    slots = ordered.reshape(lists * FAR // GROUP, GROUP)[index * (FAR // GROUP) + first]
    lift = jnp.where(ids < base, side, 1 - side) * part
    sizes = jnp.stack([base + total - own_total, own_total, base, total - own_total])
    return (
        sizes.astype(jnp.int32),
        (index % leaves).astype(jnp.int32),
        count.astype(jnp.int32),
        slots.reshape(-1).astype(jnp.int32),
        (slots + lift[:, None]).reshape(-1).astype(jnp.int32),
    )


def sketch_body(place_ref, sketch_ref, samples_ref, points_ref, mine_ref, other_ref):
    product = dot_exact(sketch_ref[...], samples_ref[...])
    rank, points_dev = product.shape
    quarter = rank // 4
    first = lax.broadcasted_iota(jnp.int32, (1, LANES), 1) < LEAF
    swap = place_ref[0] == 1
    leaves = points_dev // LEAF

    def interleave(low, high):
        even = jnp.where(first, low, pltpu.roll(high, LEAF, 1))
        odd = jnp.where(first, pltpu.roll(low, LEAF, 1), high)
        return even, odd

    for pair in range(leaves // 2):
        lanes = slice(pair * LANES, (pair + 1) * LANES)
        shares = []
        for share in range(2):
            base = 2 * quarter * share
            shares.append(
                interleave(product[base : base + quarter, lanes], product[base + quarter : base + 2 * quarter, lanes])
            )
        for member in range(2):
            at = (2 * pair + member) * quarter
            mine_ref[at : at + quarter, :] = jnp.where(swap, shares[1][member], shares[0][member])
            other_ref[at : at + quarter, :] = jnp.where(swap, shares[0][member], shares[1][member])
        x = points_ref[0:1, lanes]
        y = points_ref[1:2, lanes]
        z = points_ref[2:3, lanes]
        xy = interleave(x, y)
        zs = interleave(z, jnp.zeros_like(z))
        for member in range(2):
            at = leaves * quarter + (2 * pair + member) * 2
            mine_ref[at : at + 1, :] = xy[member]
            mine_ref[at + 1 : at + 2, :] = zs[member]
    other_ref[leaves * quarter :, :] = jnp.zeros((2 * leaves, LANES), jnp.float32)


def sketched_shares(place, sketch, samples, points):
    rank = sketch.shape[0]
    leaves = samples.shape[1] // LEAF
    return pl.pallas_call(
        sketch_body,
        in_specs=[pl.BlockSpec(memory_space=pltpu.SMEM)] + [vmem_spec] * 3,
        out_specs=[vmem_spec] * 2,
        out_shape=[
            jax.ShapeDtypeStruct((leaves * (rank // 4 + 2), LANES), jnp.float32),
            jax.ShapeDtypeStruct((leaves * (rank // 4 + 2), LANES), jnp.float32),
        ],
        compiler_params=pltpu.CompilerParams(vmem_limit_bytes=vmem_bytes),
        name="sketched_shares",
        cost_estimate=pl.CostEstimate(flops=10**6, bytes_accessed=10**4, transcendentals=0),
    )(place, sketch, samples, points)


def pack_body(asked_ref, side_ref, mine_ref, partner_ref, out_ref, *, cap, leaves):
    z_rows = mine_ref.shape[0] // leaves - 2
    side = side_ref[0]

    def one(peer, carry):
        for entry in range(2 * cap):
            leaf = asked_ref[peer, entry]
            here = side == entry // cap
            at = pl.ds(leaf * z_rows, z_rows)
            out_ref[peer, z_rows * entry : z_rows * (entry + 1), :] = jnp.where(
                here, mine_ref[at, :], partner_ref[at, :]
            )
            base = z_rows * 2 * cap + 2 * entry
            at = pl.ds(leaves * z_rows + leaf * 2, 2)
            out_ref[peer, base : base + 2, :] = jnp.where(here, mine_ref[at, :], partner_ref[at, :])
        return carry

    lax.fori_loop(0, out_ref.shape[0], one, 0)


def packed_rows(asked, side, mine, partner, cap, leaves):
    z_rows = mine.shape[0] // leaves - 2
    return pl.pallas_call(
        functools.partial(pack_body, cap=cap, leaves=leaves),
        in_specs=[pl.BlockSpec(memory_space=pltpu.SMEM)] * 2 + [vmem_spec] * 2,
        out_specs=vmem_spec,
        out_shape=jax.ShapeDtypeStruct((asked.shape[0], 2 * cap * (z_rows + 2), LANES), jnp.float32),
        compiler_params=pltpu.CompilerParams(vmem_limit_bytes=vmem_bytes),
        name="packed_rows",
    )(asked, side, mine, partner)


def payload_body(asked_ref, side_ref, rows_ref, child_ref, out_ref, *, cap):
    base = (1 - side_ref[0]) * cap

    def one(peer, carry):
        for entry in range(cap):
            out_ref[peer, LEAF * entry : LEAF * (entry + 1), :] = rows_ref[asked_ref[peer, base + entry]]
        out_ref[peer, LEAF * cap :, :] = child_ref[...]
        return carry

    lax.fori_loop(0, out_ref.shape[0], one, 0)


def payload_rows(asked, side, rows, child):
    half = asked.shape[0]
    cap = asked.shape[1] // 2
    return pl.pallas_call(
        functools.partial(payload_body, cap=cap),
        in_specs=[pl.BlockSpec(memory_space=pltpu.SMEM)] * 2 + [vmem_spec] * 2,
        out_specs=vmem_spec,
        out_shape=jax.ShapeDtypeStruct((half, cap * LEAF + child.shape[0], rows.shape[2]), jnp.float32),
        compiler_params=pltpu.CompilerParams(vmem_limit_bytes=vmem_bytes),
        name="payload_rows",
    )(asked, side, rows, child)


def two_rows(values, rows):
    leaves = values.shape[1]
    split = jnp.transpose(values.reshape(2, rows, leaves, LEAF), (2, 1, 0, 3))
    return split.reshape(leaves, rows, 2 * LEAF)


def on_device(points, samples, sketch, far_requests, far_slots, far_count, near_mask):
    samp_dev = samples.shape[0]
    leaves = samples.shape[1] // LEAF
    rank = sketch.shape[0]
    branches = lax.axis_size("leaf")
    columns = lax.axis_size("cols")
    cap = far_requests.shape[2]
    share = rank // columns
    me = lax.axis_index("leaf")
    column = lax.axis_index("cols")

    half = branches // 2
    side = me // half
    groups = [list(range(half)), list(range(half, branches))]
    mirror = [(i, (i + half) % branches) for i in range(branches)]
    side_ref = side.astype(jnp.int32).reshape(1)
    wanted = jnp.transpose(far_requests.reshape(2, half, cap), (1, 0, 2)).reshape(half, 2 * cap)
    if columns == 2:
        place = column.astype(jnp.int32).reshape(1)
        mine, other = sketched_shares(place, sketch, samples, points)
        mine = mine + lax.ppermute(other, "cols", [(0, 1), (1, 0)])
        wanted, mine = lax.optimization_barrier((wanted, mine))
    else:
        z_part = jnp.dot(sketch, samples, precision=highest)
        z_mine = exchange_sum(z_part.reshape(columns, share, leaves * LEAF), "cols")
        z_rows = two_rows(z_mine.reshape(share, leaves, LEAF), share // 2)
        planes = points.reshape(3, leaves, LEAF)
        c_rows = two_rows(
            jnp.concatenate([planes[0:1], planes[2:3], planes[1:2], jnp.zeros_like(planes[0:1])], axis=0), 2
        )
        mine = jnp.concatenate([z_rows.reshape(-1, LANES), c_rows.reshape(-1, LANES)], axis=0)

    partner = lax.ppermute(mine, "leaf", mirror)
    asked = lax.all_to_all(
        wanted, "leaf", split_axis=0, concat_axis=0, axis_index_groups=groups, tiled=True
    )
    coords = jnp.transpose(points.reshape(3, leaves, LEAF), (1, 0, 2))
    targets = jnp.transpose(coords, (0, 2, 1))
    rows = jnp.transpose(samples.reshape(samp_dev, leaves, LEAF), (1, 2, 0))

    asked, rows, targets = lax.optimization_barrier((asked, rows, targets))
    small_sent = packed_rows(asked, side_ref, mine, partner, cap, leaves)
    small_got = lax.all_to_all(
        small_sent, "leaf", split_axis=0, concat_axis=0, axis_index_groups=groups, tiled=True
    )

    rows_out, unused = lax.optimization_barrier((rows, small_sent))
    partner_rows = lax.ppermute(rows_out, "leaf", mirror)

    forward = [(i, i + 1) for i in range(branches - 1)]
    backward = [(target, source) for source, target in forward]
    width = max(samp_dev, LEAF)

    def edge(first):
        samples_edge = jnp.transpose(lax.slice_in_dim(samples, first, first + LEAF, axis=1))
        points_edge = lax.slice_in_dim(points, first, first + LEAF, axis=1)
        return jnp.concatenate(
            [
                jnp.pad(samples_edge, ((0, 0), (0, width - samp_dev))),
                jnp.pad(points_edge, ((0, 5), (0, width - LEAF))),
            ],
            axis=0,
        )

    last, first, unused = lax.optimization_barrier((edge((leaves - 1) * LEAF), edge(0), small_sent))
    low_edge = lax.ppermute(last, "leaf", forward)
    high_edge = lax.ppermute(first, "leaf", backward)

    own_asked = lax.dynamic_slice_in_dim(asked, side * cap, cap, axis=1)
    own_sent = rows_out[own_asked.reshape(-1)].reshape(half, cap, LEAF, samp_dev)
    own_sent, low_edge, high_edge, far_slots, far_count = lax.optimization_barrier(
        (own_sent, low_edge, high_edge, far_slots, far_count)
    )
    sizes, group_leaf, group_count, group_slots, group_places = group_tables(
        far_slots, far_count, side, half * cap
    )
    own_got = lax.all_to_all(
        own_sent, "leaf", split_axis=0, concat_axis=0, axis_index_groups=groups, tiled=True
    )
    own_got = own_got.reshape(half * cap, LEAF, samp_dev)

    if columns == 2:
        small_other = lax.ppermute(small_got, "cols", [(0, 1), (1, 0)])
    else:
        z_count = cap * share
        z_all = exchange_all(small_got[:, :z_count], "cols")
        z_all = z_all.reshape(columns, half, 2 * cap, share // 2, 2, LEAF)
        z_all = jnp.transpose(z_all, (1, 2, 0, 4, 3, 5)).reshape(half, 2 * cap, 2, 2, rank // 4, LEAF)
        z_all = jnp.transpose(z_all, (2, 0, 1, 4, 3, 5)).reshape(2, half, cap * rank // 2, LANES)
        c_got = small_got[:, z_count:]
        small_got = jnp.concatenate([z_all[0], c_got], axis=1)
        small_other = jnp.concatenate([z_all[1], c_got], axis=1)
        place = jnp.zeros((1,), jnp.int32)

    blocks, sketched, gram = kernel_blocks(
        sizes, group_leaf, group_count, group_places, place, small_got, small_other, targets, rank, cap
    )

    levels = leaves.bit_length()
    inverse, ratio, top_inverse, own_child = branch_factors(gram, levels, min(samp_dev, LANES))
    own_child, own_got, partner_rows = lax.optimization_barrier((own_child, own_got, partner_rows))
    payload = payload_rows(asked, side_ref, partner_rows, own_child)
    arrived = lax.all_to_all(
        payload, "leaf", split_axis=0, concat_axis=0, axis_index_groups=groups, tiled=True
    )
    ratio, low_edge, high_edge, unused = lax.optimization_barrier((ratio, low_edge, high_edge, payload))
    weights, leaf_basis = bases(inverse, ratio, top_inverse, sketched)

    rows_low, rows_high = low_edge[:LEAF, :samp_dev], high_edge[:LEAF, :samp_dev]
    coords_low, coords_high = low_edge[LEAF : LEAF + 3, :LEAF], high_edge[LEAF : LEAF + 3, :LEAF]
    near_rows = jnp.concatenate(
        [rows_low[None], rows, rows_high[None], jnp.zeros_like(rows_low)[None]], axis=0
    )
    near_coords = jnp.concatenate(
        [coords_low[None], coords, coords_high[None], jnp.zeros_like(coords_low)[None]], axis=0
    )
    near_coords = jnp.pad(near_coords, ((0, 0), (0, 5), (0, 0)))
    near_coords = jnp.concatenate([near_coords, near_coords], axis=2)
    near_sample = near_products(near_mask.reshape(-1), near_rows, near_coords, targets)


    children = arrived[:, cap * LEAF :]
    mirrored = lax.ppermute(children, "leaf", mirror)
    own_got, unused = lax.optimization_barrier((own_got, payload))
    far_start = far_own(sizes, group_leaf, group_slots, own_got, blocks, leaves)
    weights, near_sample = lax.optimization_barrier((weights, near_sample))
    far_sample, branch_samples, copies = far_partner(
        sizes, group_leaf, group_slots, arrived, blocks, far_start, weights, cap, branches
    )
    everyone = lax.all_to_all(copies, "leaf", split_axis=0, concat_axis=0, tiled=True)
    children, mirrored, unused = lax.optimization_barrier((children, mirrored, branch_samples))
    transfer_t, paths = top_factors(side_ref, children, mirrored, rank)
    top_transfer = jnp.swapaxes(transfer_t, 1, 2)
    root_sample = lax.dot_general(
        paths, everyone.reshape(branches * rank, samp_dev), tn_dims, precision=highest
    )
    return (far_sample, near_sample, leaf_basis, branch_samples, top_transfer, root_sample)


def solution(mesh):
    return jax.shard_map(
        on_device,
        mesh=mesh,
        in_specs=(
            P(None, "leaf"),
            P("cols", "leaf"),
            P(None, "cols"),
            P("leaf", None, None),
            P("leaf", None),
            P("leaf"),
            P("leaf", None),
        ),
        out_specs=(
            P("cols", "leaf"),
            P("cols", "leaf"),
            P(None, "leaf"),
            P("leaf", "cols"),
            P(),
            P(None, "cols"),
        ),
        check_vma=False,
    )
```

```python
import functools
import math

import jax
import jax.numpy as jnp
import numpy as np
from jax import lax
from jax.experimental import pallas as pl
from jax.experimental.pallas import tpu as pltpu
from jax.sharding import PartitionSpec as P

LEAF = 64
FAR = 16
GROUP = 4
BATCH = 16
LANES = 128
SUB = 8

length_scale = 0.3
shift_share = 0.05
highest = lax.Precision.HIGHEST
exponent_scale = -math.log2(math.e) / length_scale
vmem_bytes = 56 * 1024 * 1024

nt_dims = (((1,), (1,)), ((), ()))
tn_dims = (((0,), (0,)), ((), ()))


def halves(value):
    high = value.astype(jnp.bfloat16)
    low = (value - high.astype(jnp.float32)).astype(jnp.bfloat16)
    return high, low


def dot(a, b):
    return jnp.dot(a, b, preferred_element_type=jnp.float32)


def dot_exact(a, b):
    return jnp.dot(a, b, precision=highest, preferred_element_type=jnp.float32)


def dot_exact_nt(a, b):
    return lax.dot_general(a, b, nt_dims, precision=highest, preferred_element_type=jnp.float32)


def stacked_halves(value, axis):
    return jnp.concatenate(halves(value), axis=axis)


def quadrants(product):
    rows, columns = product.shape[0] // 2, product.shape[1] // 2
    top = product[:rows, :columns] + product[:rows, columns:]
    return top + (product[rows:, :columns] + product[rows:, columns:])


def dot_nt(a, b):
    return lax.dot_general(a, b, nt_dims, preferred_element_type=jnp.float32)


def kernel_half(source_rows, target, lane, valid):
    total = None
    for axis in range(3):
        difference = source_rows[axis : axis + 1, :] - target[:, axis : axis + 1]
        square = difference * difference
        total = square if total is None else total + square
    distance = total * lax.rsqrt(jnp.maximum(total, 1e-30))
    values = jnp.exp2(distance * exponent_scale)
    return jnp.where(lane < valid, values, 0.0)


def blocks_body(
    total_ref, leaf_ref, count_ref, slot_ref, place_ref,
    own_ref, other_ref, target_ref,
    both_ref, sketched_ref, gram_ref,
    packed,
    *, rank, cap,
):
    step = pl.program_id(0)
    lane = lax.broadcasted_iota(jnp.int32, (1, LANES), 1)
    first = lane < LEAF

    @pl.when(step == 0)
    def _():
        sketched_ref[...] = jnp.zeros_like(sketched_ref)
        quarter = rank // 4
        slots = packed.shape[0]
        own_at = pl.multiple_of(place_ref[0] * 2 * quarter, quarter)
        other_at = pl.multiple_of((1 - place_ref[0]) * 2 * quarter, quarter)

        def unpack(peer, carry):
            for entry in range(2 * cap):
                slot = (entry // cap) * (slots // 2) + peer * cap + entry % cap
                at = entry * quarter
                for ref, base in ((own_ref, own_at), (other_ref, other_at)):
                    value = ref[peer, at : at + quarter, :]
                    turned = pltpu.roll(value, LEAF, 1)
                    packed[slot, pl.ds(base, quarter), :] = jnp.where(first, value, turned)
                    packed[slot, pl.ds(base + quarter, quarter), :] = jnp.where(first, turned, value)
                at = 2 * cap * quarter + 2 * entry
                value = own_ref[peer, at : at + 2, :]
                turned = pltpu.roll(value, LEAF, 1)
                packed[slot, rank : rank + 1, :] = jnp.where(first, value, turned)[0:1]
                packed[slot, rank + 1 : rank + 2, :] = jnp.where(first, turned, value)[0:1]
                packed[slot, rank + 2 : rank + 3, :] = jnp.where(first, value, turned)[1:2]
            return carry

        lax.fori_loop(0, slots // (2 * cap), unpack, 0)

    @pl.when(step * BATCH < total_ref[0])
    def _():
        for member in range(BATCH):
            group = step * BATCH + member
            leaf = leaf_ref[group]
            count = count_ref[group]
            slots = [slot_ref[group * GROUP + e] for e in range(GROUP)]
            target = target_ref[leaf]
            z_parts = []
            for half in range(GROUP // 2):
                left = packed[slots[2 * half]]
                right = packed[slots[2 * half + 1]]
                both = jnp.where(first, left, right)
                values = kernel_half(both[rank : rank + 3], target, lane, (count - 2 * half) * LEAF)
                both_ref[member, :, half * LANES : (half + 1) * LANES] = stacked_halves(values, 0)
                z_parts.append(both[:rank])
            z_both = stacked_halves(jnp.concatenate(z_parts, axis=1), 0)
            by_high = dot_nt(z_both, both_ref[member, :LEAF])
            by_low = dot_nt(z_both[:rank], both_ref[member, LEAF:])
            sketched_ref[leaf] += by_high[:rank] + (by_high[rank:] + by_low)

    @pl.when(step == pl.num_programs(0) - 1)
    def _():
        for leaf in range(gram_ref.shape[0]):
            block = sketched_ref[leaf]
            gram_ref[leaf] = dot_exact_nt(block, block)


def kernel_blocks(total, group_leaf, group_count, group_slots, place, own, other, targets, rank, cap):
    leaves = targets.shape[0]
    groups = group_leaf.shape[0]
    slots = own.shape[0] * 2 * cap
    steps = groups // BATCH

    def block_index(step, total_ref, *unused):
        last = (total_ref[0] - 1) // BATCH
        return (jnp.minimum(step, last), 0, 0)

    whole = lambda *unused: (0, 0, 0)
    once = pl.Buffered(1)
    return pl.pallas_call(
        functools.partial(blocks_body, rank=rank, cap=cap),
        grid_spec=pltpu.PrefetchScalarGridSpec(
            num_scalar_prefetch=5,
            grid=(steps,),
            in_specs=[
                pl.BlockSpec(own.shape, whole, pipeline_mode=once),
                pl.BlockSpec(other.shape, whole, pipeline_mode=once),
                pl.BlockSpec(targets.shape, whole, pipeline_mode=once),
            ],
            out_specs=[
                pl.BlockSpec((BATCH, 2 * LEAF, GROUP * LEAF), block_index),
                pl.BlockSpec((leaves, rank, LEAF), whole),
                pl.BlockSpec((leaves, rank, rank), whole),
            ],
            scratch_shapes=[pltpu.VMEM((slots, rank + SUB, LANES), jnp.float32)],
        ),
        out_shape=[
            jax.ShapeDtypeStruct((groups, 2 * LEAF, GROUP * LEAF), jnp.bfloat16),
            jax.ShapeDtypeStruct((leaves, rank, LEAF), jnp.float32),
            jax.ShapeDtypeStruct((leaves, rank, rank), jnp.float32),
        ],
        compiler_params=pltpu.CompilerParams(vmem_limit_bytes=vmem_bytes),
        name="kernel_blocks",
        cost_estimate=pl.CostEstimate(
            flops=10**6, bytes_accessed=10**4, transcendentals=0
        ),
    )(total, group_leaf, group_count, group_slots, place, own, other, targets)


def far_groups(sizes_ref, leaf_ref, slot_ref, first_batch, live, blocks_ref, s_both, acc):
    step = pl.program_id(0)

    @pl.when(step * BATCH < live)
    def _():
        for member in range(BATCH):
            group = first_batch * BATCH + step * BATCH + member
            leaf = leaf_ref[group]
            slots = [slot_ref[group * GROUP + e] for e in range(GROUP)]
            rows = jnp.concatenate([s_both[slot] for slot in slots], axis=0)
            acc[leaf] += quadrants(dot(blocks_ref[member], rows))


def far_own_body(sizes_ref, leaf_ref, slot_ref, own_ref, blocks_ref, acc_ref, s_both):
    @pl.when(pl.program_id(0) == 0)
    def _():
        acc_ref[...] = jnp.zeros_like(acc_ref)

        def split(slot, carry):
            s_both[slot] = stacked_halves(own_ref[slot], 1)
            return carry

        lax.fori_loop(0, own_ref.shape[0], split, 0, unroll=8)

    far_groups(sizes_ref, leaf_ref, slot_ref, 0, sizes_ref[1], blocks_ref, s_both, acc_ref)


def far_partner_body(
    sizes_ref, leaf_ref, slot_ref,
    partner_ref, blocks_ref, start_ref, weights_ref,
    out_ref, projected_ref, copies_ref,
    s_both, acc,
    *, cap,
):
    step = pl.program_id(0)
    samp_dev = partner_ref.shape[2]

    @pl.when(step == 0)
    def _():
        acc[...] = start_ref[...]

        def split(peer, carry):
            for entry in range(cap):
                s_both[peer * cap + entry] = stacked_halves(
                    partner_ref[peer, LEAF * entry : LEAF * (entry + 1), :], 1
                )
            return carry

        lax.fori_loop(0, partner_ref.shape[0], split, 0)

    far_groups(
        sizes_ref, leaf_ref, slot_ref, sizes_ref[2] // BATCH, sizes_ref[3], blocks_ref, s_both, acc
    )

    @pl.when(step == pl.num_programs(0) - 1)
    def _():
        leaves = acc.shape[0]
        rows = acc[...].reshape(leaves * LEAF, samp_dev)
        projected = dot_exact(weights_ref[...], rows)
        projected_ref[...] = projected
        for branch in range(copies_ref.shape[0]):
            copies_ref[branch] = projected
        for pair in range(leaves // 2):
            block = acc[2 * pair : 2 * pair + 2].reshape(2 * LEAF, samp_dev)
            out_ref[:, 2 * pair * LEAF : 2 * (pair + 1) * LEAF] = block.T


def far_own(sizes, group_leaf, group_slots, own, blocks, leaves):
    part, unused, samp_dev = own.shape
    steps = leaves * FAR // GROUP // BATCH

    def block_index(step, sizes_ref, *unused):
        last = jnp.maximum(sizes_ref[1] - 1, 0) // BATCH
        return (jnp.minimum(step, last), 0, 0)

    whole = lambda *unused: (0, 0, 0)
    return pl.pallas_call(
        far_own_body,
        grid_spec=pltpu.PrefetchScalarGridSpec(
            num_scalar_prefetch=3,
            grid=(steps,),
            in_specs=[
                pl.BlockSpec(own.shape, whole, pipeline_mode=pl.Buffered(1)),
                pl.BlockSpec((BATCH, 2 * LEAF, GROUP * LEAF), block_index),
            ],
            out_specs=pl.BlockSpec((leaves, LEAF, samp_dev), whole),
            scratch_shapes=[pltpu.VMEM((part, LEAF, 2 * samp_dev), jnp.bfloat16)],
        ),
        out_shape=jax.ShapeDtypeStruct((leaves, LEAF, samp_dev), jnp.float32),
        compiler_params=pltpu.CompilerParams(vmem_limit_bytes=vmem_bytes),
        name="far_own",
        cost_estimate=pl.CostEstimate(flops=10**9, bytes_accessed=10**6, transcendentals=0),
    )(sizes, group_leaf, group_slots, own, blocks)


def far_partner(sizes, group_leaf, group_slots, partner, blocks, start, weights, cap, branches):
    leaves, unused, samp_dev = start.shape
    part = partner.shape[0] * cap
    points_dev = leaves * LEAF
    rank = weights.shape[0]
    steps = leaves * FAR // GROUP // BATCH

    def block_index(step, sizes_ref, *unused):
        last = jnp.maximum(sizes_ref[3] - 1, 0) // BATCH
        most = blocks.shape[0] // BATCH - 1
        return (jnp.minimum(sizes_ref[2] // BATCH + jnp.minimum(step, last), most), 0, 0)

    flat = lambda *unused: (0, 0)
    whole = lambda *unused: (0, 0, 0)
    once = pl.Buffered(1)
    return pl.pallas_call(
        functools.partial(far_partner_body, cap=cap),
        grid_spec=pltpu.PrefetchScalarGridSpec(
            num_scalar_prefetch=3,
            grid=(steps,),
            in_specs=[
                pl.BlockSpec(partner.shape, whole, pipeline_mode=once),
                pl.BlockSpec((BATCH, 2 * LEAF, GROUP * LEAF), block_index),
                pl.BlockSpec(start.shape, whole, pipeline_mode=once),
                pl.BlockSpec(weights.shape, flat, pipeline_mode=once),
            ],
            out_specs=[
                pl.BlockSpec((samp_dev, points_dev), flat),
                pl.BlockSpec((rank, samp_dev), flat),
                pl.BlockSpec((branches, rank, samp_dev), whole),
            ],
            scratch_shapes=[
                pltpu.VMEM((part, LEAF, 2 * samp_dev), jnp.bfloat16),
                pltpu.VMEM((leaves, LEAF, samp_dev), jnp.float32),
            ],
        ),
        out_shape=[
            jax.ShapeDtypeStruct((samp_dev, points_dev), jnp.float32),
            jax.ShapeDtypeStruct((rank, samp_dev), jnp.float32),
            jax.ShapeDtypeStruct((branches, rank, samp_dev), jnp.float32),
        ],
        compiler_params=pltpu.CompilerParams(vmem_limit_bytes=vmem_bytes),
        name="far_partner",
        cost_estimate=pl.CostEstimate(flops=10**10, bytes_accessed=10**7, transcendentals=0),
    )(sizes, group_leaf, group_slots, partner, blocks, start, weights)


NEAR_LEAVES = 8


def near_body(mask_ref, rows_ref, coords_ref, target_ref, out_ref):
    step = pl.program_id(0)
    samp_dev = rows_ref.shape[2]
    lane = lax.broadcasted_iota(jnp.int32, (1, LANES), 1)
    first = lane < LEAF
    for pair in range(NEAR_LEAVES // 2):
        results = []
        for member in range(2):
            leaf = step * NEAR_LEAVES + 2 * pair + member
            target = target_ref[leaf]
            k_parts = []
            for half in range(2):
                both = jnp.where(first, coords_ref[leaf + 2 * half], coords_ref[leaf + 2 * half + 1])
                values = kernel_half(both, target, lane, LANES)
                left = mask_ref[leaf * 3 + 2 * half].astype(jnp.float32)
                if half == 0:
                    right = mask_ref[leaf * 3 + 1].astype(jnp.float32)
                else:
                    right = jnp.float32(0.0)
                k_parts.append(stacked_halves(values * jnp.where(first, left, right), 0))
            rows = rows_ref[pl.ds(leaf, 4)].reshape(4 * LEAF, samp_dev)
            product = dot(jnp.concatenate(k_parts, axis=1), stacked_halves(rows, 1))
            results.append(quadrants(product))
        block = jnp.concatenate(results, axis=0)
        out_ref[:, 2 * pair * LEAF : 2 * (pair + 1) * LEAF] = block.T


def near_products(mask, rows, coords, targets):
    leaves = targets.shape[0]
    samp_dev = rows.shape[2]
    whole = lambda *unused: (0, 0, 0)
    return pl.pallas_call(
        near_body,
        grid_spec=pltpu.PrefetchScalarGridSpec(
            num_scalar_prefetch=1,
            grid=(leaves // NEAR_LEAVES,),
            in_specs=[
                pl.BlockSpec(rows.shape, whole),
                pl.BlockSpec(coords.shape, whole),
                pl.BlockSpec(targets.shape, whole),
            ],
            out_specs=pl.BlockSpec((samp_dev, NEAR_LEAVES * LEAF), lambda step, *unused: (0, step)),
        ),
        out_shape=jax.ShapeDtypeStruct((samp_dev, leaves * LEAF), jnp.float32),
        compiler_params=pltpu.CompilerParams(vmem_limit_bytes=vmem_bytes),
        name="near_products",
        cost_estimate=pl.CostEstimate(
            flops=10**9, bytes_accessed=10**6, transcendentals=0
        ),
    )(mask, rows, coords, targets)


def to_lanes(source, target, rank):
    nodes = source.shape[0] // rank
    target[...] = jnp.zeros_like(target)
    for r in range(rank):
        target[r, :, 0:nodes] = source[pl.ds(r, nodes, stride=rank), :].T


def from_lanes(columns, target, r, nodes, rank):
    target[pl.ds(r, nodes, stride=rank), :] = columns.T[0:nodes]


def eliminate(current, left, inverse, level, rank):
    tiles = rank // SUB
    row = lax.broadcasted_iota(jnp.int32, (SUB, LANES), 0)
    diagonal = [current[j, j : j + 1, :] for j in range(rank)]
    while len(diagonal) > 1:
        diagonal = [diagonal[i] + diagonal[i + 1] for i in range(0, len(diagonal), 2)]
    share = shift_share * diagonal[0] / rank
    shift = share + 1e-06
    a = [
        {t: current[j, SUB * t : SUB * (t + 1), :] for t in range(j // SUB, tiles)}
        for j in range(rank)
    ]
    for j in range(rank):
        a[j][j // SUB] = a[j][j // SUB] + jnp.where(row == j % SUB, shift, 0.0)
    m = []
    scales = []
    for k in range(rank):
        tk, rk = k // SUB, k % SUB
        root = lax.rsqrt(a[k][tk][rk : rk + 1, :])
        scales.append(root)
        reciprocal = root * root
        column = {t: a[k][t] * reciprocal for t in range(tk, tiles)}
        column[tk] = jnp.where(row > rk, column[tk], 0.0)
        for j in range(k + 1, rank):
            factor = a[k][j // SUB][j % SUB : j % SUB + 1, :]
            for t in range(j // SUB, tiles):
                a[j][t] = a[j][t] - column[t] * factor
        for c in range(k):
            factor = m[c][tk][rk : rk + 1, :]
            for t in range(tk, tiles):
                m[c][t] = m[c][t] - column[t] * factor
        fresh = {t: -column[t] for t in range(tk, tiles)}
        fresh[tk] = jnp.where(row == rk, 1.0, fresh[tk])
        m.append(fresh)
        if left is not None:
            for t in range(tiles):
                if t < tk:
                    value = jnp.zeros((SUB, LANES), jnp.float32)
                else:
                    value = a[k][t] * root
                if t == tk:
                    value = jnp.where(row >= rk, value, 0.0)
                left[k, SUB * t : SUB * (t + 1), :] = value
    for t in range(tiles):
        scale = jnp.concatenate(scales[SUB * t : SUB * (t + 1)], axis=0)
        for c in range(rank):
            value = m[c][t] * scale if t >= c // SUB else jnp.zeros((SUB, LANES), jnp.float32)
            inverse[c * rank + SUB * t : c * rank + SUB * (t + 1), :] = value
    return shift, share


def inverse_row(inverse, r, t, rank):
    return inverse[pl.ds(SUB * t * rank + r, SUB, stride=rank), :]


def pair_up(value, level):
    reach = LANES - (1 << level if isinstance(level, int) else lax.shift_left(1, level))
    return value + pltpu.roll(value, reach, 1)


def when(condition):
    if isinstance(condition, bool):
        return lambda body: body() if condition else None
    return pl.when(condition)


def level_fast(level, levels, current, left, inverse, squared, ratio, child, lowest, rank, child_at):
    tiles = rank // SUB
    row = lax.broadcasted_iota(jnp.int32, (SUB, LANES), 0)
    shift, share = eliminate(current, left, inverse, level, rank)
    lowest[...] = jnp.minimum(lowest[...], share)

    if child is not None:
        @when(child_at(level))
        def _():
            for r in range(rank):
                for t in range(tiles):
                    value = left[r, SUB * t : SUB * (t + 1), :]
                    if t <= r // SUB:
                        value = value - shift * inverse_row(inverse, r, t, rank)
                    child[r, SUB * t : SUB * (t + 1), :] = value

    @when(level < levels - 1)
    def _():
        for block in range(tiles):
            sums = [[None] * tiles for _ in range(SUB)]
            for r in range(SUB * block, rank):
                parts = [inverse_row(inverse, r, t, rank) for t in range(block, r // SUB + 1)]
                for q in range(SUB):
                    if SUB * block + q > r:
                        continue
                    factor = parts[0][q : q + 1, :]
                    for t in range(block, r // SUB + 1):
                        term = parts[t - block] * factor
                        sums[q][t] = term if sums[q][t] is None else sums[q][t] + term
            for q in range(SUB):
                at = (SUB * block + q) * rank
                for t in range(block, tiles):
                    squared[at + SUB * t : at + SUB * (t + 1), :] = sums[q][t]

        for q in range(rank):
            for t in range(tiles):
                if t >= q // SUB:
                    value = squared[q * rank + SUB * t : q * rank + SUB * (t + 1), :]
                else:
                    value = squared[pl.ds(SUB * t * rank + q, SUB, stride=rank), :]
                value = -shift * value
                if t == q // SUB:
                    value = value + jnp.where(row == q % SUB, 1.0, 0.0)
                if ratio is not None:
                    ratio[level, q, SUB * t : SUB * (t + 1), :] = value
                here = current[q, SUB * t : SUB * (t + 1), :] - shift * value
                current[q, SUB * t : SUB * (t + 1), :] = pair_up(here, level)


def level_plain(level, levels, current, left, inverse, squared, ratio, child, lowest, rank, child_at):
    tiles = rank // SUB
    eliminate(current, left, inverse, level, rank)

    def products(out, count, left_of, right_of):
        def block_step(block, carry):
            offset = pl.multiple_of(block * SUB, SUB)
            sums = [[None] * tiles for _ in range(SUB)]
            for r in range(count):
                parts = [left_of(r, t) for t in range(tiles)]
                heads = right_of(r, offset)
                for q in range(SUB):
                    for t in range(tiles):
                        term = parts[t] * heads[q : q + 1, :]
                        sums[q][t] = term if sums[q][t] is None else sums[q][t] + term
            for q in range(SUB):
                for t in range(tiles):
                    out(offset + q, t, sums[q][t])
            return carry

        lax.fori_loop(0, tiles, block_step, 0)

    def tile(t):
        return slice(SUB * t, SUB * (t + 1))

    def put_child(r, t, value):
        squared[pl.ds(pl.multiple_of(r * rank + SUB * t, SUB), SUB), :] = value

    products(
        put_child, rank,
        lambda k, t: current[k, tile(t), :],
        lambda k, offset: inverse[pl.ds(pl.multiple_of(k * rank + offset, SUB), SUB), :],
    )
    if child is not None:
        @when(child_at(level))
        def _():
            for r in range(rank):
                for t in range(tiles):
                    child[r, tile(t), :] = squared[r * rank + SUB * t : r * rank + SUB * (t + 1), :]

    def child_part(r, t):
        return squared[r * rank + SUB * t : r * rank + SUB * (t + 1), :]

    def put_current(q, t, value):
        current[q, tile(t), :] = pair_up(value, level)

    if ratio is not None:
        def put_ratio(c, t, value):
            ratio[level, c, tile(t), :] = value

        def inverse_head(r, offset):
            return inverse[pl.ds(offset * rank + r, SUB, stride=rank), :]

        products(put_ratio, rank, child_part, inverse_head)
    products(
        put_current, rank, child_part,
        lambda r, offset: squared[pl.ds(pl.multiple_of(r * rank + offset, SUB), SUB), :],
    )


def run_levels(source, levels, nodes, current, left, inverse, squared, ratio, child, lowest, rank, child_at, finish, unrolled=False):
    lowest[...] = jnp.full((1, LANES), 1.0, jnp.float32)

    def sweep(level_step):
        to_lanes(source, current, rank)

        def body(level, carry):
            level_step(level, levels, current, left, inverse, squared, ratio, child, lowest, rank, child_at)
            finish(level)
            return carry

        if unrolled and level_step is level_fast:
            for level in range(levels):
                body(level, 0)
        else:
            lax.fori_loop(0, levels, body, 0)

    sweep(level_fast)
    lane = lax.broadcasted_iota(jnp.int32, (1, LANES), 1)
    least = jnp.min(jnp.where(lane < nodes, lowest[...], 1.0))

    @pl.when(least < 2e-06)
    def _():
        sweep(level_plain)


def branch_body(gram_ref, inverse_ref, ratio_ref, top_ref, child_ref, current, left, inverse, squared, child, lowest, *, rank, levels):
    nodes = gram_ref.shape[0] // rank

    def finish(level):
        @pl.when(level == 0)
        def _():
            for c in range(rank):
                inverse_ref[c] = inverse[c * rank : (c + 1) * rank, :]

        @pl.when(level == levels - 1)
        def _():
            for r in range(rank):
                width = child_ref.shape[1]
                at = r * rank
                child_ref[at // width : at // width + 1, at % width : at % width + rank] = child[r].T[0:1, :]
                top_ref[r : r + 1, :] = jnp.concatenate(
                    [inverse_row(inverse, r, t, rank) for t in range(rank // SUB)], axis=0
                ).T[0:1, :]

    run_levels(
        gram_ref, levels, nodes, current, left, inverse, squared, ratio_ref, child, lowest, rank,
        lambda level: level == levels - 1, finish,
    )


vmem_spec = pl.BlockSpec(memory_space=pltpu.VMEM)


def tree_scratch(rank):
    return [
        pltpu.VMEM((rank, rank, LANES), jnp.float32),
        pltpu.VMEM((rank, rank, LANES), jnp.float32),
        pltpu.VMEM((rank * rank, LANES), jnp.float32),
        pltpu.VMEM((rank * rank, LANES), jnp.float32),
        pltpu.VMEM((rank, rank, LANES), jnp.float32),
        pltpu.VMEM((1, LANES), jnp.float32),
    ]


def branch_factors(gram, levels, width):
    leaves, rank, unused = gram.shape
    return pl.pallas_call(
        functools.partial(branch_body, rank=rank, levels=levels),
        in_specs=[vmem_spec],
        out_specs=[vmem_spec] * 4,
        out_shape=[
            jax.ShapeDtypeStruct((rank, rank, LANES), jnp.float32),
            jax.ShapeDtypeStruct((levels, rank, rank, LANES), jnp.float32),
            jax.ShapeDtypeStruct((rank, rank), jnp.float32),
            jax.ShapeDtypeStruct((rank * rank // width, width), jnp.float32),
        ],
        scratch_shapes=tree_scratch(rank),
        compiler_params=pltpu.CompilerParams(vmem_limit_bytes=vmem_bytes),
        name="branch_factors",
        cost_estimate=pl.CostEstimate(flops=10**6, bytes_accessed=10**4, transcendentals=0),
    )(gram.reshape(leaves * rank, rank))


def basis_body(inverse_ref, ratio_ref, top_ref, sketched_ref, weights_ref, basis_ref, natural, *, rank, levels):
    leaves = sketched_ref.shape[0]
    upper = [top_ref[...]]
    for level in range(levels - 2, -1, -1):
        stride = 2**level
        for c in range(rank):
            from_lanes(ratio_ref[level, c], natural, c, leaves, rank)
        fresh = []
        for node in range(leaves // stride):
            block = natural[node * stride * rank : (node * stride + 1) * rank, :]
            fresh.append(dot_exact(upper[node // 2], block))
        upper = fresh
    for r in range(rank):
        from_lanes(inverse_ref[r], natural, r, leaves, rank)
    for pair in range(leaves // 2):
        results = []
        for leaf in (2 * pair, 2 * pair + 1):
            block = sketched_ref[leaf]
            own = lax.dot_general(
                natural[leaf * rank : (leaf + 1) * rank, :], block, tn_dims,
                precision=highest, preferred_element_type=jnp.float32,
            )
            results.append(jnp.concatenate([dot_exact(upper[leaf], block), own], axis=0))
        both = jnp.concatenate(results, axis=1)
        weights_ref[:, pair * 2 * LEAF : (pair + 1) * 2 * LEAF] = both[:rank]
        basis_ref[:, pair * 2 * LEAF : (pair + 1) * 2 * LEAF] = both[rank:]


def bases(inverse, ratio, top, sketched):
    leaves, rank, unused = sketched.shape
    levels = ratio.shape[0]
    shape = jax.ShapeDtypeStruct((rank, leaves * LEAF), jnp.float32)
    return pl.pallas_call(
        functools.partial(basis_body, rank=rank, levels=levels),
        in_specs=[vmem_spec] * 4,
        out_specs=[vmem_spec] * 2,
        out_shape=[shape, shape],
        scratch_shapes=[pltpu.VMEM((leaves * rank, rank), jnp.float32)],
        compiler_params=pltpu.CompilerParams(vmem_limit_bytes=vmem_bytes),
        name="bases",
        cost_estimate=pl.CostEstimate(flops=10**9, bytes_accessed=10**6, transcendentals=0),
    )(inverse, ratio, top, sketched)


def top_body(side_ref, mine_ref, mirrored_ref, transfer_ref, paths_ref, children_ref, source, current, left, inverse, squared, child, lowest, nat_inverse, nat_child, *, rank, levels):
    half, packed_rows_each, width = mine_ref.shape
    nodes = half
    every = width // rank
    count = half * packed_rows_each
    for ref, side in ((mine_ref, side_ref[0]), (mirrored_ref, 1 - side_ref[0])):
        flat = ref[...].reshape(count, width)
        base = pl.multiple_of(side * (half * rank), half * rank)
        for part in range(every):
            children_ref[pl.ds(base + part, count, stride=every), :] = flat[:, part * rank : (part + 1) * rank]
    for node in range(nodes):
        both = children_ref[2 * node * rank : (2 * node + 2) * rank, :]
        source[node * rank : (node + 1) * rank, :] = lax.dot_general(
            both, both, tn_dims, precision=highest, preferred_element_type=jnp.float32
        )

    def finish(level):
        @when(level < levels - 1)
        def _():
            for r in range(rank):
                from_lanes(child[r], nat_child.at[level], r, nodes, rank)

        for r in range(rank):
            from_lanes(inverse[r * rank : (r + 1) * rank, :], nat_inverse.at[level], r, nodes, rank)

    run_levels(
        source, levels, nodes, current, left, inverse, squared, None, child, lowest, rank,
        lambda level: True, finish, unrolled=True,
    )
    offset = 0
    for level in range(levels):
        for node in range(nodes >> level):
            if level == 0:
                stacked = children_ref[2 * node * rank : (2 * node + 2) * rank, :]
            else:
                first = 2 * node << level - 1
                second = 2 * node + 1 << level - 1
                stacked = jnp.concatenate(
                    [
                        nat_child[level - 1, first * rank : (first + 1) * rank, :],
                        nat_child[level - 1, second * rank : (second + 1) * rank, :],
                    ],
                    axis=0,
                )
            at = (node << level) * rank
            transfer_ref[offset + node] = lax.dot_general(
                nat_inverse[level, at : at + rank, :], stacked, (((0,), (1,)), ((), ())),
                precision=highest, preferred_element_type=jnp.float32,
            )
        offset += nodes >> level
    above = [None]
    for level in range(levels - 1, -1, -1):
        offset -= nodes >> level
        fresh = []
        for node in range(nodes >> level):
            both = transfer_ref[offset + node]
            if above[0] is None:
                both = both.T
            else:
                both = lax.dot_general(
                    both, above[node], tn_dims, precision=highest, preferred_element_type=jnp.float32
                )
            fresh += [both[:rank], both[rank:]]
        above = fresh
    for branch in range(2 * nodes):
        paths_ref[branch * rank : (branch + 1) * rank, :] = above[branch]


def top_factors(side, mine, mirrored, rank):
    branches = 2 * mine.shape[0]
    levels = branches.bit_length() - 1
    nodes = branches // 2
    natural = pltpu.VMEM((levels, nodes * rank, rank), jnp.float32)
    return pl.pallas_call(
        functools.partial(top_body, rank=rank, levels=levels),
        in_specs=[pl.BlockSpec(memory_space=pltpu.SMEM), vmem_spec, vmem_spec],
        out_specs=[vmem_spec] * 2,
        out_shape=[
            jax.ShapeDtypeStruct((branches - 1, rank, 2 * rank), jnp.float32),
            jax.ShapeDtypeStruct((branches * rank, rank), jnp.float32),
        ],
        scratch_shapes=[
            pltpu.VMEM((branches * rank, rank), jnp.float32),
            pltpu.VMEM((nodes * rank, rank), jnp.float32),
        ]
        + tree_scratch(rank)
        + [natural, natural],
        compiler_params=pltpu.CompilerParams(vmem_limit_bytes=vmem_bytes),
        name="top_factors",
        cost_estimate=pl.CostEstimate(flops=10**10, bytes_accessed=10**7, transcendentals=0),
    )(side, mine, mirrored)


def exchange_sum(pieces, axis):
    count = pieces.shape[0]
    me = lax.axis_index(axis)
    mine = lax.dynamic_index_in_dim(pieces, me, 0, keepdims=False)
    for step in range(1, count):
        outgoing = lax.dynamic_index_in_dim(pieces, (me + step) % count, 0, keepdims=False)
        mine = mine + lax.ppermute(
            outgoing, axis, [(i, (i + step) % count) for i in range(count)]
        )
    return mine


def exchange_all(piece, axis):
    count = lax.axis_size(axis)
    me = lax.axis_index(axis)
    if count == 2:
        other = lax.ppermute(piece, axis, [(0, 1), (1, 0)])
        return jnp.stack([jnp.where(me == 0, piece, other), jnp.where(me == 0, other, piece)])
    result = jnp.zeros((count,) + piece.shape, piece.dtype)
    result = lax.dynamic_update_index_in_dim(result, piece, me, 0)
    for step in range(1, count):
        arrived = lax.ppermute(piece, axis, [(i, (i + step) % count) for i in range(count)])
        result = lax.dynamic_update_index_in_dim(result, arrived, (me - step) % count, 0)
    return result


def group_tables(far_slots, far_count, side, part):
    leaves = far_slots.shape[0]
    groups = -(-(leaves * (FAR // GROUP + 1) + BATCH - 1) // BATCH) * BATCH
    places = jnp.arange(FAR, dtype=jnp.int32)
    valid = places[None, :] < far_count[:, None]
    here = far_slots // part == side
    local = far_slots % part
    held = jnp.concatenate([valid & here, valid & ~here], axis=0)
    local = jnp.concatenate([local, local], axis=0)
    earlier = places[None, :] < places[:, None]
    rank = jnp.sum((held[:, None, :] & earlier[None]).astype(jnp.int32), axis=2)
    chosen = held[:, None, :] & (rank[:, None, :] == places[None, :, None])
    ordered = jnp.sum(jnp.where(chosen, local[:, None, :], 0), axis=2)
    lengths = jnp.sum(held.astype(jnp.int32), axis=1)
    lists = 2 * leaves
    per_list = (lengths + GROUP - 1) // GROUP
    before = jnp.arange(lists)[:, None] >= jnp.arange(lists)[None, :]
    ends = jnp.sum(jnp.where(before, per_list[None, :], 0), axis=1)
    own_total = ends[leaves - 1]
    total = ends[lists - 1]
    base = (own_total + BATCH - 1) // BATCH * BATCH
    ids = jnp.arange(groups, dtype=jnp.int32)
    at = jnp.where(ids < base, ids, ids - base + own_total)
    dead = ((ids < base) & (ids >= own_total)) | (at >= total)
    index = jnp.minimum(jnp.sum((ends[None, :] <= at[:, None]).astype(jnp.int32), axis=1), lists - 1)
    hit = index[:, None] == jnp.arange(lists)[None, :]
    start = jnp.sum(jnp.where(hit, (ends - per_list)[None, :], 0), axis=1)
    length = jnp.sum(jnp.where(hit, lengths[None, :], 0), axis=1)
    sub = at - start
    count = jnp.where(dead, 0, jnp.clip(length - GROUP * sub, 0, GROUP))
    first = jnp.clip(sub, 0, FAR // GROUP - 1)
    slots = ordered.reshape(lists * FAR // GROUP, GROUP)[index * (FAR // GROUP) + first]
    lift = jnp.where(ids < base, side, 1 - side) * part
    sizes = jnp.stack([base + total - own_total, own_total, base, total - own_total])
    return (
        sizes.astype(jnp.int32),
        (index % leaves).astype(jnp.int32),
        count.astype(jnp.int32),
        slots.reshape(-1).astype(jnp.int32),
        (slots + lift[:, None]).reshape(-1).astype(jnp.int32),
    )


def sketch_body(place_ref, sketch_ref, samples_ref, points_ref, mine_ref, other_ref):
    product = dot_exact(sketch_ref[...], samples_ref[...])
    rank, points_dev = product.shape
    quarter = rank // 4
    first = lax.broadcasted_iota(jnp.int32, (1, LANES), 1) < LEAF
    swap = place_ref[0] == 1
    leaves = points_dev // LEAF

    def interleave(low, high):
        even = jnp.where(first, low, pltpu.roll(high, LEAF, 1))
        odd = jnp.where(first, pltpu.roll(low, LEAF, 1), high)
        return even, odd

    for pair in range(leaves // 2):
        lanes = slice(pair * LANES, (pair + 1) * LANES)
        shares = []
        for share in range(2):
            base = 2 * quarter * share
            shares.append(
                interleave(product[base : base + quarter, lanes], product[base + quarter : base + 2 * quarter, lanes])
            )
        for member in range(2):
            at = (2 * pair + member) * quarter
            mine_ref[at : at + quarter, :] = jnp.where(swap, shares[1][member], shares[0][member])
            other_ref[at : at + quarter, :] = jnp.where(swap, shares[0][member], shares[1][member])
        x = points_ref[0:1, lanes]
        y = points_ref[1:2, lanes]
        z = points_ref[2:3, lanes]
        xy = interleave(x, y)
        zs = interleave(z, jnp.zeros_like(z))
        for member in range(2):
            at = leaves * quarter + (2 * pair + member) * 2
            mine_ref[at : at + 1, :] = xy[member]
            mine_ref[at + 1 : at + 2, :] = zs[member]
    other_ref[leaves * quarter :, :] = jnp.zeros((2 * leaves, LANES), jnp.float32)


def sketched_shares(place, sketch, samples, points):
    rank = sketch.shape[0]
    leaves = samples.shape[1] // LEAF
    return pl.pallas_call(
        sketch_body,
        in_specs=[pl.BlockSpec(memory_space=pltpu.SMEM)] + [vmem_spec] * 3,
        out_specs=[vmem_spec] * 2,
        out_shape=[
            jax.ShapeDtypeStruct((leaves * (rank // 4 + 2), LANES), jnp.float32),
            jax.ShapeDtypeStruct((leaves * (rank // 4 + 2), LANES), jnp.float32),
        ],
        compiler_params=pltpu.CompilerParams(vmem_limit_bytes=vmem_bytes),
        name="sketched_shares",
        cost_estimate=pl.CostEstimate(flops=10**6, bytes_accessed=10**4, transcendentals=0),
    )(place, sketch, samples, points)


def pack_body(asked_ref, side_ref, mine_ref, partner_ref, out_ref, *, cap, leaves):
    z_rows = mine_ref.shape[0] // leaves - 2
    side = side_ref[0]

    def one(peer, carry):
        for entry in range(2 * cap):
            leaf = asked_ref[peer, entry]
            here = side == entry // cap
            at = pl.ds(leaf * z_rows, z_rows)
            out_ref[peer, z_rows * entry : z_rows * (entry + 1), :] = jnp.where(
                here, mine_ref[at, :], partner_ref[at, :]
            )
            base = z_rows * 2 * cap + 2 * entry
            at = pl.ds(leaves * z_rows + leaf * 2, 2)
            out_ref[peer, base : base + 2, :] = jnp.where(here, mine_ref[at, :], partner_ref[at, :])
        return carry

    lax.fori_loop(0, out_ref.shape[0], one, 0)


def packed_rows(asked, side, mine, partner, cap, leaves):
    z_rows = mine.shape[0] // leaves - 2
    return pl.pallas_call(
        functools.partial(pack_body, cap=cap, leaves=leaves),
        in_specs=[pl.BlockSpec(memory_space=pltpu.SMEM)] * 2 + [vmem_spec] * 2,
        out_specs=vmem_spec,
        out_shape=jax.ShapeDtypeStruct((asked.shape[0], 2 * cap * (z_rows + 2), LANES), jnp.float32),
        compiler_params=pltpu.CompilerParams(vmem_limit_bytes=vmem_bytes),
        name="packed_rows",
    )(asked, side, mine, partner)


def payload_body(asked_ref, side_ref, rows_ref, child_ref, out_ref, *, cap):
    base = (1 - side_ref[0]) * cap

    def one(peer, carry):
        for entry in range(cap):
            out_ref[peer, LEAF * entry : LEAF * (entry + 1), :] = rows_ref[asked_ref[peer, base + entry]]
        out_ref[peer, LEAF * cap :, :] = child_ref[...]
        return carry

    lax.fori_loop(0, out_ref.shape[0], one, 0)


def payload_rows(asked, side, rows, child):
    half = asked.shape[0]
    cap = asked.shape[1] // 2
    return pl.pallas_call(
        functools.partial(payload_body, cap=cap),
        in_specs=[pl.BlockSpec(memory_space=pltpu.SMEM)] * 2 + [vmem_spec] * 2,
        out_specs=vmem_spec,
        out_shape=jax.ShapeDtypeStruct((half, cap * LEAF + child.shape[0], rows.shape[2]), jnp.float32),
        compiler_params=pltpu.CompilerParams(vmem_limit_bytes=vmem_bytes),
        name="payload_rows",
    )(asked, side, rows, child)


def two_rows(values, rows):
    leaves = values.shape[1]
    split = jnp.transpose(values.reshape(2, rows, leaves, LEAF), (2, 1, 0, 3))
    return split.reshape(leaves, rows, 2 * LEAF)


def on_device(points, samples, sketch, far_requests, far_slots, far_count, near_mask):
    samp_dev = samples.shape[0]
    leaves = samples.shape[1] // LEAF
    rank = sketch.shape[0]
    branches = lax.axis_size("leaf")
    columns = lax.axis_size("cols")
    cap = far_requests.shape[2]
    share = rank // columns
    me = lax.axis_index("leaf")
    column = lax.axis_index("cols")

    half = branches // 2
    side = me // half
    groups = [list(range(half)), list(range(half, branches))]
    mirror = [(i, (i + half) % branches) for i in range(branches)]
    side_ref = side.astype(jnp.int32).reshape(1)
    wanted = jnp.transpose(far_requests.reshape(2, half, cap), (1, 0, 2)).reshape(half, 2 * cap)
    if columns == 2:
        place = column.astype(jnp.int32).reshape(1)
        mine, other = sketched_shares(place, sketch, samples, points)
        mine = mine + lax.ppermute(other, "cols", [(0, 1), (1, 0)])
        wanted, mine = lax.optimization_barrier((wanted, mine))
    else:
        z_part = jnp.dot(sketch, samples, precision=highest)
        z_mine = exchange_sum(z_part.reshape(columns, share, leaves * LEAF), "cols")
        z_rows = two_rows(z_mine.reshape(share, leaves, LEAF), share // 2)
        planes = points.reshape(3, leaves, LEAF)
        c_rows = two_rows(
            jnp.concatenate([planes[0:1], planes[2:3], planes[1:2], jnp.zeros_like(planes[0:1])], axis=0), 2
        )
        mine = jnp.concatenate([z_rows.reshape(-1, LANES), c_rows.reshape(-1, LANES)], axis=0)

    partner = lax.ppermute(mine, "leaf", mirror)
    asked = lax.all_to_all(
        wanted, "leaf", split_axis=0, concat_axis=0, axis_index_groups=groups, tiled=True
    )
    coords = jnp.transpose(points.reshape(3, leaves, LEAF), (1, 0, 2))
    targets = jnp.transpose(coords, (0, 2, 1))
    rows = jnp.transpose(samples.reshape(samp_dev, leaves, LEAF), (1, 2, 0))

    asked, rows, targets = lax.optimization_barrier((asked, rows, targets))
    small_sent = packed_rows(asked, side_ref, mine, partner, cap, leaves)
    small_got = lax.all_to_all(
        small_sent, "leaf", split_axis=0, concat_axis=0, axis_index_groups=groups, tiled=True
    )

    rows_out, unused = lax.optimization_barrier((rows, small_sent))
    partner_rows = lax.ppermute(rows_out, "leaf", mirror)

    forward = [(i, i + 1) for i in range(branches - 1)]
    backward = [(target, source) for source, target in forward]
    width = max(samp_dev, LEAF)

    def edge(first):
        samples_edge = jnp.transpose(lax.slice_in_dim(samples, first, first + LEAF, axis=1))
        points_edge = lax.slice_in_dim(points, first, first + LEAF, axis=1)
        return jnp.concatenate(
            [
                jnp.pad(samples_edge, ((0, 0), (0, width - samp_dev))),
                jnp.pad(points_edge, ((0, 5), (0, width - LEAF))),
            ],
            axis=0,
        )

    last, first, unused = lax.optimization_barrier((edge((leaves - 1) * LEAF), edge(0), small_sent))
    low_edge = lax.ppermute(last, "leaf", forward)
    high_edge = lax.ppermute(first, "leaf", backward)

    own_asked = lax.dynamic_slice_in_dim(asked, side * cap, cap, axis=1)
    own_sent = rows_out[own_asked.reshape(-1)].reshape(half, cap, LEAF, samp_dev)
    own_sent, low_edge, high_edge, far_slots, far_count = lax.optimization_barrier(
        (own_sent, low_edge, high_edge, far_slots, far_count)
    )
    sizes, group_leaf, group_count, group_slots, group_places = group_tables(
        far_slots, far_count, side, half * cap
    )
    own_got = lax.all_to_all(
        own_sent, "leaf", split_axis=0, concat_axis=0, axis_index_groups=groups, tiled=True
    )
    own_got = own_got.reshape(half * cap, LEAF, samp_dev)

    if columns == 2:
        small_other = lax.ppermute(small_got, "cols", [(0, 1), (1, 0)])
    else:
        z_count = cap * share
        z_all = exchange_all(small_got[:, :z_count], "cols")
        z_all = z_all.reshape(columns, half, 2 * cap, share // 2, 2, LEAF)
        z_all = jnp.transpose(z_all, (1, 2, 0, 4, 3, 5)).reshape(half, 2 * cap, 2, 2, rank // 4, LEAF)
        z_all = jnp.transpose(z_all, (2, 0, 1, 4, 3, 5)).reshape(2, half, cap * rank // 2, LANES)
        c_got = small_got[:, z_count:]
        small_got = jnp.concatenate([z_all[0], c_got], axis=1)
        small_other = jnp.concatenate([z_all[1], c_got], axis=1)
        place = jnp.zeros((1,), jnp.int32)

    blocks, sketched, gram = kernel_blocks(
        sizes, group_leaf, group_count, group_places, place, small_got, small_other, targets, rank, cap
    )

    levels = leaves.bit_length()
    inverse, ratio, top_inverse, own_child = branch_factors(gram, levels, min(samp_dev, LANES))
    own_child, own_got, partner_rows = lax.optimization_barrier((own_child, own_got, partner_rows))
    payload = payload_rows(asked, side_ref, partner_rows, own_child)
    arrived = lax.all_to_all(
        payload, "leaf", split_axis=0, concat_axis=0, axis_index_groups=groups, tiled=True
    )
    ratio, low_edge, high_edge, unused = lax.optimization_barrier((ratio, low_edge, high_edge, payload))
    weights, leaf_basis = bases(inverse, ratio, top_inverse, sketched)

    rows_low, rows_high = low_edge[:LEAF, :samp_dev], high_edge[:LEAF, :samp_dev]
    coords_low, coords_high = low_edge[LEAF : LEAF + 3, :LEAF], high_edge[LEAF : LEAF + 3, :LEAF]
    near_rows = jnp.concatenate(
        [rows_low[None], rows, rows_high[None], jnp.zeros_like(rows_low)[None]], axis=0
    )
    near_coords = jnp.concatenate(
        [coords_low[None], coords, coords_high[None], jnp.zeros_like(coords_low)[None]], axis=0
    )
    near_coords = jnp.pad(near_coords, ((0, 0), (0, 5), (0, 0)))
    near_coords = jnp.concatenate([near_coords, near_coords], axis=2)
    near_sample = near_products(near_mask.reshape(-1), near_rows, near_coords, targets)


    children = arrived[:, cap * LEAF :]
    mirrored = lax.ppermute(children, "leaf", mirror)
    own_got, unused = lax.optimization_barrier((own_got, payload))
    far_start = far_own(sizes, group_leaf, group_slots, own_got, blocks, leaves)
    weights, near_sample = lax.optimization_barrier((weights, near_sample))
    far_sample, branch_samples, copies = far_partner(
        sizes, group_leaf, group_slots, arrived, blocks, far_start, weights, cap, branches
    )
    everyone = lax.all_to_all(copies, "leaf", split_axis=0, concat_axis=0, tiled=True)
    children, mirrored, unused = lax.optimization_barrier((children, mirrored, branch_samples))
    transfer_t, paths = top_factors(side_ref, children, mirrored, rank)
    top_transfer = jnp.swapaxes(transfer_t, 1, 2)
    root_sample = lax.dot_general(
        paths, everyone.reshape(branches * rank, samp_dev), tn_dims, precision=highest
    )
    return (far_sample, near_sample, leaf_basis, branch_samples, top_transfer, root_sample)


def solution(mesh):
    return jax.shard_map(
        on_device,
        mesh=mesh,
        in_specs=(
            P(None, "leaf"),
            P("cols", "leaf"),
            P(None, "cols"),
            P("leaf", None, None),
            P("leaf", None),
            P("leaf"),
            P("leaf", None),
        ),
        out_specs=(
            P("cols", "leaf"),
            P("cols", "leaf"),
            P(None, "leaf"),
            P("leaf", "cols"),
            P(),
            P(None, "cols"),
        ),
        check_vma=False,
    )
```
